32 devices in a mesh: img: 16 (over z, x, core), seq: 2 (over y).
Axes of the slice: x: 2, y: 2, z: 4, core: 2. Of those that a mesh axis runs over, the one named last changes fastest.
Arguments:
- tokens: bfloat16 [16, 16, 64, 768], P('img', 'seq'), may hold values from -6 to 6
- valid_rows: int32 [16], P('img'), may hold values from 8 to 16, as said below
- valid_cols: int32 [16], P('img'), may hold values from 32 to 64, as said below
- block_gains: bfloat16 [768, 2], replicated, may hold values from 0.5 to 1.5
- block_shifts: bfloat16 [768, 2], replicated, may hold values from -1.25 to 1.25
- qkv_weight: bfloat16 [768, 2304], replicated, may hold values from -0.21875 to 0.21875
- qv_bias: bfloat16 [768, 2], replicated, may hold values from -1.25 to 1.25
- table_rows: bfloat16 [64, 31], replicated, may hold values from -0.625 to 0.625
- table_cols: bfloat16 [64, 127], replicated, may hold values from -0.625 to 0.625
- proj_weight: bfloat16 [768, 768], replicated, may hold values from -4 to 4
- proj_bias: bfloat16 [768], replicated, may hold values from -1.25 to 1.25
- fc1_weight: bfloat16 [768, 3072], replicated, may hold values from -0.21875 to 0.21875
- fc1_bias: bfloat16 [3072], replicated, may hold values from -1.25 to 1.25
- fc2_weight: bfloat16 [3072, 768], replicated, may hold values from -0.109375 to 0.109375
- fc2_bias: bfloat16 [768], replicated, may hold values from -1.25 to 1.25
- fine_first: bfloat16 [768, 1536], replicated, may hold values from -0.21875 to 0.21875
- fine_first_bias: bfloat16 [384], replicated, may hold values from -1.25 to 1.25
- fine_norm_gain: bfloat16 [384], replicated, may hold values from 0.5 to 1.5
- fine_norm_shift: bfloat16 [384], replicated, may hold values from -1.25 to 1.25
- fine_second: bfloat16 [768, 384], replicated, may hold values from -0.3125 to 0.3125
- fine_second_bias: bfloat16 [192], replicated, may hold values from -1.25 to 1.25
- middle_up: bfloat16 [768, 1536], replicated, may hold values from -0.21875 to 0.21875
- middle_up_bias: bfloat16 [384], replicated, may hold values from -1.25 to 1.25
- lateral_fine: bfloat16 [192, 256], replicated, may hold values from -0.4375 to 0.4375
- lateral_middle: bfloat16 [384, 256], replicated, may hold values from -0.3125 to 0.3125
- lateral_coarse: bfloat16 [768, 2, 256], replicated, may hold values from -0.21875 to 0.21875
- level_gains: bfloat16 [256, 8], replicated, may hold values from 0.5 to 1.5
- level_shifts: bfloat16 [256, 8], replicated, may hold values from -1.25 to 1.25
- output_convs: bfloat16 [2304, 4, 256], replicated, may hold values from -0.125 to 0.125
- cotan_fine: bfloat16 [16, 64, 256, 256], P('img', 'seq'), may hold values from -6 to 6
- cotan_middle: bfloat16 [16, 32, 128, 256], P('img', 'seq'), may hold values from -6 to 6
- cotan_base: bfloat16 [16, 16, 64, 256], P('img', 'seq'), may hold values from -6 to 6
- cotan_coarse: bfloat16 [16, 8, 32, 256], P('img', 'seq'), may hold values from -6 to 6
Outputs:
- map_fine: bfloat16 [16, 64, 256, 256], P('img', 'seq')
- map_middle: bfloat16 [16, 32, 128, 256], P('img', 'seq')
- map_base: bfloat16 [16, 16, 64, 256], P('img', 'seq')
- map_coarse: bfloat16 [16, 8, 32, 256], P('img', 'seq')
- input_grad: float32 [16, 16, 64, 768], P('img', 'seq')
- block_gains_grad: float32 [768, 2], P('img')
- block_shifts_grad: float32 [768, 2], P('img')
- qkv_weight_grad: float32 [768, 2304], P('img')
- qv_bias_grad: float32 [768, 2], P('img')
- table_rows_grad: float32 [64, 31], P('img')
- table_cols_grad: float32 [64, 127], P('img')
- proj_weight_grad: float32 [768, 768], P('img')
- proj_bias_grad: float32 [768], P('img')
- fc1_weight_grad: float32 [768, 3072], P('img')
- fc1_bias_grad: float32 [3072], P('img')
- fc2_weight_grad: float32 [3072, 768], P('img')
- fc2_bias_grad: float32 [768], P('img')
- fine_first_grad: float32 [768, 1536], P('img')
- fine_first_bias_grad: float32 [384], P('img')
- fine_norm_gain_grad: float32 [384], P('img')
- fine_norm_shift_grad: float32 [384], P('img')
- fine_second_grad: float32 [768, 384], P('img')
- fine_second_bias_grad: float32 [192], P('img')
- middle_up_grad: float32 [768, 1536], P('img')
- middle_up_bias_grad: float32 [384], P('img')
- lateral_fine_grad: float32 [192, 256], P('img')
- lateral_middle_grad: float32 [384, 256], P('img')
- lateral_coarse_grad: float32 [768, 2, 256], P('img')
- level_gains_grad: float32 [256, 8], P('img')
- level_shifts_grad: float32 [256, 8], P('img')
- output_convs_grad: float32 [2304, 4, 256], P('img')
The draws below stay inside these ranges and needn't reach their ends.
Inputs may be any that keep to these rules, and one draw needn't show every extreme that they name: Some image has valid_rows equal to 16 and some image equal to 8. Some image has valid_cols equal to 64 and some image equal to 32.
All inputs are finite; a program needn't handle non-finite values.
Results may differ from the reference program's by a relative error of at most 0.025.
Values may be sent and summed in bfloat16 or wider, within the bound.
No kernel may reach another device: no remote copies, remote signals or barrier semaphores. Data moves between devices by JAX's collectives and lax.ppermute only.
A program may use at most 512 MiB of HBM per device.

```python
import jax
import jax.numpy as jnp
from jax import lax

D = 768
FF = 3072
HEAD = 64
HALF = 384
QUART = 192
OUT = 256
HEADS = 12
COLS = 64
ROWS = 16
IMAGES = 16


def extent_values(key, largest):
    picks = jax.random.randint(key, (IMAGES,), largest // 2, largest + 1)
    full_at = jax.random.randint(jax.random.fold_in(key, 1), (), 0, IMAGES)
    offset_at = jax.random.randint(jax.random.fold_in(key, 2), (), 1, IMAGES)
    least_at = (full_at + offset_at) % IMAGES
    places = jnp.arange(IMAGES, dtype=jnp.int32)
    picks = jnp.where(places == full_at, largest, picks)
    picks = jnp.where(places == least_at, largest // 2, picks)
    return picks.astype(jnp.int32)


def draw_valid_rows(key, part):
    return extent_values(jax.random.fold_in(key, 11), ROWS)


def draw_valid_cols(key, part):
    return extent_values(jax.random.fold_in(key, 12), COLS)


def steps_of(key, shape, cuts, low, high):
    def one(axis_at, blocks):
        heights = jax.random.uniform(jax.random.fold_in(jax.random.fold_in(key, 6), axis_at), (blocks,), jnp.float32, low / len(cuts), high / len(cuts))
        return jnp.repeat(jnp.exp(heights), shape[axis_at] // blocks).reshape((-1,) + (1,) * (len(shape) - axis_at - 1))

    level = one(*cuts[0])
    for cut in cuts[1:]:
        level = level * one(*cut)
    return level


def normal_values(key, extent, scale, reach, cuts=(), kind=jnp.bfloat16):
    values = scale * jax.random.normal(key, extent, jnp.float32)
    if cuts:
        values = values * steps_of(key, extent, cuts, -0.22, 0.18)
    return jnp.clip(values, -reach, reach).astype(kind)


def setup_inputs(seed: int = 0) -> dict:
    seeds = jax.random.split(jax.random.key(seed), 34)
    tokens = normal_values(seeds[0], (IMAGES, ROWS, COLS, D), 1.0, 6.0, ((0, 16), (1, 2)))
    valid_rows = draw_valid_rows(jax.random.fold_in(seeds[33], 71), 0)
    valid_cols = draw_valid_cols(jax.random.fold_in(seeds[33], 71), 0)
    block_gains = jnp.clip(1.0 + 0.1 * jax.random.normal(seeds[3], (D, 2), jnp.float32), 0.5, 1.5).astype(jnp.bfloat16)
    block_shifts = normal_values(seeds[4], (D, 2), 0.2, 1.25)
    qkv_weight = normal_values(seeds[5], (D, 3 * D), D ** -0.5, 0.21875)
    qv_bias = normal_values(seeds[6], (D, 2), 0.2, 1.25)
    table_rows = normal_values(seeds[7], (HEAD, 2 * ROWS - 1), 0.1, 0.625)
    table_cols = normal_values(seeds[8], (HEAD, 2 * COLS - 1), 0.1, 0.625)
    proj_weight = normal_values(seeds[9], (D, D), 2 ** -0.5, 4.0)
    proj_bias = normal_values(seeds[10], (D,), 0.2, 1.25)
    fc1_weight = normal_values(seeds[11], (D, FF), D ** -0.5, 0.21875)
    fc1_bias = normal_values(seeds[12], (FF,), 0.2, 1.25)
    fc2_weight = normal_values(seeds[13], (FF, D), FF ** -0.5, 0.109375)
    fc2_bias = normal_values(seeds[14], (D,), 0.2, 1.25)
    fine_first = normal_values(seeds[15], (D, 4 * HALF), D ** -0.5, 0.21875)
    fine_first_bias = normal_values(seeds[16], (HALF,), 0.2, 1.25)
    fine_norm_gain = jnp.clip(1.0 + 0.1 * jax.random.normal(seeds[17], (HALF,), jnp.float32), 0.5, 1.5).astype(jnp.bfloat16)
    fine_norm_shift = normal_values(seeds[18], (HALF,), 0.2, 1.25)
    fine_second = normal_values(seeds[19], (4 * QUART, HALF), HALF ** -0.5, 0.3125)
    fine_second_bias = normal_values(seeds[20], (QUART,), 0.2, 1.25)
    middle_up = normal_values(seeds[21], (D, 4 * HALF), D ** -0.5, 0.21875)
    middle_up_bias = normal_values(seeds[22], (HALF,), 0.2, 1.25)
    lateral_fine = normal_values(seeds[23], (QUART, OUT), QUART ** -0.5, 0.4375)
    lateral_middle = normal_values(seeds[24], (HALF, OUT), HALF ** -0.5, 0.3125)
    lateral_coarse = normal_values(seeds[25], (D, 2, OUT), D ** -0.5, 0.21875)
    level_gains = jnp.clip(1.0 + 0.1 * jax.random.normal(seeds[26], (OUT, 8), jnp.float32), 0.5, 1.5).astype(jnp.bfloat16)
    level_shifts = normal_values(seeds[27], (OUT, 8), 0.2, 1.25)
    output_convs = normal_values(seeds[28], (9 * OUT, 4, OUT), (9 * OUT) ** -0.5, 0.125)
    cotan_fine = normal_values(seeds[29], (IMAGES, 4 * ROWS, 4 * COLS, OUT), 1.0, 6.0, ((0, 16), (1, 2)))
    cotan_middle = normal_values(seeds[30], (IMAGES, 2 * ROWS, 2 * COLS, OUT), 1.0, 6.0, ((0, 16), (1, 2)))
    cotan_base = normal_values(seeds[31], (IMAGES, ROWS, COLS, OUT), 1.0, 6.0, ((0, 16), (1, 2)))
    cotan_coarse = normal_values(seeds[32], (IMAGES, ROWS // 2, COLS // 2, OUT), 1.0, 6.0, ((0, 16), (1, 2)))
    return {"tokens": tokens, "valid_rows": valid_rows, "valid_cols": valid_cols, "block_gains": block_gains, "block_shifts": block_shifts, "qkv_weight": qkv_weight, "qv_bias": qv_bias, "table_rows": table_rows, "table_cols": table_cols, "proj_weight": proj_weight, "proj_bias": proj_bias, "fc1_weight": fc1_weight, "fc1_bias": fc1_bias, "fc2_weight": fc2_weight, "fc2_bias": fc2_bias, "fine_first": fine_first, "fine_first_bias": fine_first_bias, "fine_norm_gain": fine_norm_gain, "fine_norm_shift": fine_norm_shift, "fine_second": fine_second, "fine_second_bias": fine_second_bias, "middle_up": middle_up, "middle_up_bias": middle_up_bias, "lateral_fine": lateral_fine, "lateral_middle": lateral_middle, "lateral_coarse": lateral_coarse, "level_gains": level_gains, "level_shifts": level_shifts, "output_convs": output_convs, "cotan_fine": cotan_fine, "cotan_middle": cotan_middle, "cotan_base": cotan_base, "cotan_coarse": cotan_coarse}


HIGH = lax.Precision.HIGHEST
NEG = -1e+30

@jax.custom_vjp
def low(v):
    return lax.optimization_barrier(v.astype(jnp.bfloat16)).astype(jnp.float32)

@jax.custom_vjp
def low_back(v):
    return v

def low_keep(v):
    return (low(v), None)

def low_pass(kept, grad):
    return (grad,)

def back_keep(v):
    return (v, None)

def back_low(kept, grad):
    return (low(grad),)
low.defvjp(low_keep, low_pass)
low_back.defvjp(back_keep, back_low)

def product(left, right):
    return jnp.dot(left, right, precision=HIGH, preferred_element_type=jnp.float32)

def normalize(values, gain_vec, shift_vec):
    average = lax.optimization_barrier(jnp.mean(values, axis=-1, keepdims=True))
    centred = values - average
    spread = lax.optimization_barrier(jnp.mean(centred * centred, axis=-1, keepdims=True))
    return centred * lax.rsqrt(spread + 1e-06) * gain_vec + shift_vec

def deconvolve(values, weight, bias_vec):
    rows_in, cols_in, channels = values.shape
    outs_chan = bias_vec.shape[0]
    spread = product(values.reshape(rows_in * cols_in, channels), weight)
    spread = spread.reshape(rows_in, cols_in, 2, 2, outs_chan).transpose(0, 2, 1, 3, 4)
    return spread.reshape(2 * rows_in, 2 * cols_in, outs_chan) + bias_vec

def conv_three(padded, weight):
    rows_out = padded.shape[0] - 2
    cols_out = padded.shape[1] - 2
    channels = padded.shape[2]
    result = jnp.zeros((rows_out * cols_out, weight.shape[1]), jnp.float32)
    for offset_row in range(3):
        for offset_col in range(3):
            window = padded[offset_row:offset_row + rows_out, offset_col:offset_col + cols_out].reshape(rows_out * cols_out, channels)
            tap_start = (3 * offset_row + offset_col) * channels
            result = result + product(window, weight[tap_start:tap_start + channels])
    return result.reshape(rows_out, cols_out, weight.shape[1])

def offsets_table(table, length):
    places = jnp.arange(length, dtype=jnp.int32)
    lookup = places[:, None] - places[None, :] + (length - 1)
    return jnp.take(table.T, lookup, axis=0)

def finish_level(values, lateral, level_at, level_gains, level_shifts, output_convs):
    rows_in, cols_in, channels = values.shape
    lateral_out = low_back(product(values.reshape(rows_in * cols_in, channels), lateral))
    lateral_out = low(normalize(lateral_out, level_gains[:, level_at], level_shifts[:, level_at]))
    padded = jnp.pad(lateral_out.reshape(rows_in, cols_in, -1), ((1, 1), (1, 1), (0, 0)))
    convolved = low_back(conv_three(padded, output_convs[:, level_at, :]))
    return normalize(convolved, level_gains[:, 4 + level_at], level_shifts[:, 4 + level_at])

def image_forward(weights, image_grid, rows_valid, cols_valid):
    block_gains, block_shifts, qkv_weight, qv_bias, table_rows, table_cols, proj_weight, proj_bias, fc1_weight, fc1_bias, fc2_weight, fc2_bias, fine_first, fine_first_bias, fine_norm_gain, fine_norm_shift, fine_second, fine_second_bias, middle_up, middle_up_bias, lateral_fine, lateral_middle, lateral_coarse, level_gains, level_shifts, output_convs = weights
    token_count = ROWS * COLS
    flat_tokens = image_grid.reshape(token_count, D)
    normed = low(normalize(flat_tokens, block_gains[:, 0], block_shifts[:, 0]))
    projected = product(normed, qkv_weight)
    queries = low_back(low(projected[:, :D] + qv_bias[:, 0]))
    keys_low = low_back(low(projected[:, D:2 * D]))
    values_low = low_back(low(projected[:, 2 * D:] + qv_bias[:, 1]))
    grid_query = queries.reshape(ROWS, COLS, HEADS, HEAD)
    rows_bias = jnp.einsum('ijhc,ikc->hijk', grid_query, offsets_table(table_rows, ROWS), precision=HIGH).reshape(HEADS, token_count, ROWS)
    cols_bias = jnp.einsum('ijhc,jkc->hijk', grid_query, offsets_table(table_cols, COLS), precision=HIGH).reshape(HEADS, token_count, COLS)
    key_ok = ((jnp.arange(ROWS, dtype=jnp.int32)[:, None] < rows_valid) & (jnp.arange(COLS, dtype=jnp.int32)[None, :] < cols_valid)).reshape(token_count)
    score_scale = HEAD ** (-0.5)

    def head_attend(pieces):
        head_query, head_keys, head_values, head_rows, head_cols = pieces
        scores = product(head_query, head_keys.T) * score_scale
        position_bias = (head_rows[:, :, None] + head_cols[:, None, :]).reshape(token_count, token_count)
        scores = low_back(jnp.where(key_ok[None, :], scores + position_bias, NEG))
        attention = low(jax.nn.softmax(scores, axis=-1))
        return product(attention, head_values)

    def by_heads(matrix):
        return matrix.reshape(token_count, HEADS, HEAD).transpose(1, 0, 2)
    attended = lax.map(jax.checkpoint(head_attend), (by_heads(queries), by_heads(keys_low), by_heads(values_low), rows_bias, cols_bias))
    attended = low_back(low(attended.transpose(1, 0, 2).reshape(token_count, D)))
    middle = flat_tokens + low_back(product(attended, proj_weight) + proj_bias)
    normed_two = low(normalize(middle, block_gains[:, 1], block_shifts[:, 1]))
    hidden = low_back(product(normed_two, fc1_weight) + fc1_bias)
    hidden = low(jax.nn.gelu(hidden, approximate=False))
    output = middle + low_back(product(hidden, fc2_weight) + fc2_bias)
    feature_map = output.reshape(ROWS, COLS, D)
    rounded = low(feature_map)
    fine_map = low_back(deconvolve(rounded, fine_first, fine_first_bias))
    fine_map = low(jax.nn.gelu(normalize(fine_map, fine_norm_gain, fine_norm_shift), approximate=False))
    fine_map = low_back(low(deconvolve(fine_map, fine_second.T, fine_second_bias)))
    middle_map = low_back(low(deconvolve(rounded, middle_up, middle_up_bias)))
    coarse_map = rounded.reshape(ROWS // 2, 2, COLS // 2, 2, D).max(axis=(1, 3))
    return (finish_level(fine_map, lateral_fine, 0, level_gains, level_shifts, output_convs), finish_level(middle_map, lateral_middle, 1, level_gains, level_shifts, output_convs), finish_level(rounded, lateral_coarse[:, 0, :], 2, level_gains, level_shifts, output_convs), finish_level(coarse_map, lateral_coarse[:, 1, :], 3, level_gains, level_shifts, output_convs))

def reference(tokens, valid_rows, valid_cols, block_gains, block_shifts, qkv_weight, qv_bias, table_rows, table_cols, proj_weight, proj_bias, fc1_weight, fc1_bias, fc2_weight, fc2_bias, fine_first, fine_first_bias, fine_norm_gain, fine_norm_shift, fine_second, fine_second_bias, middle_up, middle_up_bias, lateral_fine, lateral_middle, lateral_coarse, level_gains, level_shifts, output_convs, cotan_fine, cotan_middle, cotan_base, cotan_coarse):
    weights = tuple((weight_arg.astype(jnp.float32) for weight_arg in (block_gains, block_shifts, qkv_weight, qv_bias, table_rows, table_cols, proj_weight, proj_bias, fc1_weight, fc1_bias, fc2_weight, fc2_bias, fine_first, fine_first_bias, fine_norm_gain, fine_norm_shift, fine_second, fine_second_bias, middle_up, middle_up_bias, lateral_fine, lateral_middle, lateral_coarse, level_gains, level_shifts, output_convs)))

    def forward(weight_list, images):

        def one_image(pieces):
            image_grid, rows_valid, cols_valid = pieces
            return image_forward(weight_list, image_grid, rows_valid, cols_valid)
        return lax.map(jax.checkpoint(one_image), (images, valid_rows, valid_cols))
    level_maps, pullback = jax.vjp(forward, weights, tokens.astype(jnp.float32))
    cotangents = (cotan_fine.astype(jnp.float32), cotan_middle.astype(jnp.float32), cotan_base.astype(jnp.float32), cotan_coarse.astype(jnp.float32))
    grads, token_grad = pullback(cotangents)
    return (level_maps[0].astype(jnp.bfloat16), level_maps[1].astype(jnp.bfloat16), level_maps[2].astype(jnp.bfloat16), level_maps[3].astype(jnp.bfloat16), token_grad, grads[0], grads[1], grads[2], grads[3], grads[4], grads[5], grads[6], grads[7], grads[8], grads[9], grads[10], grads[11], grads[12], grads[13], grads[14], grads[15], grads[16], grads[17], grads[18], grads[19], grads[20], grads[21], grads[22], grads[23], grads[24], grads[25])
```

```python
import functools

import jax
import jax.numpy as jnp
from jax import lax
from jax.experimental import pallas as pl
from jax.experimental.pallas import tpu as pltpu
from jax.sharding import PartitionSpec as P

F32 = jnp.float32
BF = jnp.bfloat16
NEG = -1e30
EPS = 1e-6
SQRT_HALF = 0.7071067811865476
INV_SQRT_2PI = 0.3989422804014327
VMEM_LIMIT = 60 * 1024 * 1024


def mm(left, right):
    return lax.dot_general(left, right, (((1,), (0,)), ((), ())), preferred_element_type=F32)


def mt(left, right):
    return lax.dot_general(left, right, (((1,), (1,)), ((), ())), preferred_element_type=F32)


def tm(left, right):
    return lax.dot_general(left, right, (((0,), (0,)), ((), ())), preferred_element_type=F32)


def call(
    kernel, outs, grid=(), in_specs=None, out_specs=None, scratch=(), flops=0, name=None, aliases=None
):
    return pl.pallas_call(
        kernel,
        out_shape=outs,
        grid=grid,
        in_specs=in_specs,
        out_specs=out_specs,
        scratch_shapes=scratch,
        name=name,
        input_output_aliases=aliases or {},
        cost_estimate=pl.CostEstimate(flops=int(flops), bytes_accessed=0, transcendentals=0),
        compiler_params=pltpu.CompilerParams(vmem_limit_bytes=VMEM_LIMIT),
    )


def whole(shape):
    return pl.BlockSpec(shape, lambda *_: (0,) * len(shape))


def sds(shape, dtype):
    return jax.ShapeDtypeStruct(shape, dtype)


def stats(values):
    average = jnp.mean(values, axis=-1, keepdims=True)
    centred = values - average
    spread = jnp.mean(centred * centred, axis=-1, keepdims=True)
    inverse = lax.rsqrt(spread + EPS)
    return centred * inverse, inverse


def norm_back(grad_hat, hat, inverse):
    first = jnp.mean(grad_hat, axis=-1, keepdims=True)
    second = jnp.mean(grad_hat * hat, axis=-1, keepdims=True)
    return inverse * (grad_hat - first - hat * second)


def rowsum(values):
    return jnp.sum(values, axis=0, keepdims=True)


def gelu_pair(values):
    half = 0.5 * (1.0 + lax.erf(values * SQRT_HALF))
    slope = half + values * (jnp.exp(-0.5 * values * values) * INV_SQRT_2PI)
    return values * half, slope


def shift_matrix(size, amount):
    out_at = lax.broadcasted_iota(jnp.int32, (size, size), 0)
    in_at = lax.broadcasted_iota(jnp.int32, (size, size), 1)
    return jnp.where(in_at == out_at + amount, 1.0, 0.0).astype(BF)


def weave_matrix(size, ways, inverse=False):
    out_at = lax.broadcasted_iota(jnp.int32, (size, size), 1 if inverse else 0)
    in_at = lax.broadcasted_iota(jnp.int32, (size, size), 0 if inverse else 1)
    source = lax.rem(out_at, ways) * (size // ways) + lax.div(out_at, ways)
    return jnp.where(in_at == source, 1.0, 0.0).astype(BF)


def qkv_kernel(x_ref, w_ref, b_ref, p_ref, out_ref, n1_ref):
    @pl.when(pl.program_id(1) == 0)
    def _():
        for at in range(0, x_ref.shape[0], 32):
            hat, _ = stats(x_ref[at : at + 32, :].astype(F32))
            n1_ref[at : at + 32, :] = (hat * p_ref[0:1, :] + p_ref[2:3, :]).astype(BF)

    out_ref[...] = (mm(n1_ref[...], w_ref[...]) + b_ref[0]).astype(BF)


def qkv_call(tokens, weight, bias3, p768, first):
    rows, width = tokens.shape
    block = 512
    count = 3 - first
    return call(
        qkv_kernel,
        sds((rows, count * width), BF),
        grid=(rows // block, count),
        in_specs=[
            pl.BlockSpec((block, width), lambda i, j: (i, 0)),
            pl.BlockSpec((width, width), lambda i, j: (0, j + first)),
            pl.BlockSpec((1, 1, width), lambda i, j: (j + first, 0, 0)),
            whole(p768.shape),
        ],
        out_specs=pl.BlockSpec((block, width), lambda i, j: (i, j)),
        scratch=[pltpu.VMEM((block, width), BF)],
        flops=2 * rows * width * width * count,
        name="qkv",
    )(tokens, weight, bias3, p768)


def aug_layout(total_rows):
    low_at = 64 + total_rows
    if low_at + total_rows + 1 > 128:
        low_at = 128
    width = 128 * (2 + (low_at + total_rows) // 128)
    return low_at, width


def build_kaug(kaug_ref, k_refs, oh1_ref, oh2_ref, odd):
    lane = lax.broadcasted_iota(jnp.int32, (512, 128), 1)
    mine = (lane >= 64) if odd else (lane < 64)
    at = 0
    for k_ref in k_refs:
        for row in range(0, k_ref.shape[0], 512):
            keys = k_ref[row : row + 512, :].astype(F32)
            hot = oh1_ref[at : at + 512, :].astype(F32)
            kaug_ref[at : at + 512, 0:128] = jnp.where(mine, keys, hot).astype(BF)
            at += 512


def build_qaug(first_row, qp, tw_ref, tr_ref, qaug_ref, odd, total_rows, scale):
    low_at, width = aug_layout(total_rows)
    tokens = qp.shape[0]
    lane = lax.broadcasted_iota(jnp.int32, (64, 128), 1)
    mine = (lane >= 64) if odd else (lane < 64)
    lane_all = lax.broadcasted_iota(jnp.int32, (tokens, 128), 1)
    mine_all = (lane_all >= 64) if odd else (lane_all < 64)
    qf = qp.astype(F32)
    qm = jnp.where(mine_all, qf, 0.0).astype(BF)
    cols = mm(qm, tw_ref[...])
    rows = mm(qm, tr_ref[...])
    for i in range(tokens // 64):
        sl = slice(64 * i, 64 * i + 64)
        upper = pltpu.roll(cols[sl], 1, 1, stride=1, stride_axis=0)
        lower = pltpu.roll(cols[sl], 65, 1, stride=1, stride_axis=0)
        first = jnp.where(mine, qf[sl] * scale, lower if odd else upper)
        col_low = lower - lower.astype(BF).astype(F32)
        shift = lax.rem(first_row + i + (65 - total_rows + 128), 128)
        row_part = pltpu.roll(rows[sl], shift, 1)
        row_low = row_part - row_part.astype(BF).astype(F32)
        qaug_ref[sl, 0:128] = first.astype(BF)
        one_at = low_at + total_rows
        if low_at < 128:
            rest = jnp.where(lane == one_at, 1.0, 0.0)
            rest = jnp.where(
                (lane >= low_at) & (lane < one_at), pltpu.roll(row_low, total_rows, 1), rest
            )
            second = jnp.where(lane < 64, col_low, jnp.where(lane < low_at, row_part, rest))
            qaug_ref[sl, 128:256] = second.astype(BF)
        else:
            second = jnp.where(
                lane < 64, col_low, jnp.where(lane < 64 + total_rows, row_part, 0.0)
            )
            third = jnp.where(
                lane < total_rows,
                pltpu.roll(row_low, 64, 1),
                jnp.where(lane == total_rows, 1.0, 0.0),
            )
            qaug_ref[sl, 128:256] = second.astype(BF)
            qaug_ref[sl, 256:384] = third.astype(BF)


def attend_kernel(total_rows, scale, others, *refs):
    first_ref, q_ref, tw_ref, tr_ref, oh1_ref, oh2_ref = refs[:6]
    k_refs = refs[6 : 6 + others]
    v_refs = refs[6 + others : 6 + 2 * others]
    o_ref, qaug_out, lse_ref, kaug_ref, v_ref, p_ref, ot_ref = refs[6 + 2 * others :]
    first_row = first_ref[0]
    tokens = q_ref.shape[0]
    keys = kaug_ref.shape[0]

    @pl.when(pl.program_id(0) == 0)
    def _():
        kaug_ref[:, 128:] = oh2_ref[...]

    at = 0
    for ref in v_refs:
        v_ref[at : at + ref.shape[0], :] = ref[...]
        at += ref.shape[0]
    qp = q_ref[...]
    for odd in (0, 1):
        build_kaug(kaug_ref, k_refs, oh1_ref, oh2_ref, odd)
        build_qaug(first_row, qp, tw_ref, tr_ref, qaug_out.at[odd], odd, total_rows, scale)
        for t in range(0, tokens, 256):
            scores = mt(kaug_ref[...], qaug_out[odd, t : t + 256, :])
            top = jnp.max(scores, axis=0, keepdims=True)
            total = jnp.zeros((1, 256), F32)
            for c in range(0, keys, 128):
                weight = jnp.exp(scores[c : c + 128] - top)
                total = total + rowsum(weight)
                p_ref[c : c + 128, :] = weight.astype(BF)
            lse_ref[0, odd : odd + 1, t : t + 256] = top + jnp.log(total)
            out_t = tm(v_ref[...], p_ref[...])
            ot_ref[64 * odd : 64 * odd + 64, t : t + 256] = (
                out_t[64 * odd : 64 * odd + 64] / total
            )
    o_ref[...] = ot_ref[...].T.astype(BF)


def attend_call(first, qkv_own, kv_others, tables, oh1, oh2, total_rows, heads):
    tokens = qkv_own.shape[0]
    width = qkv_own.shape[1] // 3
    keys = oh1.shape[0]
    aug = 128 + oh2.shape[1]
    pairs = width // 128
    tw, tr = tables
    parts = 1 + (1 if kv_others is not None else 0)
    in_specs = [
        pl.BlockSpec(memory_space=pltpu.SMEM),
        pl.BlockSpec((tokens, 128), lambda h: (0, h)),
        whole(tw.shape),
        whole(tr.shape),
        whole(oh1.shape),
        whole(oh2.shape),
    ]
    k_args, v_args, k_specs, v_specs = [qkv_own], [qkv_own], [], []
    k_specs.append(pl.BlockSpec((tokens, 128), lambda h: (0, h + pairs)))
    v_specs.append(pl.BlockSpec((tokens, 128), lambda h: (0, h + 2 * pairs)))
    if kv_others is not None:
        k_args.append(kv_others)
        v_args.append(kv_others)
        k_specs.append(pl.BlockSpec((keys - tokens, 128), lambda h: (0, h)))
        v_specs.append(pl.BlockSpec((keys - tokens, 128), lambda h: (0, h + pairs)))
    scale = (width // heads) ** -0.5
    return call(
        functools.partial(attend_kernel, total_rows, scale, parts),
        [
            sds((tokens, width), BF),
            sds((heads, tokens, aug), BF),
            sds((pairs, 2, tokens), F32),
        ],
        grid=(pairs,),
        in_specs=in_specs + k_specs + v_specs,
        out_specs=[
            pl.BlockSpec((tokens, 128), lambda h: (0, h)),
            pl.BlockSpec((2, tokens, aug), lambda h: (h, 0, 0)),
            pl.BlockSpec((1, 2, tokens), lambda h: (h, 0, 0)),
        ],
        scratch=[
            pltpu.VMEM((keys, aug), BF),
            pltpu.VMEM((keys, 128), BF),
            pltpu.VMEM((keys, 256), BF),
            pltpu.VMEM((128, tokens), F32),
        ],
        flops=12e9,
        name="attend",
    )(first, qkv_own, tw, tr, oh1, oh2, *k_args, *v_args)


def mlp_kernel(
    x_ref, o_ref, wp_ref, w1_ref, b1_ref, w2_ref, p_ref, x1_ref, g_ref, gp_ref, y_ref, n2_ref, acc_ref
):
    step = pl.program_id(0)
    tokens = x_ref.shape[0]

    @pl.when(step == 0)
    def _():
        product = mm(o_ref[...], wp_ref[...])
        for at in range(0, tokens, 32):
            sl = slice(at, at + 32)
            middle = x_ref[sl, :].astype(F32) + (product[sl] + p_ref[6:7, :])
            x1_ref[sl, :] = middle
            hat, _ = stats(middle)
            n2_ref[sl, :] = (hat * p_ref[1:2, :] + p_ref[3:4, :]).astype(BF)

    hidden = mm(n2_ref[...], w1_ref[...])
    for at in range(0, tokens, 32):
        sl = slice(at, at + 32)
        value, slope = gelu_pair(hidden[sl] + b1_ref[...])
        g_ref[sl, :] = value.astype(BF)
        gp_ref[sl, :] = slope.astype(BF)
    part = mm(g_ref[...], w2_ref[...])

    @pl.when(step == 0)
    def _():
        acc_ref[...] = part

    @pl.when(step > 0)
    def _():
        acc_ref[...] += part

    @pl.when(step == pl.num_programs(0) - 1)
    def _():
        y_ref[...] = (x1_ref[...] + (acc_ref[...] + p_ref[7:8, :])).astype(BF)


def mlp_call(tokens, attended, wp, w1, b1, w2, p768):
    rows, width = tokens.shape
    hidden = w1.shape[1]
    return call(
        mlp_kernel,
        [sds((rows, width), F32), sds((rows, hidden), BF), sds((rows, hidden), BF), sds((rows, width), BF)],
        grid=(hidden // width,),
        in_specs=[
            whole((rows, width)),
            whole((rows, width)),
            whole(wp.shape),
            pl.BlockSpec((width, width), lambda s: (0, s)),
            pl.BlockSpec((1, width), lambda s: (0, s)),
            pl.BlockSpec((width, width), lambda s: (s, 0)),
            whole(p768.shape),
        ],
        out_specs=[
            whole((rows, width)),
            pl.BlockSpec((rows, width), lambda s: (0, s)),
            pl.BlockSpec((rows, width), lambda s: (0, s)),
            whole((rows, width)),
        ],
        scratch=[pltpu.VMEM((rows, width), BF), pltpu.VMEM((rows, width), F32)],
        flops=11e9,
        name="mlp",
    )(tokens, attended, wp, w1, b1, w2, p768)


def pool_matrix(a, b, rows, cols):
    count = rows * cols // 4
    out_at = lax.broadcasted_iota(jnp.int32, (count, rows * cols), 0)
    in_at = lax.broadcasted_iota(jnp.int32, (count, rows * cols), 1)
    half = cols // 2
    source = (2 * lax.div(out_at, half) + a) * cols + 2 * lax.rem(out_at, half) + b
    return jnp.where(in_at == source, 1.0, 0.0).astype(BF)


def lateral_norm(product, gain, shift, write):
    for at in range(0, product.shape[0], 64):
        hat, _ = stats(product[at : at + 64])
        write(at, (hat * gain + shift).astype(BF))


def pyramid_kernel(
    lr, cols, y_ref, ff_ref, fs_ref, mu_ref, lf_ref, lm_ref, lc0_ref, lc1_ref, p384_ref, fsb_ref, p256_ref,
    zf_ref, zm_ref, zb_ref, zc_ref, plane_ref, mplane_ref, f2_ref,
):
    tokens = lr * cols
    y = y_ref[...]
    half = mu_ref.shape[1] // 2
    quart = fs_ref.shape[0] // 4

    for b in (0, 1):
        first = mm(y, ff_ref[:, half * b : half * b + half])
        for at in range(0, tokens, 64):
            sl = slice(at, at + 64)
            hat, _ = stats(first[sl] + p384_ref[0:1, :])
            value = hat * p384_ref[1:2, :] + p384_ref[2:3, :]
            f2_ref[sl, :] = (0.5 * value * (1.0 + lax.erf(value * SQRT_HALF))).astype(BF)

        for c in (0, 1):
            for d in (0, 1):
                at_row = (2 * c + d) * quart
                third = (mt(f2_ref[...], fs_ref[at_row : at_row + quart, :]) + fsb_ref[...]).astype(BF)
                product = mm(third, lf_ref[...])

                def write(at, values):
                    plane_ref[c, 2 * b + d, at : at + 64, :] = values

                lateral_norm(product, p256_ref[0:1, :], p256_ref[8:9, :], write)

        middle = (mm(y, mu_ref[:, half * b : half * b + half]) + p384_ref[3:4, :]).astype(BF)
        product = mm(middle, lm_ref[...])

        def write_middle(at, values):
            mplane_ref[b, at : at + 64, :] = values

        lateral_norm(product, p256_ref[1:2, :], p256_ref[9:10, :], write_middle)

    weave4 = weave_matrix(4 * cols, 4)
    weave2 = weave_matrix(2 * cols, 2)
    for i in range(lr):
        sl = slice(i * cols, (i + 1) * cols)
        for c in (0, 1):
            planes = jnp.concatenate([plane_ref[c, k, sl, :] for k in range(4)], axis=0)
            zf_ref[i, c] = mm(weave4, planes).astype(BF)
        planes = jnp.concatenate([mplane_ref[k, sl, :] for k in range(2)], axis=0)
        zm_ref[i, 0] = mm(weave2, planes).astype(BF)

    @pl.when(pl.program_id(0) == 0)
    def _():
        product = mm(y, lc0_ref[...])

        def write_base(at, values):
            zb_ref[at : at + 64, :] = values

        lateral_norm(product, p256_ref[2:3, :], p256_ref[10:11, :], write_base)
        pooled = mm(pool_matrix(0, 0, lr, cols), y)
        for a, b in ((0, 1), (1, 0), (1, 1)):
            pooled = jnp.maximum(pooled, mm(pool_matrix(a, b, lr, cols), y))
        product = mm(pooled.astype(BF), lc1_ref[...])

        def write_coarse(at, values):
            zc_ref[at : at + 64, :] = values

        lateral_norm(product, p256_ref[3:4, :], p256_ref[11:12, :], write_coarse)


def pyramid_call(y, lr, cols, ff, fs, mu, lf, lm, lc0, lc1, p384, fsb, p256):
    tokens, width = y.shape
    outs = lf.shape[1]
    half2 = ff.shape[1] // 2
    return call(
        functools.partial(pyramid_kernel, lr, cols),
        [
            sds((lr, 4, 4 * cols, outs), BF),
            sds((lr, 2, 2 * cols, outs), BF),
            sds((tokens, outs), BF),
            sds((tokens // 4, outs), BF),
        ],
        grid=(2,),
        in_specs=[
            whole(y.shape),
            pl.BlockSpec((width, half2), lambda a: (0, a)),
            whole(fs.shape),
            pl.BlockSpec((width, half2), lambda a: (0, a)),
            whole(lf.shape),
            whole(lm.shape),
            whole(lc0.shape),
            whole(lc1.shape),
            whole(p384.shape),
            whole(fsb.shape),
            whole(p256.shape),
        ],
        out_specs=[
            pl.BlockSpec((lr, 2, 4 * cols, outs), lambda a: (0, a, 0, 0)),
            pl.BlockSpec((lr, 1, 2 * cols, outs), lambda a: (0, a, 0, 0)),
            whole((tokens, outs)),
            whole((tokens // 4, outs)),
        ],
        scratch=[
            pltpu.VMEM((2, 4, tokens, outs), BF),
            pltpu.VMEM((2, tokens, outs), BF),
            pltpu.VMEM((tokens, half2 // 2), BF),
        ],
        flops=8e9,
        name="pyramid",
    )(y, ff, fs, mu, lf, lm, lc0, lc1, p384, fsb, p256)


def fill_padded(step, block, rows, src_ref, rim_ref, pad_ref, left, right):
    def put(at, row):
        pad_ref[at] = jnp.concatenate(
            [mm(left, row).astype(BF), row, mm(right, row).astype(BF)], axis=1
        )

    @pl.when(step == 0)
    def _():
        put(0, rim_ref[0])
        put(1, src_ref[0])

    def body(k, carry):
        at = step * block + k
        put(at + 2, src_ref[at + 1])
        return carry

    lax.fori_loop(0, block - 1, body, 0)

    @pl.when(step == rows // block - 1)
    def _():
        put(rows + 1, rim_ref[1])

    @pl.when(step < rows // block - 1)
    def _():
        at = step * block + block - 1
        put(at + 2, src_ref[at + 1])


def conv_kernel(
    level, block, shards, z_ref, rim_ref, w_ref, cot_ref, p_ref, *refs
):
    map_ref, dr_ref, dw_ref, sums_ref, pad_ref, dwt_ref, acc_ref, pack_ref = refs[-8:]
    step = pl.program_id(0)
    rows, cols, chan = z_ref.shape
    pixels = block * cols
    fill_padded(
        step, block, rows, z_ref, rim_ref, pad_ref, shift_matrix(cols, -1), shift_matrix(cols, 1)
    )
    windows = [
        pad_ref[pl.ds(step * block + a, block)].reshape(pixels, 3 * chan) for a in range(3)
    ]
    result = mm(windows[0], w_ref[0, 0])
    for a in (1, 2):
        result = result + mm(windows[a], w_ref[0, a])
    acc_ref[...] = result.reshape(block, cols, chan)
    gain = p_ref[4 + level : 5 + level, :]
    shift = p_ref[12 + level : 13 + level, :]
    part = min(cols, 64)
    per_row = cols // part

    def body(k, carry):
        sum_gain, sum_shift = carry
        for q in range(per_row):
            at = slice(q * part, (q + 1) * part)
            hat, inverse = stats(acc_ref[k, at, :])
            map_ref[k, at, :] = (hat * gain + shift).astype(BF)
            cot = cot_ref[k, at, :].astype(F32)
            sum_gain = sum_gain + rowsum(cot * hat)
            sum_shift = sum_shift + rowsum(cot)
            dr_ref[k, at, :] = norm_back(cot * gain, hat, inverse).astype(BF)
        return sum_gain, sum_shift

    zero = jnp.zeros((1, chan), F32)
    sum_gain, sum_shift = lax.fori_loop(0, block, body, (zero, zero))

    @pl.when(step == 0)
    def _():
        sums_ref[...] = jnp.zeros_like(sums_ref)
        dwt_ref[...] = jnp.zeros_like(dwt_ref)

    sums_ref[0:1, :] += sum_gain
    sums_ref[1:2, :] += sum_shift
    grad_t = dr_ref[...].reshape(pixels, chan).T
    for a in range(3):
        dwt_ref[a] += mm(grad_t, windows[a])

    @pl.when(step == pl.num_programs(0) - 1)
    def _():
        unit = chan * 3 // shards
        for a in range(3):
            grad = dwt_ref[a].T
            for m in range(shards):
                piece = a * shards + m
                to = piece // 3
                lane = chan * (piece % 3)
                pack_ref[to * unit : to * unit + unit, lane : lane + chan] = grad[
                    m * unit : m * unit + unit
                ]
        dw_ref[...] = pack_ref[...].astype(BF)


def conv_call(level, z, rims, weights, cot, p256, block, shards, packed):
    rows, cols, chan = z.shape
    before = [] if packed is None else [packed]
    spec = pl.BlockSpec((block, cols, chan), lambda s: (s, 0, 0))
    return call(
        functools.partial(conv_kernel, level, block, shards),
        [
            sds((rows, cols, chan), BF),
            sds((rows, cols, chan), BF),
            sds((3 * chan, 4 * 3 * chan), BF),
            sds((8, chan), F32),
        ],
        grid=(rows // block,),
        in_specs=[
            whole(z.shape),
            whole(rims.shape),
            pl.BlockSpec((1, 3, 3 * chan, chan), lambda s: (level, 0, 0, 0)),
            spec,
            whole(p256.shape),
        ]
        + [pl.BlockSpec(memory_space=pl.ANY)] * len(before),
        out_specs=[
            spec,
            spec,
            pl.BlockSpec((3 * chan, 3 * chan), lambda s: (0, level)),
            whole((8, chan)),
        ],
        scratch=[
            pltpu.VMEM((rows + 2, cols, 3 * chan), BF),
            pltpu.VMEM((3, chan, 3 * chan), F32),
            pltpu.VMEM((block, cols, chan), F32),
            pltpu.VMEM((3 * chan, 3 * chan), F32),
        ],
        flops=4 * 9 * rows * cols * chan * chan,
        name=f"conv{level}",
        aliases={5: 2} if before else {},
    )(z, rims, weights, cot, p256, *before)


def conv_back_kernel(ways, block, dr_ref, rim_ref, w_ref, dz_ref, pad_ref):
    step = pl.program_id(0)
    rows, cols, chan = dr_ref.shape
    pixels = block * cols
    fill_padded(
        step, block, rows, dr_ref, rim_ref, pad_ref, shift_matrix(cols, 1), shift_matrix(cols, -1)
    )
    result = None
    for a in range(3):
        window = pad_ref[pl.ds(step * block + 2 - a, block)].reshape(pixels, 3 * chan)
        for b in range(3):
            part = mt(
                window[:, b * chan : (b + 1) * chan], w_ref[0, a, b * chan : (b + 1) * chan, :]
            )
            result = part if result is None else result + part
    low = result.astype(BF)
    if ways == 1:
        dz_ref[...] = low.reshape(dz_ref.shape)
        return
    unweave = weave_matrix(cols, ways, inverse=True)
    base = cols // ways
    for k in range(block):
        planes = mm(unweave, low[k * cols : (k + 1) * cols]).astype(BF)
        token_row, offset = k // ways, k % ways
        for w in range(ways):
            dz_ref[offset, w, token_row * base : (token_row + 1) * base, :] = planes[
                w * base : (w + 1) * base
            ]


def conv_back_call(level, dr, rims, weights, ways, block):
    rows, cols, chan = dr.shape
    if ways == 1:
        out = sds((rows * cols, chan), BF)
        spec = pl.BlockSpec((block * cols, chan), lambda s: (s, 0))
    else:
        tokens = rows * cols // (ways * ways)
        out = sds((ways, ways, tokens, chan), BF)
        spec = pl.BlockSpec(
            (ways, ways, block * cols // (ways * ways), chan), lambda s: (0, 0, s, 0)
        )
    return call(
        functools.partial(conv_back_kernel, ways, block),
        out,
        grid=(rows // block,),
        in_specs=[
            whole(dr.shape),
            whole(rims.shape),
            pl.BlockSpec((1, 3, 3 * chan, chan), lambda s: (level, 0, 0, 0)),
        ],
        out_specs=spec,
        scratch=[pltpu.VMEM((rows + 2, cols, 3 * chan), BF)],
        flops=2 * 9 * rows * cols * chan * chan,
        name=f"conv_back{level}",
    )(dr, rims, weights)


def lateral_back(product, read, gain, dl_ref):
    chan = product.shape[1]
    sum_gain = jnp.zeros((1, chan), F32)
    sum_shift = jnp.zeros((1, chan), F32)
    for at in range(0, product.shape[0], 64):
        hat, inverse = stats(product[at : at + 64])
        grad = read(at)
        sum_gain = sum_gain + rowsum(grad * hat)
        sum_shift = sum_shift + rowsum(grad)
        dl_ref[at : at + 64, :] = norm_back(grad * gain, hat, inverse).astype(BF)
    return sum_gain, sum_shift


def pyramid_back_kernel(
    lr, cols, y_ref, ff_ref, fs_ref, mu_ref, lf_ref, lm_ref, lc0_ref, lc1_ref, p384_ref, fsb_ref, p256_ref,
    dzf_ref, dzm_ref, dzb_ref, dzc_ref, place_ref,
    dy_ref, pack_ref, s384_ref, s192_ref, s256_ref,
    yt_ref, hat_ref, slope_ref, inv_ref, f2_ref, df2_ref, df1_ref, dl_ref, fs_acc, lf_acc, lm_acc,
    dcol_ref, drest_ref, sem,
):
    step = pl.program_id(0)
    tokens = lr * cols
    half = ff_ref.shape[1]
    chan = lf_ref.shape[1]

    def col_copy(at, which):
        return pltpu.make_async_copy(
            dcol_ref.at[which, at],
            pack_ref.at[:, pl.ds((4 * which + at) * half, half)],
            sem.at[4 * which + at],
        )

    rest = drest_ref.shape[1]
    rest_copy = pltpu.make_async_copy(drest_ref, pack_ref.at[:, pl.ds(8 * half, rest)], sem.at[8])
    quart = fs_ref.shape[0] // 4

    @pl.when(step == 0)
    def _():
        yt_ref[...] = y_ref[...].T
        for ref in (fs_acc, lf_acc, lm_acc, s384_ref, s192_ref, s256_ref):
            ref[...] = jnp.zeros_like(ref)
        product = mm(y_ref[...], lc0_ref[...])
        sg, ss = lateral_back(
            product, lambda at: dzb_ref[at : at + 64, :].astype(F32), p256_ref[2:3, :], dl_ref
        )
        s256_ref[2:3, :] = sg
        s256_ref[10:11, :] = ss
        drest_ref[:, half : half + chan] = mm(yt_ref[...], dl_ref[...]).astype(BF)
        dy_ref[...] = mt(dl_ref[...], lc0_ref[...])
        picks = [mm(pool_matrix(a, b, lr, cols), y_ref[...]) for a in (0, 1) for b in (0, 1)]
        top = jnp.maximum(jnp.maximum(picks[0], picks[1]), jnp.maximum(picks[2], picks[3]))
        low = top.astype(BF)
        product = mm(low, lc1_ref[...])
        sg, ss = lateral_back(
            product, lambda at: dzc_ref[at : at + 64, :].astype(F32), p256_ref[3:4, :], dl_ref
        )
        s256_ref[3:4, :] = sg
        s256_ref[11:12, :] = ss
        grad = dl_ref[0 : tokens // 4, :]
        drest_ref[:, half + chan : half + 2 * chan] = tm(low, grad).astype(BF)
        dtop = mt(grad, lc1_ref[...])
        hits = [jnp.where(pick == top, 1.0, 0.0) for pick in picks]
        dtop = dtop / (hits[0] + hits[1] + hits[2] + hits[3])
        for index, hit in enumerate(hits):
            share = dtop * hit
            upper = share.astype(BF)
            lower = (share - upper.astype(F32)).astype(BF)
            spread = pool_matrix(index // 2, index % 2, lr, cols)
            dy_ref[...] += tm(spread, upper) + tm(spread, lower)

    first = mm(y_ref[...], ff_ref[...])
    for at in range(0, tokens, 64):
        sl = slice(at, at + 64)
        hat, inverse = stats(first[sl] + p384_ref[0:1, :])
        hat_ref[sl, :] = hat
        inv_ref[sl, :] = jnp.broadcast_to(inverse, (64, 128))
        value, slope = gelu_pair(hat * p384_ref[1:2, :] + p384_ref[2:3, :])
        f2_ref[sl, :] = value.astype(BF)
        slope_ref[sl, :] = slope
    for c in (0, 1):
        for d in (0, 1):
            at_row = (2 * c + d) * quart
            weight = fs_ref[at_row : at_row + quart, :]
            third = (mt(f2_ref[...], weight) + fsb_ref[...]).astype(BF)
            product = mm(third, lf_ref[...])
            sg, ss = lateral_back(
                product,
                lambda at: dzf_ref[0, c, 0, d, at : at + 64, :].astype(F32),
                p256_ref[0:1, :],
                dl_ref,
            )
            s256_ref[0:1, :] += sg
            s256_ref[8:9, :] += ss
            lf_acc[...] += tm(third, dl_ref[...])
            dthird = mt(dl_ref[...], lf_ref[...]).astype(BF)
            s192_ref[0:1, :] += rowsum(dthird.astype(F32))
            fs_acc[at_row : at_row + quart, :] += tm(dthird, f2_ref[...])
            part = mm(dthird, weight)
            if c + d == 0:
                df2_ref[...] = part
            else:
                df2_ref[...] += part
    zero = jnp.zeros((1, df2_ref.shape[1]), F32)
    sum_gain, sum_shift, sum_bias = zero, zero, zero
    for at in range(0, tokens, 64):
        sl = slice(at, at + 64)
        hat = hat_ref[sl, :]
        grad = df2_ref[sl, :] * slope_ref[sl, :]
        sum_gain = sum_gain + rowsum(grad * hat)
        sum_shift = sum_shift + rowsum(grad)
        low = norm_back(grad * p384_ref[1:2, :], hat, inv_ref[sl, 0:1]).astype(BF)
        sum_bias = sum_bias + rowsum(low.astype(F32))
        df1_ref[sl, :] = low
    s384_ref[0:1, :] += sum_bias
    s384_ref[1:2, :] += sum_gain
    s384_ref[2:3, :] += sum_shift
    dcol_ref[0, step] = mm(yt_ref[...], df1_ref[...]).astype(BF)
    col_copy(step, 0).start()
    dy_ref[...] += mt(df1_ref[...], ff_ref[...])

    middle = (mm(y_ref[...], mu_ref[...]) + p384_ref[3:4, :]).astype(BF)
    product = mm(middle, lm_ref[...])
    sg, ss = lateral_back(
        product,
        lambda at: dzm_ref[0, 0, at : at + 64, :].astype(F32),
        p256_ref[1:2, :],
        dl_ref,
    )
    s256_ref[1:2, :] += sg
    s256_ref[9:10, :] += ss
    lm_acc[...] += tm(middle, dl_ref[...])
    dmiddle = mt(dl_ref[...], lm_ref[...]).astype(BF)
    s384_ref[3:4, :] += rowsum(dmiddle.astype(F32))
    dcol_ref[1, step] = mm(yt_ref[...], dmiddle).astype(BF)
    col_copy(step, 1).start()
    dy_ref[...] += mt(dmiddle, mu_ref[...])

    @pl.when(step == pl.num_programs(0) - 1)
    def _():
        drest_ref[:, 0:half] = fs_acc[...].astype(BF)
        laterals = jnp.concatenate([lf_acc[...], lm_acc[...]], axis=0).astype(BF)
        drest_ref[:, half + 2 * chan : half + 3 * chan] = mm(place_ref[...], laterals).astype(BF)
        rest_copy.start()
        for which in (0, 1):
            for at in range(4):
                col_copy(at, which).wait()
        rest_copy.wait()


def pyramid_back_call(
    y, lr, cols, ff, fs, mu, lf, lm, lc0, lc1, p384, fsb, p256, dzf, dzm, dzb, dzc, place, lanes
):
    tokens, width = y.shape
    half = fs.shape[1]
    quart = fsb.shape[1]
    outs = lf.shape[1]
    col_block = pl.BlockSpec((width, half), lambda s: (0, s))
    return call(
        functools.partial(pyramid_back_kernel, lr, cols),
        [
            sds((tokens, width), F32),
            sds((width, lanes), BF),
            sds((8, half), F32),
            sds((8, quart), F32),
            sds((16, outs), F32),
        ],
        grid=(4,),
        in_specs=[
            whole(y.shape),
            col_block,
            whole(fs.shape),
            col_block,
            whole(lf.shape),
            whole(lm.shape),
            whole(lc0.shape),
            whole(lc1.shape),
            whole(p384.shape),
            whole(fsb.shape),
            whole(p256.shape),
            pl.BlockSpec((1, 2, 1, 2, tokens, outs), lambda s: (s // 2, 0, s % 2, 0, 0, 0)),
            pl.BlockSpec((1, 1, tokens, outs), lambda s: (s // 2, s % 2, 0, 0)),
            whole(dzb.shape),
            whole(dzc.shape),
            whole(place.shape),
        ],
        out_specs=[
            whole((tokens, width)),
            pl.BlockSpec(memory_space=pl.ANY),
            whole((8, half)),
            whole((8, quart)),
            whole((16, outs)),
        ],
        scratch=[
            pltpu.VMEM((width, tokens), BF),
            pltpu.VMEM((tokens, half), F32),
            pltpu.VMEM((tokens, half), F32),
            pltpu.VMEM((tokens, 128), F32),
            pltpu.VMEM((tokens, half), BF),
            pltpu.VMEM((tokens, half), F32),
            pltpu.VMEM((tokens, half), BF),
            pltpu.VMEM((tokens, outs), BF),
            pltpu.VMEM(fs.shape, F32),
            pltpu.VMEM(lf.shape, F32),
            pltpu.VMEM(lm.shape, F32),
            pltpu.VMEM((2, 4, width, half), BF),
            pltpu.VMEM((width, half + 3 * outs), BF),
            pltpu.SemaphoreType.DMA((9,)),
        ],
        flops=20e9,
        name="pyramid_back",
    )(
        y, ff, fs, mu, lf, lm, lc0, lc1, p384, fsb, p256,
        dzf.reshape(2, 2, 2, 2, tokens, outs), dzm, dzb, dzc, place,
    )


def mlp_back_kernel(
    shards, offset,
    dy_ref, g_ref, gp_ref, w1_ref, w2_ref, x1_ref, o_ref, wp_ref, p_ref, s384_ref, s192_ref, s256_ref, levels_ref,
    hot256_ref, hot384_ref, hot192_ref, old_ref,
    pack_ref, dx1_ref, do_ref,
    n2t_ref, d2_ref, dn2_ref, low_ref, sums_ref, vec_ref, dw1_ref, dw2f_ref, dw2_ref, dwp_ref, vlow_ref, sem,
):
    step = pl.program_id(0)
    steps = pl.num_programs(0)
    tokens, width = dy_ref.shape
    unit = width // shards
    hidden = 4 * width

    def w1_copy(at):
        return pltpu.make_async_copy(
            dw1_ref.at[at], pack_ref.at[:, pl.ds(offset + at * width, width)], sem.at[at]
        )

    def w2_copy(at):
        rows = width // 4
        return pltpu.make_async_copy(
            dw2_ref.at[at],
            pack_ref.at[pl.ds(at * rows, rows), pl.ds(offset + hidden, hidden)],
            sem.at[4 + at],
        )

    wp_copy = pltpu.make_async_copy(
        dwp_ref, pack_ref.at[:, pl.ds(offset + 2 * hidden, width)], sem.at[8]
    )
    vec_copy = pltpu.make_async_copy(
        vlow_ref, pack_ref.at[:, pl.ds(offset + 2 * hidden + width, 128)], sem.at[9]
    )

    @pl.when(step == 0)
    def _():
        sums_ref[...] = jnp.zeros_like(sums_ref)
        vec_ref[...] = jnp.zeros_like(vec_ref)
        total = jnp.zeros((1, width), F32)
        for at in range(0, tokens, 32):
            sl = slice(at, at + 32)
            hat, _ = stats(x1_ref[sl, :])
            low_ref[sl, :] = (hat * p_ref[1:2, :] + p_ref[3:4, :]).astype(BF)
            low = dy_ref[sl, :].astype(BF)
            d2_ref[sl, :] = low
            total = total + rowsum(low.astype(F32))
        sums_ref[7:8, :] = total
        n2t_ref[...] = low_ref[...].T

    dw2 = tm(g_ref[...], d2_ref[...])
    dg = mt(d2_ref[...], w2_ref[...])
    for at in range(0, tokens, 32):
        sl = slice(at, at + 32)
        low_ref[sl, :] = (dg[sl] * gp_ref[sl, :].astype(F32)).astype(BF)
    db1 = tm(low_ref[...], jnp.ones((tokens, 128), BF))
    lane = lax.broadcasted_iota(jnp.int32, (unit, 128), 1)
    rows4 = width // 4
    for q in range(shards // 4):
        entry = jnp.zeros((unit, 128), F32)
        for k in range(4):
            sl = slice((4 * q + k) * unit, (4 * q + k + 1) * unit)
            dw2f_ref[q * unit : q * unit + unit, k * width : (k + 1) * width] = dw2[sl]
            entry = jnp.where(lane == 40 + k, db1[sl], entry)
        vec_ref[pl.ds(pl.multiple_of(step * rows4 + q * unit, 8), unit), :] += entry
    dw2_ref[step] = dw2f_ref[...].astype(BF)
    w2_copy(step).start()
    dw1_ref[step] = mm(n2t_ref[...], low_ref[...]).astype(BF)
    w1_copy(step).start()
    part = mt(low_ref[...], w1_ref[...])

    @pl.when(step == 0)
    def _():
        dn2_ref[...] = part

    @pl.when(step > 0)
    def _():
        dn2_ref[...] += part

    @pl.when(step == steps - 1)
    def _():
        zero = jnp.zeros((1, width), F32)
        sum_gain, sum_shift, sum_bias = zero, zero, zero
        for at in range(0, tokens, 32):
            sl = slice(at, at + 32)
            hat, inverse = stats(x1_ref[sl, :])
            grad = dn2_ref[sl, :]
            sum_gain = sum_gain + rowsum(grad * hat)
            sum_shift = sum_shift + rowsum(grad)
            dx1 = dy_ref[sl, :] + norm_back(grad * p_ref[1:2, :], hat, inverse)
            dx1_ref[sl, :] = dx1
            low = dx1.astype(BF)
            sum_bias = sum_bias + rowsum(low.astype(F32))
            d2_ref[sl, :] = low
        sums_ref[1:2, :] = sum_gain
        sums_ref[3:4, :] = sum_shift
        sums_ref[6:7, :] = sum_bias
        dwp_ref[...] = tm(o_ref[...], d2_ref[...]).astype(BF)
        wp_copy.start()
        do_ref[...] = mt(d2_ref[...], wp_ref[...]).astype(BF)

        def lanes_of(rows, before):
            after = 128 - before - rows.shape[0]
            parts = [jnp.zeros((before, rows.shape[1]), F32)] if before else []
            parts += [rows, jnp.zeros((after, rows.shape[1]), F32)]
            return jnp.concatenate(parts, axis=0)

        spread = mt(hot256_ref[...], lanes_of(s256_ref[...], 8).astype(BF))
        spread = spread + mt(hot256_ref[...], lanes_of(levels_ref[...], 24).astype(BF))
        spread = spread + mt(hot384_ref[...], lanes_of(s384_ref[...], 32).astype(BF))
        spread = spread + mt(hot192_ref[...], lanes_of(s192_ref[...], 48).astype(BF))
        spread = spread + lanes_of(sums_ref[...], 0).T
        vlow_ref[...] = (vec_ref[...] + spread).astype(BF)
        vec_copy.start()
        for at in range(4):
            w1_copy(at).wait()
            w2_copy(at).wait()
        wp_copy.wait()
        vec_copy.wait()


def mlp_back_call(
    dy, g, gp, w1, w2, x1, attended, wp, p768, s384, s192, s256, levels, hots, packed, offset, shards
):
    rows, width = dy.shape
    hidden = g.shape[1]
    full = whole((rows, width))
    column = pl.BlockSpec((rows, width), lambda s: (0, s))
    smalls = [p768, s384, s192, s256, levels, *hots]
    return call(
        functools.partial(mlp_back_kernel, shards, offset),
        [
            sds(packed.shape, BF),
            sds((rows, width), F32),
            sds((rows, width), BF),
        ],
        grid=(hidden // width,),
        in_specs=[
            full,
            column,
            column,
            pl.BlockSpec((width, width), lambda s: (0, s)),
            pl.BlockSpec((width, width), lambda s: (s, 0)),
            full,
            full,
            whole((width, width)),
        ]
        + [whole(a.shape) for a in smalls]
        + [pl.BlockSpec(memory_space=pl.ANY)],
        out_specs=[pl.BlockSpec(memory_space=pl.ANY), full, full],
        scratch=[
            pltpu.VMEM((width, rows), BF),
            pltpu.VMEM((rows, width), BF),
            pltpu.VMEM((rows, width), F32),
            pltpu.VMEM((rows, width), BF),
            pltpu.VMEM((8, width), F32),
            pltpu.VMEM((width, 128), F32),
            pltpu.VMEM((4, width, width), BF),
            pltpu.VMEM((width // 4, hidden), F32),
            pltpu.VMEM((4, width // 4, hidden), BF),
            pltpu.VMEM((width, width), BF),
            pltpu.VMEM((width, 128), BF),
            pltpu.SemaphoreType.DMA((10,)),
        ],
        flops=22e9,
        name="mlp_back",
        aliases={16: 0},
    )(dy, g, gp, w1, w2, x1, attended, wp, *smalls, packed)


def roll_back(values, amount):
    moved = jnp.concatenate(
        [
            pltpu.roll(values[8 * g : 8 * g + 8], (amount - 7 - 8 * g) % 128, 1)
            for g in range(values.shape[0] // 8)
        ],
        axis=0,
    )
    left = 7 - lax.rem(lax.broadcasted_iota(jnp.int32, values.shape, 0), 8)
    for step in (1, 2, 4):
        moved = jnp.where((left & step) > 0, pltpu.roll(moved, step, 1), moved)
    return moved


def attend_back_kernel(total_rows, scale, others, *refs):
    first_ref, q_ref, qaug_ref, do_ref, o_ref, lse_ref, tab_ref, oh1_ref, oh2_ref = refs[:9]
    k_refs = refs[9 : 9 + others]
    v_refs = refs[9 + others : 9 + 2 * others]
    rest = refs[9 + 2 * others :]
    dq_ref, dtab_ref = rest[:2]
    dk_refs = rest[2 : 2 + others]
    dv_refs = rest[2 + others : 2 + 2 * others]
    kaug_ref, v_ref, p_ref, ds_ref, dqt_ref, df_ref = rest[2 + 2 * others :]
    first_row = first_ref[0]
    tokens = q_ref.shape[0]
    keys = kaug_ref.shape[0]

    @pl.when(pl.program_id(0) == 0)
    def _():
        kaug_ref[:, 128:] = oh2_ref[...]
        dtab_ref[...] = jnp.zeros_like(dtab_ref)

    at = 0
    for ref in v_refs:
        v_ref[at : at + ref.shape[0], :] = ref[...]
        at += ref.shape[0]
    lane_all = lax.broadcasted_iota(jnp.int32, (tokens, 128), 1)
    lane = lax.broadcasted_iota(jnp.int32, (64, 128), 1)
    qf = q_ref[...].astype(F32)
    dof = do_ref[...].astype(F32)
    delta_t = (dof * o_ref[...].astype(F32)).T
    dk = None
    dv = None
    dq = None
    for odd in (0, 1):
        mine_all = (lane_all >= 64) if odd else (lane_all < 64)
        other = (lane < 64) if odd else (lane >= 64)
        build_kaug(kaug_ref, k_refs, oh1_ref, oh2_ref, odd)
        qm = jnp.where(mine_all, qf, 0.0).astype(BF)
        dom = jnp.where(mine_all, dof, 0.0).astype(BF)
        delta = rowsum(delta_t[64 * odd : 64 * odd + 64])
        for t in range(0, tokens, 256):
            sl = slice(t, t + 256)
            scores = mt(kaug_ref[...], qaug_ref[odd, sl, :])
            dweight = mt(v_ref[...], dom[sl])
            lse = lse_ref[0, odd : odd + 1, sl]
            for c in range(0, keys, 128):
                weight = jnp.exp(scores[c : c + 128] - lse)
                p_ref[c : c + 128, :] = weight.astype(BF)
                ds_ref[c : c + 128, :] = (weight * (dweight[c : c + 128] - delta[:, sl])).astype(BF)
            dk_part = mm(ds_ref[...], qm[sl])
            dv_part = mm(p_ref[...], dom[sl])
            dk = dk_part if dk is None else dk + dk_part
            dv = dv_part if dv is None else dv + dv_part
            dqt_ref[:, sl] = tm(kaug_ref[...], ds_ref[...])
        dqa = dqt_ref[0:256, :].T
        for i in range(tokens // 64):
            sl = slice(64 * i, 64 * i + 64)
            cols = roll_back(jnp.where(other, dqa[sl, 0:128], 0.0), 63 if odd else 127)
            shift = lax.rem(63 + total_rows - (first_row + i) + 128, 128)
            rows = pltpu.roll(
                jnp.where((lane >= 64) & (lane < 64 + total_rows), dqa[sl, 128:256], 0.0), shift, 1
            )
            df_ref[sl, 0:128] = cols.astype(BF)
            df_ref[sl, 128:256] = rows.astype(BF)
        from_tables = mt(df_ref[...], tab_ref[...])
        part = jnp.where(mine_all, dqa[:, 0:128] * scale + from_tables, 0.0)
        dq = part if dq is None else dq + part
        dtab_ref[...] += tm(qm, df_ref[...])
    dq_ref[...] = dq.astype(BF)
    at = 0
    for dk_ref, dv_ref in zip(dk_refs, dv_refs):
        count = dk_ref.shape[0]
        dk_ref[...] = (dk[at : at + count] * scale).astype(BF)
        dv_ref[...] = dv[at : at + count].astype(BF)
        at += count


def attend_back_call(first, qkv_own, kv_others, qaug, dout, attended, lse, tab, oh1, oh2, total_rows, heads):
    tokens = qkv_own.shape[0]
    width = qkv_own.shape[1] // 3
    keys = oh1.shape[0]
    aug = 128 + oh2.shape[1]
    pairs = width // 128
    parts = 1 + (1 if kv_others is not None else 0)
    own = pl.BlockSpec((tokens, 128), lambda h: (0, h))
    far = pl.BlockSpec((max(keys - tokens, 16), 128), lambda h: (0, h))
    in_specs = [
        pl.BlockSpec(memory_space=pltpu.SMEM),
        own,
        pl.BlockSpec((2, tokens, aug), lambda h: (h, 0, 0)),
        own,
        own,
        pl.BlockSpec((1, 2, tokens), lambda h: (h, 0, 0)),
        whole(tab.shape),
        whole(oh1.shape),
        whole(oh2.shape),
    ]
    k_args, v_args, k_specs, v_specs = [qkv_own], [qkv_own], [], []
    k_specs.append(pl.BlockSpec((tokens, 128), lambda h: (0, h + pairs)))
    v_specs.append(pl.BlockSpec((tokens, 128), lambda h: (0, h + 2 * pairs)))
    g_shapes, g_specs = [sds((tokens, width), BF)], [own]
    if kv_others is not None:
        k_args.append(kv_others)
        v_args.append(kv_others)
        k_specs.append(far)
        v_specs.append(pl.BlockSpec((keys - tokens, 128), lambda h: (0, h + pairs)))
        g_shapes.append(sds((keys - tokens, width), BF))
        g_specs.append(far)
    scale = (width // heads) ** -0.5
    return call(
        functools.partial(attend_back_kernel, total_rows, scale, parts),
        [sds((tokens, width), BF), sds((128, 256), F32)] + g_shapes + g_shapes,
        grid=(pairs,),
        in_specs=in_specs + k_specs + v_specs,
        out_specs=[own, whole((128, 256))] + g_specs + g_specs,
        scratch=[
            pltpu.VMEM((keys, aug), BF),
            pltpu.VMEM((keys, 128), BF),
            pltpu.VMEM((keys, 256), BF),
            pltpu.VMEM((keys, 256), BF),
            pltpu.VMEM((aug, tokens), F32),
            pltpu.VMEM((tokens, 256), BF),
        ],
        flops=30e9,
        name="attend_back",
    )(first, qkv_own, qaug, dout, attended, lse, tab, oh1, oh2, *k_args, *v_args)


def qkv_back_kernel(
    x_ref, dq_ref, dk_ref, dv_ref, rk_ref, rv_ref, w_ref, dx1_ref, p_ref, dtab_ref, hot_ref,
    pack_ref, dx_ref, nt_ref, low_ref, dn_ref, sums_ref, dw_ref, extra_ref, sem,
):
    step = pl.program_id(0)
    tokens, width = x_ref.shape

    def w_copy(at):
        return pltpu.make_async_copy(
            dw_ref.at[at], pack_ref.at[:, pl.ds(at * width, width)], sem.at[at]
        )

    extra_copy = pltpu.make_async_copy(extra_ref, pack_ref.at[:, pl.ds(3 * width, 384)], sem.at[3])

    @pl.when(step == 0)
    def _():
        sums_ref[...] = jnp.zeros_like(sums_ref)
        for at in range(0, tokens, 32):
            sl = slice(at, at + 32)
            hat, _ = stats(x_ref[sl, :].astype(F32))
            low_ref[sl, :] = (hat * p_ref[0:1, :] + p_ref[2:3, :]).astype(BF)
        nt_ref[...] = low_ref[...].T
        low_ref[...] = dq_ref[...]
        sums_ref[4:5, :] = rowsum(dq_ref[...].astype(F32))
        both = dtab_ref[...]
        tables = (both[0:64] + both[64:128]).astype(BF)
        extra_ref[:, 128:384] = mm(hot_ref[...], tables).astype(BF)

    def gather(own_ref, recv_ref):
        total = own_ref[...].astype(F32)
        for d in range(recv_ref.shape[0]):
            total = total + recv_ref[d].astype(F32)
        low_ref[...] = total.astype(BF)

    @pl.when(step == 1)
    def _():
        gather(dk_ref, rk_ref)

    @pl.when(step == 2)
    def _():
        gather(dv_ref, rv_ref)
        sums_ref[5:6, :] = rowsum(low_ref[...].astype(F32))

    dw_ref[step] = mm(nt_ref[...], low_ref[...]).astype(BF)
    w_copy(step).start()
    part = mt(low_ref[...], w_ref[...])

    @pl.when(step == 0)
    def _():
        dn_ref[...] = part

    @pl.when(step > 0)
    def _():
        dn_ref[...] += part

    @pl.when(step == 2)
    def _():
        zero = jnp.zeros((1, width), F32)
        sum_gain, sum_shift = zero, zero
        for at in range(0, tokens, 32):
            sl = slice(at, at + 32)
            hat, inverse = stats(x_ref[sl, :].astype(F32))
            grad = dn_ref[sl, :]
            sum_gain = sum_gain + rowsum(grad * hat)
            sum_shift = sum_shift + rowsum(grad)
            dx_ref[sl, :] = dx1_ref[sl, :] + norm_back(grad * p_ref[0:1, :], hat, inverse)
        sums_ref[0:1, :] = sum_gain
        sums_ref[2:3, :] = sum_shift
        padded = jnp.concatenate([sums_ref[...], jnp.zeros((120, width), F32)], axis=0)
        extra_ref[:, 0:128] = padded.T.astype(BF)
        extra_copy.start()
        for at in range(3):
            w_copy(at).wait()
        extra_copy.wait()


def qkv_back_call(tokens, dq, dk, dv, recv_k, recv_v, weight, dx1, p768, dtab, hot):
    rows, width = tokens.shape
    full = whole((rows, width))
    return call(
        qkv_back_kernel,
        [sds((width, 3 * width + 384), BF), sds((rows, width), F32)],
        grid=(3,),
        in_specs=[
            full,
            full,
            full,
            full,
            whole(recv_k.shape),
            whole(recv_v.shape),
            pl.BlockSpec((width, width), lambda s: (0, s)),
            full,
            whole(p768.shape),
            whole(dtab.shape),
            whole(hot.shape),
        ],
        out_specs=[pl.BlockSpec(memory_space=pl.ANY), full],
        scratch=[
            pltpu.VMEM((width, rows), BF),
            pltpu.VMEM((rows, width), BF),
            pltpu.VMEM((rows, width), F32),
            pltpu.VMEM((8, width), F32),
            pltpu.VMEM((3, width, width), BF),
            pltpu.VMEM((width, 384), BF),
            pltpu.SemaphoreType.DMA((4,)),
        ],
        flops=4e9,
        name="qkv_back",
    )(tokens, dq, dk, dv, recv_k, recv_v, weight, dx1, p768, dtab, hot)


def rim_exchange(levels, axis):
    peers = lax.axis_size(axis)
    chan = levels[0].shape[-1]
    counts = [level.shape[1] for level in levels]
    lasts = jnp.concatenate([level[-1] for level in levels], axis=0)
    firsts = jnp.concatenate([level[0] for level in levels], axis=0)
    if peers == 2:
        me = lax.axis_index(axis)
        got = lax.ppermute(jnp.where(me == 0, lasts, firsts), axis, [(0, 1), (1, 0)])
        nothing = jnp.zeros_like(got)
        before = jnp.where(me == 1, got, nothing)
        after = jnp.where(me == 0, got, nothing)
    else:
        before = lax.ppermute(lasts, axis, [(i, i + 1) for i in range(peers - 1)])
        after = lax.ppermute(firsts, axis, [(i + 1, i) for i in range(peers - 1)])
    both = jnp.stack([before, after])
    rims, at = [], 0
    for count in counts:
        rims.append(both[:, at : at + count])
        at += count
    return rims


def seq_total(part):
    peers = lax.axis_size("seq")
    if peers == 2:
        other = lax.ppermute(part, "seq", [(0, 1), (1, 0)])
        return part.astype(F32) + other.astype(F32)
    return lax.psum(part, "seq").astype(F32)


def per_device(
    tokens, valid_rows, valid_cols, block_gains, block_shifts, qkv_weight, qv_bias, table_rows, table_cols,
    proj_weight, proj_bias, fc1_weight, fc1_bias, fc2_weight, fc2_bias, fine_first, fine_first_bias,
    fine_norm_gain, fine_norm_shift, fine_second, fine_second_bias, middle_up, middle_up_bias, lateral_fine,
    lateral_middle, lateral_coarse, level_gains, level_shifts, output_convs, cotan_fine, cotan_middle,
    cotan_base, cotan_coarse,
):
    lr, cols, width = tokens.shape[1:]
    head = table_rows.shape[0]
    heads = width // head
    peers = lax.axis_size("seq")
    shards = lax.axis_size("img")
    me = lax.axis_index("seq")
    total_rows = lr * peers
    count = lr * cols
    chan = lateral_fine.shape[1]
    first_row = me * lr
    first = first_row.astype(jnp.int32).reshape(1)
    flat = tokens[0].reshape(count, width)

    far = [
        lax.ppermute(flat, "seq", [(i, (i + d) % peers) for i in range(peers)])
        for d in range(1, peers)
    ]
    far_tokens = jnp.concatenate(far, axis=0) if len(far) > 1 else (far[0] if far else None)

    p768 = jnp.stack(
        [
            block_gains[:, 0], block_gains[:, 1], block_shifts[:, 0], block_shifts[:, 1],
            qv_bias[:, 0], qv_bias[:, 1], proj_bias, fc2_bias,
        ]
    ).astype(F32)
    bias3 = jnp.stack([qv_bias[:, 0], jnp.zeros_like(proj_bias), qv_bias[:, 1]]).astype(F32)[:, None, :]
    b1 = fc1_bias.astype(F32)[None]
    p384 = jnp.stack([fine_first_bias, fine_norm_gain, fine_norm_shift, middle_up_bias]).astype(F32)
    fsb = fine_second_bias.astype(F32)[None]
    p256 = jnp.concatenate([level_gains.T, level_shifts.T]).astype(F32)
    conv_weights = output_convs.transpose(1, 0, 2).reshape(4, 3, 3 * chan, chan)
    lc0, lc1 = lateral_coarse[:, 0, :], lateral_coarse[:, 1, :]

    def turned(table):
        back = table[:, ::-1]
        back = jnp.pad(back, ((0, 0), (0, 128 - back.shape[1])))
        return jnp.concatenate([back, back], axis=0)

    tw, tr = turned(table_cols), turned(table_rows)

    low_at, aug = aug_layout(total_rows)
    ranks = jnp.stack([(me - d) % peers for d in range(peers)])
    key_rows = (ranks[:, None] * lr + jnp.arange(lr)[None, :])[:, :, None]
    key_rows = jnp.broadcast_to(key_rows, (peers, lr, cols)).reshape(-1, 1)
    key_cols = jnp.broadcast_to(jnp.arange(cols)[None, None, :], (peers, lr, cols)).reshape(-1, 1)
    lane = jnp.arange(128)[None, :]
    oh1 = (lane % 64 == key_cols).astype(BF)
    lane = jnp.arange(aug - 128)[None, :]
    hot = (lane < 64) & (lane == key_cols)
    hot = hot | ((lane >= 64) & (lane < 64 + total_rows) & (lane - 64 == key_rows))
    off = low_at
    hot = hot | ((lane >= off) & (lane < off + total_rows) & (lane - off == key_rows))
    bad = (key_rows >= valid_rows[0]) | (key_cols >= valid_cols[0])
    oh2 = jnp.where(bad & (lane == off + total_rows), NEG, hot.astype(F32)).astype(BF)

    qkv_own = qkv_call(flat, qkv_weight, bias3, p768, 0)
    kv_far = qkv_call(far_tokens, qkv_weight, bias3, p768, 1) if far else None
    attended, qaug, lse = attend_call(
        first, qkv_own, kv_far, (tw, tr), oh1, oh2, total_rows, heads
    )
    x1, hidden, slope, y = mlp_call(flat, attended, proj_weight, fc1_weight, b1, fc2_weight, p768)

    zf, zm, zb, zc = pyramid_call(
        y, lr, cols, fine_first, fine_second, middle_up, lateral_fine, lateral_middle, lc0, lc1, p384, fsb, p256
    )
    levels = [
        zf.reshape(4 * lr, 4 * cols, chan),
        zm.reshape(2 * lr, 2 * cols, chan),
        zb.reshape(lr, cols, chan),
        zc.reshape(lr // 2, cols // 2, chan),
    ]
    rims = rim_exchange(levels, "seq")
    cots = [c[0] for c in (cotan_fine, cotan_middle, cotan_base, cotan_coarse)]
    maps, drs, level_sums = [None] * 4, [None] * 4, [None] * 4
    packed = None
    for level in (3, 2, 1, 0):
        z = levels[level]
        block = min(z.shape[0], max(1, 2048 // z.shape[1]))
        maps[level], drs[level], packed, level_sums[level] = conv_call(
            level, z, rims[level], conv_weights, cots[level], p256, block, shards, packed
        )

    conv_low = lax.psum_scatter(packed, "img", scatter_dimension=0, tiled=True)
    drims = rim_exchange(drs, "seq")
    dzs = []
    for level, ways in enumerate((4, 2, 1, 1)):
        dr = drs[level]
        block = min(dr.shape[0], max(1, 2048 // dr.shape[1]))
        dzs.append(conv_back_call(level, dr, drims[level], conv_weights, ways, block))

    unit = width // shards
    packed_row = jnp.arange(width)[:, None]
    shard_at, within = packed_row // unit, packed_row % unit

    def placed(size):
        own = size // shards
        at = jnp.arange(size)[None, :]
        return ((within < own) & (at == shard_at * own + within)).astype(BF)

    quart, half = lateral_fine.shape[0], lateral_middle.shape[0]
    own_q, own_h = quart // shards, half // shards
    at = jnp.arange(quart + half)[None, :]
    source = jnp.where(
        within < own_q,
        shard_at * own_q + within,
        jnp.where(within < own_q + own_h, quart + shard_at * own_h + within - own_q, -1),
    )
    place = (at == source).astype(BF)
    hots = (placed(chan), placed(half), placed(quart))
    offset = 9 * half + 3 * chan
    lanes = offset + 9 * width + 128
    dy, wide, s384, s192, s256 = pyramid_back_call(
        y, lr, cols, fine_first, fine_second, middle_up, lateral_fine, lateral_middle, lc0, lc1, p384, fsb, p256,
        *dzs, place, lanes,
    )

    level_rows = jnp.concatenate(
        [level_sums[k][0:1] for k in range(4)] + [level_sums[k][1:2] for k in range(4)]
    )
    wide, dx1, dout = mlp_back_call(
        dy, hidden, slope, fc1_weight, fc2_weight, x1, attended, proj_weight, p768,
        s384, s192, s256, level_rows, hots, wide, offset, shards,
    )
    wide_low = lax.psum_scatter(wide, "img", scatter_dimension=0, tiled=True)
    back = attend_back_call(
        first, qkv_own, kv_far, qaug, dout, attended, lse,
        jnp.concatenate([tw, tr], axis=1), oh1, oh2, total_rows, heads,
    )
    dq, dtab = back[:2]
    if far:
        dk, dk_far, dv, dv_far = back[2:]

        def send(parts):
            return jnp.stack(
                [
                    lax.ppermute(
                        parts[(d - 1) * count : d * count],
                        "seq",
                        [(i, (i - d) % peers) for i in range(peers)],
                    )
                    for d in range(1, peers)
                ]
            )

        recv_k, recv_v = send(dk_far), send(dv_far)
    else:
        dk, dv = back[2:]
        recv_k = recv_v = jnp.zeros((1, count, width), BF)
    last, dx = qkv_back_call(
        flat, dq, dk, dv, recv_k, recv_v, qkv_weight, dx1, p768, dtab, placed(head)
    )
    last, wide_low = lax.optimization_barrier((last, wide_low))
    last_low = lax.psum_scatter(last, "img", scatter_dimension=0, tiled=True)
    conv_total = seq_total(conv_low)
    wide_total = seq_total(wide_low)
    last_total = seq_total(last_low)

    def taken(total, start, size):
        return total[:, start : start + size]

    g_ff = taken(wide_total, 0, 4 * half)
    g_mu = taken(wide_total, 4 * half, 4 * half)
    g_fs = taken(wide_total, 8 * half, half)
    g_lc = jnp.stack(
        [taken(wide_total, 9 * half, chan), taken(wide_total, 9 * half + chan, chan)], axis=1
    )
    laterals = taken(wide_total, 9 * half + 2 * chan, chan)
    g_lf, g_lm = laterals[:own_q], laterals[own_q : own_q + own_h]
    g_w1 = taken(wide_total, offset, 4 * width)
    g_w2 = (
        taken(wide_total, offset + 4 * width, 4 * width)
        .reshape(unit, 4, width).transpose(1, 0, 2).reshape(4 * unit, width)
    )
    g_wp = taken(wide_total, offset + 8 * width, width)
    vec = taken(wide_total, offset + 9 * width, 128)
    own_c = chan // shards
    g_lg = jnp.concatenate([vec[:own_c, 8:12], vec[:own_c, 24:28]], axis=1)
    g_ls = jnp.concatenate([vec[:own_c, 16:20], vec[:own_c, 28:32]], axis=1)
    g_ffb, g_fng, g_fns, g_mub = (vec[:own_h, 32 + k] for k in range(4))
    g_fsb = vec[:own_q, 48]
    g_b1 = vec[:, 40:44].T.reshape(-1)
    g_pb, g_b2 = vec[:, 6], vec[:, 7]
    g_qkv = last_total[:, : 3 * width]
    late = last_total[:, 3 * width : 3 * width + 128]
    g_bg = jnp.stack([late[:, 0], vec[:, 1]], axis=1)
    g_bs = jnp.stack([late[:, 2], vec[:, 3]], axis=1)
    g_qvb = late[:, 4:6]
    own_t = head // shards
    tabs = last_total[:own_t, 3 * width + 128 :]
    g_tc = tabs[:, : 2 * cols - 1][:, ::-1]
    g_tr = tabs[:, 128 : 128 + 2 * total_rows - 1][:, ::-1]
    g_conv = (
        conv_total.reshape(unit, 4, 3, chan).transpose(2, 0, 1, 3).reshape(3 * unit, 4, chan)
    )
    return (
        maps[0][None], maps[1][None], maps[2][None], maps[3][None],
        dx.reshape(1, lr, cols, width),
        g_bg, g_bs, g_qkv, g_qvb, g_tr, g_tc, g_wp, g_pb, g_w1, g_b1, g_w2, g_b2, g_ff, g_ffb, g_fng, g_fns,
        g_fs, g_fsb, g_mu, g_mub, g_lf, g_lm, g_lc, g_lg, g_ls, g_conv,
    )


def solution(mesh):
    image = P("img", "seq", None, None)
    in_specs = (image, P("img"), P("img")) + (P(),) * 26 + (image,) * 4
    ranks = (2, 2, 2, 2, 2, 2, 2, 1, 2, 1, 2, 1, 2, 1, 1, 1, 2, 1, 2, 1, 2, 2, 3, 2, 2, 3)
    out_specs = (image,) * 5 + tuple(P(*(("img",) + (None,) * (r - 1))) for r in ranks)
    return jax.shard_map(
        per_device, mesh=mesh, in_specs=in_specs, out_specs=out_specs, check_vma=False
    )
```

```python
import functools

import jax
import jax.numpy as jnp
from jax import lax
from jax.experimental import pallas as pl
from jax.experimental.pallas import tpu as pltpu
from jax.sharding import PartitionSpec as P

F32 = jnp.float32
BF = jnp.bfloat16
NEG = -1e30
EPS = 1e-6
SQRT_HALF = 0.7071067811865476
INV_SQRT_2PI = 0.3989422804014327
VMEM_LIMIT = 60 * 1024 * 1024


def mm(left, right):
    return lax.dot_general(left, right, (((1,), (0,)), ((), ())), preferred_element_type=F32)


def mt(left, right):
    return lax.dot_general(left, right, (((1,), (1,)), ((), ())), preferred_element_type=F32)


def tm(left, right):
    return lax.dot_general(left, right, (((0,), (0,)), ((), ())), preferred_element_type=F32)


def call(
    kernel, outs, grid=(), in_specs=None, out_specs=None, scratch=(), flops=0, name=None, aliases=None
):
    return pl.pallas_call(
        kernel,
        out_shape=outs,
        grid=grid,
        in_specs=in_specs,
        out_specs=out_specs,
        scratch_shapes=scratch,
        name=name,
        input_output_aliases=aliases or {},
        cost_estimate=pl.CostEstimate(flops=int(flops) // COST_SHARE, bytes_accessed=0, transcendentals=0),
        compiler_params=pltpu.CompilerParams(vmem_limit_bytes=VMEM_LIMIT),
    )


def whole(shape):
    return pl.BlockSpec(shape, lambda *_: (0,) * len(shape))


def sds(shape, dtype):
    return jax.ShapeDtypeStruct(shape, dtype)


def stats(values):
    average = jnp.mean(values, axis=-1, keepdims=True)
    centred = values - average
    spread = jnp.mean(centred * centred, axis=-1, keepdims=True)
    inverse = lax.rsqrt(spread + EPS)
    return centred * inverse, inverse


def norm_back(grad_hat, hat, inverse):
    first = jnp.mean(grad_hat, axis=-1, keepdims=True)
    second = jnp.mean(grad_hat * hat, axis=-1, keepdims=True)
    return inverse * (grad_hat - first - hat * second)


def rowsum(values):
    return jnp.sum(values, axis=0, keepdims=True)


UNROLL = 64
COST_SHARE = 100
CONV_PIXELS = 1024
MOVE_ROWS = 8
BACK_PIXELS = 2048


def by_chunks(total, size, body, carry=0, unroll=None):
    unroll = max(1, min(unroll or UNROLL, total // size))

    def step(k, inner):
        for u in range(unroll):
            out = body(pl.ds(pl.multiple_of((k * unroll + u) * size, size), size), inner)
            inner = inner if out is None else out
        return inner

    if unroll == total // size:
        return step(0, carry)
    return lax.fori_loop(0, total // size // unroll, step, carry)


def put_shards(source, keep_ref, send_ref, lanes, shards, first, core, sem):
    unit = source.shape[0] // shards
    for s in range(shards):
        at = first + s
        rows = pl.ds(pl.multiple_of(lax.div(at, 2) * unit, unit), unit)
        piece = source.at[pl.ds(s * unit, unit)]

        @pl.when(lax.rem(at, 2) == core)
        def _():
            pltpu.make_async_copy(piece, keep_ref.at[rows, lanes], sem).start()

        @pl.when(lax.rem(at, 2) != core)
        def _():
            pltpu.make_async_copy(piece, send_ref.at[rows, lanes], sem).start()


def wait_shards(source, sem):
    pltpu.make_async_copy(source, source, sem).wait()


def repeat(count, body):
    for k in range(count):
        body(k, 0)


def gelu_pair(values):
    half = 0.5 * (1.0 + lax.erf(values * SQRT_HALF))
    slope = half + values * (jnp.exp(-0.5 * values * values) * INV_SQRT_2PI)
    return values * half, slope


def shift_matrix(size, amount):
    out_at = lax.broadcasted_iota(jnp.int32, (size, size), 0)
    in_at = lax.broadcasted_iota(jnp.int32, (size, size), 1)
    return jnp.where(in_at == out_at + amount, 1.0, 0.0).astype(BF)


def weave_matrix(size, ways, inverse=False):
    out_at = lax.broadcasted_iota(jnp.int32, (size, size), 1 if inverse else 0)
    in_at = lax.broadcasted_iota(jnp.int32, (size, size), 0 if inverse else 1)
    source = lax.rem(out_at, ways) * (size // ways) + lax.div(out_at, ways)
    return jnp.where(in_at == source, 1.0, 0.0).astype(BF)


def qkv_kernel(x_ref, w_ref, b_ref, p_ref, out_ref, n1_ref):
    @pl.when(pl.program_id(1) == 0)
    def _():
        def norm(sl, carry):
            hat, _ = stats(x_ref[sl, :].astype(F32))
            n1_ref[sl, :] = (hat * p_ref[0:1, :] + p_ref[2:3, :]).astype(BF)

        by_chunks(x_ref.shape[0], 32, norm)

    out_ref[...] = (mm(n1_ref[...], w_ref[...]) + b_ref[0]).astype(BF)


def qkv_call(tokens, weight, bias3, p768, first):
    rows, width = tokens.shape
    block = 512
    count = 3 - first
    return call(
        qkv_kernel,
        sds((rows, count * width), BF),
        grid=(rows // block, count),
        in_specs=[
            pl.BlockSpec((block, width), lambda i, j: (i, 0)),
            pl.BlockSpec((width, width), lambda i, j: (0, j + first)),
            pl.BlockSpec((1, 1, width), lambda i, j: (j + first, 0, 0)),
            whole(p768.shape),
        ],
        out_specs=pl.BlockSpec((block, width), lambda i, j: (i, j)),
        scratch=[pltpu.VMEM((block, width), BF)],
        flops=2 * rows * width * width * count,
        name="qkv",
    )(tokens, weight, bias3, p768)


def aug_layout(total_rows):
    low_at = 64 + total_rows
    if low_at + total_rows + 1 > 128:
        low_at = 128
    width = 128 * (2 + (low_at + total_rows) // 128)
    return low_at, width


def build_kaug(kaug_ref, k_refs, oh1_ref, oh2_ref, odd):
    lane = lax.broadcasted_iota(jnp.int32, (512, 128), 1)
    mine = (lane >= 64) if odd else (lane < 64)
    at = 0
    for k_ref in k_refs:
        for row in range(0, k_ref.shape[0], 512):
            keys = k_ref[row : row + 512, :].astype(F32)
            hot = oh1_ref[at : at + 512, :].astype(F32)
            kaug_ref[at : at + 512, 0:128] = jnp.where(mine, keys, hot).astype(BF)
            at += 512


def build_qaug(first_row, qp, tw_ref, tr_ref, qaug_ref, odd, total_rows, scale):
    low_at, width = aug_layout(total_rows)
    tokens = qp.shape[0]
    lane = lax.broadcasted_iota(jnp.int32, (64, 128), 1)
    mine = (lane >= 64) if odd else (lane < 64)
    lane_all = lax.broadcasted_iota(jnp.int32, (tokens, 128), 1)
    mine_all = (lane_all >= 64) if odd else (lane_all < 64)
    qf = qp.astype(F32)
    qm = jnp.where(mine_all, qf, 0.0).astype(BF)
    cols = mm(qm, tw_ref[...])
    rows = mm(qm, tr_ref[...])
    for i in range(tokens // 64):
        sl = slice(64 * i, 64 * i + 64)
        upper = pltpu.roll(cols[sl], 1, 1, stride=1, stride_axis=0)
        lower = pltpu.roll(cols[sl], 65, 1, stride=1, stride_axis=0)
        first = jnp.where(mine, qf[sl] * scale, lower if odd else upper)
        col_low = lower - lower.astype(BF).astype(F32)
        shift = lax.rem(first_row + i + (65 - total_rows + 128), 128)
        row_part = pltpu.roll(rows[sl], shift, 1)
        row_low = row_part - row_part.astype(BF).astype(F32)
        qaug_ref[sl, 0:128] = first.astype(BF)
        one_at = low_at + total_rows
        if low_at < 128:
            rest = jnp.where(lane == one_at, 1.0, 0.0)
            rest = jnp.where(
                (lane >= low_at) & (lane < one_at), pltpu.roll(row_low, total_rows, 1), rest
            )
            second = jnp.where(lane < 64, col_low, jnp.where(lane < low_at, row_part, rest))
            qaug_ref[sl, 128:256] = second.astype(BF)
        else:
            second = jnp.where(
                lane < 64, col_low, jnp.where(lane < 64 + total_rows, row_part, 0.0)
            )
            third = jnp.where(
                lane < total_rows,
                pltpu.roll(row_low, 64, 1),
                jnp.where(lane == total_rows, 1.0, 0.0),
            )
            qaug_ref[sl, 128:256] = second.astype(BF)
            qaug_ref[sl, 256:384] = third.astype(BF)


def attend_kernel(total_rows, scale, others, *refs):
    first_ref, q_ref, tw_ref, tr_ref, oh1_ref, oh2_ref = refs[:6]
    k_refs = refs[6 : 6 + others]
    v_refs = refs[6 + others : 6 + 2 * others]
    o_ref, qaug_out, lse_ref, kaug_ref, v_ref, p_ref, ot_ref, scores_ref = refs[6 + 2 * others :]
    first_row = first_ref[0]
    tokens = q_ref.shape[0]
    keys = kaug_ref.shape[0]

    @pl.when(pl.program_id(0) == 0)
    def _():
        kaug_ref[:, 128:] = oh2_ref[...]

    at = 0
    for ref in v_refs:
        v_ref[at : at + ref.shape[0], :] = ref[...]
        at += ref.shape[0]
    qp = q_ref[...]
    for odd in (0, 1):
        build_kaug(kaug_ref, k_refs, oh1_ref, oh2_ref, odd)
        build_qaug(first_row, qp, tw_ref, tr_ref, qaug_out.at[odd], odd, total_rows, scale)

        def queries(t, carry):
            sl = pl.ds(pl.multiple_of(t * 256, 256), 256)
            scores_ref[...] = mt(kaug_ref[...], qaug_out[odd, sl, :])

            def highest(rows, top):
                return jnp.maximum(top, jnp.max(scores_ref[rows, :], axis=0, keepdims=True))

            top = by_chunks(keys, 128, highest, jnp.full((1, 256), NEG, F32))

            def weigh(rows, total):
                weight = jnp.exp(scores_ref[rows, :] - top)
                p_ref[rows, :] = weight.astype(BF)
                return total + rowsum(weight)

            total = by_chunks(keys, 128, weigh, jnp.zeros((1, 256), F32))
            lse_ref[0, odd : odd + 1, sl] = top + jnp.log(total)
            out_t = tm(v_ref[...], p_ref[...])
            ot_ref[64 * odd : 64 * odd + 64, sl] = out_t[64 * odd : 64 * odd + 64] / total
            return carry

        repeat(tokens // 256, queries)
    o_ref[...] = ot_ref[...].T.astype(BF)


def attend_call(first, qkv_own, kv_others, tables, oh1, oh2, total_rows, heads):
    tokens = qkv_own.shape[0]
    width = qkv_own.shape[1] // 3
    keys = oh1.shape[0]
    aug = 128 + oh2.shape[1]
    pairs = width // 128
    tw, tr = tables
    parts = 1 + (1 if kv_others is not None else 0)
    in_specs = [
        pl.BlockSpec(memory_space=pltpu.SMEM),
        pl.BlockSpec((tokens, 128), lambda h: (0, h)),
        whole(tw.shape),
        whole(tr.shape),
        whole(oh1.shape),
        whole(oh2.shape),
    ]
    k_args, v_args, k_specs, v_specs = [qkv_own], [qkv_own], [], []
    k_specs.append(pl.BlockSpec((tokens, 128), lambda h: (0, h + pairs)))
    v_specs.append(pl.BlockSpec((tokens, 128), lambda h: (0, h + 2 * pairs)))
    if kv_others is not None:
        k_args.append(kv_others)
        v_args.append(kv_others)
        k_specs.append(pl.BlockSpec((keys - tokens, 128), lambda h: (0, h)))
        v_specs.append(pl.BlockSpec((keys - tokens, 128), lambda h: (0, h + pairs)))
    scale = (width // heads) ** -0.5
    return call(
        functools.partial(attend_kernel, total_rows, scale, parts),
        [
            sds((tokens, width), BF),
            sds((heads, tokens, aug), BF),
            sds((pairs, 2, tokens), F32),
        ],
        grid=(pairs,),
        in_specs=in_specs + k_specs + v_specs,
        out_specs=[
            pl.BlockSpec((tokens, 128), lambda h: (0, h)),
            pl.BlockSpec((2, tokens, aug), lambda h: (h, 0, 0)),
            pl.BlockSpec((1, 2, tokens), lambda h: (h, 0, 0)),
        ],
        scratch=[
            pltpu.VMEM((keys, aug), BF),
            pltpu.VMEM((keys, 128), BF),
            pltpu.VMEM((keys, 256), BF),
            pltpu.VMEM((128, tokens), F32),
            pltpu.VMEM((keys, 256), F32),
        ],
        flops=25e9,
        name="attend",
    )(first, qkv_own, tw, tr, oh1, oh2, *k_args, *v_args)


def mlp_kernel(
    x_ref, o_ref, wp_ref, w1_ref, b1_ref, w2_ref, p_ref, x1_ref, g_ref, gp_ref, y_ref, n2_ref, acc_ref,
    hidden_ref,
):
    step = pl.program_id(0)
    tokens = x_ref.shape[0]

    @pl.when(step == 0)
    def _():
        product = mm(o_ref[...], wp_ref[...])
        acc_ref[...] = product

        def norm(sl, carry):
            middle = x_ref[sl, :].astype(F32) + (acc_ref[sl, :] + p_ref[6:7, :])
            x1_ref[sl, :] = middle
            acc_ref[sl, :] = jnp.zeros_like(middle)
            hat, _ = stats(middle)
            n2_ref[sl, :] = (hat * p_ref[1:2, :] + p_ref[3:4, :]).astype(BF)

        by_chunks(tokens, 32, norm)

    hidden_ref[...] = mm(n2_ref[...], w1_ref[...])

    def act(sl, carry):
        value, slope = gelu_pair(hidden_ref[sl, :] + b1_ref[...])
        g_ref[sl, :] = value.astype(BF)
        gp_ref[sl, :] = slope.astype(BF)

    by_chunks(tokens, 32, act)
    acc_ref[...] += mm(g_ref[...], w2_ref[...])

    @pl.when(step == pl.num_programs(0) - 1)
    def _():
        y_ref[...] = (x1_ref[...] + (acc_ref[...] + p_ref[7:8, :])).astype(BF)


def mlp_call(tokens, attended, wp, w1, b1, w2, p768):
    rows, width = tokens.shape
    hidden = w1.shape[1]
    return call(
        mlp_kernel,
        [sds((rows, width), F32), sds((rows, hidden), BF), sds((rows, hidden), BF), sds((rows, width), BF)],
        grid=(hidden // width,),
        in_specs=[
            whole((rows, width)),
            whole((rows, width)),
            whole(wp.shape),
            pl.BlockSpec((width, width), lambda s: (0, s)),
            pl.BlockSpec((1, width), lambda s: (0, s)),
            pl.BlockSpec((width, width), lambda s: (s, 0)),
            whole(p768.shape),
        ],
        out_specs=[
            whole((rows, width)),
            pl.BlockSpec((rows, width), lambda s: (0, s)),
            pl.BlockSpec((rows, width), lambda s: (0, s)),
            whole((rows, width)),
        ],
        scratch=[
            pltpu.VMEM((rows, width), BF),
            pltpu.VMEM((rows, width), F32),
            pltpu.VMEM((rows, width), F32),
        ],
        flops=14e9,
        name="mlp",
    )(tokens, attended, wp, w1, b1, w2, p768)


def pool_matrix(a, b, rows, cols):
    count = rows * cols // 4
    out_at = lax.broadcasted_iota(jnp.int32, (count, rows * cols), 0)
    in_at = lax.broadcasted_iota(jnp.int32, (count, rows * cols), 1)
    half = cols // 2
    source = (2 * lax.div(out_at, half) + a) * cols + 2 * lax.rem(out_at, half) + b
    return jnp.where(in_at == source, 1.0, 0.0).astype(BF)


def lateral_norm(product_ref, count, gain, shift, write):
    def norm(sl, carry):
        hat, _ = stats(product_ref[sl, :])
        write(sl, (hat * gain + shift).astype(BF))

    by_chunks(count, 64, norm)


def pyramid_kernel(
    lr, cols, y_ref, ff_ref, fs_ref, mu_ref, lf_ref, lm_ref, lc0_ref, lc1_ref, p384_ref, fsb_ref, p256_ref,
    zf_ref, zm_ref, zb_ref, zc_ref, plane_ref, mplane_ref, f2_ref, first_ref, product_ref,
    third_ref, stack_ref,
):
    tokens = lr * cols
    half = mu_ref.shape[1] // 2
    quart = fs_ref.shape[0] // 4

    def offset(b, carry):
        columns = pl.ds(pl.multiple_of(b * half, half), half)
        first_ref[...] = mm(y_ref[...], ff_ref[:, columns])

        def norm(sl, inner):
            hat, _ = stats(first_ref[sl, :] + p384_ref[0:1, :])
            value = hat * p384_ref[1:2, :] + p384_ref[2:3, :]
            f2_ref[sl, :] = (0.5 * value * (1.0 + lax.erf(value * SQRT_HALF))).astype(BF)

        by_chunks(tokens, 64, norm)

        for k in range(4):
            third_ref[k * tokens : (k + 1) * tokens, :] = (
                mt(f2_ref[...], fs_ref[k * quart : (k + 1) * quart, :]) + fsb_ref[...]
            ).astype(BF)
        stack_ref[...] = mm(third_ref[...], lf_ref[...])
        for k in range(4):

            def write(sl, values):
                plane_ref[k // 2, 2 * b + k % 2, sl, :] = values

            part = stack_ref.at[k * tokens : (k + 1) * tokens]
            lateral_norm(part, tokens, p256_ref[0:1, :], p256_ref[8:9, :], write)
        middle = (mm(y_ref[...], mu_ref[:, columns]) + p384_ref[3:4, :]).astype(BF)
        product_ref[...] = mm(middle, lm_ref[...])

        def write_middle(sl, values):
            mplane_ref[b, sl, :] = values

        lateral_norm(product_ref, tokens, p256_ref[1:2, :], p256_ref[9:10, :], write_middle)
        return carry

    repeat(2, offset)
    weave4 = weave_matrix(4 * cols, 4)
    weave2 = weave_matrix(2 * cols, 2)

    def weave(i, carry):
        sl = pl.ds(pl.multiple_of(i * cols, cols), cols)
        for c in (0, 1):
            planes = jnp.concatenate([plane_ref[c, k, sl, :] for k in range(4)], axis=0)
            zf_ref[i, c] = mm(weave4, planes).astype(BF)
        planes = jnp.concatenate([mplane_ref[k, sl, :] for k in range(2)], axis=0)
        zm_ref[i, 0] = mm(weave2, planes).astype(BF)
        return carry

    repeat(lr, weave)

    @pl.when(pl.program_id(0) == 0)
    def _():
        product_ref[...] = mm(y_ref[...], lc0_ref[...])

        def write_base(sl, values):
            zb_ref[sl, :] = values

        lateral_norm(product_ref, tokens, p256_ref[2:3, :], p256_ref[10:11, :], write_base)
        pooled = pool_picks(y_ref, pick_ref=None, rows=lr, cols=cols)
        product_ref[0 : tokens // 4, :] = mm(pooled.astype(BF), lc1_ref[...])

        def write_coarse(sl, values):
            zc_ref[sl, :] = values

        lateral_norm(product_ref, tokens // 4, p256_ref[3:4, :], p256_ref[11:12, :], write_coarse)


def pool_picks(y_ref, pick_ref, rows, cols):
    def pick(k, top):
        values = mm(pool_matrix(k // 2, k % 2, rows, cols), y_ref[...])
        if pick_ref is not None:
            pick_ref[k] = values
        return jnp.maximum(top, values)

    low = jnp.full((rows * cols // 4, y_ref.shape[1]), -jnp.inf, F32)
    for k in range(4):
        low = pick(k, low)
    return low


def pyramid_call(y, lr, cols, ff, fs, mu, lf, lm, lc0, lc1, p384, fsb, p256):
    tokens, width = y.shape
    outs = lf.shape[1]
    half2 = ff.shape[1] // 2
    return call(
        functools.partial(pyramid_kernel, lr, cols),
        [
            sds((lr, 4, 4 * cols, outs), BF),
            sds((lr, 2, 2 * cols, outs), BF),
            sds((tokens, outs), BF),
            sds((tokens // 4, outs), BF),
        ],
        grid=(2,),
        in_specs=[
            whole(y.shape),
            pl.BlockSpec((width, half2), lambda a: (0, a)),
            whole(fs.shape),
            pl.BlockSpec((width, half2), lambda a: (0, a)),
            whole(lf.shape),
            whole(lm.shape),
            whole(lc0.shape),
            whole(lc1.shape),
            whole(p384.shape),
            whole(fsb.shape),
            whole(p256.shape),
        ],
        out_specs=[
            pl.BlockSpec((lr, 2, 4 * cols, outs), lambda a: (0, a, 0, 0)),
            pl.BlockSpec((lr, 1, 2 * cols, outs), lambda a: (0, a, 0, 0)),
            whole((tokens, outs)),
            whole((tokens // 4, outs)),
        ],
        scratch=[
            pltpu.VMEM((2, 4, tokens, outs), BF),
            pltpu.VMEM((2, tokens, outs), BF),
            pltpu.VMEM((tokens, half2 // 2), BF),
            pltpu.VMEM((tokens, half2 // 2), F32),
            pltpu.VMEM((tokens, outs), F32),
            pltpu.VMEM((4 * tokens, fs.shape[0] // 4), BF),
            pltpu.VMEM((4 * tokens, outs), F32),
        ],
        flops=20e9,
        name="pyramid",
    )(y, ff, fs, mu, lf, lm, lc0, lc1, p384, fsb, p256)


def fill_padded(step, block, src_ref, rim_ref, pad_ref, left, right):
    rows, cols, chan = src_ref.shape

    @pl.when(step == 0)
    def _():
        pad_ref[0, :, chan : 2 * chan] = rim_ref[0]
        pad_ref[rows + 1, :, chan : 2 * chan] = rim_ref[1]

        def copy(row, carry):
            pad_ref[row + 1, :, chan : 2 * chan] = src_ref[row]
            return carry

        lax.fori_loop(0, rows, copy, 0)

    def move(at):
        row = pad_ref[at, :, chan : 2 * chan]
        pad_ref[at, :, 0:chan] = mm(left, row).astype(BF)
        pad_ref[at, :, 2 * chan :] = mm(right, row).astype(BF)

    start = step * block
    group = min(block, MOVE_ROWS)

    @pl.when(step == 0)
    def _():
        move(0)
        move(1)

    def move_group(k, carry):
        for q in range(group):
            move(start + 2 + k * group + q)
        return carry

    lax.fori_loop(0, block // group, move_group, 0)


def conv_kernel(level, block, z_ref, rim_ref, w_ref, cot_ref, p_ref, *refs):
    map_ref, dr_ref, dw_ref, sums_ref, pad_ref, dwt_ref, gradt_ref = refs[-7:]
    step = pl.program_id(0)
    rows, cols, chan = z_ref.shape
    fill_padded(
        step, block, z_ref, rim_ref, pad_ref, shift_matrix(cols, -1), shift_matrix(cols, 1)
    )
    gain = p_ref[4 + level : 5 + level, :]
    shift = p_ref[12 + level : 13 + level, :]
    few = min(block, max(1, (CONV_PIXELS if rows * cols > 4096 else CONV_PIXELS // 2) // cols))
    pixels = few * cols

    @pl.when(step == 0)
    def _():
        sums_ref[...] = jnp.zeros_like(sums_ref)
        dwt_ref[...] = jnp.zeros_like(dwt_ref)

    def forward(k, carry):
        sum_gain, sum_shift = carry
        row = step * block + k * few
        result = None
        for a in range(3):
            part = mm(pad_ref[pl.ds(row + a, few)].reshape(pixels, 3 * chan), w_ref[0, a])
            result = part if result is None else result + part
        base = pl.multiple_of(k * pixels, pixels)
        for q in range(0, pixels, 64):
            sl = pl.ds(base + q, 64)
            hat, inverse = stats(result[q : q + 64])
            map_ref[sl, :] = (hat * gain + shift).astype(BF)
            cot = cot_ref[sl, :].astype(F32)
            sum_gain = sum_gain + rowsum(cot * hat)
            sum_shift = sum_shift + rowsum(cot)
            dr_ref[sl, :] = norm_back(cot * gain, hat, inverse).astype(BF)
        gradt_ref[:, pl.ds(base, pixels)] = dr_ref[pl.ds(base, pixels), :].T
        return sum_gain, sum_shift

    zero = jnp.zeros((1, chan), F32)
    sum_gain, sum_shift = lax.fori_loop(0, block // few, forward, (zero, zero))
    sums_ref[0:1, :] += sum_gain
    sums_ref[1:2, :] += sum_shift

    def add_grad(k, carry):
        a, b = lax.div(k, 3), lax.rem(k, 3)
        lanes = pl.ds(pl.multiple_of(b * chan, chan), chan)
        window = pad_ref[pl.ds(step * block + a, block), :, lanes].reshape(block * cols, chan)
        dwt_ref[k] += mm(gradt_ref[...], window)
        return carry

    lax.fori_loop(0, 9, add_grad, 0)

    @pl.when(step == pl.num_programs(0) - 1)
    def _():
        def turn(k, carry):
            dw_ref[pl.ds(pl.multiple_of(k * chan, chan), chan), :] = dwt_ref[k].T.astype(BF)
            return carry

        lax.fori_loop(0, 9, turn, 0)


def conv_call(level, z, rims, weights, cot, p256, block, packed):
    rows, cols, chan = z.shape
    before = [] if packed is None else [packed]
    spec = pl.BlockSpec((block * cols, chan), lambda s: (s, 0))
    return call(
        functools.partial(conv_kernel, level, block),
        [
            sds((rows * cols, chan), BF),
            sds((rows * cols, chan), BF),
            sds((9 * chan, 4 * chan), BF),
            sds((8, chan), F32),
        ],
        grid=(rows // block,),
        in_specs=[
            whole(z.shape),
            whole(rims.shape),
            pl.BlockSpec((1, 3, 3 * chan, chan), lambda s: (level, 0, 0, 0)),
            spec,
            whole(p256.shape),
        ]
        + [pl.BlockSpec(memory_space=pl.ANY)] * len(before),
        out_specs=[
            spec,
            spec,
            pl.BlockSpec((9 * chan, chan), lambda s: (0, level)),
            whole((8, chan)),
        ],
        scratch=[
            pltpu.VMEM((rows + 2, cols, 3 * chan), BF),
            pltpu.VMEM((9, chan, chan), F32),
            pltpu.VMEM((chan, block * cols), BF),
        ],
        flops=5 * 9 * rows * cols * chan * chan,
        name=f"conv{level}",
        aliases={5: 2} if before else {},
    )(z, rims, weights, cot.reshape(rows * cols, chan), p256, *before)


def conv_back_kernel(ways, block, dr_ref, rim_ref, w_ref, dz_ref, pad_ref):
    step = pl.program_id(0)
    rows, cols, chan = dr_ref.shape
    fill_padded(
        step, block, dr_ref, rim_ref, pad_ref, shift_matrix(cols, 1), shift_matrix(cols, -1)
    )
    few = min(block, max(1, BACK_PIXELS // cols))
    pixels = few * cols
    base = cols // ways
    unweave = weave_matrix(cols, ways, inverse=True)

    def back(k, carry):
        row = step * block + k * few
        result = None
        for a in range(3):
            for b in range(3):
                window = pad_ref[pl.ds(row + 2 - a, few), :, b * chan : (b + 1) * chan]
                part = mt(
                    window.reshape(pixels, chan), w_ref[0, a, b * chan : (b + 1) * chan, :]
                )
                result = part if result is None else result + part
        low = result.astype(BF)
        if ways == 1:
            dz_ref[pl.ds(pl.multiple_of(k * pixels, pixels), pixels), :] = low
            return carry
        for q in range(few):
            planes = mm(unweave, low[q * cols : (q + 1) * cols]).astype(BF)
            inner = k * few + q
            at = pl.ds(pl.multiple_of(lax.div(inner, ways) * base, base), base)
            for w in range(ways):
                dz_ref[lax.rem(inner, ways), w, at, :] = planes[w * base : (w + 1) * base]
        return carry

    lax.fori_loop(0, block // few, back, 0)


def conv_back_call(level, dr, rims, weights, ways, block):
    rows, cols, chan = dr.shape
    if ways == 1:
        out = sds((rows * cols, chan), BF)
        spec = pl.BlockSpec((block * cols, chan), lambda s: (s, 0))
    else:
        tokens = rows * cols // (ways * ways)
        out = sds((ways, ways, tokens, chan), BF)
        spec = pl.BlockSpec(
            (ways, ways, block * cols // (ways * ways), chan), lambda s: (0, 0, s, 0)
        )
    return call(
        functools.partial(conv_back_kernel, ways, block),
        out,
        grid=(rows // block,),
        in_specs=[
            whole(dr.shape),
            whole(rims.shape),
            pl.BlockSpec((1, 3, 3 * chan, chan), lambda s: (level, 0, 0, 0)),
        ],
        out_specs=spec,
        scratch=[pltpu.VMEM((rows + 2, cols, 3 * chan), BF)],
        flops=3 * 9 * rows * cols * chan * chan,
        name=f"conv_back{level}",
    )(dr, rims, weights)


def lateral_back(product_ref, count, read, gain, dl_ref):
    zero = jnp.zeros((1, product_ref.shape[1]), F32)

    def chunk(sl, carry):
        hat, inverse = stats(product_ref[sl, :])
        grad = read(sl)
        dl_ref[sl, :] = norm_back(grad * gain, hat, inverse).astype(BF)
        return carry[0] + rowsum(grad * hat), carry[1] + rowsum(grad)

    return by_chunks(count, 64, chunk, (zero, zero))


def pyramid_back_kernel(
    lr, cols, shards, core_ref, y_ref, ff_ref, fs_ref, mu_ref, lf_ref, lm_ref, lc0_ref, lc1_ref, p384_ref,
    fsb_ref, p256_ref, dzf_ref, dzm_ref, dzb_ref, dzc_ref, place_ref,
    dy_ref, keep_ref, send_ref, s384_ref, s192_ref, s256_ref,
    yt_ref, hat_ref, slope_ref, inv_ref, f2_ref, df2_ref, df1_ref, dl_ref, fs_acc, lf_acc, lm_acc,
    dcol_ref, drest_ref, product_ref, pick_ref, third_ref, stack_ref, dls_ref, sem,
):
    step = pl.program_id(0)
    tokens = lr * cols
    quart = fs_ref.shape[0] // 4
    half = ff_ref.shape[1]
    chan = lf_ref.shape[1]

    core = core_ref[0]
    rest = drest_ref.shape[1]

    @pl.when(step == 0)
    def _():
        yt_ref[...] = y_ref[...].T
        for ref in (fs_acc, lf_acc, lm_acc, s384_ref, s192_ref, s256_ref):
            ref[...] = jnp.zeros_like(ref)
        product_ref[...] = mm(y_ref[...], lc0_ref[...])
        sg, ss = lateral_back(
            product_ref, tokens, lambda sl: dzb_ref[sl, :].astype(F32), p256_ref[2:3, :], dl_ref
        )
        s256_ref[2:3, :] = sg
        s256_ref[10:11, :] = ss
        drest_ref[:, half : half + chan] = mm(yt_ref[...], dl_ref[...]).astype(BF)
        dy_ref[...] = mt(dl_ref[...], lc0_ref[...])
        top = pool_picks(y_ref, pick_ref, lr, cols)
        low = top.astype(BF)
        product_ref[0 : tokens // 4, :] = mm(low, lc1_ref[...])
        sg, ss = lateral_back(
            product_ref, tokens // 4, lambda sl: dzc_ref[sl, :].astype(F32), p256_ref[3:4, :], dl_ref
        )
        s256_ref[3:4, :] = sg
        s256_ref[11:12, :] = ss
        grad = dl_ref[0 : tokens // 4, :]
        drest_ref[:, half + chan : half + 2 * chan] = tm(low, grad).astype(BF)
        dtop = mt(grad, lc1_ref[...])
        hits = jnp.zeros_like(top)
        for k in range(4):
            hits = hits + jnp.where(pick_ref[k] == top, 1.0, 0.0)
        dtop = dtop / hits

        def share_out(k, carry):
            share = jnp.where(pick_ref[k] == top, dtop, 0.0)
            upper = share.astype(BF)
            lower = (share - upper.astype(F32)).astype(BF)
            spread = pool_matrix(k // 2, k % 2, lr, cols)
            dy_ref[...] += tm(spread, upper) + tm(spread, lower)
            return carry

        repeat(4, share_out)

    df2_ref[...] = mm(y_ref[...], ff_ref[...])

    def norm(sl, carry):
        hat, inverse = stats(df2_ref[sl, :] + p384_ref[0:1, :])
        hat_ref[sl, :] = hat
        inv_ref[sl, :] = jnp.broadcast_to(inverse, (64, 128))
        value, slope = gelu_pair(hat * p384_ref[1:2, :] + p384_ref[2:3, :])
        f2_ref[sl, :] = value.astype(BF)
        slope_ref[sl, :] = slope
        df2_ref[sl, :] = jnp.zeros_like(hat)

    by_chunks(tokens, 64, norm)

    for k in range(4):
        third_ref[k * tokens : (k + 1) * tokens, :] = (
            mt(f2_ref[...], fs_ref[k * quart : (k + 1) * quart, :]) + fsb_ref[...]
        ).astype(BF)
    stack_ref[...] = mm(third_ref[...], lf_ref[...])
    for k in range(4):
        sg, ss = lateral_back(
            stack_ref.at[k * tokens : (k + 1) * tokens],
            tokens,
            lambda sl: dzf_ref[0, k // 2, 0, k % 2, sl, :].astype(F32),
            p256_ref[0:1, :],
            dls_ref.at[k * tokens : (k + 1) * tokens],
        )
        s256_ref[0:1, :] += sg
        s256_ref[8:9, :] += ss
    lf_acc[...] += tm(third_ref[...], dls_ref[...])
    third_ref[...] = mt(dls_ref[...], lf_ref[...]).astype(BF)
    s192_ref[0:1, :] += rowsum(third_ref[...].astype(F32))
    for k in range(4):
        rows = slice(k * quart, (k + 1) * quart)
        fs_acc[rows, :] += tm(third_ref[k * tokens : (k + 1) * tokens, :], f2_ref[...])
        df2_ref[...] += mm(third_ref[k * tokens : (k + 1) * tokens, :], fs_ref[rows, :])
    zero = jnp.zeros((1, half), F32)

    def first_back(sl, carry):
        sum_gain, sum_shift, sum_bias = carry
        hat = hat_ref[sl, :]
        grad = df2_ref[sl, :] * slope_ref[sl, :]
        low = norm_back(grad * p384_ref[1:2, :], hat, inv_ref[sl, 0:1]).astype(BF)
        df1_ref[sl, :] = low
        return (
            sum_gain + rowsum(grad * hat),
            sum_shift + rowsum(grad),
            sum_bias + rowsum(low.astype(F32)),
        )

    sum_gain, sum_shift, sum_bias = by_chunks(tokens, 64, first_back, (zero, zero, zero))
    s384_ref[0:1, :] += sum_bias
    s384_ref[1:2, :] += sum_gain
    s384_ref[2:3, :] += sum_shift
    dcol_ref[step, :, 0:half] = mm(yt_ref[...], df1_ref[...]).astype(BF)
    dy_ref[...] += mt(df1_ref[...], ff_ref[...])

    f2_ref[...] = (mm(y_ref[...], mu_ref[...]) + p384_ref[3:4, :]).astype(BF)
    product_ref[...] = mm(f2_ref[...], lm_ref[...])
    sg, ss = lateral_back(
        product_ref, tokens, lambda sl: dzm_ref[0, 0, sl, :].astype(F32), p256_ref[1:2, :], dl_ref
    )
    s256_ref[1:2, :] += sg
    s256_ref[9:10, :] += ss
    lm_acc[...] += tm(f2_ref[...], dl_ref[...])
    df1_ref[...] = mt(dl_ref[...], lm_ref[...]).astype(BF)
    s384_ref[3:4, :] += rowsum(df1_ref[...].astype(F32))
    dcol_ref[step, :, half:] = mm(yt_ref[...], df1_ref[...]).astype(BF)
    lanes = pl.ds(pl.multiple_of(step * 2 * half, 2 * half), 2 * half)
    put_shards(dcol_ref.at[step], keep_ref, send_ref, lanes, shards, 0, core, sem.at[step])
    dy_ref[...] += mt(df1_ref[...], mu_ref[...])

    @pl.when(step == pl.num_programs(0) - 1)
    def _():
        drest_ref[:, 0:half] = fs_acc[...].astype(BF)
        laterals = jnp.concatenate([lf_acc[...], lm_acc[...]], axis=0).astype(BF)
        drest_ref[:, half + 2 * chan : half + 3 * chan] = mm(place_ref[...], laterals).astype(BF)
        put_shards(
            drest_ref, keep_ref, send_ref, pl.ds(8 * half, rest), shards, 0, core, sem.at[4]
        )
        for at in range(4):
            wait_shards(dcol_ref.at[at], sem.at[at])
        wait_shards(drest_ref, sem.at[4])


def pyramid_back_call(
    y, lr, cols, ff, fs, mu, lf, lm, lc0, lc1, p384, fsb, p256, dzf, dzm, dzb, dzc, place, core, shards
):
    tokens, width = y.shape
    half = fs.shape[1]
    quart = fsb.shape[1]
    outs = lf.shape[1]
    col_block = pl.BlockSpec((width, half), lambda s: (0, s))
    return call(
        functools.partial(pyramid_back_kernel, lr, cols, shards),
        [
            sds((tokens, width), F32),
            sds((width // 2, 9 * half + 3 * outs), BF),
            sds((width // 2, 9 * half + 3 * outs), BF),
            sds((8, half), F32),
            sds((8, quart), F32),
            sds((16, outs), F32),
        ],
        grid=(4,),
        in_specs=[
            pl.BlockSpec(memory_space=pltpu.SMEM),
            whole(y.shape),
            col_block,
            whole(fs.shape),
            col_block,
            whole(lf.shape),
            whole(lm.shape),
            whole(lc0.shape),
            whole(lc1.shape),
            whole(p384.shape),
            whole(fsb.shape),
            whole(p256.shape),
            pl.BlockSpec((1, 2, 1, 2, tokens, outs), lambda s: (s // 2, 0, s % 2, 0, 0, 0)),
            pl.BlockSpec((1, 1, tokens, outs), lambda s: (s // 2, s % 2, 0, 0)),
            whole(dzb.shape),
            whole(dzc.shape),
            whole(place.shape),
        ],
        out_specs=[
            whole((tokens, width)),
            pl.BlockSpec(memory_space=pl.ANY),
            pl.BlockSpec(memory_space=pl.ANY),
            whole((8, half)),
            whole((8, quart)),
            whole((16, outs)),
        ],
        scratch=[
            pltpu.VMEM((width, tokens), BF),
            pltpu.VMEM((tokens, half), F32),
            pltpu.VMEM((tokens, half), F32),
            pltpu.VMEM((tokens, 128), F32),
            pltpu.VMEM((tokens, half), BF),
            pltpu.VMEM((tokens, half), F32),
            pltpu.VMEM((tokens, half), BF),
            pltpu.VMEM((tokens, outs), BF),
            pltpu.VMEM(fs.shape, F32),
            pltpu.VMEM(lf.shape, F32),
            pltpu.VMEM(lm.shape, F32),
            pltpu.VMEM((4, width, 2 * half), BF),
            pltpu.VMEM((width, half + 3 * outs), BF),
            pltpu.VMEM((tokens, outs), F32),
            pltpu.VMEM((4, tokens // 4, width), F32),
            pltpu.VMEM((4 * tokens, quart), BF),
            pltpu.VMEM((4 * tokens, outs), F32),
            pltpu.VMEM((4 * tokens, outs), BF),
            pltpu.SemaphoreType.DMA((5,)),
        ],
        flops=45e9,
        name="pyramid_back",
    )(
        core, y, ff, fs, mu, lf, lm, lc0, lc1, p384, fsb, p256,
        dzf.reshape(2, 2, 2, 2, tokens, outs), dzm, dzb, dzc, place,
    )


def mlp_back_kernel(
    shards,
    core_ref, dy_ref, g_ref, gp_ref, w1_ref, w2_ref, x1_ref, o_ref, wp_ref, p_ref, s384_ref, s192_ref, s256_ref, levels_ref,
    hot256_ref, hot384_ref, hot192_ref,
    keep_ref, send_ref, keep2_ref, send2_ref, dx1_ref, do_ref,
    n2t_ref, d2_ref, dn2_ref, low_ref, sums_ref, vec_ref, dw1_ref, dw2_ref, rest_ref, temp_ref, sem,
):
    step = pl.program_id(0)
    steps = pl.num_programs(0)
    tokens, width = dy_ref.shape
    unit = width // shards
    hidden = 4 * width

    core = core_ref[0]

    @pl.when(step == 0)
    def _():
        sums_ref[...] = jnp.zeros_like(sums_ref)
        vec_ref[...] = jnp.zeros_like(vec_ref)
        dn2_ref[...] = jnp.zeros_like(dn2_ref)

        def norm(sl, total):
            hat, _ = stats(x1_ref[sl, :])
            low_ref[sl, :] = (hat * p_ref[1:2, :] + p_ref[3:4, :]).astype(BF)
            low = dy_ref[sl, :].astype(BF)
            d2_ref[sl, :] = low
            return total + rowsum(low.astype(F32))

        sums_ref[7:8, :] = by_chunks(tokens, 32, norm, jnp.zeros((1, width), F32))
        n2t_ref[...] = low_ref[...].T

    dw2_ref[step] = tm(g_ref[...], d2_ref[...]).astype(BF)
    put_shards(
        dw2_ref.at[step], keep2_ref, send2_ref, pl.ds(0, width), shards // 4, step * (shards // 4), core,
        sem.at[5 + step],
    )
    temp_ref[...] = mt(d2_ref[...], w2_ref[...])

    def act(sl, carry):
        low_ref[sl, :] = (temp_ref[sl, :] * gp_ref[sl, :].astype(F32)).astype(BF)

    by_chunks(tokens, 32, act)
    db1 = tm(low_ref[...], jnp.ones((tokens, 128), BF))
    lane = lax.broadcasted_iota(jnp.int32, (unit, 128), 1)
    for q in range(shards // 4):
        entry = jnp.zeros((unit, 128), F32)
        for k in range(4):
            sl = slice((4 * q + k) * unit, (4 * q + k + 1) * unit)
            entry = jnp.where(lane == 40 + k, db1[sl], entry)
        vec_ref[pl.ds(pl.multiple_of(step * (width // 4) + q * unit, 8), unit), :] += entry
    dw1_ref[step] = mm(n2t_ref[...], low_ref[...]).astype(BF)
    lanes = pl.ds(pl.multiple_of(step * width, width), width)
    put_shards(dw1_ref.at[step], keep_ref, send_ref, lanes, shards, 0, core, sem.at[step])
    dn2_ref[...] += mt(low_ref[...], w1_ref[...])

    @pl.when(step == steps - 1)
    def _():
        zero = jnp.zeros((1, width), F32)

        def back(sl, carry):
            hat, inverse = stats(x1_ref[sl, :])
            grad = dn2_ref[sl, :]
            dx1 = dy_ref[sl, :] + norm_back(grad * p_ref[1:2, :], hat, inverse)
            dx1_ref[sl, :] = dx1
            low = dx1.astype(BF)
            d2_ref[sl, :] = low
            return (
                carry[0] + rowsum(grad * hat),
                carry[1] + rowsum(grad),
                carry[2] + rowsum(low.astype(F32)),
            )

        sum_gain, sum_shift, sum_bias = by_chunks(tokens, 32, back, (zero, zero, zero))
        sums_ref[1:2, :] = sum_gain
        sums_ref[3:4, :] = sum_shift
        sums_ref[6:7, :] = sum_bias
        rest_ref[:, 0:width] = tm(o_ref[...], d2_ref[...]).astype(BF)
        do_ref[...] = mt(d2_ref[...], wp_ref[...]).astype(BF)

        def lanes_of(rows, before):
            after = 128 - before - rows.shape[0]
            parts = [jnp.zeros((before, rows.shape[1]), F32)] if before else []
            parts += [rows, jnp.zeros((after, rows.shape[1]), F32)]
            return jnp.concatenate(parts, axis=0)

        spread = mt(hot256_ref[...], lanes_of(s256_ref[...], 8).astype(BF))
        spread = spread + mt(hot256_ref[...], lanes_of(levels_ref[...], 24).astype(BF))
        spread = spread + mt(hot384_ref[...], lanes_of(s384_ref[...], 32).astype(BF))
        spread = spread + mt(hot192_ref[...], lanes_of(s192_ref[...], 48).astype(BF))
        spread = spread + lanes_of(sums_ref[...], 0).T
        rest_ref[:, width:] = (vec_ref[...] + spread).astype(BF)
        put_shards(
            rest_ref, keep_ref, send_ref, pl.ds(hidden, width + 128), shards, 0, core, sem.at[4]
        )
        for at in range(4):
            wait_shards(dw1_ref.at[at], sem.at[at])
            wait_shards(dw2_ref.at[at], sem.at[5 + at])
        wait_shards(rest_ref, sem.at[4])


def mlp_back_call(
    dy, g, gp, w1, w2, x1, attended, wp, p768, s384, s192, s256, levels, hots, core, shards
):
    rows, width = dy.shape
    hidden = g.shape[1]
    full = whole((rows, width))
    column = pl.BlockSpec((rows, width), lambda s: (0, s))
    smalls = [p768, s384, s192, s256, levels, *hots]
    return call(
        functools.partial(mlp_back_kernel, shards),
        [
            sds((width // 2, hidden + width + 128), BF),
            sds((width // 2, hidden + width + 128), BF),
            sds((hidden // 2, width), BF),
            sds((hidden // 2, width), BF),
            sds((rows, width), F32),
            sds((rows, width), BF),
        ],
        grid=(hidden // width,),
        in_specs=[
            pl.BlockSpec(memory_space=pltpu.SMEM),
            full,
            column,
            column,
            pl.BlockSpec((width, width), lambda s: (0, s)),
            pl.BlockSpec((width, width), lambda s: (s, 0)),
            full,
            full,
            whole((width, width)),
        ]
        + [whole(a.shape) for a in smalls],
        out_specs=[
            pl.BlockSpec(memory_space=pl.ANY),
            pl.BlockSpec(memory_space=pl.ANY),
            pl.BlockSpec(memory_space=pl.ANY),
            pl.BlockSpec(memory_space=pl.ANY),
            full,
            full,
        ],
        scratch=[
            pltpu.VMEM((width, rows), BF),
            pltpu.VMEM((rows, width), BF),
            pltpu.VMEM((rows, width), F32),
            pltpu.VMEM((rows, width), BF),
            pltpu.VMEM((8, width), F32),
            pltpu.VMEM((width, 128), F32),
            pltpu.VMEM((4, width, width), BF),
            pltpu.VMEM((4, width, width), BF),
            pltpu.VMEM((width, width + 128), BF),
            pltpu.VMEM((rows, width), F32),
            pltpu.SemaphoreType.DMA((9,)),
        ],
        flops=25e9,
        name="mlp_back",
    )(core, dy, g, gp, w1, w2, x1, attended, wp, *smalls)


def roll_back(values, amount):
    moved = jnp.concatenate(
        [
            pltpu.roll(values[8 * g : 8 * g + 8], (amount - 7 - 8 * g) % 128, 1)
            for g in range(values.shape[0] // 8)
        ],
        axis=0,
    )
    left = 7 - lax.rem(lax.broadcasted_iota(jnp.int32, values.shape, 0), 8)
    for step in (1, 2, 4):
        moved = jnp.where((left & step) > 0, pltpu.roll(moved, step, 1), moved)
    return moved


def attend_back_kernel(total_rows, scale, others, *refs):
    first_ref, q_ref, qaug_ref, do_ref, o_ref, lse_ref, tab_ref, oh1_ref, oh2_ref, before_ref = refs[:10]
    k_refs = refs[10 : 10 + others]
    v_refs = refs[10 + others : 10 + 2 * others]
    rest = refs[-15:]
    (
        dqkv_ref, dtab_ref, kaug_ref, v_ref, p_ref, ds_ref, dqt_ref, df_ref, qm_ref, dom_ref, delta_ref,
        scores_ref, dweight_ref, dk_acc, dv_acc,
    ) = rest
    first_row = first_ref[0]
    tokens = q_ref.shape[0]
    keys = kaug_ref.shape[0]

    @pl.when(pl.program_id(0) == 0)
    def _():
        kaug_ref[:, 128:] = oh2_ref[...]
        dtab_ref[...] = before_ref[...]

    at = 0
    for ref in v_refs:
        v_ref[at : at + ref.shape[0], :] = ref[...]
        at += ref.shape[0]
    lane_all = lax.broadcasted_iota(jnp.int32, (tokens, 128), 1)
    lane = lax.broadcasted_iota(jnp.int32, (64, 128), 1)
    qf = q_ref[...].astype(F32)
    dof = do_ref[...].astype(F32)
    delta_t = (dof * o_ref[...].astype(F32)).T
    dk_acc[...] = jnp.zeros_like(dk_acc)
    dv_acc[...] = jnp.zeros_like(dv_acc)
    dq = None
    for odd in (0, 1):
        mine_all = (lane_all >= 64) if odd else (lane_all < 64)
        other = (lane < 64) if odd else (lane >= 64)
        build_kaug(kaug_ref, k_refs, oh1_ref, oh2_ref, odd)
        qm = jnp.where(mine_all, qf, 0.0).astype(BF)
        dom = jnp.where(mine_all, dof, 0.0).astype(BF)
        delta = rowsum(delta_t[64 * odd : 64 * odd + 64])
        qm_ref[...] = qm
        dom_ref[...] = dom
        delta_ref[...] = delta

        def queries(t, carry):
            sl = pl.ds(pl.multiple_of(t * 256, 256), 256)
            scores_ref[...] = mt(kaug_ref[...], qaug_ref[odd, sl, :])
            dweight_ref[...] = mt(v_ref[...], dom_ref[sl, :])
            lse = lse_ref[0, odd : odd + 1, sl]
            shift = delta_ref[:, sl]

            def weigh(rows, inner):
                weight = jnp.exp(scores_ref[rows, :] - lse)
                p_ref[rows, :] = weight.astype(BF)
                ds_ref[rows, :] = (weight * (dweight_ref[rows, :] - shift)).astype(BF)

            by_chunks(keys, 128, weigh)
            dk_acc[...] += mm(ds_ref[...], qm_ref[sl, :])
            dv_acc[...] += mm(p_ref[...], dom_ref[sl, :])
            dqt_ref[:, sl] = tm(kaug_ref[...], ds_ref[...])
            return carry

        repeat(tokens // 256, queries)
        dqa = dqt_ref[0:256, :].T
        for i in range(tokens // 64):
            sl = slice(64 * i, 64 * i + 64)
            cols = roll_back(jnp.where(other, dqa[sl, 0:128], 0.0), 63 if odd else 127)
            shift = lax.rem(63 + total_rows - (first_row + i) + 128, 128)
            rows = pltpu.roll(
                jnp.where((lane >= 64) & (lane < 64 + total_rows), dqa[sl, 128:256], 0.0), shift, 1
            )
            df_ref[sl, 0:128] = cols.astype(BF)
            df_ref[sl, 128:256] = rows.astype(BF)
        from_tables = mt(df_ref[...], tab_ref[...])
        part = jnp.where(mine_all, dqa[:, 0:128] * scale + from_tables, 0.0)
        dq = part if dq is None else dq + part
        dtab_ref[...] += tm(qm, df_ref[...])
    dqkv_ref[0, 0:tokens, :] = dq.astype(BF)
    dqkv_ref[1] = (dk_acc[...] * scale).astype(BF)
    dqkv_ref[2] = dv_acc[...].astype(BF)


def attend_back_call(
    first, qkv_own, kv_others, qaug, dout, attended, lse, tab, oh1, oh2, dtab, total_rows, heads, part, parts, grads
):
    tokens = qkv_own.shape[0]
    width = qkv_own.shape[1] // 3
    keys = oh1.shape[0]
    aug = 128 + oh2.shape[1]
    pairs = width // 128
    count = pairs // parts
    base = part * count
    sources = 1 + (1 if kv_others is not None else 0)
    own = pl.BlockSpec((tokens, 128), lambda h: (0, h + base))
    in_specs = [
        pl.BlockSpec(memory_space=pltpu.SMEM),
        own,
        pl.BlockSpec((2, tokens, aug), lambda h: (h + base, 0, 0)),
        own,
        own,
        pl.BlockSpec((1, 2, tokens), lambda h: (h + base, 0, 0)),
        whole(tab.shape),
        whole(oh1.shape),
        whole(oh2.shape),
        whole(dtab.shape),
    ]
    k_args, v_args, k_specs, v_specs = [qkv_own], [qkv_own], [], []
    k_specs.append(pl.BlockSpec((tokens, 128), lambda h: (0, h + base + pairs)))
    v_specs.append(pl.BlockSpec((tokens, 128), lambda h: (0, h + base + 2 * pairs)))
    if kv_others is not None:
        k_args.append(kv_others)
        v_args.append(kv_others)
        k_specs.append(pl.BlockSpec((keys - tokens, 128), lambda h: (0, h + base)))
        v_specs.append(pl.BlockSpec((keys - tokens, 128), lambda h: (0, h + base + pairs)))
    scale = (width // heads) ** -0.5
    earlier = [] if grads is None else [grads]
    return call(
        functools.partial(attend_back_kernel, total_rows, scale, sources),
        [sds((3, keys, width), BF), sds((128, 256), F32)],
        grid=(count,),
        in_specs=in_specs + k_specs + v_specs + [pl.BlockSpec(memory_space=pl.ANY)] * len(earlier),
        out_specs=[pl.BlockSpec((3, keys, 128), lambda h: (0, 0, h + base)), whole((128, 256))],
        scratch=[
            pltpu.VMEM((keys, aug), BF),
            pltpu.VMEM((keys, 128), BF),
            pltpu.VMEM((keys, 256), BF),
            pltpu.VMEM((keys, 256), BF),
            pltpu.VMEM((aug, tokens), F32),
            pltpu.VMEM((tokens, 256), BF),
            pltpu.VMEM((tokens, 128), BF),
            pltpu.VMEM((tokens, 128), BF),
            pltpu.VMEM((1, tokens), F32),
            pltpu.VMEM((keys, 256), F32),
            pltpu.VMEM((keys, 256), F32),
            pltpu.VMEM((keys, 128), F32),
            pltpu.VMEM((keys, 128), F32),
        ],
        flops=30e9 / parts,
        name="attend_back",
        aliases={10 + 2 * sources: 0} if earlier else {},
    )(first, qkv_own, qaug, dout, attended, lse, tab, oh1, oh2, dtab, *k_args, *v_args, *earlier)


def qkv_back_kernel(
    x_ref, dqkv_ref, w_ref, dx1_ref, p_ref, dtab_ref, hot_ref,
    pack_ref, dx_ref, far_ref, nt_ref, low_ref, dn_ref, sums_ref, dw_ref, out_ref, extra_ref, sem,
):
    step = pl.program_id(0)
    tokens, width = x_ref.shape

    def w_copy(at):
        return pltpu.make_async_copy(
            out_ref.at[at], pack_ref.at[:, pl.ds(at * width, width)], sem.at[at]
        )

    extra_copy = pltpu.make_async_copy(extra_ref, pack_ref.at[:, pl.ds(3 * width, 384)], sem.at[3])

    def norm_chunk(sl, carry):
        hat, _ = stats(x_ref[sl, :].astype(F32))
        low_ref[sl, :] = (hat * p_ref[0:1, :] + p_ref[2:3, :]).astype(BF)

    by_chunks(tokens, 32, norm_chunk)
    nt_ref[...] = low_ref[...].T

    @pl.when(step == 0)
    def _():
        sums_ref[...] = jnp.zeros_like(sums_ref)
        sums_ref[4:5, :] = rowsum(dqkv_ref[0].astype(F32))
        both = dtab_ref[...]
        tables = (both[0:64] + both[64:128]).astype(BF)
        extra_ref[:, 128:384] = mm(hot_ref[...], tables).astype(BF)
        dw_ref[...] = jnp.zeros_like(dw_ref)

    dn_ref[...] = jnp.zeros_like(dn_ref)

    def product(at, carry):
        lanes = pl.ds(pl.multiple_of(at * width, width), width)
        dw_ref[at] += mm(nt_ref[...], dqkv_ref[at])
        dn_ref[...] += mt(dqkv_ref[at], w_ref[:, lanes])
        return carry

    lax.fori_loop(jnp.where(step == 0, 0, 1), 3, product, 0)
    sums_ref[5:6, :] += rowsum(dqkv_ref[2].astype(F32))

    def back_chunk(sl, carry):
        sum_gain, sum_shift = carry
        hat, inverse = stats(x_ref[sl, :].astype(F32))
        grad = dn_ref[sl, :]
        dn_ref[sl, :] = norm_back(grad * p_ref[0:1, :], hat, inverse)
        return sum_gain + rowsum(grad * hat), sum_shift + rowsum(grad)

    zero = jnp.zeros((1, width), F32)
    sum_gain, sum_shift = by_chunks(tokens, 32, back_chunk, (zero, zero))
    sums_ref[0:1, :] += sum_gain
    sums_ref[2:3, :] += sum_shift

    @pl.when(step == 0)
    def _():
        dx_ref[...] = dx1_ref[...] + dn_ref[...]

    far_ref[...] = dn_ref[...].astype(BF)

    @pl.when(step == pl.num_programs(0) - 1)
    def _():
        def put(at, carry):
            out_ref[at] = dw_ref[at].astype(BF)
            w_copy(at).start()
            return carry

        lax.fori_loop(0, 3, put, 0)
        padded = jnp.concatenate([sums_ref[...], jnp.zeros((120, width), F32)], axis=0)
        extra_ref[:, 0:128] = padded.T.astype(BF)
        extra_copy.start()
        for at in range(3):
            w_copy(at).wait()
        extra_copy.wait()


def qkv_back_call(tokens, dqkv, weight, dx1, p768, dtab, hot):
    rows, width = dx1.shape
    blocks = tokens.shape[0] // rows
    full = whole((rows, width))
    block = pl.BlockSpec((rows, width), lambda s: (s, 0))
    return call(
        qkv_back_kernel,
        [
            sds((width, 3 * width + 384), BF),
            sds((rows, width), F32),
            sds(((max(blocks, 2) - 1) * rows, width), BF),
        ],
        grid=(blocks,),
        in_specs=[
            block,
            pl.BlockSpec((3, rows, width), lambda s: (0, s, 0)),
            whole(weight.shape),
            full,
            whole(p768.shape),
            whole(dtab.shape),
            whole(hot.shape),
        ],
        out_specs=[
            pl.BlockSpec(memory_space=pl.ANY),
            full,
            pl.BlockSpec((rows, width), lambda s: (jnp.maximum(s - 1, 0), 0)),
        ],
        scratch=[
            pltpu.VMEM((width, rows), BF),
            pltpu.VMEM((rows, width), BF),
            pltpu.VMEM((rows, width), F32),
            pltpu.VMEM((8, width), F32),
            pltpu.VMEM((3, width, width), F32),
            pltpu.VMEM((3, width, width), BF),
            pltpu.VMEM((width, 384), BF),
            pltpu.SemaphoreType.DMA((4,)),
        ],
        flops=8e9,
        name="qkv_back",
    )(tokens, dqkv, weight, dx1, p768, dtab, hot)


def rim_exchange(levels, axis):
    peers = lax.axis_size(axis)
    chan = levels[0].shape[-1]
    counts = [level.shape[1] for level in levels]
    lasts = jnp.concatenate([level[-1] for level in levels], axis=0)
    firsts = jnp.concatenate([level[0] for level in levels], axis=0)
    if peers == 2:
        me = lax.axis_index(axis)
        got = lax.ppermute(jnp.where(me == 0, lasts, firsts), axis, [(0, 1), (1, 0)])
        nothing = jnp.zeros_like(got)
        before = jnp.where(me == 1, got, nothing)
        after = jnp.where(me == 0, got, nothing)
    else:
        before = lax.ppermute(lasts, axis, [(i, i + 1) for i in range(peers - 1)])
        after = lax.ppermute(firsts, axis, [(i + 1, i) for i in range(peers - 1)])
    both = jnp.stack([before, after])
    rims, at = [], 0
    for count in counts:
        rims.append(both[:, at : at + count])
        at += count
    return rims


class Halving:
    def __init__(self, keep, send):
        bits = lax.axis_size("img").bit_length() - 1
        self.left = list(range(1, bits))[::-1]
        self.shape = (2,) * (bits - 1) + (keep.shape[0] >> (bits - 1), keep.shape[1])
        self.keep, self.first = keep.reshape(self.shape), send.reshape(self.shape)

    def lanes(self):
        first, second = Halving.__new__(Halving), Halving.__new__(Halving)
        middle = self.shape[-1] // 256 * 128
        for part, cut in ((first, slice(0, middle)), (second, slice(middle, None))):
            part.left = list(self.left)
            part.terms = [term[..., cut] for term in self.terms]
        return first, second

    def split(self, step):
        if step == 0:
            self.route = ("img", [(i, i ^ 1) for i in range(lax.axis_size("img"))])
            return self.first
        terms = self.terms
        if step == "y":
            at, mine, axis, pairs = len(self.left), lax.axis_index("seq"), "seq", [(0, 1), (1, 0)]
            shape = terms[0].shape
            terms = [t.reshape(shape[:-2] + (2, shape[-2] // 2, shape[-1])) for t in terms]
        else:
            at, mine, axis = self.left.index(step), (lax.axis_index("img") >> step) & 1, "img"
            pairs = [(i, i ^ (1 << step)) for i in range(lax.axis_size("img"))]
            self.left.remove(step)
        self.route = (axis, pairs)

        def half(which):
            parts = [lax.dynamic_index_in_dim(t, which, at, keepdims=False) for t in terms]
            return (parts[0].astype(F32) + parts[1].astype(F32)).astype(BF)

        self.keep = half(mine)
        return half(1 - mine)


def swap(steps, after=()):
    if lax.axis_size("seq") != 2:
        steps = [(h, step) for h, step in steps if step != "y"]
    sends = [h.split(step) for h, step in steps]
    keeps = [h.keep for h, _ in steps]
    sends, keeps, after = lax.optimization_barrier((sends, keeps, after))
    for (h, _), send, keep in zip(steps, sends, keeps):
        h.terms = [keep, lax.ppermute(flat(send), *h.route).reshape(send.shape)]
    return [h for h, _ in steps], after


def flat(values):
    return values.reshape(-1, values.shape[-1])


def last_swap(group):
    left = group[0].left
    count = 1 << len(left)
    base = left[-1]
    mine = (lax.axis_index("img") >> base) & (count - 1)
    shards = lax.axis_size("img")
    terms = [
        jnp.concatenate(
            [h.terms[k].reshape((count,) + h.terms[k].shape[len(left) :]) for h in group], axis=-1
        )
        for k in (0, 1)
    ]

    def part(which):
        parts = [lax.dynamic_index_in_dim(t, which, 0, keepdims=False) for t in terms]
        return (parts[0].astype(F32) + parts[1].astype(F32)).astype(BF)

    total = part(mine).astype(F32)
    for d in range(1, count):
        pairs = [(i, i ^ (d << base)) for i in range(shards)]
        total = total + lax.ppermute(part(mine ^ d), "img", pairs).astype(F32)
    grad = total.astype(BF)
    if lax.axis_size("seq") != 2:
        return lax.psum(grad, "seq").astype(F32)
    row = lax.axis_index("seq")
    other = lax.ppermute(grad, "seq", [(0, 1), (1, 0)])
    first = jnp.where(row == 0, grad, other)
    second = jnp.where(row == 0, other, grad)
    return jnp.concatenate([first, second], axis=0).astype(F32)


def settle(moving, done=()):
    terms, _ = lax.optimization_barrier(([h.terms for h in moving], done))
    for h, arrived in zip(moving, terms):
        h.terms = arrived


def seq_total(part):
    peers = lax.axis_size("seq")
    if peers == 2:
        other = lax.ppermute(part, "seq", [(0, 1), (1, 0)])
        return part.astype(F32) + other.astype(F32)
    return lax.psum(part, "seq").astype(F32)


def per_device(
    tokens, valid_rows, valid_cols, block_gains, block_shifts, qkv_weight, qv_bias, table_rows, table_cols,
    proj_weight, proj_bias, fc1_weight, fc1_bias, fc2_weight, fc2_bias, fine_first, fine_first_bias,
    fine_norm_gain, fine_norm_shift, fine_second, fine_second_bias, middle_up, middle_up_bias, lateral_fine,
    lateral_middle, lateral_coarse, level_gains, level_shifts, output_convs, cotan_fine, cotan_middle,
    cotan_base, cotan_coarse,
):
    lr, cols, width = tokens.shape[1:]
    head = table_rows.shape[0]
    heads = width // head
    peers = lax.axis_size("seq")
    shards = lax.axis_size("img")
    me = lax.axis_index("seq")
    total_rows = lr * peers
    count = lr * cols
    chan = lateral_fine.shape[1]
    first_row = me * lr
    first = first_row.astype(jnp.int32).reshape(1)
    own_tokens = tokens[0].reshape(count, width)

    far = [
        lax.ppermute(own_tokens, "seq", [(i, (i + d) % peers) for i in range(peers)])
        for d in range(1, peers)
    ]
    far_tokens = jnp.concatenate(far, axis=0) if len(far) > 1 else (far[0] if far else None)
    all_tokens = jnp.concatenate([own_tokens] + far, axis=0)

    p768 = jnp.stack(
        [
            block_gains[:, 0], block_gains[:, 1], block_shifts[:, 0], block_shifts[:, 1],
            qv_bias[:, 0], qv_bias[:, 1], proj_bias, fc2_bias,
        ]
    ).astype(F32)
    bias3 = jnp.stack([qv_bias[:, 0], jnp.zeros_like(proj_bias), qv_bias[:, 1]]).astype(F32)[:, None, :]
    qkv_own = qkv_call(own_tokens, qkv_weight, bias3, p768, 0)
    (
        fc1_bias, fine_first_bias, fine_norm_gain, fine_norm_shift, middle_up_bias, fine_second_bias, level_gains,
        level_shifts, table_cols, table_rows, valid_rows, qkv_own,
    ) = lax.optimization_barrier(
        (
            fc1_bias, fine_first_bias, fine_norm_gain, fine_norm_shift, middle_up_bias, fine_second_bias,
            level_gains, level_shifts, table_cols, table_rows, valid_rows, qkv_own,
        )
    )
    b1 = fc1_bias.astype(F32)[None]
    p384 = jnp.stack([fine_first_bias, fine_norm_gain, fine_norm_shift, middle_up_bias]).astype(F32)
    fsb = fine_second_bias.astype(F32)[None]
    p256 = jnp.concatenate([level_gains.T, level_shifts.T]).astype(F32)
    lc0, lc1 = lateral_coarse[:, 0, :], lateral_coarse[:, 1, :]

    def turned(table):
        back = table[:, ::-1]
        back = jnp.pad(back, ((0, 0), (0, 128 - back.shape[1])))
        return jnp.concatenate([back, back], axis=0)

    tw, tr = turned(table_cols), turned(table_rows)

    low_at, aug = aug_layout(total_rows)
    ranks = jnp.stack([(me - d) % peers for d in range(peers)])
    key_rows = (ranks[:, None] * lr + jnp.arange(lr)[None, :])[:, :, None]
    key_rows = jnp.broadcast_to(key_rows, (peers, lr, cols)).reshape(-1, 1)
    key_cols = jnp.broadcast_to(jnp.arange(cols)[None, None, :], (peers, lr, cols)).reshape(-1, 1)
    lane = jnp.arange(128)[None, :]
    oh1 = (lane % 64 == key_cols).astype(BF)
    lane = jnp.arange(aug - 128)[None, :]
    hot = (lane < 64) & (lane == key_cols)
    hot = hot | ((lane >= 64) & (lane < 64 + total_rows) & (lane - 64 == key_rows))
    off = low_at
    hot = hot | ((lane >= off) & (lane < off + total_rows) & (lane - off == key_rows))
    bad = (key_rows >= valid_rows[0]) | (key_cols >= valid_cols[0])
    oh2 = jnp.where(bad & (lane == off + total_rows), NEG, hot.astype(F32)).astype(BF)

    kv_far = qkv_call(far_tokens, qkv_weight, bias3, p768, 1) if far else None
    attended, qaug, lse = attend_call(
        first, qkv_own, kv_far, (tw, tr), oh1, oh2, total_rows, heads
    )
    x1, hidden, slope, y = mlp_call(own_tokens, attended, proj_weight, fc1_weight, b1, fc2_weight, p768)

    zf, zm, zb, zc = pyramid_call(
        y, lr, cols, fine_first, fine_second, middle_up, lateral_fine, lateral_middle, lc0, lc1, p384, fsb, p256
    )
    levels = [
        zf.reshape(4 * lr, 4 * cols, chan),
        zm.reshape(2 * lr, 2 * cols, chan),
        zb.reshape(lr, cols, chan),
        zc.reshape(lr // 2, cols // 2, chan),
    ]
    later, _ = lax.optimization_barrier((output_convs, zc))
    conv_weights = later.transpose(1, 0, 2).reshape(4, 3, 3 * chan, chan)
    rims = rim_exchange(levels, "seq")
    cots = [c[0] for c in (cotan_fine, cotan_middle, cotan_base, cotan_coarse)]
    maps, drs, level_sums = [None] * 4, [None] * 4, [None] * 4
    packed = None
    for level in (3, 2, 1, 0):
        z = levels[level]
        block = min(z.shape[0], max(1, 2048 // z.shape[1]))
        map_low, dr, packed, level_sums[level] = conv_call(
            level, z, rims[level], conv_weights, cots[level], p256, block, packed
        )
        maps[level], drs[level] = map_low.reshape(z.shape), dr.reshape(z.shape)

    conv_low = lax.psum_scatter(packed, "img", scatter_dimension=0, tiled=True)
    drims = rim_exchange(drs, "seq")
    dzs = []
    for level, ways in enumerate((4, 2, 1, 1)):
        dr = drs[level]
        block = min(dr.shape[0], max(1, 2048 // dr.shape[1]))
        dzs.append(conv_back_call(level, dr, drims[level], conv_weights, ways, block))

    unit = width // shards
    packed_row, _ = lax.optimization_barrier((jnp.arange(width)[:, None], level_sums[0]))
    shard_at, within = packed_row // unit, packed_row % unit

    def placed(size):
        own = size // shards
        at = jnp.arange(size)[None, :]
        return ((within < own) & (at == shard_at * own + within)).astype(BF)

    quart, half = lateral_fine.shape[0], lateral_middle.shape[0]
    own_q, own_h = quart // shards, half // shards
    at = jnp.arange(quart + half)[None, :]
    source = jnp.where(
        within < own_q,
        shard_at * own_q + within,
        jnp.where(within < own_q + own_h, quart + shard_at * own_h + within - own_q, -1),
    )
    place = (at == source).astype(BF)
    hots = (placed(chan), placed(half), placed(quart))
    core = (lax.axis_index("img") & 1).astype(jnp.int32).reshape(1)
    dy, low_keep, low_send, s384, s192, s256 = pyramid_back_call(
        y, lr, cols, fine_first, fine_second, middle_up, lateral_fine, lateral_middle, lc0, lc1, p384, fsb, p256,
        *dzs, place, core, shards,
    )
    pyramid_sum = Halving(low_keep, low_send)
    moving, dy = swap([(pyramid_sum, 0)], dy)

    level_rows = jnp.concatenate(
        [level_sums[k][0:1] for k in range(4)] + [level_sums[k][1:2] for k in range(4)]
    )
    high_keep, high_send, keep2, send2, dx1, dout = mlp_back_call(
        dy, hidden, slope, fc1_weight, fc2_weight, x1, attended, proj_weight, p768,
        s384, s192, s256, level_rows, hots, core, shards,
    )
    settle(moving, dout)
    one, two = pyramid_sum.lanes()
    three, four = Halving(high_keep, high_send), Halving(keep2, send2)
    tables = jnp.concatenate([tw, tr], axis=1)

    def attend_part(dout_now, dtab, part, grads):
        return attend_back_call(
            first, qkv_own, kv_far, qaug, dout_now, attended, lse, tables, oh1, oh2, dtab,
            total_rows, heads, part, 2, grads,
        )

    _, (dout, conv_low) = swap([(one, 1), (two, "y"), (three, 0), (four, 0)], (dout, conv_low))
    dqkv, dtab = attend_part(dout, jnp.zeros((128, 256), F32), 0, None)
    settle([three, four], dtab)
    _, dtab = swap([(three, 1), (four, "y")], dtab)
    dqkv, dtab = attend_part(dout, dtab, 1, dqkv)
    settle([one, two], dtab)
    _, dtab = swap([(one, "y"), (two, 1)], dtab)
    last, dx, dx_far = qkv_back_call(
        all_tokens, dqkv, qkv_weight, dx1, p768, dtab, placed(head)
    )
    last_low = lax.psum_scatter(last, "img", scatter_dimension=0, tiled=True)
    for d in range(1, peers):
        part = dx_far[(d - 1) * count : d * count]
        dx = dx + lax.ppermute(part, "seq", [(i, (i - d) % peers) for i in range(peers)])
    conv_low, _ = lax.optimization_barrier((conv_low, last))
    conv_total = seq_total(conv_low)
    settle([one, two, three, four], last)
    swap([(three, "y"), (four, 1)])
    settle([three, four])
    low_total, high_total = last_swap([one, two]), last_swap([three])
    g_w2 = last_swap([four])
    last_low, low_total, high_total, g_w2 = lax.optimization_barrier(
        (last_low, low_total, high_total, g_w2)
    )
    last_total = seq_total(last_low)

    def taken(total, start, size):
        return total[:, start : start + size]

    g_ff = jnp.concatenate([taken(low_total, 2 * k * half, half) for k in range(4)], axis=1)
    g_mu = jnp.concatenate([taken(low_total, (2 * k + 1) * half, half) for k in range(4)], axis=1)
    g_fs = taken(low_total, 8 * half, half)
    g_lc = jnp.stack(
        [taken(low_total, 9 * half, chan), taken(low_total, 9 * half + chan, chan)], axis=1
    )
    laterals = taken(low_total, 9 * half + 2 * chan, chan)
    g_lf, g_lm = laterals[:own_q], laterals[own_q : own_q + own_h]
    g_w1 = taken(high_total, 0, 4 * width)
    g_wp = taken(high_total, 4 * width, width)
    vec = taken(high_total, 5 * width, 128)
    own_c = chan // shards
    g_lg = jnp.concatenate([vec[:own_c, 8:12], vec[:own_c, 24:28]], axis=1)
    g_ls = jnp.concatenate([vec[:own_c, 16:20], vec[:own_c, 28:32]], axis=1)
    g_ffb, g_fng, g_fns, g_mub = (vec[:own_h, 32 + k] for k in range(4))
    g_fsb = vec[:own_q, 48]
    g_b1 = vec[:, 40:44].T.reshape(-1)
    g_pb, g_b2 = vec[:, 6], vec[:, 7]
    g_qkv = last_total[:, : 3 * width]
    late = last_total[:, 3 * width : 3 * width + 128]
    g_bg = jnp.stack([late[:, 0], vec[:, 1]], axis=1)
    g_bs = jnp.stack([late[:, 2], vec[:, 3]], axis=1)
    g_qvb = late[:, 4:6]
    own_t = head // shards
    tabs = last_total[:own_t, 3 * width + 128 :]
    g_tc = tabs[:, : 2 * cols - 1][:, ::-1]
    g_tr = tabs[:, 128 : 128 + 2 * total_rows - 1][:, ::-1]
    g_conv = conv_total.reshape(-1, 4, chan)
    return (
        maps[0][None], maps[1][None], maps[2][None], maps[3][None],
        dx.reshape(1, lr, cols, width),
        g_bg, g_bs, g_qkv, g_qvb, g_tr, g_tc, g_wp, g_pb, g_w1, g_b1, g_w2, g_b2, g_ff, g_ffb, g_fng, g_fns,
        g_fs, g_fsb, g_mu, g_mub, g_lf, g_lm, g_lc, g_lg, g_ls, g_conv,
    )


def solution(mesh):
    image = P("img", "seq", None, None)
    in_specs = (image, P("img"), P("img")) + (P(),) * 26 + (image,) * 4
    ranks = (2, 2, 2, 2, 2, 2, 2, 1, 2, 1, 2, 1, 2, 1, 1, 1, 2, 1, 2, 1, 2, 2, 3, 2, 2, 3)
    out_specs = (image,) * 5 + tuple(P(*(("img",) + (None,) * (r - 1))) for r in ranks)
    return jax.shard_map(
        per_device, mesh=mesh, in_specs=in_specs, out_specs=out_specs, check_vma=False
    )
```

```python
import functools

import jax
import jax.numpy as jnp
from jax import lax
from jax.experimental import pallas as pl
from jax.experimental.pallas import tpu as pltpu
from jax.sharding import PartitionSpec as P

F32 = jnp.float32
BF = jnp.bfloat16
NEG = -1e30
EPS = 1e-6
SQRT_HALF = 0.7071067811865476
INV_SQRT_2PI = 0.3989422804014327
VMEM_LIMIT = 60 * 1024 * 1024


def mm(left, right):
    return lax.dot_general(left, right, (((1,), (0,)), ((), ())), preferred_element_type=F32)


def mt(left, right):
    return lax.dot_general(left, right, (((1,), (1,)), ((), ())), preferred_element_type=F32)


def tm(left, right):
    return lax.dot_general(left, right, (((0,), (0,)), ((), ())), preferred_element_type=F32)


def call(
    kernel, outs, grid=(), in_specs=None, out_specs=None, scratch=(), flops=0, name=None, aliases=None
):
    return pl.pallas_call(
        kernel,
        out_shape=outs,
        grid=grid,
        in_specs=in_specs,
        out_specs=out_specs,
        scratch_shapes=scratch,
        name=name,
        input_output_aliases=aliases or {},
        cost_estimate=pl.CostEstimate(flops=int(flops) // COST_SHARE, bytes_accessed=0, transcendentals=0),
        compiler_params=pltpu.CompilerParams(vmem_limit_bytes=VMEM_LIMIT),
    )


def whole(shape):
    return pl.BlockSpec(shape, lambda *_: (0,) * len(shape))


def sds(shape, dtype):
    return jax.ShapeDtypeStruct(shape, dtype)


def stats(values):
    average = jnp.mean(values, axis=-1, keepdims=True)
    centred = values - average
    spread = jnp.mean(centred * centred, axis=-1, keepdims=True)
    inverse = lax.rsqrt(spread + EPS)
    return centred * inverse, inverse


def norm_back(grad_hat, hat, inverse):
    first = jnp.mean(grad_hat, axis=-1, keepdims=True)
    second = jnp.mean(grad_hat * hat, axis=-1, keepdims=True)
    return inverse * (grad_hat - first - hat * second)


def rowsum(values):
    return jnp.sum(values, axis=0, keepdims=True)


UNROLL = 64
COST_SHARE = 100
CONV_PIXELS = 1024
MOVE_ROWS = 8
BACK_PIXELS = 2048


def by_chunks(total, size, body, carry=0, unroll=None):
    unroll = max(1, min(unroll or UNROLL, total // size))

    def step(k, inner):
        for u in range(unroll):
            out = body(pl.ds(pl.multiple_of((k * unroll + u) * size, size), size), inner)
            inner = inner if out is None else out
        return inner

    if unroll == total // size:
        return step(0, carry)
    return lax.fori_loop(0, total // size // unroll, step, carry)


def put_shards(source, keep_ref, send_ref, lanes, shards, first, core, sem):
    unit = source.shape[0] // shards
    for s in range(shards):
        at = first + s
        rows = pl.ds(pl.multiple_of(lax.div(at, 2) * unit, unit), unit)
        piece = source.at[pl.ds(s * unit, unit)]

        @pl.when(lax.rem(at, 2) == core)
        def _():
            pltpu.make_async_copy(piece, keep_ref.at[rows, lanes], sem).start()

        @pl.when(lax.rem(at, 2) != core)
        def _():
            pltpu.make_async_copy(piece, send_ref.at[rows, lanes], sem).start()


def wait_shards(source, sem):
    pltpu.make_async_copy(source, source, sem).wait()


def repeat(count, body):
    for k in range(count):
        body(k, 0)


def gelu_pair(values):
    half = 0.5 * (1.0 + lax.erf(values * SQRT_HALF))
    slope = half + values * (jnp.exp(-0.5 * values * values) * INV_SQRT_2PI)
    return values * half, slope


def shift_matrix(size, amount):
    out_at = lax.broadcasted_iota(jnp.int32, (size, size), 0)
    in_at = lax.broadcasted_iota(jnp.int32, (size, size), 1)
    return jnp.where(in_at == out_at + amount, 1.0, 0.0).astype(BF)


def weave_matrix(size, ways, inverse=False):
    out_at = lax.broadcasted_iota(jnp.int32, (size, size), 1 if inverse else 0)
    in_at = lax.broadcasted_iota(jnp.int32, (size, size), 0 if inverse else 1)
    source = lax.rem(out_at, ways) * (size // ways) + lax.div(out_at, ways)
    return jnp.where(in_at == source, 1.0, 0.0).astype(BF)


def qkv_kernel(x_ref, w_ref, b_ref, p_ref, out_ref, n1_ref):
    @pl.when(pl.program_id(1) == 0)
    def _():
        def norm(sl, carry):
            hat, _ = stats(x_ref[sl, :].astype(F32))
            n1_ref[sl, :] = (hat * p_ref[0:1, :] + p_ref[2:3, :]).astype(BF)

        by_chunks(x_ref.shape[0], 32, norm)

    out_ref[...] = (mm(n1_ref[...], w_ref[...]) + b_ref[0]).astype(BF)


def qkv_call(tokens, weight, bias3, p768, first):
    rows, width = tokens.shape
    block = 512
    count = 3 - first
    return call(
        qkv_kernel,
        sds((rows, count * width), BF),
        grid=(rows // block, count),
        in_specs=[
            pl.BlockSpec((block, width), lambda i, j: (i, 0)),
            pl.BlockSpec((width, width), lambda i, j: (0, j + first)),
            pl.BlockSpec((1, 1, width), lambda i, j: (j + first, 0, 0)),
            whole(p768.shape),
        ],
        out_specs=pl.BlockSpec((block, width), lambda i, j: (i, j)),
        scratch=[pltpu.VMEM((block, width), BF)],
        flops=2 * rows * width * width * count,
        name="qkv",
    )(tokens, weight, bias3, p768)


def aug_layout(total_rows):
    low_at = 64 + total_rows
    if low_at + total_rows + 1 > 128:
        low_at = 128
    width = 128 * (2 + (low_at + total_rows) // 128)
    return low_at, width


def build_kaug(kaug_ref, k_refs, oh1_ref, oh2_ref, odd):
    lane = lax.broadcasted_iota(jnp.int32, (512, 128), 1)
    mine = (lane >= 64) if odd else (lane < 64)
    at = 0
    for k_ref in k_refs:
        for row in range(0, k_ref.shape[0], 512):
            keys = k_ref[row : row + 512, :].astype(F32)
            hot = oh1_ref[at : at + 512, :].astype(F32)
            kaug_ref[at : at + 512, 0:128] = jnp.where(mine, keys, hot).astype(BF)
            at += 512


def build_qaug(first_row, qp, tw_ref, tr_ref, qaug_ref, odd, total_rows, scale):
    low_at, width = aug_layout(total_rows)
    tokens = qp.shape[0]
    lane = lax.broadcasted_iota(jnp.int32, (64, 128), 1)
    mine = (lane >= 64) if odd else (lane < 64)
    lane_all = lax.broadcasted_iota(jnp.int32, (tokens, 128), 1)
    mine_all = (lane_all >= 64) if odd else (lane_all < 64)
    qf = qp.astype(F32)
    qm = jnp.where(mine_all, qf, 0.0).astype(BF)
    cols = mm(qm, tw_ref[...])
    rows = mm(qm, tr_ref[...])
    for i in range(tokens // 64):
        sl = slice(64 * i, 64 * i + 64)
        upper = pltpu.roll(cols[sl], 1, 1, stride=1, stride_axis=0)
        lower = pltpu.roll(cols[sl], 65, 1, stride=1, stride_axis=0)
        first = jnp.where(mine, qf[sl] * scale, lower if odd else upper)
        col_low = lower - lower.astype(BF).astype(F32)
        shift = lax.rem(first_row + i + (65 - total_rows + 128), 128)
        row_part = pltpu.roll(rows[sl], shift, 1)
        row_low = row_part - row_part.astype(BF).astype(F32)
        qaug_ref[sl, 0:128] = first.astype(BF)
        one_at = low_at + total_rows
        if low_at < 128:
            rest = jnp.where(lane == one_at, 1.0, 0.0)
            rest = jnp.where(
                (lane >= low_at) & (lane < one_at), pltpu.roll(row_low, total_rows, 1), rest
            )
            second = jnp.where(lane < 64, col_low, jnp.where(lane < low_at, row_part, rest))
            qaug_ref[sl, 128:256] = second.astype(BF)
        else:
            second = jnp.where(
                lane < 64, col_low, jnp.where(lane < 64 + total_rows, row_part, 0.0)
            )
            third = jnp.where(
                lane < total_rows,
                pltpu.roll(row_low, 64, 1),
                jnp.where(lane == total_rows, 1.0, 0.0),
            )
            qaug_ref[sl, 128:256] = second.astype(BF)
            qaug_ref[sl, 256:384] = third.astype(BF)


def attend_kernel(total_rows, scale, others, *refs):
    first_ref, q_ref, tw_ref, tr_ref, oh1_ref, oh2_ref = refs[:6]
    k_refs = refs[6 : 6 + others]
    v_refs = refs[6 + others : 6 + 2 * others]
    o_ref, qaug_out, lse_ref, kaug_ref, v_ref, p_ref, ot_ref, scores_ref = refs[6 + 2 * others :]
    first_row = first_ref[0]
    tokens = q_ref.shape[0]
    keys = kaug_ref.shape[0]

    @pl.when(pl.program_id(0) == 0)
    def _():
        kaug_ref[:, 128:] = oh2_ref[...]

    at = 0
    for ref in v_refs:
        v_ref[at : at + ref.shape[0], :] = ref[...]
        at += ref.shape[0]
    qp = q_ref[...]
    for odd in (0, 1):
        build_kaug(kaug_ref, k_refs, oh1_ref, oh2_ref, odd)
        build_qaug(first_row, qp, tw_ref, tr_ref, qaug_out.at[odd], odd, total_rows, scale)

        def queries(t, carry):
            sl = pl.ds(pl.multiple_of(t * 256, 256), 256)
            scores_ref[...] = mt(kaug_ref[...], qaug_out[odd, sl, :])

            def highest(rows, top):
                return jnp.maximum(top, jnp.max(scores_ref[rows, :], axis=0, keepdims=True))

            top = by_chunks(keys, 128, highest, jnp.full((1, 256), NEG, F32))

            def weigh(rows, total):
                weight = jnp.exp(scores_ref[rows, :] - top)
                p_ref[rows, :] = weight.astype(BF)
                return total + rowsum(weight)

            total = by_chunks(keys, 128, weigh, jnp.zeros((1, 256), F32))
            lse_ref[0, odd : odd + 1, sl] = top + jnp.log(total)
            out_t = tm(v_ref[...], p_ref[...])
            ot_ref[64 * odd : 64 * odd + 64, sl] = out_t[64 * odd : 64 * odd + 64] / total
            return carry

        repeat(tokens // 256, queries)
    o_ref[...] = ot_ref[...].T.astype(BF)


def attend_call(first, qkv_own, kv_others, tables, oh1, oh2, total_rows, heads):
    tokens = qkv_own.shape[0]
    width = qkv_own.shape[1] // 3
    keys = oh1.shape[0]
    aug = 128 + oh2.shape[1]
    pairs = width // 128
    tw, tr = tables
    parts = 1 + (1 if kv_others is not None else 0)
    in_specs = [
        pl.BlockSpec(memory_space=pltpu.SMEM),
        pl.BlockSpec((tokens, 128), lambda h: (0, h)),
        whole(tw.shape),
        whole(tr.shape),
        whole(oh1.shape),
        whole(oh2.shape),
    ]
    k_args, v_args, k_specs, v_specs = [qkv_own], [qkv_own], [], []
    k_specs.append(pl.BlockSpec((tokens, 128), lambda h: (0, h + pairs)))
    v_specs.append(pl.BlockSpec((tokens, 128), lambda h: (0, h + 2 * pairs)))
    if kv_others is not None:
        k_args.append(kv_others)
        v_args.append(kv_others)
        k_specs.append(pl.BlockSpec((keys - tokens, 128), lambda h: (0, h)))
        v_specs.append(pl.BlockSpec((keys - tokens, 128), lambda h: (0, h + pairs)))
    scale = (width // heads) ** -0.5
    return call(
        functools.partial(attend_kernel, total_rows, scale, parts),
        [
            sds((tokens, width), BF),
            sds((heads, tokens, aug), BF),
            sds((pairs, 2, tokens), F32),
        ],
        grid=(pairs,),
        in_specs=in_specs + k_specs + v_specs,
        out_specs=[
            pl.BlockSpec((tokens, 128), lambda h: (0, h)),
            pl.BlockSpec((2, tokens, aug), lambda h: (h, 0, 0)),
            pl.BlockSpec((1, 2, tokens), lambda h: (h, 0, 0)),
        ],
        scratch=[
            pltpu.VMEM((keys, aug), BF),
            pltpu.VMEM((keys, 128), BF),
            pltpu.VMEM((keys, 256), BF),
            pltpu.VMEM((128, tokens), F32),
            pltpu.VMEM((keys, 256), F32),
        ],
        flops=25e9,
        name="attend",
    )(first, qkv_own, tw, tr, oh1, oh2, *k_args, *v_args)


def mlp_kernel(
    x_ref, o_ref, wp_ref, w1_ref, b1_ref, w2_ref, p_ref, x1_ref, g_ref, gp_ref, y_ref, n2_ref, acc_ref,
    hidden_ref,
):
    step = pl.program_id(0)
    tokens = x_ref.shape[0]

    @pl.when(step == 0)
    def _():
        product = mm(o_ref[...], wp_ref[...])
        acc_ref[...] = product

        def norm(sl, carry):
            middle = x_ref[sl, :].astype(F32) + (acc_ref[sl, :] + p_ref[6:7, :])
            x1_ref[sl, :] = middle
            acc_ref[sl, :] = jnp.zeros_like(middle)
            hat, _ = stats(middle)
            n2_ref[sl, :] = (hat * p_ref[1:2, :] + p_ref[3:4, :]).astype(BF)

        by_chunks(tokens, 32, norm)

    hidden_ref[...] = mm(n2_ref[...], w1_ref[...])

    def act(sl, carry):
        value, slope = gelu_pair(hidden_ref[sl, :] + b1_ref[...])
        g_ref[sl, :] = value.astype(BF)
        gp_ref[sl, :] = slope.astype(BF)

    by_chunks(tokens, 32, act)
    acc_ref[...] += mm(g_ref[...], w2_ref[...])

    @pl.when(step == pl.num_programs(0) - 1)
    def _():
        y_ref[...] = (x1_ref[...] + (acc_ref[...] + p_ref[7:8, :])).astype(BF)


def mlp_call(tokens, attended, wp, w1, b1, w2, p768):
    rows, width = tokens.shape
    hidden = w1.shape[1]
    return call(
        mlp_kernel,
        [sds((rows, width), F32), sds((rows, hidden), BF), sds((rows, hidden), BF), sds((rows, width), BF)],
        grid=(hidden // width,),
        in_specs=[
            whole((rows, width)),
            whole((rows, width)),
            whole(wp.shape),
            pl.BlockSpec((width, width), lambda s: (0, s)),
            pl.BlockSpec((1, width), lambda s: (0, s)),
            pl.BlockSpec((width, width), lambda s: (s, 0)),
            whole(p768.shape),
        ],
        out_specs=[
            whole((rows, width)),
            pl.BlockSpec((rows, width), lambda s: (0, s)),
            pl.BlockSpec((rows, width), lambda s: (0, s)),
            whole((rows, width)),
        ],
        scratch=[
            pltpu.VMEM((rows, width), BF),
            pltpu.VMEM((rows, width), F32),
            pltpu.VMEM((rows, width), F32),
        ],
        flops=14e9,
        name="mlp",
    )(tokens, attended, wp, w1, b1, w2, p768)


def pool_matrix(a, b, rows, cols):
    count = rows * cols // 4
    out_at = lax.broadcasted_iota(jnp.int32, (count, rows * cols), 0)
    in_at = lax.broadcasted_iota(jnp.int32, (count, rows * cols), 1)
    half = cols // 2
    source = (2 * lax.div(out_at, half) + a) * cols + 2 * lax.rem(out_at, half) + b
    return jnp.where(in_at == source, 1.0, 0.0).astype(BF)


def lateral_norm(product_ref, count, gain, shift, write):
    def norm(sl, carry):
        hat, _ = stats(product_ref[sl, :])
        write(sl, (hat * gain + shift).astype(BF))

    by_chunks(count, 64, norm)


def pyramid_kernel(
    lr, cols, y_ref, ff_ref, fs_ref, mu_ref, lf_ref, lm_ref, lc0_ref, lc1_ref, p384_ref, fsb_ref, p256_ref,
    zf_ref, zm_ref, zb_ref, zc_ref, plane_ref, mplane_ref, f2_ref, first_ref, product_ref,
    third_ref, stack_ref,
):
    tokens = lr * cols
    half = mu_ref.shape[1] // 2
    quart = fs_ref.shape[0] // 4

    def offset(b, carry):
        columns = pl.ds(pl.multiple_of(b * half, half), half)
        first_ref[...] = mm(y_ref[...], ff_ref[:, columns])

        def norm(sl, inner):
            hat, _ = stats(first_ref[sl, :] + p384_ref[0:1, :])
            value = hat * p384_ref[1:2, :] + p384_ref[2:3, :]
            f2_ref[sl, :] = (0.5 * value * (1.0 + lax.erf(value * SQRT_HALF))).astype(BF)

        by_chunks(tokens, 64, norm)

        for k in range(4):
            third_ref[k * tokens : (k + 1) * tokens, :] = (
                mt(f2_ref[...], fs_ref[k * quart : (k + 1) * quart, :]) + fsb_ref[...]
            ).astype(BF)
        stack_ref[...] = mm(third_ref[...], lf_ref[...])
        for k in range(4):

            def write(sl, values):
                plane_ref[k // 2, 2 * b + k % 2, sl, :] = values

            part = stack_ref.at[k * tokens : (k + 1) * tokens]
            lateral_norm(part, tokens, p256_ref[0:1, :], p256_ref[8:9, :], write)
        middle = (mm(y_ref[...], mu_ref[:, columns]) + p384_ref[3:4, :]).astype(BF)
        product_ref[...] = mm(middle, lm_ref[...])

        def write_middle(sl, values):
            mplane_ref[b, sl, :] = values

        lateral_norm(product_ref, tokens, p256_ref[1:2, :], p256_ref[9:10, :], write_middle)
        return carry

    repeat(2, offset)
    weave4 = weave_matrix(4 * cols, 4)
    weave2 = weave_matrix(2 * cols, 2)

    def weave(i, carry):
        sl = pl.ds(pl.multiple_of(i * cols, cols), cols)
        for c in (0, 1):
            planes = jnp.concatenate([plane_ref[c, k, sl, :] for k in range(4)], axis=0)
            zf_ref[i, c] = mm(weave4, planes).astype(BF)
        planes = jnp.concatenate([mplane_ref[k, sl, :] for k in range(2)], axis=0)
        zm_ref[i, 0] = mm(weave2, planes).astype(BF)
        return carry

    repeat(lr, weave)

    @pl.when(pl.program_id(0) == 0)
    def _():
        product_ref[...] = mm(y_ref[...], lc0_ref[...])

        def write_base(sl, values):
            zb_ref[sl, :] = values

        lateral_norm(product_ref, tokens, p256_ref[2:3, :], p256_ref[10:11, :], write_base)
        pooled = pool_picks(y_ref, pick_ref=None, rows=lr, cols=cols)
        product_ref[0 : tokens // 4, :] = mm(pooled.astype(BF), lc1_ref[...])

        def write_coarse(sl, values):
            zc_ref[sl, :] = values

        lateral_norm(product_ref, tokens // 4, p256_ref[3:4, :], p256_ref[11:12, :], write_coarse)


def pool_picks(y_ref, pick_ref, rows, cols):
    def pick(k, top):
        values = mm(pool_matrix(k // 2, k % 2, rows, cols), y_ref[...])
        if pick_ref is not None:
            pick_ref[k] = values
        return jnp.maximum(top, values)

    low = jnp.full((rows * cols // 4, y_ref.shape[1]), -jnp.inf, F32)
    for k in range(4):
        low = pick(k, low)
    return low


def pyramid_call(y, lr, cols, ff, fs, mu, lf, lm, lc0, lc1, p384, fsb, p256):
    tokens, width = y.shape
    outs = lf.shape[1]
    half2 = ff.shape[1] // 2
    return call(
        functools.partial(pyramid_kernel, lr, cols),
        [
            sds((lr, 4, 4 * cols, outs), BF),
            sds((lr, 2, 2 * cols, outs), BF),
            sds((tokens, outs), BF),
            sds((tokens // 4, outs), BF),
        ],
        grid=(2,),
        in_specs=[
            whole(y.shape),
            pl.BlockSpec((width, half2), lambda a: (0, a)),
            whole(fs.shape),
            pl.BlockSpec((width, half2), lambda a: (0, a)),
            whole(lf.shape),
            whole(lm.shape),
            whole(lc0.shape),
            whole(lc1.shape),
            whole(p384.shape),
            whole(fsb.shape),
            whole(p256.shape),
        ],
        out_specs=[
            pl.BlockSpec((lr, 2, 4 * cols, outs), lambda a: (0, a, 0, 0)),
            pl.BlockSpec((lr, 1, 2 * cols, outs), lambda a: (0, a, 0, 0)),
            whole((tokens, outs)),
            whole((tokens // 4, outs)),
        ],
        scratch=[
            pltpu.VMEM((2, 4, tokens, outs), BF),
            pltpu.VMEM((2, tokens, outs), BF),
            pltpu.VMEM((tokens, half2 // 2), BF),
            pltpu.VMEM((tokens, half2 // 2), F32),
            pltpu.VMEM((tokens, outs), F32),
            pltpu.VMEM((4 * tokens, fs.shape[0] // 4), BF),
            pltpu.VMEM((4 * tokens, outs), F32),
        ],
        flops=20e9,
        name="pyramid",
    )(y, ff, fs, mu, lf, lm, lc0, lc1, p384, fsb, p256)


def fill_padded(step, block, src_ref, rim_ref, pad_ref, left, right):
    rows, cols, chan = src_ref.shape

    @pl.when(step == 0)
    def _():
        pad_ref[0, :, chan : 2 * chan] = rim_ref[0]
        pad_ref[rows + 1, :, chan : 2 * chan] = rim_ref[1]

        def copy(row, carry):
            pad_ref[row + 1, :, chan : 2 * chan] = src_ref[row]
            return carry

        lax.fori_loop(0, rows, copy, 0)

    def move(at):
        row = pad_ref[at, :, chan : 2 * chan]
        pad_ref[at, :, 0:chan] = mm(left, row).astype(BF)
        pad_ref[at, :, 2 * chan :] = mm(right, row).astype(BF)

    start = step * block
    group = min(block, MOVE_ROWS)

    @pl.when(step == 0)
    def _():
        move(0)
        move(1)

    def move_group(k, carry):
        for q in range(group):
            move(start + 2 + k * group + q)
        return carry

    lax.fori_loop(0, block // group, move_group, 0)


def conv_kernel(level, block, z_ref, rim_ref, w_ref, cot_ref, p_ref, *refs):
    map_ref, dr_ref, dw_ref, sums_ref, pad_ref, dwt_ref, gradt_ref = refs[-7:]
    step = pl.program_id(0)
    rows, cols, chan = z_ref.shape
    fill_padded(
        step, block, z_ref, rim_ref, pad_ref, shift_matrix(cols, -1), shift_matrix(cols, 1)
    )
    gain = p_ref[4 + level : 5 + level, :]
    shift = p_ref[12 + level : 13 + level, :]
    few = min(block, max(1, (CONV_PIXELS if rows * cols > 4096 else CONV_PIXELS // 2) // cols))
    pixels = few * cols

    @pl.when(step == 0)
    def _():
        sums_ref[...] = jnp.zeros_like(sums_ref)
        dwt_ref[...] = jnp.zeros_like(dwt_ref)

    def forward(k, carry):
        sum_gain, sum_shift = carry
        row = step * block + k * few
        result = None
        for a in range(3):
            part = mm(pad_ref[pl.ds(row + a, few)].reshape(pixels, 3 * chan), w_ref[0, a])
            result = part if result is None else result + part
        base = pl.multiple_of(k * pixels, pixels)
        for q in range(0, pixels, 64):
            sl = pl.ds(base + q, 64)
            hat, inverse = stats(result[q : q + 64])
            map_ref[sl, :] = (hat * gain + shift).astype(BF)
            cot = cot_ref[sl, :].astype(F32)
            sum_gain = sum_gain + rowsum(cot * hat)
            sum_shift = sum_shift + rowsum(cot)
            dr_ref[sl, :] = norm_back(cot * gain, hat, inverse).astype(BF)
        gradt_ref[:, pl.ds(base, pixels)] = dr_ref[pl.ds(base, pixels), :].T
        return sum_gain, sum_shift

    zero = jnp.zeros((1, chan), F32)
    sum_gain, sum_shift = lax.fori_loop(0, block // few, forward, (zero, zero))
    sums_ref[0:1, :] += sum_gain
    sums_ref[1:2, :] += sum_shift

    def add_grad(k, carry):
        a, b = lax.div(k, 3), lax.rem(k, 3)
        lanes = pl.ds(pl.multiple_of(b * chan, chan), chan)
        window = pad_ref[pl.ds(step * block + a, block), :, lanes].reshape(block * cols, chan)
        dwt_ref[k] += mm(gradt_ref[...], window)
        return carry

    lax.fori_loop(0, 9, add_grad, 0)

    @pl.when(step == pl.num_programs(0) - 1)
    def _():
        def turn(k, carry):
            dw_ref[pl.ds(pl.multiple_of(k * chan, chan), chan), :] = dwt_ref[k].T.astype(BF)
            return carry

        lax.fori_loop(0, 9, turn, 0)


def conv_call(level, z, rims, weights, cot, p256, block, packed):
    rows, cols, chan = z.shape
    before = [] if packed is None else [packed]
    spec = pl.BlockSpec((block * cols, chan), lambda s: (s, 0))
    return call(
        functools.partial(conv_kernel, level, block),
        [
            sds((rows * cols, chan), BF),
            sds((rows * cols, chan), BF),
            sds((9 * chan, 4 * chan), BF),
            sds((8, chan), F32),
        ],
        grid=(rows // block,),
        in_specs=[
            whole(z.shape),
            whole(rims.shape),
            pl.BlockSpec((1, 3, 3 * chan, chan), lambda s: (level, 0, 0, 0)),
            spec,
            whole(p256.shape),
        ]
        + [pl.BlockSpec(memory_space=pl.ANY)] * len(before),
        out_specs=[
            spec,
            spec,
            pl.BlockSpec((9 * chan, chan), lambda s: (0, level)),
            whole((8, chan)),
        ],
        scratch=[
            pltpu.VMEM((rows + 2, cols, 3 * chan), BF),
            pltpu.VMEM((9, chan, chan), F32),
            pltpu.VMEM((chan, block * cols), BF),
        ],
        flops=5 * 9 * rows * cols * chan * chan,
        name=f"conv{level}",
        aliases={5: 2} if before else {},
    )(z, rims, weights, cot.reshape(rows * cols, chan), p256, *before)


def conv_back_kernel(ways, block, dr_ref, rim_ref, w_ref, dz_ref, pad_ref):
    step = pl.program_id(0)
    rows, cols, chan = dr_ref.shape
    fill_padded(
        step, block, dr_ref, rim_ref, pad_ref, shift_matrix(cols, 1), shift_matrix(cols, -1)
    )
    few = min(block, max(1, BACK_PIXELS // cols))
    pixels = few * cols
    base = cols // ways
    unweave = weave_matrix(cols, ways, inverse=True)

    def back(k, carry):
        row = step * block + k * few
        result = None
        for a in range(3):
            for b in range(3):
                window = pad_ref[pl.ds(row + 2 - a, few), :, b * chan : (b + 1) * chan]
                part = mt(
                    window.reshape(pixels, chan), w_ref[0, a, b * chan : (b + 1) * chan, :]
                )
                result = part if result is None else result + part
        low = result.astype(BF)
        if ways == 1:
            dz_ref[pl.ds(pl.multiple_of(k * pixels, pixels), pixels), :] = low
            return carry
        for q in range(few):
            planes = mm(unweave, low[q * cols : (q + 1) * cols]).astype(BF)
            inner = k * few + q
            at = pl.ds(pl.multiple_of(lax.div(inner, ways) * base, base), base)
            for w in range(ways):
                dz_ref[lax.rem(inner, ways), w, at, :] = planes[w * base : (w + 1) * base]
        return carry

    lax.fori_loop(0, block // few, back, 0)


def conv_back_call(level, dr, rims, weights, ways, block):
    rows, cols, chan = dr.shape
    if ways == 1:
        out = sds((rows * cols, chan), BF)
        spec = pl.BlockSpec((block * cols, chan), lambda s: (s, 0))
    else:
        tokens = rows * cols // (ways * ways)
        out = sds((ways, ways, tokens, chan), BF)
        spec = pl.BlockSpec(
            (ways, ways, block * cols // (ways * ways), chan), lambda s: (0, 0, s, 0)
        )
    return call(
        functools.partial(conv_back_kernel, ways, block),
        out,
        grid=(rows // block,),
        in_specs=[
            whole(dr.shape),
            whole(rims.shape),
            pl.BlockSpec((1, 3, 3 * chan, chan), lambda s: (level, 0, 0, 0)),
        ],
        out_specs=spec,
        scratch=[pltpu.VMEM((rows + 2, cols, 3 * chan), BF)],
        flops=3 * 9 * rows * cols * chan * chan,
        name=f"conv_back{level}",
    )(dr, rims, weights)


def lateral_back(product_ref, count, read, gain, dl_ref):
    zero = jnp.zeros((1, product_ref.shape[1]), F32)

    def chunk(sl, carry):
        hat, inverse = stats(product_ref[sl, :])
        grad = read(sl)
        dl_ref[sl, :] = norm_back(grad * gain, hat, inverse).astype(BF)
        return carry[0] + rowsum(grad * hat), carry[1] + rowsum(grad)

    return by_chunks(count, 64, chunk, (zero, zero))


def pyramid_back_kernel(
    lr, cols, y_ref, ff_ref, fs_ref, mu_ref, lf_ref, lm_ref, lc0_ref, lc1_ref, p384_ref,
    fsb_ref, p256_ref, dzf_ref, dzm_ref, dzb_ref, dzc_ref, place_ref,
    dy_ref, pack_ref, s384_ref, s192_ref, s256_ref,
    yt_ref, hat_ref, slope_ref, inv_ref, f2_ref, df2_ref, df1_ref, dl_ref, fs_acc, lf_acc, lm_acc,
    dcol_ref, drest_ref, product_ref, pick_ref, third_ref, stack_ref, dls_ref, sem,
):
    step = pl.program_id(0)
    tokens = lr * cols
    quart = fs_ref.shape[0] // 4
    half = ff_ref.shape[1]
    chan = lf_ref.shape[1]

    rest = drest_ref.shape[1]

    def col_copy(at):
        lanes = pl.ds(pl.multiple_of(at * 2 * half, 2 * half), 2 * half)
        return pltpu.make_async_copy(dcol_ref.at[at], pack_ref.at[:, lanes], sem.at[at])

    rest_copy = pltpu.make_async_copy(drest_ref, pack_ref.at[:, pl.ds(8 * half, rest)], sem.at[4])

    @pl.when(step == 0)
    def _():
        yt_ref[...] = y_ref[...].T
        for ref in (fs_acc, lf_acc, lm_acc, s384_ref, s192_ref, s256_ref):
            ref[...] = jnp.zeros_like(ref)
        product_ref[...] = mm(y_ref[...], lc0_ref[...])
        sg, ss = lateral_back(
            product_ref, tokens, lambda sl: dzb_ref[sl, :].astype(F32), p256_ref[2:3, :], dl_ref
        )
        s256_ref[2:3, :] = sg
        s256_ref[10:11, :] = ss
        drest_ref[:, half : half + chan] = mm(yt_ref[...], dl_ref[...]).astype(BF)
        dy_ref[...] = mt(dl_ref[...], lc0_ref[...])
        top = pool_picks(y_ref, pick_ref, lr, cols)
        low = top.astype(BF)
        product_ref[0 : tokens // 4, :] = mm(low, lc1_ref[...])
        sg, ss = lateral_back(
            product_ref, tokens // 4, lambda sl: dzc_ref[sl, :].astype(F32), p256_ref[3:4, :], dl_ref
        )
        s256_ref[3:4, :] = sg
        s256_ref[11:12, :] = ss
        grad = dl_ref[0 : tokens // 4, :]
        drest_ref[:, half + chan : half + 2 * chan] = tm(low, grad).astype(BF)
        dtop = mt(grad, lc1_ref[...])
        hits = jnp.zeros_like(top)
        for k in range(4):
            hits = hits + jnp.where(pick_ref[k] == top, 1.0, 0.0)
        dtop = dtop / hits

        def share_out(k, carry):
            share = jnp.where(pick_ref[k] == top, dtop, 0.0)
            upper = share.astype(BF)
            lower = (share - upper.astype(F32)).astype(BF)
            spread = pool_matrix(k // 2, k % 2, lr, cols)
            dy_ref[...] += tm(spread, upper) + tm(spread, lower)
            return carry

        repeat(4, share_out)

    df2_ref[...] = mm(y_ref[...], ff_ref[...])

    def norm(sl, carry):
        hat, inverse = stats(df2_ref[sl, :] + p384_ref[0:1, :])
        hat_ref[sl, :] = hat
        inv_ref[sl, :] = jnp.broadcast_to(inverse, (64, 128))
        value, slope = gelu_pair(hat * p384_ref[1:2, :] + p384_ref[2:3, :])
        f2_ref[sl, :] = value.astype(BF)
        slope_ref[sl, :] = slope
        df2_ref[sl, :] = jnp.zeros_like(hat)

    by_chunks(tokens, 64, norm)

    for k in range(4):
        third_ref[k * tokens : (k + 1) * tokens, :] = (
            mt(f2_ref[...], fs_ref[k * quart : (k + 1) * quart, :]) + fsb_ref[...]
        ).astype(BF)
    stack_ref[...] = mm(third_ref[...], lf_ref[...])
    for k in range(4):
        sg, ss = lateral_back(
            stack_ref.at[k * tokens : (k + 1) * tokens],
            tokens,
            lambda sl: dzf_ref[0, k // 2, 0, k % 2, sl, :].astype(F32),
            p256_ref[0:1, :],
            dls_ref.at[k * tokens : (k + 1) * tokens],
        )
        s256_ref[0:1, :] += sg
        s256_ref[8:9, :] += ss
    lf_acc[...] += tm(third_ref[...], dls_ref[...])
    third_ref[...] = mt(dls_ref[...], lf_ref[...]).astype(BF)
    s192_ref[0:1, :] += rowsum(third_ref[...].astype(F32))
    for k in range(4):
        rows = slice(k * quart, (k + 1) * quart)
        fs_acc[rows, :] += tm(third_ref[k * tokens : (k + 1) * tokens, :], f2_ref[...])
        df2_ref[...] += mm(third_ref[k * tokens : (k + 1) * tokens, :], fs_ref[rows, :])
    zero = jnp.zeros((1, half), F32)

    def first_back(sl, carry):
        sum_gain, sum_shift, sum_bias = carry
        hat = hat_ref[sl, :]
        grad = df2_ref[sl, :] * slope_ref[sl, :]
        low = norm_back(grad * p384_ref[1:2, :], hat, inv_ref[sl, 0:1]).astype(BF)
        df1_ref[sl, :] = low
        return (
            sum_gain + rowsum(grad * hat),
            sum_shift + rowsum(grad),
            sum_bias + rowsum(low.astype(F32)),
        )

    sum_gain, sum_shift, sum_bias = by_chunks(tokens, 64, first_back, (zero, zero, zero))
    s384_ref[0:1, :] += sum_bias
    s384_ref[1:2, :] += sum_gain
    s384_ref[2:3, :] += sum_shift
    dcol_ref[step, :, 0:half] = mm(yt_ref[...], df1_ref[...]).astype(BF)
    dy_ref[...] += mt(df1_ref[...], ff_ref[...])

    f2_ref[...] = (mm(y_ref[...], mu_ref[...]) + p384_ref[3:4, :]).astype(BF)
    product_ref[...] = mm(f2_ref[...], lm_ref[...])
    sg, ss = lateral_back(
        product_ref, tokens, lambda sl: dzm_ref[0, 0, sl, :].astype(F32), p256_ref[1:2, :], dl_ref
    )
    s256_ref[1:2, :] += sg
    s256_ref[9:10, :] += ss
    lm_acc[...] += tm(f2_ref[...], dl_ref[...])
    df1_ref[...] = mt(dl_ref[...], lm_ref[...]).astype(BF)
    s384_ref[3:4, :] += rowsum(df1_ref[...].astype(F32))
    dcol_ref[step, :, half:] = mm(yt_ref[...], df1_ref[...]).astype(BF)
    col_copy(step).start()
    dy_ref[...] += mt(df1_ref[...], mu_ref[...])

    @pl.when(step == pl.num_programs(0) - 1)
    def _():
        drest_ref[:, 0:half] = fs_acc[...].astype(BF)
        laterals = jnp.concatenate([lf_acc[...], lm_acc[...]], axis=0).astype(BF)
        drest_ref[:, half + 2 * chan : half + 3 * chan] = mm(place_ref[...], laterals).astype(BF)
        rest_copy.start()
        for at in range(4):
            col_copy(at).wait()
        rest_copy.wait()


def pyramid_back_call(
    y, lr, cols, ff, fs, mu, lf, lm, lc0, lc1, p384, fsb, p256, dzf, dzm, dzb, dzc, place
):
    tokens, width = y.shape
    half = fs.shape[1]
    quart = fsb.shape[1]
    outs = lf.shape[1]
    col_block = pl.BlockSpec((width, half), lambda s: (0, s))
    return call(
        functools.partial(pyramid_back_kernel, lr, cols),
        [
            sds((tokens, width), F32),
            sds((width, 9 * half + 3 * outs), BF),
            sds((8, half), F32),
            sds((8, quart), F32),
            sds((16, outs), F32),
        ],
        grid=(4,),
        in_specs=[
            whole(y.shape),
            col_block,
            whole(fs.shape),
            col_block,
            whole(lf.shape),
            whole(lm.shape),
            whole(lc0.shape),
            whole(lc1.shape),
            whole(p384.shape),
            whole(fsb.shape),
            whole(p256.shape),
            pl.BlockSpec((1, 2, 1, 2, tokens, outs), lambda s: (s // 2, 0, s % 2, 0, 0, 0)),
            pl.BlockSpec((1, 1, tokens, outs), lambda s: (s // 2, s % 2, 0, 0)),
            whole(dzb.shape),
            whole(dzc.shape),
            whole(place.shape),
        ],
        out_specs=[
            whole((tokens, width)),
            pl.BlockSpec(memory_space=pl.ANY),
            whole((8, half)),
            whole((8, quart)),
            whole((16, outs)),
        ],
        scratch=[
            pltpu.VMEM((width, tokens), BF),
            pltpu.VMEM((tokens, half), F32),
            pltpu.VMEM((tokens, half), F32),
            pltpu.VMEM((tokens, 128), F32),
            pltpu.VMEM((tokens, half), BF),
            pltpu.VMEM((tokens, half), F32),
            pltpu.VMEM((tokens, half), BF),
            pltpu.VMEM((tokens, outs), BF),
            pltpu.VMEM(fs.shape, F32),
            pltpu.VMEM(lf.shape, F32),
            pltpu.VMEM(lm.shape, F32),
            pltpu.VMEM((4, width, 2 * half), BF),
            pltpu.VMEM((width, half + 3 * outs), BF),
            pltpu.VMEM((tokens, outs), F32),
            pltpu.VMEM((4, tokens // 4, width), F32),
            pltpu.VMEM((4 * tokens, quart), BF),
            pltpu.VMEM((4 * tokens, outs), F32),
            pltpu.VMEM((4 * tokens, outs), BF),
            pltpu.SemaphoreType.DMA((5,)),
        ],
        flops=45e9,
        name="pyramid_back",
    )(
        y, ff, fs, mu, lf, lm, lc0, lc1, p384, fsb, p256,
        dzf.reshape(2, 2, 2, 2, tokens, outs), dzm, dzb, dzc, place,
    )


def mlp_back_kernel(
    shards,
    core_ref, dy_ref, g_ref, gp_ref, w1_ref, w2_ref, x1_ref, o_ref, wp_ref, p_ref, s384_ref, s192_ref, s256_ref, levels_ref,
    hot256_ref, hot384_ref, hot192_ref,
    keep_ref, send_ref, keep2_ref, send2_ref, dx1_ref, do_ref,
    n2t_ref, d2_ref, dn2_ref, low_ref, sums_ref, vec_ref, dw1_ref, dw2_ref, rest_ref, temp_ref, sem,
):
    step = pl.program_id(0)
    steps = pl.num_programs(0)
    tokens, width = dy_ref.shape
    unit = width // shards
    hidden = 4 * width

    core = core_ref[0]

    @pl.when(step == 0)
    def _():
        sums_ref[...] = jnp.zeros_like(sums_ref)
        vec_ref[...] = jnp.zeros_like(vec_ref)
        dn2_ref[...] = jnp.zeros_like(dn2_ref)

        def norm(sl, total):
            hat, _ = stats(x1_ref[sl, :])
            low_ref[sl, :] = (hat * p_ref[1:2, :] + p_ref[3:4, :]).astype(BF)
            low = dy_ref[sl, :].astype(BF)
            d2_ref[sl, :] = low
            return total + rowsum(low.astype(F32))

        sums_ref[7:8, :] = by_chunks(tokens, 32, norm, jnp.zeros((1, width), F32))
        n2t_ref[...] = low_ref[...].T

    dw2_ref[step] = tm(g_ref[...], d2_ref[...]).astype(BF)
    put_shards(
        dw2_ref.at[step], keep2_ref, send2_ref, pl.ds(0, width), shards // 4, step * (shards // 4), core,
        sem.at[5 + step],
    )
    temp_ref[...] = mt(d2_ref[...], w2_ref[...])

    def act(sl, carry):
        low_ref[sl, :] = (temp_ref[sl, :] * gp_ref[sl, :].astype(F32)).astype(BF)

    by_chunks(tokens, 32, act)
    db1 = tm(low_ref[...], jnp.ones((tokens, 128), BF))
    lane = lax.broadcasted_iota(jnp.int32, (unit, 128), 1)
    for q in range(shards // 4):
        entry = jnp.zeros((unit, 128), F32)
        for k in range(4):
            sl = slice((4 * q + k) * unit, (4 * q + k + 1) * unit)
            entry = jnp.where(lane == 40 + k, db1[sl], entry)
        vec_ref[pl.ds(pl.multiple_of(step * (width // 4) + q * unit, 8), unit), :] += entry
    dw1_ref[step] = mm(n2t_ref[...], low_ref[...]).astype(BF)
    lanes = pl.ds(pl.multiple_of(step * width, width), width)
    put_shards(dw1_ref.at[step], keep_ref, send_ref, lanes, shards, 0, core, sem.at[step])
    dn2_ref[...] += mt(low_ref[...], w1_ref[...])

    @pl.when(step == steps - 1)
    def _():
        zero = jnp.zeros((1, width), F32)

        def back(sl, carry):
            hat, inverse = stats(x1_ref[sl, :])
            grad = dn2_ref[sl, :]
            dx1 = dy_ref[sl, :] + norm_back(grad * p_ref[1:2, :], hat, inverse)
            dx1_ref[sl, :] = dx1
            low = dx1.astype(BF)
            d2_ref[sl, :] = low
            return (
                carry[0] + rowsum(grad * hat),
                carry[1] + rowsum(grad),
                carry[2] + rowsum(low.astype(F32)),
            )

        sum_gain, sum_shift, sum_bias = by_chunks(tokens, 32, back, (zero, zero, zero))
        sums_ref[1:2, :] = sum_gain
        sums_ref[3:4, :] = sum_shift
        sums_ref[6:7, :] = sum_bias
        rest_ref[:, 0:width] = tm(o_ref[...], d2_ref[...]).astype(BF)
        do_ref[...] = mt(d2_ref[...], wp_ref[...]).astype(BF)

        def lanes_of(rows, before):
            after = 128 - before - rows.shape[0]
            parts = [jnp.zeros((before, rows.shape[1]), F32)] if before else []
            parts += [rows, jnp.zeros((after, rows.shape[1]), F32)]
            return jnp.concatenate(parts, axis=0)

        spread = mt(hot256_ref[...], lanes_of(s256_ref[...], 8).astype(BF))
        spread = spread + mt(hot256_ref[...], lanes_of(levels_ref[...], 24).astype(BF))
        spread = spread + mt(hot384_ref[...], lanes_of(s384_ref[...], 32).astype(BF))
        spread = spread + mt(hot192_ref[...], lanes_of(s192_ref[...], 48).astype(BF))
        spread = spread + lanes_of(sums_ref[...], 0).T
        rest_ref[:, width:] = (vec_ref[...] + spread).astype(BF)
        put_shards(
            rest_ref, keep_ref, send_ref, pl.ds(hidden, width + 128), shards, 0, core, sem.at[4]
        )
        for at in range(4):
            wait_shards(dw1_ref.at[at], sem.at[at])
            wait_shards(dw2_ref.at[at], sem.at[5 + at])
        wait_shards(rest_ref, sem.at[4])


def mlp_back_call(
    dy, g, gp, w1, w2, x1, attended, wp, p768, s384, s192, s256, levels, hots, core, shards
):
    rows, width = dy.shape
    hidden = g.shape[1]
    full = whole((rows, width))
    column = pl.BlockSpec((rows, width), lambda s: (0, s))
    smalls = [p768, s384, s192, s256, levels, *hots]
    return call(
        functools.partial(mlp_back_kernel, shards),
        [
            sds((width // 2, hidden + width + 128), BF),
            sds((width // 2, hidden + width + 128), BF),
            sds((hidden // 2, width), BF),
            sds((hidden // 2, width), BF),
            sds((rows, width), F32),
            sds((rows, width), BF),
        ],
        grid=(hidden // width,),
        in_specs=[
            pl.BlockSpec(memory_space=pltpu.SMEM),
            full,
            column,
            column,
            pl.BlockSpec((width, width), lambda s: (0, s)),
            pl.BlockSpec((width, width), lambda s: (s, 0)),
            full,
            full,
            whole((width, width)),
        ]
        + [whole(a.shape) for a in smalls],
        out_specs=[
            pl.BlockSpec(memory_space=pl.ANY),
            pl.BlockSpec(memory_space=pl.ANY),
            pl.BlockSpec(memory_space=pl.ANY),
            pl.BlockSpec(memory_space=pl.ANY),
            full,
            full,
        ],
        scratch=[
            pltpu.VMEM((width, rows), BF),
            pltpu.VMEM((rows, width), BF),
            pltpu.VMEM((rows, width), F32),
            pltpu.VMEM((rows, width), BF),
            pltpu.VMEM((8, width), F32),
            pltpu.VMEM((width, 128), F32),
            pltpu.VMEM((4, width, width), BF),
            pltpu.VMEM((4, width, width), BF),
            pltpu.VMEM((width, width + 128), BF),
            pltpu.VMEM((rows, width), F32),
            pltpu.SemaphoreType.DMA((9,)),
        ],
        flops=25e9,
        name="mlp_back",
    )(core, dy, g, gp, w1, w2, x1, attended, wp, *smalls)


def roll_back(values, amount):
    moved = jnp.concatenate(
        [
            pltpu.roll(values[8 * g : 8 * g + 8], (amount - 7 - 8 * g) % 128, 1)
            for g in range(values.shape[0] // 8)
        ],
        axis=0,
    )
    left = 7 - lax.rem(lax.broadcasted_iota(jnp.int32, values.shape, 0), 8)
    for step in (1, 2, 4):
        moved = jnp.where((left & step) > 0, pltpu.roll(moved, step, 1), moved)
    return moved


def attend_back_kernel(total_rows, scale, others, *refs):
    first_ref, q_ref, qaug_ref, do_ref, o_ref, lse_ref, tab_ref, oh1_ref, oh2_ref, before_ref = refs[:10]
    k_refs = refs[10 : 10 + others]
    v_refs = refs[10 + others : 10 + 2 * others]
    rest = refs[-15:]
    (
        dqkv_ref, dtab_ref, kaug_ref, v_ref, p_ref, ds_ref, dqt_ref, df_ref, qm_ref, dom_ref, delta_ref,
        scores_ref, dweight_ref, dk_acc, dv_acc,
    ) = rest
    first_row = first_ref[0]
    tokens = q_ref.shape[0]
    keys = kaug_ref.shape[0]

    @pl.when(pl.program_id(0) == 0)
    def _():
        kaug_ref[:, 128:] = oh2_ref[...]
        dtab_ref[...] = before_ref[...]

    at = 0
    for ref in v_refs:
        v_ref[at : at + ref.shape[0], :] = ref[...]
        at += ref.shape[0]
    lane_all = lax.broadcasted_iota(jnp.int32, (tokens, 128), 1)
    lane = lax.broadcasted_iota(jnp.int32, (64, 128), 1)
    qf = q_ref[...].astype(F32)
    dof = do_ref[...].astype(F32)
    delta_t = (dof * o_ref[...].astype(F32)).T
    dk_acc[...] = jnp.zeros_like(dk_acc)
    dv_acc[...] = jnp.zeros_like(dv_acc)
    dq = None
    for odd in (0, 1):
        mine_all = (lane_all >= 64) if odd else (lane_all < 64)
        other = (lane < 64) if odd else (lane >= 64)
        build_kaug(kaug_ref, k_refs, oh1_ref, oh2_ref, odd)
        qm = jnp.where(mine_all, qf, 0.0).astype(BF)
        dom = jnp.where(mine_all, dof, 0.0).astype(BF)
        delta = rowsum(delta_t[64 * odd : 64 * odd + 64])
        qm_ref[...] = qm
        dom_ref[...] = dom
        delta_ref[...] = delta

        def queries(t, carry):
            sl = pl.ds(pl.multiple_of(t * 256, 256), 256)
            scores_ref[...] = mt(kaug_ref[...], qaug_ref[odd, sl, :])
            dweight_ref[...] = mt(v_ref[...], dom_ref[sl, :])
            lse = lse_ref[0, odd : odd + 1, sl]
            shift = delta_ref[:, sl]

            def weigh(rows, inner):
                weight = jnp.exp(scores_ref[rows, :] - lse)
                p_ref[rows, :] = weight.astype(BF)
                ds_ref[rows, :] = (weight * (dweight_ref[rows, :] - shift)).astype(BF)

            by_chunks(keys, 128, weigh)
            dk_acc[...] += mm(ds_ref[...], qm_ref[sl, :])
            dv_acc[...] += mm(p_ref[...], dom_ref[sl, :])
            dqt_ref[:, sl] = tm(kaug_ref[...], ds_ref[...])
            return carry

        repeat(tokens // 256, queries)
        dqa = dqt_ref[0:256, :].T
        for i in range(tokens // 64):
            sl = slice(64 * i, 64 * i + 64)
            cols = roll_back(jnp.where(other, dqa[sl, 0:128], 0.0), 63 if odd else 127)
            shift = lax.rem(63 + total_rows - (first_row + i) + 128, 128)
            rows = pltpu.roll(
                jnp.where((lane >= 64) & (lane < 64 + total_rows), dqa[sl, 128:256], 0.0), shift, 1
            )
            df_ref[sl, 0:128] = cols.astype(BF)
            df_ref[sl, 128:256] = rows.astype(BF)
        from_tables = mt(df_ref[...], tab_ref[...])
        part = jnp.where(mine_all, dqa[:, 0:128] * scale + from_tables, 0.0)
        dq = part if dq is None else dq + part
        dtab_ref[...] += tm(qm, df_ref[...])
    dqkv_ref[0, 0:tokens, :] = dq.astype(BF)
    dqkv_ref[1] = (dk_acc[...] * scale).astype(BF)
    dqkv_ref[2] = dv_acc[...].astype(BF)


def attend_back_call(
    first, qkv_own, kv_others, qaug, dout, attended, lse, tab, oh1, oh2, dtab, total_rows, heads, part, parts, grads
):
    tokens = qkv_own.shape[0]
    width = qkv_own.shape[1] // 3
    keys = oh1.shape[0]
    aug = 128 + oh2.shape[1]
    pairs = width // 128
    count = pairs // parts
    base = part * count
    sources = 1 + (1 if kv_others is not None else 0)
    own = pl.BlockSpec((tokens, 128), lambda h: (0, h + base))
    in_specs = [
        pl.BlockSpec(memory_space=pltpu.SMEM),
        own,
        pl.BlockSpec((2, tokens, aug), lambda h: (h + base, 0, 0)),
        own,
        own,
        pl.BlockSpec((1, 2, tokens), lambda h: (h + base, 0, 0)),
        whole(tab.shape),
        whole(oh1.shape),
        whole(oh2.shape),
        whole(dtab.shape),
    ]
    k_args, v_args, k_specs, v_specs = [qkv_own], [qkv_own], [], []
    k_specs.append(pl.BlockSpec((tokens, 128), lambda h: (0, h + base + pairs)))
    v_specs.append(pl.BlockSpec((tokens, 128), lambda h: (0, h + base + 2 * pairs)))
    if kv_others is not None:
        k_args.append(kv_others)
        v_args.append(kv_others)
        k_specs.append(pl.BlockSpec((keys - tokens, 128), lambda h: (0, h + base)))
        v_specs.append(pl.BlockSpec((keys - tokens, 128), lambda h: (0, h + base + pairs)))
    scale = (width // heads) ** -0.5
    earlier = [] if grads is None else [grads]
    return call(
        functools.partial(attend_back_kernel, total_rows, scale, sources),
        [sds((3, keys, width), BF), sds((128, 256), F32)],
        grid=(count,),
        in_specs=in_specs + k_specs + v_specs + [pl.BlockSpec(memory_space=pl.ANY)] * len(earlier),
        out_specs=[pl.BlockSpec((3, keys, 128), lambda h: (0, 0, h + base)), whole((128, 256))],
        scratch=[
            pltpu.VMEM((keys, aug), BF),
            pltpu.VMEM((keys, 128), BF),
            pltpu.VMEM((keys, 256), BF),
            pltpu.VMEM((keys, 256), BF),
            pltpu.VMEM((aug, tokens), F32),
            pltpu.VMEM((tokens, 256), BF),
            pltpu.VMEM((tokens, 128), BF),
            pltpu.VMEM((tokens, 128), BF),
            pltpu.VMEM((1, tokens), F32),
            pltpu.VMEM((keys, 256), F32),
            pltpu.VMEM((keys, 256), F32),
            pltpu.VMEM((keys, 128), F32),
            pltpu.VMEM((keys, 128), F32),
        ],
        flops=30e9 / parts,
        name="attend_back",
        aliases={10 + 2 * sources: 0} if earlier else {},
    )(first, qkv_own, qaug, dout, attended, lse, tab, oh1, oh2, dtab, *k_args, *v_args, *earlier)


def qkv_back_kernel(
    x_ref, dqkv_ref, w_ref, dx1_ref, p_ref, dtab_ref, hot_ref,
    pack_ref, dx_ref, far_ref, nt_ref, low_ref, dn_ref, sums_ref, dw_ref, out_ref, extra_ref, sem,
):
    step = pl.program_id(0)
    tokens, width = x_ref.shape

    def w_copy(at):
        return pltpu.make_async_copy(
            out_ref.at[at], pack_ref.at[:, pl.ds(at * width, width)], sem.at[at]
        )

    extra_copy = pltpu.make_async_copy(extra_ref, pack_ref.at[:, pl.ds(3 * width, 384)], sem.at[3])

    def norm_chunk(sl, carry):
        hat, _ = stats(x_ref[sl, :].astype(F32))
        low_ref[sl, :] = (hat * p_ref[0:1, :] + p_ref[2:3, :]).astype(BF)

    by_chunks(tokens, 32, norm_chunk)
    nt_ref[...] = low_ref[...].T

    @pl.when(step == 0)
    def _():
        sums_ref[...] = jnp.zeros_like(sums_ref)
        sums_ref[4:5, :] = rowsum(dqkv_ref[0].astype(F32))
        both = dtab_ref[...]
        tables = (both[0:64] + both[64:128]).astype(BF)
        extra_ref[:, 128:384] = mm(hot_ref[...], tables).astype(BF)
        dw_ref[...] = jnp.zeros_like(dw_ref)

    dn_ref[...] = jnp.zeros_like(dn_ref)

    def product(at, carry):
        lanes = pl.ds(pl.multiple_of(at * width, width), width)
        dw_ref[at] += mm(nt_ref[...], dqkv_ref[at])
        dn_ref[...] += mt(dqkv_ref[at], w_ref[:, lanes])
        return carry

    lax.fori_loop(jnp.where(step == 0, 0, 1), 3, product, 0)
    sums_ref[5:6, :] += rowsum(dqkv_ref[2].astype(F32))

    def back_chunk(sl, carry):
        sum_gain, sum_shift = carry
        hat, inverse = stats(x_ref[sl, :].astype(F32))
        grad = dn_ref[sl, :]
        dn_ref[sl, :] = norm_back(grad * p_ref[0:1, :], hat, inverse)
        return sum_gain + rowsum(grad * hat), sum_shift + rowsum(grad)

    zero = jnp.zeros((1, width), F32)
    sum_gain, sum_shift = by_chunks(tokens, 32, back_chunk, (zero, zero))
    sums_ref[0:1, :] += sum_gain
    sums_ref[2:3, :] += sum_shift

    @pl.when(step == 0)
    def _():
        dx_ref[...] = dx1_ref[...] + dn_ref[...]

    far_ref[...] = dn_ref[...].astype(BF)

    @pl.when(step == pl.num_programs(0) - 1)
    def _():
        def put(at, carry):
            out_ref[at] = dw_ref[at].astype(BF)
            w_copy(at).start()
            return carry

        lax.fori_loop(0, 3, put, 0)
        padded = jnp.concatenate([sums_ref[...], jnp.zeros((120, width), F32)], axis=0)
        extra_ref[:, 0:128] = padded.T.astype(BF)
        extra_copy.start()
        for at in range(3):
            w_copy(at).wait()
        extra_copy.wait()


def qkv_back_call(tokens, dqkv, weight, dx1, p768, dtab, hot):
    rows, width = dx1.shape
    blocks = tokens.shape[0] // rows
    full = whole((rows, width))
    block = pl.BlockSpec((rows, width), lambda s: (s, 0))
    return call(
        qkv_back_kernel,
        [
            sds((width, 3 * width + 384), BF),
            sds((rows, width), F32),
            sds(((max(blocks, 2) - 1) * rows, width), BF),
        ],
        grid=(blocks,),
        in_specs=[
            block,
            pl.BlockSpec((3, rows, width), lambda s: (0, s, 0)),
            whole(weight.shape),
            full,
            whole(p768.shape),
            whole(dtab.shape),
            whole(hot.shape),
        ],
        out_specs=[
            pl.BlockSpec(memory_space=pl.ANY),
            full,
            pl.BlockSpec((rows, width), lambda s: (jnp.maximum(s - 1, 0), 0)),
        ],
        scratch=[
            pltpu.VMEM((width, rows), BF),
            pltpu.VMEM((rows, width), BF),
            pltpu.VMEM((rows, width), F32),
            pltpu.VMEM((8, width), F32),
            pltpu.VMEM((3, width, width), F32),
            pltpu.VMEM((3, width, width), BF),
            pltpu.VMEM((width, 384), BF),
            pltpu.SemaphoreType.DMA((4,)),
        ],
        flops=8e9,
        name="qkv_back",
    )(tokens, dqkv, weight, dx1, p768, dtab, hot)


def rim_exchange(levels, axis):
    peers = lax.axis_size(axis)
    chan = levels[0].shape[-1]
    counts = [level.shape[1] for level in levels]
    lasts = jnp.concatenate([level[-1] for level in levels], axis=0)
    firsts = jnp.concatenate([level[0] for level in levels], axis=0)
    if peers == 2:
        me = lax.axis_index(axis)
        got = lax.ppermute(jnp.where(me == 0, lasts, firsts), axis, [(0, 1), (1, 0)])
        nothing = jnp.zeros_like(got)
        before = jnp.where(me == 1, got, nothing)
        after = jnp.where(me == 0, got, nothing)
    else:
        before = lax.ppermute(lasts, axis, [(i, i + 1) for i in range(peers - 1)])
        after = lax.ppermute(firsts, axis, [(i + 1, i) for i in range(peers - 1)])
    both = jnp.stack([before, after])
    rims, at = [], 0
    for count in counts:
        rims.append(both[:, at : at + count])
        at += count
    return rims


class Halving:
    def __init__(self, keep, send):
        bits = lax.axis_size("img").bit_length() - 1
        self.left = list(range(1, bits))[::-1]
        self.shape = (2,) * (bits - 1) + (keep.shape[0] >> (bits - 1), keep.shape[1])
        self.keep, self.first = keep.reshape(self.shape), send.reshape(self.shape)

    def split(self, step):
        if step == 0:
            self.route = ("img", [(i, i ^ 1) for i in range(lax.axis_size("img"))])
            return self.first
        terms = self.terms
        if step == "y":
            at, mine, axis, pairs = len(self.left), lax.axis_index("seq"), "seq", [(0, 1), (1, 0)]
            shape = terms[0].shape
            terms = [t.reshape(shape[:-2] + (2, shape[-2] // 2, shape[-1])) for t in terms]
        else:
            at, mine, axis = self.left.index(step), (lax.axis_index("img") >> step) & 1, "img"
            pairs = [(i, i ^ (1 << step)) for i in range(lax.axis_size("img"))]
            self.left.remove(step)
        self.route = (axis, pairs)

        def half(which):
            parts = [lax.dynamic_index_in_dim(t, which, at, keepdims=False) for t in terms]
            return (parts[0].astype(F32) + parts[1].astype(F32)).astype(BF)

        self.keep = half(mine)
        return half(1 - mine)


def swap(steps, after=()):
    if lax.axis_size("seq") != 2:
        steps = [(h, step) for h, step in steps if step != "y"]
    sends = [h.split(step) for h, step in steps]
    keeps = [h.keep for h, _ in steps]
    sends, keeps, after = lax.optimization_barrier((sends, keeps, after))
    for (h, _), send, keep in zip(steps, sends, keeps):
        h.terms = [keep, lax.ppermute(flat(send), *h.route).reshape(send.shape)]
    return [h for h, _ in steps], after


def flat(values):
    return values.reshape(-1, values.shape[-1])


def last_swap(group):
    left = group[0].left
    count = 1 << len(left)
    base = left[-1]
    mine = (lax.axis_index("img") >> base) & (count - 1)
    shards = lax.axis_size("img")
    terms = [
        jnp.concatenate(
            [h.terms[k].reshape((count,) + h.terms[k].shape[len(left) :]) for h in group], axis=-1
        )
        for k in (0, 1)
    ]

    def part(which):
        parts = [lax.dynamic_index_in_dim(t, which, 0, keepdims=False) for t in terms]
        return (parts[0].astype(F32) + parts[1].astype(F32)).astype(BF)

    total = part(mine).astype(F32)
    for d in range(1, count):
        pairs = [(i, i ^ (d << base)) for i in range(shards)]
        total = total + lax.ppermute(part(mine ^ d), "img", pairs).astype(F32)
    grad = total.astype(BF)
    if lax.axis_size("seq") != 2:
        return lax.psum(grad, "seq").astype(F32)
    row = lax.axis_index("seq")
    other = lax.ppermute(grad, "seq", [(0, 1), (1, 0)])
    first = jnp.where(row == 0, grad, other)
    second = jnp.where(row == 0, other, grad)
    return jnp.concatenate([first, second], axis=0).astype(F32)


def settle(moving, done=()):
    terms, _ = lax.optimization_barrier(([h.terms for h in moving], done))
    for h, arrived in zip(moving, terms):
        h.terms = arrived


def seq_total(part):
    peers = lax.axis_size("seq")
    if peers == 2:
        other = lax.ppermute(part, "seq", [(0, 1), (1, 0)])
        return part.astype(F32) + other.astype(F32)
    return lax.psum(part, "seq").astype(F32)


def per_device(
    tokens, valid_rows, valid_cols, block_gains, block_shifts, qkv_weight, qv_bias, table_rows, table_cols,
    proj_weight, proj_bias, fc1_weight, fc1_bias, fc2_weight, fc2_bias, fine_first, fine_first_bias,
    fine_norm_gain, fine_norm_shift, fine_second, fine_second_bias, middle_up, middle_up_bias, lateral_fine,
    lateral_middle, lateral_coarse, level_gains, level_shifts, output_convs, cotan_fine, cotan_middle,
    cotan_base, cotan_coarse,
):
    lr, cols, width = tokens.shape[1:]
    head = table_rows.shape[0]
    heads = width // head
    peers = lax.axis_size("seq")
    shards = lax.axis_size("img")
    me = lax.axis_index("seq")
    total_rows = lr * peers
    count = lr * cols
    chan = lateral_fine.shape[1]
    first_row = me * lr
    first = first_row.astype(jnp.int32).reshape(1)
    own_tokens = tokens[0].reshape(count, width)

    far = [
        lax.ppermute(own_tokens, "seq", [(i, (i + d) % peers) for i in range(peers)])
        for d in range(1, peers)
    ]
    far_tokens = jnp.concatenate(far, axis=0) if len(far) > 1 else (far[0] if far else None)
    all_tokens = jnp.concatenate([own_tokens] + far, axis=0)

    p768 = jnp.stack(
        [
            block_gains[:, 0], block_gains[:, 1], block_shifts[:, 0], block_shifts[:, 1],
            qv_bias[:, 0], qv_bias[:, 1], proj_bias, fc2_bias,
        ]
    ).astype(F32)
    bias3 = jnp.stack([qv_bias[:, 0], jnp.zeros_like(proj_bias), qv_bias[:, 1]]).astype(F32)[:, None, :]
    qkv_own = qkv_call(own_tokens, qkv_weight, bias3, p768, 0)
    (
        fc1_bias, fine_first_bias, fine_norm_gain, fine_norm_shift, middle_up_bias, fine_second_bias, level_gains,
        level_shifts, table_cols, table_rows, valid_rows, qkv_own,
    ) = lax.optimization_barrier(
        (
            fc1_bias, fine_first_bias, fine_norm_gain, fine_norm_shift, middle_up_bias, fine_second_bias,
            level_gains, level_shifts, table_cols, table_rows, valid_rows, qkv_own,
        )
    )
    b1 = fc1_bias.astype(F32)[None]
    p384 = jnp.stack([fine_first_bias, fine_norm_gain, fine_norm_shift, middle_up_bias]).astype(F32)
    fsb = fine_second_bias.astype(F32)[None]
    p256 = jnp.concatenate([level_gains.T, level_shifts.T]).astype(F32)
    lc0, lc1 = lateral_coarse[:, 0, :], lateral_coarse[:, 1, :]

    def turned(table):
        back = table[:, ::-1]
        back = jnp.pad(back, ((0, 0), (0, 128 - back.shape[1])))
        return jnp.concatenate([back, back], axis=0)

    tw, tr = turned(table_cols), turned(table_rows)

    low_at, aug = aug_layout(total_rows)
    ranks = jnp.stack([(me - d) % peers for d in range(peers)])
    key_rows = (ranks[:, None] * lr + jnp.arange(lr)[None, :])[:, :, None]
    key_rows = jnp.broadcast_to(key_rows, (peers, lr, cols)).reshape(-1, 1)
    key_cols = jnp.broadcast_to(jnp.arange(cols)[None, None, :], (peers, lr, cols)).reshape(-1, 1)
    lane = jnp.arange(128)[None, :]
    oh1 = (lane % 64 == key_cols).astype(BF)
    lane = jnp.arange(aug - 128)[None, :]
    hot = (lane < 64) & (lane == key_cols)
    hot = hot | ((lane >= 64) & (lane < 64 + total_rows) & (lane - 64 == key_rows))
    off = low_at
    hot = hot | ((lane >= off) & (lane < off + total_rows) & (lane - off == key_rows))
    bad = (key_rows >= valid_rows[0]) | (key_cols >= valid_cols[0])
    oh2 = jnp.where(bad & (lane == off + total_rows), NEG, hot.astype(F32)).astype(BF)

    kv_far = qkv_call(far_tokens, qkv_weight, bias3, p768, 1) if far else None
    attended, qaug, lse = attend_call(
        first, qkv_own, kv_far, (tw, tr), oh1, oh2, total_rows, heads
    )
    x1, hidden, slope, y = mlp_call(own_tokens, attended, proj_weight, fc1_weight, b1, fc2_weight, p768)

    zf, zm, zb, zc = pyramid_call(
        y, lr, cols, fine_first, fine_second, middle_up, lateral_fine, lateral_middle, lc0, lc1, p384, fsb, p256
    )
    levels = [
        zf.reshape(4 * lr, 4 * cols, chan),
        zm.reshape(2 * lr, 2 * cols, chan),
        zb.reshape(lr, cols, chan),
        zc.reshape(lr // 2, cols // 2, chan),
    ]
    later, _ = lax.optimization_barrier((output_convs, zc))
    conv_weights = later.transpose(1, 0, 2).reshape(4, 3, 3 * chan, chan)
    rims = rim_exchange(levels, "seq")
    cots = [c[0] for c in (cotan_fine, cotan_middle, cotan_base, cotan_coarse)]
    maps, drs, level_sums = [None] * 4, [None] * 4, [None] * 4
    packed = None
    for level in (3, 2, 1, 0):
        z = levels[level]
        block = min(z.shape[0], max(1, 2048 // z.shape[1]))
        map_low, dr, packed, level_sums[level] = conv_call(
            level, z, rims[level], conv_weights, cots[level], p256, block, packed
        )
        maps[level], drs[level] = map_low.reshape(z.shape), dr.reshape(z.shape)

    conv_low = lax.psum_scatter(packed, "img", scatter_dimension=0, tiled=True)
    drims = rim_exchange(drs, "seq")
    unit = width // shards
    packed_row, _ = lax.optimization_barrier((jnp.arange(width)[:, None], level_sums[0]))
    shard_at, within = packed_row // unit, packed_row % unit

    def placed(size):
        own = size // shards
        at = jnp.arange(size)[None, :]
        return ((within < own) & (at == shard_at * own + within)).astype(BF)

    quart, half = lateral_fine.shape[0], lateral_middle.shape[0]
    own_q, own_h = quart // shards, half // shards
    at = jnp.arange(quart + half)[None, :]
    source = jnp.where(
        within < own_q,
        shard_at * own_q + within,
        jnp.where(within < own_q + own_h, quart + shard_at * own_h + within - own_q, -1),
    )
    place = (at == source).astype(BF)
    hots = (placed(chan), placed(half), placed(quart))
    drims, hots, place = lax.optimization_barrier((drims, hots, place))
    dzs = []
    for level, ways in enumerate((4, 2, 1, 1)):
        dr = drs[level]
        block = min(dr.shape[0], max(1, 2048 // dr.shape[1]))
        dzs.append(conv_back_call(level, dr, drims[level], conv_weights, ways, block))

    core = (lax.axis_index("img") & 1).astype(jnp.int32).reshape(1)
    dy, low_pack, s384, s192, s256 = pyramid_back_call(
        y, lr, cols, fine_first, fine_second, middle_up, lateral_fine, lateral_middle, lc0, lc1, p384, fsb, p256,
        *dzs, place,
    )
    low_pack, conv_low = lax.optimization_barrier((low_pack, conv_low))
    low_low = lax.psum_scatter(low_pack, "img", scatter_dimension=0, tiled=True)

    level_rows = jnp.concatenate(
        [level_sums[k][0:1] for k in range(4)] + [level_sums[k][1:2] for k in range(4)]
    )
    high_keep, high_send, keep2, send2, dx1, dout = mlp_back_call(
        dy, hidden, slope, fc1_weight, fc2_weight, x1, attended, proj_weight, p768,
        s384, s192, s256, level_rows, hots, core, shards,
    )
    three, four = Halving(high_keep, high_send), Halving(keep2, send2)
    tables = jnp.concatenate([tw, tr], axis=1)

    def attend_part(dout_now, dtab, part, grads):
        return attend_back_call(
            first, qkv_own, kv_far, qaug, dout_now, attended, lse, tables, oh1, oh2, dtab,
            total_rows, heads, part, 2, grads,
        )

    _, dout = swap([(three, 0), (four, 0)], dout)
    dqkv, dtab = attend_part(dout, jnp.zeros((128, 256), F32), 0, None)
    settle([three, four], dtab)
    _, dtab = swap([(three, 1), (four, "y")], dtab)
    dqkv, dtab = attend_part(dout, dtab, 1, dqkv)
    last, dx, dx_far = qkv_back_call(
        all_tokens, dqkv, qkv_weight, dx1, p768, dtab, placed(head)
    )
    last, low_low = lax.optimization_barrier((last, low_low))
    last_low = lax.psum_scatter(last, "img", scatter_dimension=0, tiled=True)
    settle([three, four], last)
    swap([(three, "y"), (four, 1)])
    settle([three, four])
    dx_far, _ = lax.optimization_barrier((dx_far, [h.terms for h in (three, four)]))
    high_total, g_w2 = last_swap([three]), last_swap([four])
    for d in range(1, peers):
        part = dx_far[(d - 1) * count : d * count]
        dx = dx + lax.ppermute(part, "seq", [(i, (i - d) % peers) for i in range(peers)])
    conv_total, low_total = seq_total(conv_low), seq_total(low_low)
    last_low, conv_total, low_total, high_total, g_w2, dx = lax.optimization_barrier(
        (last_low, conv_total, low_total, high_total, g_w2, dx)
    )
    last_total = seq_total(last_low)

    def taken(total, start, size):
        return total[:, start : start + size]

    g_ff = jnp.concatenate([taken(low_total, 2 * k * half, half) for k in range(4)], axis=1)
    g_mu = jnp.concatenate([taken(low_total, (2 * k + 1) * half, half) for k in range(4)], axis=1)
    g_fs = taken(low_total, 8 * half, half)
    g_lc = jnp.stack(
        [taken(low_total, 9 * half, chan), taken(low_total, 9 * half + chan, chan)], axis=1
    )
    laterals = taken(low_total, 9 * half + 2 * chan, chan)
    g_lf, g_lm = laterals[:own_q], laterals[own_q : own_q + own_h]
    g_w1 = taken(high_total, 0, 4 * width)
    g_wp = taken(high_total, 4 * width, width)
    vec = taken(high_total, 5 * width, 128)
    own_c = chan // shards
    g_lg = jnp.concatenate([vec[:own_c, 8:12], vec[:own_c, 24:28]], axis=1)
    g_ls = jnp.concatenate([vec[:own_c, 16:20], vec[:own_c, 28:32]], axis=1)
    g_ffb, g_fng, g_fns, g_mub = (vec[:own_h, 32 + k] for k in range(4))
    g_fsb = vec[:own_q, 48]
    g_b1 = vec[:, 40:44].T.reshape(-1)
    g_pb, g_b2 = vec[:, 6], vec[:, 7]
    g_qkv = last_total[:, : 3 * width]
    late = last_total[:, 3 * width : 3 * width + 128]
    g_bg = jnp.stack([late[:, 0], vec[:, 1]], axis=1)
    g_bs = jnp.stack([late[:, 2], vec[:, 3]], axis=1)
    g_qvb = late[:, 4:6]
    own_t = head // shards
    tabs = last_total[:own_t, 3 * width + 128 :]
    g_tc = tabs[:, : 2 * cols - 1][:, ::-1]
    g_tr = tabs[:, 128 : 128 + 2 * total_rows - 1][:, ::-1]
    g_conv = conv_total.reshape(-1, 4, chan)
    return (
        maps[0][None], maps[1][None], maps[2][None], maps[3][None],
        dx.reshape(1, lr, cols, width),
        g_bg, g_bs, g_qkv, g_qvb, g_tr, g_tc, g_wp, g_pb, g_w1, g_b1, g_w2, g_b2, g_ff, g_ffb, g_fng, g_fns,
        g_fs, g_fsb, g_mu, g_mub, g_lf, g_lm, g_lc, g_lg, g_ls, g_conv,
    )


def solution(mesh):
    image = P("img", "seq", None, None)
    in_specs = (image, P("img"), P("img")) + (P(),) * 26 + (image,) * 4
    ranks = (2, 2, 2, 2, 2, 2, 2, 1, 2, 1, 2, 1, 2, 1, 1, 1, 2, 1, 2, 1, 2, 2, 3, 2, 2, 3)
    out_specs = (image,) * 5 + tuple(P(*(("img",) + (None,) * (r - 1))) for r in ranks)
    return jax.shard_map(
        per_device, mesh=mesh, in_specs=in_specs, out_specs=out_specs, check_vma=False
    )
```

```python
import functools

import jax
import jax.numpy as jnp
from jax import lax
from jax.experimental import pallas as pl
from jax.experimental.pallas import tpu as pltpu
from jax.sharding import PartitionSpec as P

F32 = jnp.float32
BF = jnp.bfloat16
NEG = -1e30
EPS = 1e-6
SQRT_HALF = 0.7071067811865476
INV_SQRT_2PI = 0.3989422804014327
VMEM_LIMIT = 60 * 1024 * 1024


def mm(left, right):
    return lax.dot_general(left, right, (((1,), (0,)), ((), ())), preferred_element_type=F32)


def mt(left, right):
    return lax.dot_general(left, right, (((1,), (1,)), ((), ())), preferred_element_type=F32)


def tm(left, right):
    return lax.dot_general(left, right, (((0,), (0,)), ((), ())), preferred_element_type=F32)


def call(
    kernel, outs, grid=(), in_specs=None, out_specs=None, scratch=(), flops=0, name=None, aliases=None
):
    return pl.pallas_call(
        kernel,
        out_shape=outs,
        grid=grid,
        in_specs=in_specs,
        out_specs=out_specs,
        scratch_shapes=scratch,
        name=name,
        input_output_aliases=aliases or {},
        cost_estimate=pl.CostEstimate(flops=int(flops) // COST_SHARE, bytes_accessed=0, transcendentals=0),
        compiler_params=pltpu.CompilerParams(vmem_limit_bytes=VMEM_LIMIT),
    )


def whole(shape):
    return pl.BlockSpec(shape, lambda *_: (0,) * len(shape))


def sds(shape, dtype):
    return jax.ShapeDtypeStruct(shape, dtype)


def stats(values):
    average = jnp.mean(values, axis=-1, keepdims=True)
    centred = values - average
    spread = jnp.mean(centred * centred, axis=-1, keepdims=True)
    inverse = lax.rsqrt(spread + EPS)
    return centred * inverse, inverse


def norm_back(grad_hat, hat, inverse):
    first = jnp.mean(grad_hat, axis=-1, keepdims=True)
    second = jnp.mean(grad_hat * hat, axis=-1, keepdims=True)
    return inverse * (grad_hat - first - hat * second)


def rowsum(values):
    return jnp.sum(values, axis=0, keepdims=True)


UNROLL = 64
COST_SHARE = 100
CONV_PIXELS = 1024
MOVE_ROWS = 8
BACK_PIXELS = 2048


def by_chunks(total, size, body, carry=0, unroll=None):
    unroll = max(1, min(unroll or UNROLL, total // size))

    def step(k, inner):
        for u in range(unroll):
            out = body(pl.ds(pl.multiple_of((k * unroll + u) * size, size), size), inner)
            inner = inner if out is None else out
        return inner

    if unroll == total // size:
        return step(0, carry)
    return lax.fori_loop(0, total // size // unroll, step, carry)


def put_shards(source, keep_ref, send_ref, lanes, shards, first, core, sem):
    unit = source.shape[0] // shards
    for s in range(shards):
        at = first + s
        rows = pl.ds(pl.multiple_of(lax.div(at, 2) * unit, unit), unit)
        piece = source.at[pl.ds(s * unit, unit)]

        @pl.when(lax.rem(at, 2) == core)
        def _():
            pltpu.make_async_copy(piece, keep_ref.at[rows, lanes], sem).start()

        @pl.when(lax.rem(at, 2) != core)
        def _():
            pltpu.make_async_copy(piece, send_ref.at[rows, lanes], sem).start()


def wait_shards(source, sem):
    pltpu.make_async_copy(source, source, sem).wait()


def repeat(count, body):
    for k in range(count):
        body(k, 0)


def gelu_pair(values):
    half = 0.5 * (1.0 + lax.erf(values * SQRT_HALF))
    slope = half + values * (jnp.exp(-0.5 * values * values) * INV_SQRT_2PI)
    return values * half, slope


def shift_matrix(size, amount):
    out_at = lax.broadcasted_iota(jnp.int32, (size, size), 0)
    in_at = lax.broadcasted_iota(jnp.int32, (size, size), 1)
    return jnp.where(in_at == out_at + amount, 1.0, 0.0).astype(BF)


def weave_matrix(size, ways, inverse=False):
    out_at = lax.broadcasted_iota(jnp.int32, (size, size), 1 if inverse else 0)
    in_at = lax.broadcasted_iota(jnp.int32, (size, size), 0 if inverse else 1)
    source = lax.rem(out_at, ways) * (size // ways) + lax.div(out_at, ways)
    return jnp.where(in_at == source, 1.0, 0.0).astype(BF)


def qkv_kernel(x_ref, w_ref, b_ref, p_ref, out_ref, n1_ref):
    @pl.when(pl.program_id(1) == 0)
    def _():
        def norm(sl, carry):
            hat, _ = stats(x_ref[sl, :].astype(F32))
            n1_ref[sl, :] = (hat * p_ref[0:1, :] + p_ref[2:3, :]).astype(BF)

        by_chunks(x_ref.shape[0], 32, norm)

    out_ref[...] = (mm(n1_ref[...], w_ref[...]) + b_ref[0]).astype(BF)


def qkv_call(tokens, weight, bias3, p768, first):
    rows, width = tokens.shape
    block = 512
    count = 3 - first
    return call(
        qkv_kernel,
        sds((rows, count * width), BF),
        grid=(rows // block, count),
        in_specs=[
            pl.BlockSpec((block, width), lambda i, j: (i, 0)),
            pl.BlockSpec((width, width), lambda i, j: (0, j + first)),
            pl.BlockSpec((1, 1, width), lambda i, j: (j + first, 0, 0)),
            whole(p768.shape),
        ],
        out_specs=pl.BlockSpec((block, width), lambda i, j: (i, j)),
        scratch=[pltpu.VMEM((block, width), BF)],
        flops=2 * rows * width * width * count,
        name="qkv",
    )(tokens, weight, bias3, p768)


def aug_layout(total_rows):
    low_at = 64 + total_rows
    if low_at + total_rows + 1 > 128:
        low_at = 128
    width = 128 * (2 + (low_at + total_rows) // 128)
    return low_at, width


def build_kaug(kaug_ref, k_refs, oh1_ref, oh2_ref, odd):
    lane = lax.broadcasted_iota(jnp.int32, (512, 128), 1)
    mine = (lane >= 64) if odd else (lane < 64)
    at = 0
    for k_ref in k_refs:
        for row in range(0, k_ref.shape[0], 512):
            keys = k_ref[row : row + 512, :].astype(F32)
            hot = oh1_ref[at : at + 512, :].astype(F32)
            kaug_ref[at : at + 512, 0:128] = jnp.where(mine, keys, hot).astype(BF)
            at += 512


def build_qaug(first_row, qp, tw_ref, tr_ref, qaug_ref, odd, total_rows, scale):
    low_at, width = aug_layout(total_rows)
    tokens = qp.shape[0]
    lane = lax.broadcasted_iota(jnp.int32, (64, 128), 1)
    mine = (lane >= 64) if odd else (lane < 64)
    lane_all = lax.broadcasted_iota(jnp.int32, (tokens, 128), 1)
    mine_all = (lane_all >= 64) if odd else (lane_all < 64)
    qf = qp.astype(F32)
    qm = jnp.where(mine_all, qf, 0.0).astype(BF)
    cols = mm(qm, tw_ref[...])
    rows = mm(qm, tr_ref[...])
    for i in range(tokens // 64):
        sl = slice(64 * i, 64 * i + 64)
        upper = pltpu.roll(cols[sl], 1, 1, stride=1, stride_axis=0)
        lower = pltpu.roll(cols[sl], 65, 1, stride=1, stride_axis=0)
        first = jnp.where(mine, qf[sl] * scale, lower if odd else upper)
        col_low = lower - lower.astype(BF).astype(F32)
        shift = lax.rem(first_row + i + (65 - total_rows + 128), 128)
        row_part = pltpu.roll(rows[sl], shift, 1)
        row_low = row_part - row_part.astype(BF).astype(F32)
        qaug_ref[sl, 0:128] = first.astype(BF)
        one_at = low_at + total_rows
        if low_at < 128:
            rest = jnp.where(lane == one_at, 1.0, 0.0)
            rest = jnp.where(
                (lane >= low_at) & (lane < one_at), pltpu.roll(row_low, total_rows, 1), rest
            )
            second = jnp.where(lane < 64, col_low, jnp.where(lane < low_at, row_part, rest))
            qaug_ref[sl, 128:256] = second.astype(BF)
        else:
            second = jnp.where(
                lane < 64, col_low, jnp.where(lane < 64 + total_rows, row_part, 0.0)
            )
            third = jnp.where(
                lane < total_rows,
                pltpu.roll(row_low, 64, 1),
                jnp.where(lane == total_rows, 1.0, 0.0),
            )
            qaug_ref[sl, 128:256] = second.astype(BF)
            qaug_ref[sl, 256:384] = third.astype(BF)


def attend_kernel(total_rows, scale, others, *refs):
    first_ref, q_ref, tw_ref, tr_ref, oh1_ref, oh2_ref = refs[:6]
    k_refs = refs[6 : 6 + others]
    v_refs = refs[6 + others : 6 + 2 * others]
    o_ref, qaug_out, lse_ref, kaug_ref, v_ref, p_ref, ot_ref, scores_ref = refs[6 + 2 * others :]
    first_row = first_ref[0]
    tokens = q_ref.shape[0]
    keys = kaug_ref.shape[0]

    @pl.when(pl.program_id(0) == 0)
    def _():
        kaug_ref[:, 128:] = oh2_ref[...]

    at = 0
    for ref in v_refs:
        v_ref[at : at + ref.shape[0], :] = ref[...]
        at += ref.shape[0]
    qp = q_ref[...]
    for odd in (0, 1):
        build_kaug(kaug_ref, k_refs, oh1_ref, oh2_ref, odd)
        build_qaug(first_row, qp, tw_ref, tr_ref, qaug_out.at[odd], odd, total_rows, scale)

        def queries(t, carry):
            sl = pl.ds(pl.multiple_of(t * 256, 256), 256)
            scores_ref[...] = mt(kaug_ref[...], qaug_out[odd, sl, :])

            def highest(rows, top):
                return jnp.maximum(top, jnp.max(scores_ref[rows, :], axis=0, keepdims=True))

            top = by_chunks(keys, 128, highest, jnp.full((1, 256), NEG, F32))

            def weigh(rows, total):
                weight = jnp.exp(scores_ref[rows, :] - top)
                p_ref[rows, :] = weight.astype(BF)
                return total + rowsum(weight)

            total = by_chunks(keys, 128, weigh, jnp.zeros((1, 256), F32))
            lse_ref[0, odd : odd + 1, sl] = top + jnp.log(total)
            out_t = tm(v_ref[...], p_ref[...])
            ot_ref[64 * odd : 64 * odd + 64, sl] = out_t[64 * odd : 64 * odd + 64] / total
            return carry

        repeat(tokens // 256, queries)
    o_ref[...] = ot_ref[...].T.astype(BF)


def attend_call(first, qkv_own, kv_others, tables, oh1, oh2, total_rows, heads):
    tokens = qkv_own.shape[0]
    width = qkv_own.shape[1] // 3
    keys = oh1.shape[0]
    aug = 128 + oh2.shape[1]
    pairs = width // 128
    tw, tr = tables
    parts = 1 + (1 if kv_others is not None else 0)
    in_specs = [
        pl.BlockSpec(memory_space=pltpu.SMEM),
        pl.BlockSpec((tokens, 128), lambda h: (0, h)),
        whole(tw.shape),
        whole(tr.shape),
        whole(oh1.shape),
        whole(oh2.shape),
    ]
    k_args, v_args, k_specs, v_specs = [qkv_own], [qkv_own], [], []
    k_specs.append(pl.BlockSpec((tokens, 128), lambda h: (0, h + pairs)))
    v_specs.append(pl.BlockSpec((tokens, 128), lambda h: (0, h + 2 * pairs)))
    if kv_others is not None:
        k_args.append(kv_others)
        v_args.append(kv_others)
        k_specs.append(pl.BlockSpec((keys - tokens, 128), lambda h: (0, h)))
        v_specs.append(pl.BlockSpec((keys - tokens, 128), lambda h: (0, h + pairs)))
    scale = (width // heads) ** -0.5
    return call(
        functools.partial(attend_kernel, total_rows, scale, parts),
        [
            sds((tokens, width), BF),
            sds((heads, tokens, aug), BF),
            sds((pairs, 2, tokens), F32),
        ],
        grid=(pairs,),
        in_specs=in_specs + k_specs + v_specs,
        out_specs=[
            pl.BlockSpec((tokens, 128), lambda h: (0, h)),
            pl.BlockSpec((2, tokens, aug), lambda h: (h, 0, 0)),
            pl.BlockSpec((1, 2, tokens), lambda h: (h, 0, 0)),
        ],
        scratch=[
            pltpu.VMEM((keys, aug), BF),
            pltpu.VMEM((keys, 128), BF),
            pltpu.VMEM((keys, 256), BF),
            pltpu.VMEM((128, tokens), F32),
            pltpu.VMEM((keys, 256), F32),
        ],
        flops=25e9,
        name="attend",
    )(first, qkv_own, tw, tr, oh1, oh2, *k_args, *v_args)


def mlp_kernel(
    x_ref, o_ref, wp_ref, w1_ref, b1_ref, w2_ref, p_ref, x1_ref, g_ref, gp_ref, y_ref, n2_ref, acc_ref,
    hidden_ref,
):
    step = pl.program_id(0)
    tokens = x_ref.shape[0]

    @pl.when(step == 0)
    def _():
        product = mm(o_ref[...], wp_ref[...])
        acc_ref[...] = product

        def norm(sl, carry):
            middle = x_ref[sl, :].astype(F32) + (acc_ref[sl, :] + p_ref[6:7, :])
            x1_ref[sl, :] = middle
            acc_ref[sl, :] = jnp.zeros_like(middle)
            hat, _ = stats(middle)
            n2_ref[sl, :] = (hat * p_ref[1:2, :] + p_ref[3:4, :]).astype(BF)

        by_chunks(tokens, 32, norm)

    hidden_ref[...] = mm(n2_ref[...], w1_ref[...])

    def act(sl, carry):
        value, slope = gelu_pair(hidden_ref[sl, :] + b1_ref[...])
        g_ref[sl, :] = value.astype(BF)
        gp_ref[sl, :] = slope.astype(BF)

    by_chunks(tokens, 32, act)
    acc_ref[...] += mm(g_ref[...], w2_ref[...])

    @pl.when(step == pl.num_programs(0) - 1)
    def _():
        y_ref[...] = (x1_ref[...] + (acc_ref[...] + p_ref[7:8, :])).astype(BF)


def mlp_call(tokens, attended, wp, w1, b1, w2, p768):
    rows, width = tokens.shape
    hidden = w1.shape[1]
    return call(
        mlp_kernel,
        [sds((rows, width), F32), sds((rows, hidden), BF), sds((rows, hidden), BF), sds((rows, width), BF)],
        grid=(hidden // width,),
        in_specs=[
            whole((rows, width)),
            whole((rows, width)),
            whole(wp.shape),
            pl.BlockSpec((width, width), lambda s: (0, s)),
            pl.BlockSpec((1, width), lambda s: (0, s)),
            pl.BlockSpec((width, width), lambda s: (s, 0)),
            whole(p768.shape),
        ],
        out_specs=[
            whole((rows, width)),
            pl.BlockSpec((rows, width), lambda s: (0, s)),
            pl.BlockSpec((rows, width), lambda s: (0, s)),
            whole((rows, width)),
        ],
        scratch=[
            pltpu.VMEM((rows, width), BF),
            pltpu.VMEM((rows, width), F32),
            pltpu.VMEM((rows, width), F32),
        ],
        flops=14e9,
        name="mlp",
    )(tokens, attended, wp, w1, b1, w2, p768)


def pool_matrix(a, b, rows, cols):
    count = rows * cols // 4
    out_at = lax.broadcasted_iota(jnp.int32, (count, rows * cols), 0)
    in_at = lax.broadcasted_iota(jnp.int32, (count, rows * cols), 1)
    half = cols // 2
    source = (2 * lax.div(out_at, half) + a) * cols + 2 * lax.rem(out_at, half) + b
    return jnp.where(in_at == source, 1.0, 0.0).astype(BF)


def lateral_norm(product_ref, count, gain, shift, write):
    def norm(sl, carry):
        hat, _ = stats(product_ref[sl, :])
        write(sl, (hat * gain + shift).astype(BF))

    by_chunks(count, 64, norm)


def pyramid_kernel(
    lr, cols, y_ref, ff_ref, fs_ref, mu_ref, lf_ref, lm_ref, lc0_ref, lc1_ref, p384_ref, fsb_ref, p256_ref,
    zf_ref, zm_ref, zb_ref, zc_ref, plane_ref, mplane_ref, f2_ref, first_ref, product_ref,
    third_ref, stack_ref,
):
    tokens = lr * cols
    half = mu_ref.shape[1] // 2
    quart = fs_ref.shape[0] // 4

    def offset(b, carry):
        columns = pl.ds(pl.multiple_of(b * half, half), half)
        first_ref[...] = mm(y_ref[...], ff_ref[:, columns])

        def norm(sl, inner):
            hat, _ = stats(first_ref[sl, :] + p384_ref[0:1, :])
            value = hat * p384_ref[1:2, :] + p384_ref[2:3, :]
            f2_ref[sl, :] = (0.5 * value * (1.0 + lax.erf(value * SQRT_HALF))).astype(BF)

        by_chunks(tokens, 64, norm)

        for k in range(4):
            third_ref[k * tokens : (k + 1) * tokens, :] = (
                mt(f2_ref[...], fs_ref[k * quart : (k + 1) * quart, :]) + fsb_ref[...]
            ).astype(BF)
        stack_ref[...] = mm(third_ref[...], lf_ref[...])
        for k in range(4):

            def write(sl, values):
                plane_ref[k // 2, 2 * b + k % 2, sl, :] = values

            part = stack_ref.at[k * tokens : (k + 1) * tokens]
            lateral_norm(part, tokens, p256_ref[0:1, :], p256_ref[8:9, :], write)
        middle = (mm(y_ref[...], mu_ref[:, columns]) + p384_ref[3:4, :]).astype(BF)
        product_ref[...] = mm(middle, lm_ref[...])

        def write_middle(sl, values):
            mplane_ref[b, sl, :] = values

        lateral_norm(product_ref, tokens, p256_ref[1:2, :], p256_ref[9:10, :], write_middle)
        return carry

    repeat(2, offset)
    weave4 = weave_matrix(4 * cols, 4)
    weave2 = weave_matrix(2 * cols, 2)

    def weave(i, carry):
        sl = pl.ds(pl.multiple_of(i * cols, cols), cols)
        for c in (0, 1):
            planes = jnp.concatenate([plane_ref[c, k, sl, :] for k in range(4)], axis=0)
            zf_ref[i, c] = mm(weave4, planes).astype(BF)
        planes = jnp.concatenate([mplane_ref[k, sl, :] for k in range(2)], axis=0)
        zm_ref[i, 0] = mm(weave2, planes).astype(BF)
        return carry

    repeat(lr, weave)

    @pl.when(pl.program_id(0) == 0)
    def _():
        product_ref[...] = mm(y_ref[...], lc0_ref[...])

        def write_base(sl, values):
            zb_ref[sl, :] = values

        lateral_norm(product_ref, tokens, p256_ref[2:3, :], p256_ref[10:11, :], write_base)
        pooled = pool_picks(y_ref, pick_ref=None, rows=lr, cols=cols)
        product_ref[0 : tokens // 4, :] = mm(pooled.astype(BF), lc1_ref[...])

        def write_coarse(sl, values):
            zc_ref[sl, :] = values

        lateral_norm(product_ref, tokens // 4, p256_ref[3:4, :], p256_ref[11:12, :], write_coarse)


def pool_picks(y_ref, pick_ref, rows, cols):
    def pick(k, top):
        values = mm(pool_matrix(k // 2, k % 2, rows, cols), y_ref[...])
        if pick_ref is not None:
            pick_ref[k] = values
        return jnp.maximum(top, values)

    low = jnp.full((rows * cols // 4, y_ref.shape[1]), -jnp.inf, F32)
    for k in range(4):
        low = pick(k, low)
    return low


def pyramid_call(y, lr, cols, ff, fs, mu, lf, lm, lc0, lc1, p384, fsb, p256):
    tokens, width = y.shape
    outs = lf.shape[1]
    half2 = ff.shape[1] // 2
    return call(
        functools.partial(pyramid_kernel, lr, cols),
        [
            sds((lr, 4, 4 * cols, outs), BF),
            sds((lr, 2, 2 * cols, outs), BF),
            sds((tokens, outs), BF),
            sds((tokens // 4, outs), BF),
        ],
        grid=(2,),
        in_specs=[
            whole(y.shape),
            pl.BlockSpec((width, half2), lambda a: (0, a)),
            whole(fs.shape),
            pl.BlockSpec((width, half2), lambda a: (0, a)),
            whole(lf.shape),
            whole(lm.shape),
            whole(lc0.shape),
            whole(lc1.shape),
            whole(p384.shape),
            whole(fsb.shape),
            whole(p256.shape),
        ],
        out_specs=[
            pl.BlockSpec((lr, 2, 4 * cols, outs), lambda a: (0, a, 0, 0)),
            pl.BlockSpec((lr, 1, 2 * cols, outs), lambda a: (0, a, 0, 0)),
            whole((tokens, outs)),
            whole((tokens // 4, outs)),
        ],
        scratch=[
            pltpu.VMEM((2, 4, tokens, outs), BF),
            pltpu.VMEM((2, tokens, outs), BF),
            pltpu.VMEM((tokens, half2 // 2), BF),
            pltpu.VMEM((tokens, half2 // 2), F32),
            pltpu.VMEM((tokens, outs), F32),
            pltpu.VMEM((4 * tokens, fs.shape[0] // 4), BF),
            pltpu.VMEM((4 * tokens, outs), F32),
        ],
        flops=20e9,
        name="pyramid",
    )(y, ff, fs, mu, lf, lm, lc0, lc1, p384, fsb, p256)


def fill_padded(step, block, src_ref, rim_ref, pad_ref, left, right):
    rows, cols, chan = src_ref.shape

    @pl.when(step == 0)
    def _():
        pad_ref[0, :, chan : 2 * chan] = rim_ref[0]
        pad_ref[rows + 1, :, chan : 2 * chan] = rim_ref[1]

        def copy(row, carry):
            pad_ref[row + 1, :, chan : 2 * chan] = src_ref[row]
            return carry

        lax.fori_loop(0, rows, copy, 0)

    def move(at):
        row = pad_ref[at, :, chan : 2 * chan]
        pad_ref[at, :, 0:chan] = mm(left, row).astype(BF)
        pad_ref[at, :, 2 * chan :] = mm(right, row).astype(BF)

    start = step * block
    group = min(block, MOVE_ROWS)

    @pl.when(step == 0)
    def _():
        move(0)
        move(1)

    def move_group(k, carry):
        for q in range(group):
            move(start + 2 + k * group + q)
        return carry

    lax.fori_loop(0, block // group, move_group, 0)


def conv_rows(rows, cols, block):
    return min(block, max(1, (CONV_PIXELS if rows * cols > 4096 else CONV_PIXELS // 2) // cols))


def conv_kernel(level, block, z_ref, rim_ref, w_ref, cot_ref, p_ref, *refs):
    map_ref, dr_ref, dw_ref, sums_ref, pad_ref, dwt_ref, gradt_ref = refs[-7:]
    step = pl.program_id(0)
    rows, cols, chan = z_ref.shape
    fill_padded(
        step, block, z_ref, rim_ref, pad_ref, shift_matrix(cols, -1), shift_matrix(cols, 1)
    )
    gain = p_ref[4 + level : 5 + level, :]
    shift = p_ref[12 + level : 13 + level, :]
    few = conv_rows(rows, cols, block)
    pixels = few * cols

    @pl.when(step == 0)
    def _():
        sums_ref[...] = jnp.zeros_like(sums_ref)
        dwt_ref[...] = jnp.zeros_like(dwt_ref)
        gradt_ref[...] = jnp.zeros_like(gradt_ref)

    def add_grad(row):
        for a in range(3):
            for b in range(3):
                window = pad_ref[pl.ds(row + a, few), :, b * chan : (b + 1) * chan]
                dwt_ref[3 * a + b] += mm(gradt_ref[...], window.reshape(pixels, chan))

    def forward(k, carry):
        sum_gain, sum_shift = carry
        row = step * block + k * few
        result = None
        for a in range(3):
            part = mm(pad_ref[pl.ds(row + a, few)].reshape(pixels, 3 * chan), w_ref[0, a])
            result = part if result is None else result + part
        base = pl.multiple_of(k * pixels, pixels)
        add_grad(jnp.maximum(row - few, 0))
        for q in range(0, pixels, 64):
            sl = pl.ds(base + q, 64)
            hat, inverse = stats(result[q : q + 64])
            map_ref[sl, :] = (hat * gain + shift).astype(BF)
            cot = cot_ref[sl, :].astype(F32)
            sum_gain = sum_gain + rowsum(cot * hat)
            sum_shift = sum_shift + rowsum(cot)
            dr_ref[sl, :] = norm_back(cot * gain, hat, inverse).astype(BF)
        gradt_ref[...] = dr_ref[pl.ds(base, pixels), :].T
        return sum_gain, sum_shift

    zero = jnp.zeros((1, chan), F32)
    sum_gain, sum_shift = lax.fori_loop(0, block // few, forward, (zero, zero))
    sums_ref[0:1, :] += sum_gain
    sums_ref[1:2, :] += sum_shift

    @pl.when(step == pl.num_programs(0) - 1)
    def _():
        add_grad(rows - few)

        def turn(k, carry):
            dw_ref[pl.ds(pl.multiple_of(k * chan, chan), chan), :] = dwt_ref[k].T.astype(BF)
            return carry

        lax.fori_loop(0, 9, turn, 0)


def conv_call(level, z, rims, weights, cot, p256, block, packed):
    rows, cols, chan = z.shape
    before = [] if packed is None else [packed]
    spec = pl.BlockSpec((block * cols, chan), lambda s: (s, 0))
    return call(
        functools.partial(conv_kernel, level, block),
        [
            sds((rows * cols, chan), BF),
            sds((rows * cols, chan), BF),
            sds((9 * chan, 4 * chan), BF),
            sds((8, chan), F32),
        ],
        grid=(rows // block,),
        in_specs=[
            whole(z.shape),
            whole(rims.shape),
            pl.BlockSpec((1, 3, 3 * chan, chan), lambda s: (level, 0, 0, 0)),
            spec,
            whole(p256.shape),
        ]
        + [pl.BlockSpec(memory_space=pl.ANY)] * len(before),
        out_specs=[
            spec,
            spec,
            pl.BlockSpec((9 * chan, chan), lambda s: (0, level)),
            whole((8, chan)),
        ],
        scratch=[
            pltpu.VMEM((rows + 2, cols, 3 * chan), BF),
            pltpu.VMEM((9, chan, chan), F32),
            pltpu.VMEM((chan, conv_rows(rows, cols, block) * cols), BF),
        ],
        flops=5 * 9 * rows * cols * chan * chan,
        name=f"conv{level}",
        aliases={5: 2} if before else {},
    )(z, rims, weights, cot.reshape(rows * cols, chan), p256, *before)


def conv_back_kernel(ways, block, dr_ref, rim_ref, w_ref, dz_ref, pad_ref):
    step = pl.program_id(0)
    rows, cols, chan = dr_ref.shape
    fill_padded(
        step, block, dr_ref, rim_ref, pad_ref, shift_matrix(cols, 1), shift_matrix(cols, -1)
    )
    few = min(block, max(1, BACK_PIXELS // cols))
    pixels = few * cols
    base = cols // ways
    unweave = weave_matrix(cols, ways, inverse=True)

    def back(k, carry):
        row = step * block + k * few
        result = None
        for a in range(3):
            for b in range(3):
                window = pad_ref[pl.ds(row + 2 - a, few), :, b * chan : (b + 1) * chan]
                part = mt(
                    window.reshape(pixels, chan), w_ref[0, a, b * chan : (b + 1) * chan, :]
                )
                result = part if result is None else result + part
        low = result.astype(BF)
        if ways == 1:
            dz_ref[pl.ds(pl.multiple_of(k * pixels, pixels), pixels), :] = low
            return carry
        for q in range(few):
            planes = mm(unweave, low[q * cols : (q + 1) * cols]).astype(BF)
            inner = k * few + q
            at = pl.ds(pl.multiple_of(lax.div(inner, ways) * base, base), base)
            for w in range(ways):
                dz_ref[lax.rem(inner, ways), w, at, :] = planes[w * base : (w + 1) * base]
        return carry

    lax.fori_loop(0, block // few, back, 0)


def conv_back_call(level, dr, rims, weights, ways, block):
    rows, cols, chan = dr.shape
    if ways == 1:
        out = sds((rows * cols, chan), BF)
        spec = pl.BlockSpec((block * cols, chan), lambda s: (s, 0))
    else:
        tokens = rows * cols // (ways * ways)
        out = sds((ways, ways, tokens, chan), BF)
        spec = pl.BlockSpec(
            (ways, ways, block * cols // (ways * ways), chan), lambda s: (0, 0, s, 0)
        )
    return call(
        functools.partial(conv_back_kernel, ways, block),
        out,
        grid=(rows // block,),
        in_specs=[
            whole(dr.shape),
            whole(rims.shape),
            pl.BlockSpec((1, 3, 3 * chan, chan), lambda s: (level, 0, 0, 0)),
        ],
        out_specs=spec,
        scratch=[pltpu.VMEM((rows + 2, cols, 3 * chan), BF)],
        flops=3 * 9 * rows * cols * chan * chan,
        name=f"conv_back{level}",
    )(dr, rims, weights)


def lateral_back(product_ref, count, read, gain, dl_ref):
    zero = jnp.zeros((1, product_ref.shape[1]), F32)

    def chunk(sl, carry):
        hat, inverse = stats(product_ref[sl, :])
        grad = read(sl)
        dl_ref[sl, :] = norm_back(grad * gain, hat, inverse).astype(BF)
        return carry[0] + rowsum(grad * hat), carry[1] + rowsum(grad)

    return by_chunks(count, 64, chunk, (zero, zero))


def pyramid_back_kernel(
    lr, cols, y_ref, ff_ref, fs_ref, mu_ref, lf_ref, lm_ref, lc0_ref, lc1_ref, p384_ref,
    fsb_ref, p256_ref, dzf_ref, dzm_ref, dzb_ref, dzc_ref, place_ref,
    dy_ref, pack_ref, s384_ref, s192_ref, s256_ref,
    yt_ref, hat_ref, slope_ref, inv_ref, f2_ref, df2_ref, df1_ref, dl_ref, fs_acc, lf_acc, lm_acc,
    dcol_ref, drest_ref, product_ref, pick_ref, third_ref, stack_ref, dls_ref, sem,
):
    step = pl.program_id(0)
    tokens = lr * cols
    quart = fs_ref.shape[0] // 4
    half = ff_ref.shape[1]
    chan = lf_ref.shape[1]

    rest = drest_ref.shape[1]

    def col_copy(at):
        lanes = pl.ds(pl.multiple_of(at * 2 * half, 2 * half), 2 * half)
        return pltpu.make_async_copy(dcol_ref.at[at], pack_ref.at[:, lanes], sem.at[at])

    rest_copy = pltpu.make_async_copy(drest_ref, pack_ref.at[:, pl.ds(8 * half, rest)], sem.at[4])

    @pl.when(step == 0)
    def _():
        yt_ref[...] = y_ref[...].T
        for ref in (fs_acc, lf_acc, lm_acc, s384_ref, s192_ref, s256_ref):
            ref[...] = jnp.zeros_like(ref)
        product_ref[...] = mm(y_ref[...], lc0_ref[...])
        sg, ss = lateral_back(
            product_ref, tokens, lambda sl: dzb_ref[sl, :].astype(F32), p256_ref[2:3, :], dl_ref
        )
        s256_ref[2:3, :] = sg
        s256_ref[10:11, :] = ss
        drest_ref[:, half : half + chan] = mm(yt_ref[...], dl_ref[...]).astype(BF)
        dy_ref[...] = mt(dl_ref[...], lc0_ref[...])
        top = pool_picks(y_ref, pick_ref, lr, cols)
        low = top.astype(BF)
        product_ref[0 : tokens // 4, :] = mm(low, lc1_ref[...])
        sg, ss = lateral_back(
            product_ref, tokens // 4, lambda sl: dzc_ref[sl, :].astype(F32), p256_ref[3:4, :], dl_ref
        )
        s256_ref[3:4, :] = sg
        s256_ref[11:12, :] = ss
        grad = dl_ref[0 : tokens // 4, :]
        drest_ref[:, half + chan : half + 2 * chan] = tm(low, grad).astype(BF)
        dtop = mt(grad, lc1_ref[...])
        hits = jnp.zeros_like(top)
        for k in range(4):
            hits = hits + jnp.where(pick_ref[k] == top, 1.0, 0.0)
        dtop = dtop / hits

        def share_out(k, carry):
            share = jnp.where(pick_ref[k] == top, dtop, 0.0)
            upper = share.astype(BF)
            lower = (share - upper.astype(F32)).astype(BF)
            spread = pool_matrix(k // 2, k % 2, lr, cols)
            dy_ref[...] += tm(spread, upper) + tm(spread, lower)
            return carry

        repeat(4, share_out)

    df2_ref[...] = mm(y_ref[...], ff_ref[...])

    def norm(sl, carry):
        hat, inverse = stats(df2_ref[sl, :] + p384_ref[0:1, :])
        hat_ref[sl, :] = hat
        inv_ref[sl, :] = jnp.broadcast_to(inverse, (64, 128))
        value, slope = gelu_pair(hat * p384_ref[1:2, :] + p384_ref[2:3, :])
        f2_ref[sl, :] = value.astype(BF)
        slope_ref[sl, :] = slope
        df2_ref[sl, :] = jnp.zeros_like(hat)

    by_chunks(tokens, 64, norm)

    for k in range(4):
        third_ref[k * tokens : (k + 1) * tokens, :] = (
            mt(f2_ref[...], fs_ref[k * quart : (k + 1) * quart, :]) + fsb_ref[...]
        ).astype(BF)
    stack_ref[...] = mm(third_ref[...], lf_ref[...])
    for k in range(4):
        sg, ss = lateral_back(
            stack_ref.at[k * tokens : (k + 1) * tokens],
            tokens,
            lambda sl: dzf_ref[0, k // 2, 0, k % 2, sl, :].astype(F32),
            p256_ref[0:1, :],
            dls_ref.at[k * tokens : (k + 1) * tokens],
        )
        s256_ref[0:1, :] += sg
        s256_ref[8:9, :] += ss
    lf_acc[...] += tm(third_ref[...], dls_ref[...])
    third_ref[...] = mt(dls_ref[...], lf_ref[...]).astype(BF)
    s192_ref[0:1, :] += rowsum(third_ref[...].astype(F32))
    for k in range(4):
        rows = slice(k * quart, (k + 1) * quart)
        fs_acc[rows, :] += tm(third_ref[k * tokens : (k + 1) * tokens, :], f2_ref[...])
        df2_ref[...] += mm(third_ref[k * tokens : (k + 1) * tokens, :], fs_ref[rows, :])
    zero = jnp.zeros((1, half), F32)

    def first_back(sl, carry):
        sum_gain, sum_shift, sum_bias = carry
        hat = hat_ref[sl, :]
        grad = df2_ref[sl, :] * slope_ref[sl, :]
        low = norm_back(grad * p384_ref[1:2, :], hat, inv_ref[sl, 0:1]).astype(BF)
        df1_ref[sl, :] = low
        return (
            sum_gain + rowsum(grad * hat),
            sum_shift + rowsum(grad),
            sum_bias + rowsum(low.astype(F32)),
        )

    sum_gain, sum_shift, sum_bias = by_chunks(tokens, 64, first_back, (zero, zero, zero))
    s384_ref[0:1, :] += sum_bias
    s384_ref[1:2, :] += sum_gain
    s384_ref[2:3, :] += sum_shift
    dcol_ref[step, :, 0:half] = mm(yt_ref[...], df1_ref[...]).astype(BF)
    dy_ref[...] += mt(df1_ref[...], ff_ref[...])

    f2_ref[...] = (mm(y_ref[...], mu_ref[...]) + p384_ref[3:4, :]).astype(BF)
    product_ref[...] = mm(f2_ref[...], lm_ref[...])
    sg, ss = lateral_back(
        product_ref, tokens, lambda sl: dzm_ref[0, 0, sl, :].astype(F32), p256_ref[1:2, :], dl_ref
    )
    s256_ref[1:2, :] += sg
    s256_ref[9:10, :] += ss
    lm_acc[...] += tm(f2_ref[...], dl_ref[...])
    df1_ref[...] = mt(dl_ref[...], lm_ref[...]).astype(BF)
    s384_ref[3:4, :] += rowsum(df1_ref[...].astype(F32))
    dcol_ref[step, :, half:] = mm(yt_ref[...], df1_ref[...]).astype(BF)
    col_copy(step).start()
    dy_ref[...] += mt(df1_ref[...], mu_ref[...])

    @pl.when(step == pl.num_programs(0) - 1)
    def _():
        drest_ref[:, 0:half] = fs_acc[...].astype(BF)
        laterals = jnp.concatenate([lf_acc[...], lm_acc[...]], axis=0).astype(BF)
        drest_ref[:, half + 2 * chan : half + 3 * chan] = mm(place_ref[...], laterals).astype(BF)
        rest_copy.start()
        for at in range(4):
            col_copy(at).wait()
        rest_copy.wait()


def pyramid_back_call(
    y, lr, cols, ff, fs, mu, lf, lm, lc0, lc1, p384, fsb, p256, dzf, dzm, dzb, dzc, place
):
    tokens, width = y.shape
    half = fs.shape[1]
    quart = fsb.shape[1]
    outs = lf.shape[1]
    col_block = pl.BlockSpec((width, half), lambda s: (0, s))
    return call(
        functools.partial(pyramid_back_kernel, lr, cols),
        [
            sds((tokens, width), F32),
            sds((width, 9 * half + 3 * outs), BF),
            sds((8, half), F32),
            sds((8, quart), F32),
            sds((16, outs), F32),
        ],
        grid=(4,),
        in_specs=[
            whole(y.shape),
            col_block,
            whole(fs.shape),
            col_block,
            whole(lf.shape),
            whole(lm.shape),
            whole(lc0.shape),
            whole(lc1.shape),
            whole(p384.shape),
            whole(fsb.shape),
            whole(p256.shape),
            pl.BlockSpec((1, 2, 1, 2, tokens, outs), lambda s: (s // 2, 0, s % 2, 0, 0, 0)),
            pl.BlockSpec((1, 1, tokens, outs), lambda s: (s // 2, s % 2, 0, 0)),
            whole(dzb.shape),
            whole(dzc.shape),
            whole(place.shape),
        ],
        out_specs=[
            whole((tokens, width)),
            pl.BlockSpec(memory_space=pl.ANY),
            whole((8, half)),
            whole((8, quart)),
            whole((16, outs)),
        ],
        scratch=[
            pltpu.VMEM((width, tokens), BF),
            pltpu.VMEM((tokens, half), F32),
            pltpu.VMEM((tokens, half), F32),
            pltpu.VMEM((tokens, 128), F32),
            pltpu.VMEM((tokens, half), BF),
            pltpu.VMEM((tokens, half), F32),
            pltpu.VMEM((tokens, half), BF),
            pltpu.VMEM((tokens, outs), BF),
            pltpu.VMEM(fs.shape, F32),
            pltpu.VMEM(lf.shape, F32),
            pltpu.VMEM(lm.shape, F32),
            pltpu.VMEM((4, width, 2 * half), BF),
            pltpu.VMEM((width, half + 3 * outs), BF),
            pltpu.VMEM((tokens, outs), F32),
            pltpu.VMEM((4, tokens // 4, width), F32),
            pltpu.VMEM((4 * tokens, quart), BF),
            pltpu.VMEM((4 * tokens, outs), F32),
            pltpu.VMEM((4 * tokens, outs), BF),
            pltpu.SemaphoreType.DMA((5,)),
        ],
        flops=45e9,
        name="pyramid_back",
    )(
        y, ff, fs, mu, lf, lm, lc0, lc1, p384, fsb, p256,
        dzf.reshape(2, 2, 2, 2, tokens, outs), dzm, dzb, dzc, place,
    )


def mlp_back_kernel(
    shards,
    core_ref, dy_ref, g_ref, gp_ref, w1_ref, w2_ref, x1_ref, o_ref, wp_ref, p_ref, s384_ref, s192_ref, s256_ref, levels_ref,
    hot256_ref, hot384_ref, hot192_ref,
    keep_ref, send_ref, keep2_ref, send2_ref, dx1_ref, do_ref,
    n2t_ref, d2_ref, dn2_ref, low_ref, sums_ref, vec_ref, dw1_ref, dw2_ref, rest_ref, temp_ref, sem,
):
    step = pl.program_id(0)
    steps = pl.num_programs(0)
    tokens, width = dy_ref.shape
    unit = width // shards
    hidden = 4 * width

    core = core_ref[0]

    @pl.when(step == 0)
    def _():
        sums_ref[...] = jnp.zeros_like(sums_ref)
        vec_ref[...] = jnp.zeros_like(vec_ref)
        dn2_ref[...] = jnp.zeros_like(dn2_ref)

        def norm(sl, total):
            hat, _ = stats(x1_ref[sl, :])
            low_ref[sl, :] = (hat * p_ref[1:2, :] + p_ref[3:4, :]).astype(BF)
            low = dy_ref[sl, :].astype(BF)
            d2_ref[sl, :] = low
            return total + rowsum(low.astype(F32))

        sums_ref[7:8, :] = by_chunks(tokens, 32, norm, jnp.zeros((1, width), F32))
        n2t_ref[...] = low_ref[...].T

    dw2_ref[step] = tm(g_ref[...], d2_ref[...]).astype(BF)
    put_shards(
        dw2_ref.at[step], keep2_ref, send2_ref, pl.ds(0, width), shards // 4, step * (shards // 4), core,
        sem.at[5 + step],
    )
    temp_ref[...] = mt(d2_ref[...], w2_ref[...])

    def act(sl, carry):
        low_ref[sl, :] = (temp_ref[sl, :] * gp_ref[sl, :].astype(F32)).astype(BF)

    by_chunks(tokens, 32, act)
    db1 = tm(low_ref[...], jnp.ones((tokens, 128), BF))
    lane = lax.broadcasted_iota(jnp.int32, (unit, 128), 1)
    for q in range(shards // 4):
        entry = jnp.zeros((unit, 128), F32)
        for k in range(4):
            sl = slice((4 * q + k) * unit, (4 * q + k + 1) * unit)
            entry = jnp.where(lane == 40 + k, db1[sl], entry)
        vec_ref[pl.ds(pl.multiple_of(step * (width // 4) + q * unit, 8), unit), :] += entry
    dw1_ref[step] = mm(n2t_ref[...], low_ref[...]).astype(BF)
    lanes = pl.ds(pl.multiple_of(step * width, width), width)
    put_shards(dw1_ref.at[step], keep_ref, send_ref, lanes, shards, 0, core, sem.at[step])
    dn2_ref[...] += mt(low_ref[...], w1_ref[...])

    @pl.when(step == steps - 1)
    def _():
        zero = jnp.zeros((1, width), F32)

        def back(sl, carry):
            hat, inverse = stats(x1_ref[sl, :])
            grad = dn2_ref[sl, :]
            dx1 = dy_ref[sl, :] + norm_back(grad * p_ref[1:2, :], hat, inverse)
            dx1_ref[sl, :] = dx1
            low = dx1.astype(BF)
            d2_ref[sl, :] = low
            return (
                carry[0] + rowsum(grad * hat),
                carry[1] + rowsum(grad),
                carry[2] + rowsum(low.astype(F32)),
            )

        sum_gain, sum_shift, sum_bias = by_chunks(tokens, 32, back, (zero, zero, zero))
        sums_ref[1:2, :] = sum_gain
        sums_ref[3:4, :] = sum_shift
        sums_ref[6:7, :] = sum_bias
        rest_ref[:, 0:width] = tm(o_ref[...], d2_ref[...]).astype(BF)
        do_ref[...] = mt(d2_ref[...], wp_ref[...]).astype(BF)

        def lanes_of(rows, before):
            after = 128 - before - rows.shape[0]
            parts = [jnp.zeros((before, rows.shape[1]), F32)] if before else []
            parts += [rows, jnp.zeros((after, rows.shape[1]), F32)]
            return jnp.concatenate(parts, axis=0)

        spread = mt(hot256_ref[...], lanes_of(s256_ref[...], 8).astype(BF))
        spread = spread + mt(hot256_ref[...], lanes_of(levels_ref[...], 24).astype(BF))
        spread = spread + mt(hot384_ref[...], lanes_of(s384_ref[...], 32).astype(BF))
        spread = spread + mt(hot192_ref[...], lanes_of(s192_ref[...], 48).astype(BF))
        spread = spread + lanes_of(sums_ref[...], 0).T
        rest_ref[:, width:] = (vec_ref[...] + spread).astype(BF)
        put_shards(
            rest_ref, keep_ref, send_ref, pl.ds(hidden, width + 128), shards, 0, core, sem.at[4]
        )
        for at in range(4):
            wait_shards(dw1_ref.at[at], sem.at[at])
            wait_shards(dw2_ref.at[at], sem.at[5 + at])
        wait_shards(rest_ref, sem.at[4])


def mlp_back_call(
    dy, g, gp, w1, w2, x1, attended, wp, p768, s384, s192, s256, levels, hots, core, shards
):
    rows, width = dy.shape
    hidden = g.shape[1]
    full = whole((rows, width))
    column = pl.BlockSpec((rows, width), lambda s: (0, s))
    smalls = [p768, s384, s192, s256, levels, *hots]
    return call(
        functools.partial(mlp_back_kernel, shards),
        [
            sds((width // 2, hidden + width + 128), BF),
            sds((width // 2, hidden + width + 128), BF),
            sds((hidden // 2, width), BF),
            sds((hidden // 2, width), BF),
            sds((rows, width), F32),
            sds((rows, width), BF),
        ],
        grid=(hidden // width,),
        in_specs=[
            pl.BlockSpec(memory_space=pltpu.SMEM),
            full,
            column,
            column,
            pl.BlockSpec((width, width), lambda s: (0, s)),
            pl.BlockSpec((width, width), lambda s: (s, 0)),
            full,
            full,
            whole((width, width)),
        ]
        + [whole(a.shape) for a in smalls],
        out_specs=[
            pl.BlockSpec(memory_space=pl.ANY),
            pl.BlockSpec(memory_space=pl.ANY),
            pl.BlockSpec(memory_space=pl.ANY),
            pl.BlockSpec(memory_space=pl.ANY),
            full,
            full,
        ],
        scratch=[
            pltpu.VMEM((width, rows), BF),
            pltpu.VMEM((rows, width), BF),
            pltpu.VMEM((rows, width), F32),
            pltpu.VMEM((rows, width), BF),
            pltpu.VMEM((8, width), F32),
            pltpu.VMEM((width, 128), F32),
            pltpu.VMEM((4, width, width), BF),
            pltpu.VMEM((4, width, width), BF),
            pltpu.VMEM((width, width + 128), BF),
            pltpu.VMEM((rows, width), F32),
            pltpu.SemaphoreType.DMA((9,)),
        ],
        flops=25e9,
        name="mlp_back",
    )(core, dy, g, gp, w1, w2, x1, attended, wp, *smalls)


def roll_back(values, amount):
    moved = jnp.concatenate(
        [
            pltpu.roll(values[8 * g : 8 * g + 8], (amount - 7 - 8 * g) % 128, 1)
            for g in range(values.shape[0] // 8)
        ],
        axis=0,
    )
    left = 7 - lax.rem(lax.broadcasted_iota(jnp.int32, values.shape, 0), 8)
    for step in (1, 2, 4):
        moved = jnp.where((left & step) > 0, pltpu.roll(moved, step, 1), moved)
    return moved


def attend_back_kernel(total_rows, scale, others, *refs):
    first_ref, q_ref, qaug_ref, do_ref, o_ref, lse_ref, tab_ref, oh1_ref, oh2_ref, before_ref = refs[:10]
    k_refs = refs[10 : 10 + others]
    v_refs = refs[10 + others : 10 + 2 * others]
    rest = refs[-15:]
    (
        dqkv_ref, dtab_ref, kaug_ref, v_ref, p_ref, ds_ref, dqt_ref, df_ref, qm_ref, dom_ref, delta_ref,
        scores_ref, dweight_ref, dk_acc, dv_acc,
    ) = rest
    first_row = first_ref[0]
    tokens = q_ref.shape[0]
    keys = kaug_ref.shape[0]

    @pl.when(pl.program_id(0) == 0)
    def _():
        kaug_ref[:, 128:] = oh2_ref[...]
        dtab_ref[...] = before_ref[...]

    at = 0
    for ref in v_refs:
        v_ref[at : at + ref.shape[0], :] = ref[...]
        at += ref.shape[0]
    lane_all = lax.broadcasted_iota(jnp.int32, (tokens, 128), 1)
    lane = lax.broadcasted_iota(jnp.int32, (64, 128), 1)
    qf = q_ref[...].astype(F32)
    dof = do_ref[...].astype(F32)
    delta_t = (dof * o_ref[...].astype(F32)).T
    dk_acc[...] = jnp.zeros_like(dk_acc)
    dv_acc[...] = jnp.zeros_like(dv_acc)
    dq = None
    for odd in (0, 1):
        mine_all = (lane_all >= 64) if odd else (lane_all < 64)
        other = (lane < 64) if odd else (lane >= 64)
        build_kaug(kaug_ref, k_refs, oh1_ref, oh2_ref, odd)
        qm = jnp.where(mine_all, qf, 0.0).astype(BF)
        dom = jnp.where(mine_all, dof, 0.0).astype(BF)
        delta = rowsum(delta_t[64 * odd : 64 * odd + 64])
        qm_ref[...] = qm
        dom_ref[...] = dom
        delta_ref[...] = delta

        def queries(t, carry):
            sl = pl.ds(pl.multiple_of(t * 256, 256), 256)
            scores_ref[...] = mt(kaug_ref[...], qaug_ref[odd, sl, :])
            dweight_ref[...] = mt(v_ref[...], dom_ref[sl, :])
            lse = lse_ref[0, odd : odd + 1, sl]
            shift = delta_ref[:, sl]

            def weigh(rows, inner):
                weight = jnp.exp(scores_ref[rows, :] - lse)
                p_ref[rows, :] = weight.astype(BF)
                ds_ref[rows, :] = (weight * (dweight_ref[rows, :] - shift)).astype(BF)

            by_chunks(keys, 128, weigh)
            dk_acc[...] += mm(ds_ref[...], qm_ref[sl, :])
            dv_acc[...] += mm(p_ref[...], dom_ref[sl, :])
            dqt_ref[:, sl] = tm(kaug_ref[...], ds_ref[...])
            return carry

        repeat(tokens // 256, queries)
        dqa = dqt_ref[0:256, :].T
        for i in range(tokens // 64):
            sl = slice(64 * i, 64 * i + 64)
            cols = roll_back(jnp.where(other, dqa[sl, 0:128], 0.0), 63 if odd else 127)
            shift = lax.rem(63 + total_rows - (first_row + i) + 128, 128)
            rows = pltpu.roll(
                jnp.where((lane >= 64) & (lane < 64 + total_rows), dqa[sl, 128:256], 0.0), shift, 1
            )
            df_ref[sl, 0:128] = cols.astype(BF)
            df_ref[sl, 128:256] = rows.astype(BF)
        from_tables = mt(df_ref[...], tab_ref[...])
        part = jnp.where(mine_all, dqa[:, 0:128] * scale + from_tables, 0.0)
        dq = part if dq is None else dq + part
        dtab_ref[...] += tm(qm, df_ref[...])
    dqkv_ref[0, 0:tokens, :] = dq.astype(BF)
    dqkv_ref[1] = (dk_acc[...] * scale).astype(BF)
    dqkv_ref[2] = dv_acc[...].astype(BF)


def attend_back_call(
    first, qkv_own, kv_others, qaug, dout, attended, lse, tab, oh1, oh2, dtab, total_rows, heads, part, parts, grads
):
    tokens = qkv_own.shape[0]
    width = qkv_own.shape[1] // 3
    keys = oh1.shape[0]
    aug = 128 + oh2.shape[1]
    pairs = width // 128
    count = pairs // parts
    base = part * count
    sources = 1 + (1 if kv_others is not None else 0)
    own = pl.BlockSpec((tokens, 128), lambda h: (0, h + base))
    in_specs = [
        pl.BlockSpec(memory_space=pltpu.SMEM),
        own,
        pl.BlockSpec((2, tokens, aug), lambda h: (h + base, 0, 0)),
        own,
        own,
        pl.BlockSpec((1, 2, tokens), lambda h: (h + base, 0, 0)),
        whole(tab.shape),
        whole(oh1.shape),
        whole(oh2.shape),
        whole(dtab.shape),
    ]
    k_args, v_args, k_specs, v_specs = [qkv_own], [qkv_own], [], []
    k_specs.append(pl.BlockSpec((tokens, 128), lambda h: (0, h + base + pairs)))
    v_specs.append(pl.BlockSpec((tokens, 128), lambda h: (0, h + base + 2 * pairs)))
    if kv_others is not None:
        k_args.append(kv_others)
        v_args.append(kv_others)
        k_specs.append(pl.BlockSpec((keys - tokens, 128), lambda h: (0, h + base)))
        v_specs.append(pl.BlockSpec((keys - tokens, 128), lambda h: (0, h + base + pairs)))
    scale = (width // heads) ** -0.5
    earlier = [] if grads is None else [grads]
    return call(
        functools.partial(attend_back_kernel, total_rows, scale, sources),
        [sds((3, keys, width), BF), sds((128, 256), F32)],
        grid=(count,),
        in_specs=in_specs + k_specs + v_specs + [pl.BlockSpec(memory_space=pl.ANY)] * len(earlier),
        out_specs=[pl.BlockSpec((3, keys, 128), lambda h: (0, 0, h + base)), whole((128, 256))],
        scratch=[
            pltpu.VMEM((keys, aug), BF),
            pltpu.VMEM((keys, 128), BF),
            pltpu.VMEM((keys, 256), BF),
            pltpu.VMEM((keys, 256), BF),
            pltpu.VMEM((aug, tokens), F32),
            pltpu.VMEM((tokens, 256), BF),
            pltpu.VMEM((tokens, 128), BF),
            pltpu.VMEM((tokens, 128), BF),
            pltpu.VMEM((1, tokens), F32),
            pltpu.VMEM((keys, 256), F32),
            pltpu.VMEM((keys, 256), F32),
            pltpu.VMEM((keys, 128), F32),
            pltpu.VMEM((keys, 128), F32),
        ],
        flops=30e9 / parts,
        name="attend_back",
        aliases={10 + 2 * sources: 0} if earlier else {},
    )(first, qkv_own, qaug, dout, attended, lse, tab, oh1, oh2, dtab, *k_args, *v_args, *earlier)


def qkv_back_kernel(
    x_ref, dqkv_ref, w_ref, dx1_ref, p_ref, dtab_ref, hot_ref,
    pack_ref, dx_ref, far_ref, nt_ref, low_ref, dn_ref, sums_ref, dw_ref, out_ref, extra_ref, sem,
):
    step = pl.program_id(0)
    tokens, width = x_ref.shape

    def w_copy(at):
        return pltpu.make_async_copy(
            out_ref.at[at], pack_ref.at[:, pl.ds(at * width, width)], sem.at[at]
        )

    extra_copy = pltpu.make_async_copy(extra_ref, pack_ref.at[:, pl.ds(3 * width, 384)], sem.at[3])

    def norm_chunk(sl, carry):
        hat, _ = stats(x_ref[sl, :].astype(F32))
        low_ref[sl, :] = (hat * p_ref[0:1, :] + p_ref[2:3, :]).astype(BF)

    by_chunks(tokens, 32, norm_chunk)
    nt_ref[...] = low_ref[...].T

    @pl.when(step == 0)
    def _():
        sums_ref[...] = jnp.zeros_like(sums_ref)
        sums_ref[4:5, :] = rowsum(dqkv_ref[0].astype(F32))
        both = dtab_ref[...]
        tables = (both[0:64] + both[64:128]).astype(BF)
        extra_ref[:, 128:384] = mm(hot_ref[...], tables).astype(BF)
        dw_ref[...] = jnp.zeros_like(dw_ref)

    dn_ref[...] = jnp.zeros_like(dn_ref)

    def product(at, carry):
        lanes = pl.ds(pl.multiple_of(at * width, width), width)
        dw_ref[at] += mm(nt_ref[...], dqkv_ref[at])
        dn_ref[...] += mt(dqkv_ref[at], w_ref[:, lanes])
        return carry

    lax.fori_loop(jnp.where(step == 0, 0, 1), 3, product, 0)
    sums_ref[5:6, :] += rowsum(dqkv_ref[2].astype(F32))

    def back_chunk(sl, carry):
        sum_gain, sum_shift = carry
        hat, inverse = stats(x_ref[sl, :].astype(F32))
        grad = dn_ref[sl, :]
        dn_ref[sl, :] = norm_back(grad * p_ref[0:1, :], hat, inverse)
        return sum_gain + rowsum(grad * hat), sum_shift + rowsum(grad)

    zero = jnp.zeros((1, width), F32)
    sum_gain, sum_shift = by_chunks(tokens, 32, back_chunk, (zero, zero))
    sums_ref[0:1, :] += sum_gain
    sums_ref[2:3, :] += sum_shift

    @pl.when(step == 0)
    def _():
        dx_ref[...] = dx1_ref[...] + dn_ref[...]

    far_ref[...] = dn_ref[...].astype(BF)

    @pl.when(step == pl.num_programs(0) - 1)
    def _():
        def put(at, carry):
            out_ref[at] = dw_ref[at].astype(BF)
            w_copy(at).start()
            return carry

        lax.fori_loop(0, 3, put, 0)
        padded = jnp.concatenate([sums_ref[...], jnp.zeros((120, width), F32)], axis=0)
        extra_ref[:, 0:128] = padded.T.astype(BF)
        extra_copy.start()
        for at in range(3):
            w_copy(at).wait()
        extra_copy.wait()


def qkv_back_call(tokens, dqkv, weight, dx1, p768, dtab, hot):
    rows, width = dx1.shape
    blocks = tokens.shape[0] // rows
    full = whole((rows, width))
    block = pl.BlockSpec((rows, width), lambda s: (s, 0))
    return call(
        qkv_back_kernel,
        [
            sds((width, 3 * width + 384), BF),
            sds((rows, width), F32),
            sds(((max(blocks, 2) - 1) * rows, width), BF),
        ],
        grid=(blocks,),
        in_specs=[
            block,
            pl.BlockSpec((3, rows, width), lambda s: (0, s, 0)),
            whole(weight.shape),
            full,
            whole(p768.shape),
            whole(dtab.shape),
            whole(hot.shape),
        ],
        out_specs=[
            pl.BlockSpec(memory_space=pl.ANY),
            full,
            pl.BlockSpec((rows, width), lambda s: (jnp.maximum(s - 1, 0), 0)),
        ],
        scratch=[
            pltpu.VMEM((width, rows), BF),
            pltpu.VMEM((rows, width), BF),
            pltpu.VMEM((rows, width), F32),
            pltpu.VMEM((8, width), F32),
            pltpu.VMEM((3, width, width), F32),
            pltpu.VMEM((3, width, width), BF),
            pltpu.VMEM((width, 384), BF),
            pltpu.SemaphoreType.DMA((4,)),
        ],
        flops=8e9,
        name="qkv_back",
    )(tokens, dqkv, weight, dx1, p768, dtab, hot)


def rim_exchange(levels, axis):
    peers = lax.axis_size(axis)
    chan = levels[0].shape[-1]
    counts = [level.shape[1] for level in levels]
    lasts = jnp.concatenate([level[-1] for level in levels], axis=0)
    firsts = jnp.concatenate([level[0] for level in levels], axis=0)
    if peers == 2:
        me = lax.axis_index(axis)
        got = lax.ppermute(jnp.where(me == 0, lasts, firsts), axis, [(0, 1), (1, 0)])
        nothing = jnp.zeros_like(got)
        before = jnp.where(me == 1, got, nothing)
        after = jnp.where(me == 0, got, nothing)
    else:
        before = lax.ppermute(lasts, axis, [(i, i + 1) for i in range(peers - 1)])
        after = lax.ppermute(firsts, axis, [(i + 1, i) for i in range(peers - 1)])
    both = jnp.stack([before, after])
    rims, at = [], 0
    for count in counts:
        rims.append(both[:, at : at + count])
        at += count
    return rims


class Halving:
    def __init__(self, keep, send):
        bits = lax.axis_size("img").bit_length() - 1
        self.left = list(range(1, bits))[::-1]
        self.shape = (2,) * (bits - 1) + (keep.shape[0] >> (bits - 1), keep.shape[1])
        self.keep, self.first = keep.reshape(self.shape), send.reshape(self.shape)

    def split(self, step):
        if step == 0:
            self.route = ("img", [(i, i ^ 1) for i in range(lax.axis_size("img"))])
            return self.first
        terms = self.terms
        if step == "y":
            at, mine, axis, pairs = len(self.left), lax.axis_index("seq"), "seq", [(0, 1), (1, 0)]
            shape = terms[0].shape
            terms = [t.reshape(shape[:-2] + (2, shape[-2] // 2, shape[-1])) for t in terms]
        else:
            at, mine, axis = self.left.index(step), (lax.axis_index("img") >> step) & 1, "img"
            pairs = [(i, i ^ (1 << step)) for i in range(lax.axis_size("img"))]
            self.left.remove(step)
        self.route = (axis, pairs)

        def half(which):
            parts = [lax.dynamic_index_in_dim(t, which, at, keepdims=False) for t in terms]
            return (parts[0].astype(F32) + parts[1].astype(F32)).astype(BF)

        self.keep = half(mine)
        return half(1 - mine)


def swap(steps, after=()):
    if lax.axis_size("seq") != 2:
        steps = [(h, step) for h, step in steps if step != "y"]
    sends = [h.split(step) for h, step in steps]
    keeps = [h.keep for h, _ in steps]
    sends, keeps, after = lax.optimization_barrier((sends, keeps, after))
    for (h, _), send, keep in zip(steps, sends, keeps):
        h.terms = [keep, lax.ppermute(flat(send), *h.route).reshape(send.shape)]
    return [h for h, _ in steps], after


def flat(values):
    return values.reshape(-1, values.shape[-1])


def last_swap(group):
    left = group[0].left
    count = 1 << len(left)
    base = left[-1]
    mine = (lax.axis_index("img") >> base) & (count - 1)
    shards = lax.axis_size("img")
    terms = [
        jnp.concatenate(
            [h.terms[k].reshape((count,) + h.terms[k].shape[len(left) :]) for h in group], axis=-1
        )
        for k in (0, 1)
    ]

    def part(which):
        parts = [lax.dynamic_index_in_dim(t, which, 0, keepdims=False) for t in terms]
        return (parts[0].astype(F32) + parts[1].astype(F32)).astype(BF)

    total = part(mine).astype(F32)
    for d in range(1, count):
        pairs = [(i, i ^ (d << base)) for i in range(shards)]
        total = total + lax.ppermute(part(mine ^ d), "img", pairs).astype(F32)
    grad = total.astype(BF)
    if lax.axis_size("seq") != 2:
        return lax.psum(grad, "seq").astype(F32)
    row = lax.axis_index("seq")
    other = lax.ppermute(grad, "seq", [(0, 1), (1, 0)])
    first = jnp.where(row == 0, grad, other)
    second = jnp.where(row == 0, other, grad)
    return jnp.concatenate([first, second], axis=0).astype(F32)


def settle(moving, done=()):
    terms, _ = lax.optimization_barrier(([h.terms for h in moving], done))
    for h, arrived in zip(moving, terms):
        h.terms = arrived


def seq_total(part):
    peers = lax.axis_size("seq")
    if peers == 2:
        other = lax.ppermute(part, "seq", [(0, 1), (1, 0)])
        return part.astype(F32) + other.astype(F32)
    return lax.psum(part, "seq").astype(F32)


def per_device(
    tokens, valid_rows, valid_cols, block_gains, block_shifts, qkv_weight, qv_bias, table_rows, table_cols,
    proj_weight, proj_bias, fc1_weight, fc1_bias, fc2_weight, fc2_bias, fine_first, fine_first_bias,
    fine_norm_gain, fine_norm_shift, fine_second, fine_second_bias, middle_up, middle_up_bias, lateral_fine,
    lateral_middle, lateral_coarse, level_gains, level_shifts, output_convs, cotan_fine, cotan_middle,
    cotan_base, cotan_coarse,
):
    lr, cols, width = tokens.shape[1:]
    head = table_rows.shape[0]
    heads = width // head
    peers = lax.axis_size("seq")
    shards = lax.axis_size("img")
    me = lax.axis_index("seq")
    total_rows = lr * peers
    count = lr * cols
    chan = lateral_fine.shape[1]
    first_row = me * lr
    first = first_row.astype(jnp.int32).reshape(1)
    own_tokens = tokens[0].reshape(count, width)

    far = [
        lax.ppermute(own_tokens, "seq", [(i, (i + d) % peers) for i in range(peers)])
        for d in range(1, peers)
    ]
    far_tokens = jnp.concatenate(far, axis=0) if len(far) > 1 else (far[0] if far else None)

    p768 = jnp.stack(
        [
            block_gains[:, 0], block_gains[:, 1], block_shifts[:, 0], block_shifts[:, 1],
            qv_bias[:, 0], qv_bias[:, 1], proj_bias, fc2_bias,
        ]
    ).astype(F32)
    bias3 = jnp.stack([qv_bias[:, 0], jnp.zeros_like(proj_bias), qv_bias[:, 1]]).astype(F32)[:, None, :]
    qkv_own = qkv_call(own_tokens, qkv_weight, bias3, p768, 0)
    (
        fc1_bias, fine_first_bias, fine_norm_gain, fine_norm_shift, middle_up_bias, fine_second_bias, level_gains,
        level_shifts, table_cols, table_rows, valid_rows, qkv_own,
    ) = lax.optimization_barrier(
        (
            fc1_bias, fine_first_bias, fine_norm_gain, fine_norm_shift, middle_up_bias, fine_second_bias,
            level_gains, level_shifts, table_cols, table_rows, valid_rows, qkv_own,
        )
    )
    b1 = fc1_bias.astype(F32)[None]
    p384 = jnp.stack([fine_first_bias, fine_norm_gain, fine_norm_shift, middle_up_bias]).astype(F32)
    fsb = fine_second_bias.astype(F32)[None]
    p256 = jnp.concatenate([level_gains.T, level_shifts.T]).astype(F32)
    lc0, lc1 = lateral_coarse[:, 0, :], lateral_coarse[:, 1, :]

    def turned(table):
        back = table[:, ::-1]
        back = jnp.pad(back, ((0, 0), (0, 128 - back.shape[1])))
        return jnp.concatenate([back, back], axis=0)

    tw, tr = turned(table_cols), turned(table_rows)

    low_at, aug = aug_layout(total_rows)
    ranks = jnp.stack([(me - d) % peers for d in range(peers)])
    key_rows = (ranks[:, None] * lr + jnp.arange(lr)[None, :])[:, :, None]
    key_rows = jnp.broadcast_to(key_rows, (peers, lr, cols)).reshape(-1, 1)
    key_cols = jnp.broadcast_to(jnp.arange(cols)[None, None, :], (peers, lr, cols)).reshape(-1, 1)
    lane = jnp.arange(128)[None, :]
    oh1 = (lane % 64 == key_cols).astype(BF)
    lane = jnp.arange(aug - 128)[None, :]
    hot = (lane < 64) & (lane == key_cols)
    hot = hot | ((lane >= 64) & (lane < 64 + total_rows) & (lane - 64 == key_rows))
    off = low_at
    hot = hot | ((lane >= off) & (lane < off + total_rows) & (lane - off == key_rows))
    bad = (key_rows >= valid_rows[0]) | (key_cols >= valid_cols[0])
    oh2 = jnp.where(bad & (lane == off + total_rows), NEG, hot.astype(F32)).astype(BF)

    kv_far = qkv_call(far_tokens, qkv_weight, bias3, p768, 1) if far else None
    attended, qaug, lse = attend_call(
        first, qkv_own, kv_far, (tw, tr), oh1, oh2, total_rows, heads
    )
    x1, hidden, slope, y = mlp_call(own_tokens, attended, proj_weight, fc1_weight, b1, fc2_weight, p768)

    zf, zm, zb, zc = pyramid_call(
        y, lr, cols, fine_first, fine_second, middle_up, lateral_fine, lateral_middle, lc0, lc1, p384, fsb, p256
    )
    levels = [
        zf.reshape(4 * lr, 4 * cols, chan),
        zm.reshape(2 * lr, 2 * cols, chan),
        zb.reshape(lr, cols, chan),
        zc.reshape(lr // 2, cols // 2, chan),
    ]
    later, _ = lax.optimization_barrier((output_convs, zc))
    conv_weights = later.transpose(1, 0, 2).reshape(4, 3, 3 * chan, chan)
    rims = rim_exchange(levels, "seq")
    cots = [c[0] for c in (cotan_fine, cotan_middle, cotan_base, cotan_coarse)]
    maps, drs, level_sums = [None] * 4, [None] * 4, [None] * 4
    packed = None
    for level in (3, 2, 1, 0):
        z = levels[level]
        block = min(z.shape[0], max(1, 2048 // z.shape[1]))
        map_low, dr, packed, level_sums[level] = conv_call(
            level, z, rims[level], conv_weights, cots[level], p256, block, packed
        )
        maps[level], drs[level] = map_low.reshape(z.shape), dr.reshape(z.shape)

    conv_low = lax.psum_scatter(packed, "img", scatter_dimension=0, tiled=True)
    drims = rim_exchange(drs, "seq")
    unit = width // shards
    packed_row, _ = lax.optimization_barrier((jnp.arange(width)[:, None], level_sums[0]))
    shard_at, within = packed_row // unit, packed_row % unit

    def placed(size):
        own = size // shards
        at = jnp.arange(size)[None, :]
        return ((within < own) & (at == shard_at * own + within)).astype(BF)

    quart, half = lateral_fine.shape[0], lateral_middle.shape[0]
    own_q, own_h = quart // shards, half // shards
    at = jnp.arange(quart + half)[None, :]
    source = jnp.where(
        within < own_q,
        shard_at * own_q + within,
        jnp.where(within < own_q + own_h, quart + shard_at * own_h + within - own_q, -1),
    )
    place = (at == source).astype(BF)
    hots = (placed(chan), placed(half), placed(quart))
    all_tokens = jnp.concatenate([own_tokens] + far, axis=0)
    tables = jnp.concatenate([tw, tr], axis=1)
    level_rows = jnp.concatenate(
        [level_sums[k][0:1] for k in range(4)] + [level_sums[k][1:2] for k in range(4)]
    )
    drims, hots, place, all_tokens, tables, level_rows, head_hot = lax.optimization_barrier(
        (drims, hots, place, all_tokens, tables, level_rows, placed(head))
    )
    dzs = []
    for level, ways in enumerate((4, 2, 1, 1)):
        dr = drs[level]
        block = min(dr.shape[0], max(1, 2048 // dr.shape[1]))
        dzs.append(conv_back_call(level, dr, drims[level], conv_weights, ways, block))

    core = (lax.axis_index("img") & 1).astype(jnp.int32).reshape(1)
    dy, low_pack, s384, s192, s256 = pyramid_back_call(
        y, lr, cols, fine_first, fine_second, middle_up, lateral_fine, lateral_middle, lc0, lc1, p384, fsb, p256,
        *dzs, place,
    )
    low_pack, conv_low = lax.optimization_barrier((low_pack, conv_low))
    low_low = lax.psum_scatter(low_pack, "img", scatter_dimension=0, tiled=True)

    high_keep, high_send, keep2, send2, dx1, dout = mlp_back_call(
        dy, hidden, slope, fc1_weight, fc2_weight, x1, attended, proj_weight, p768,
        s384, s192, s256, level_rows, hots, core, shards,
    )
    three, four = Halving(high_keep, high_send), Halving(keep2, send2)

    def attend_part(dout_now, dtab, part, grads):
        return attend_back_call(
            first, qkv_own, kv_far, qaug, dout_now, attended, lse, tables, oh1, oh2, dtab,
            total_rows, heads, part, 2, grads,
        )

    _, dout = swap([(three, 0), (four, 0)], dout)
    dqkv, dtab = attend_part(dout, jnp.zeros((128, 256), F32), 0, None)
    settle([three, four], dtab)
    _, dtab = swap([(three, 1), (four, "y")], dtab)
    dqkv, dtab = attend_part(dout, dtab, 1, dqkv)
    last, dx, dx_far = qkv_back_call(
        all_tokens, dqkv, qkv_weight, dx1, p768, dtab, head_hot
    )
    last, low_low = lax.optimization_barrier((last, low_low))
    last_low = lax.psum_scatter(last, "img", scatter_dimension=0, tiled=True)
    settle([three, four], last)
    swap([(three, "y"), (four, 1)])
    settle([three, four])
    (dx_far, conv_low, low_low), _ = lax.optimization_barrier(
        ((dx_far, conv_low, low_low), [h.terms for h in (three, four)])
    )
    high_total, g_w2 = last_swap([three]), last_swap([four])
    for d in range(1, peers):
        part = dx_far[(d - 1) * count : d * count]
        dx = dx + lax.ppermute(part, "seq", [(i, (i - d) % peers) for i in range(peers)])
    conv_total, low_total = seq_total(conv_low), seq_total(low_low)
    last_low, conv_total, low_total, high_total, g_w2, dx = lax.optimization_barrier(
        (last_low, conv_total, low_total, high_total, g_w2, dx)
    )
    last_total = seq_total(last_low)

    def taken(total, start, size):
        return total[:, start : start + size]

    g_ff = jnp.concatenate([taken(low_total, 2 * k * half, half) for k in range(4)], axis=1)
    g_mu = jnp.concatenate([taken(low_total, (2 * k + 1) * half, half) for k in range(4)], axis=1)
    g_fs = taken(low_total, 8 * half, half)
    g_lc = jnp.stack(
        [taken(low_total, 9 * half, chan), taken(low_total, 9 * half + chan, chan)], axis=1
    )
    laterals = taken(low_total, 9 * half + 2 * chan, chan)
    g_lf, g_lm = laterals[:own_q], laterals[own_q : own_q + own_h]
    g_w1 = taken(high_total, 0, 4 * width)
    g_wp = taken(high_total, 4 * width, width)
    vec = taken(high_total, 5 * width, 128)
    own_c = chan // shards
    g_lg = jnp.concatenate([vec[:own_c, 8:12], vec[:own_c, 24:28]], axis=1)
    g_ls = jnp.concatenate([vec[:own_c, 16:20], vec[:own_c, 28:32]], axis=1)
    g_ffb, g_fng, g_fns, g_mub = (vec[:own_h, 32 + k] for k in range(4))
    g_fsb = vec[:own_q, 48]
    g_b1 = vec[:, 40:44].T.reshape(-1)
    g_pb, g_b2 = vec[:, 6], vec[:, 7]
    g_qkv = last_total[:, : 3 * width]
    late = last_total[:, 3 * width : 3 * width + 128]
    g_bg = jnp.stack([late[:, 0], vec[:, 1]], axis=1)
    g_bs = jnp.stack([late[:, 2], vec[:, 3]], axis=1)
    g_qvb = late[:, 4:6]
    own_t = head // shards
    tabs = last_total[:own_t, 3 * width + 128 :]
    g_tc = tabs[:, : 2 * cols - 1][:, ::-1]
    g_tr = tabs[:, 128 : 128 + 2 * total_rows - 1][:, ::-1]
    g_conv = conv_total.reshape(-1, 4, chan)
    return (
        maps[0][None], maps[1][None], maps[2][None], maps[3][None],
        dx.reshape(1, lr, cols, width),
        g_bg, g_bs, g_qkv, g_qvb, g_tr, g_tc, g_wp, g_pb, g_w1, g_b1, g_w2, g_b2, g_ff, g_ffb, g_fng, g_fns,
        g_fs, g_fsb, g_mu, g_mub, g_lf, g_lm, g_lc, g_lg, g_ls, g_conv,
    )


def solution(mesh):
    image = P("img", "seq", None, None)
    in_specs = (image, P("img"), P("img")) + (P(),) * 26 + (image,) * 4
    ranks = (2, 2, 2, 2, 2, 2, 2, 1, 2, 1, 2, 1, 2, 1, 1, 1, 2, 1, 2, 1, 2, 2, 3, 2, 2, 3)
    out_specs = (image,) * 5 + tuple(P(*(("img",) + (None,) * (r - 1))) for r in ranks)
    return jax.shard_map(
        per_device, mesh=mesh, in_specs=in_specs, out_specs=out_specs, check_vma=False
    )
```

```python
import functools

import jax
import jax.numpy as jnp
from jax import lax
from jax.experimental import pallas as pl
from jax.experimental.pallas import tpu as pltpu
from jax.sharding import PartitionSpec as P

F32 = jnp.float32
BF = jnp.bfloat16
NEG = -1e30
EPS = 1e-6
SQRT_HALF = 0.7071067811865476
INV_SQRT_2PI = 0.3989422804014327
VMEM_LIMIT = 60 * 1024 * 1024


def mm(left, right):
    return lax.dot_general(left, right, (((1,), (0,)), ((), ())), preferred_element_type=F32)


def mt(left, right):
    return lax.dot_general(left, right, (((1,), (1,)), ((), ())), preferred_element_type=F32)


def tm(left, right):
    return lax.dot_general(left, right, (((0,), (0,)), ((), ())), preferred_element_type=F32)


def call(
    kernel, outs, grid=(), in_specs=None, out_specs=None, scratch=(), flops=0, name=None, aliases=None
):
    return pl.pallas_call(
        kernel,
        out_shape=outs,
        grid=grid,
        in_specs=in_specs,
        out_specs=out_specs,
        scratch_shapes=scratch,
        name=name,
        input_output_aliases=aliases or {},
        cost_estimate=pl.CostEstimate(flops=int(flops) // COST_SHARE, bytes_accessed=0, transcendentals=0),
        compiler_params=pltpu.CompilerParams(vmem_limit_bytes=VMEM_LIMIT),
    )


def whole(shape):
    return pl.BlockSpec(shape, lambda *_: (0,) * len(shape))


def sds(shape, dtype):
    return jax.ShapeDtypeStruct(shape, dtype)


def stats(values):
    average = jnp.mean(values, axis=-1, keepdims=True)
    centred = values - average
    spread = jnp.mean(centred * centred, axis=-1, keepdims=True)
    inverse = lax.rsqrt(spread + EPS)
    return centred * inverse, inverse


def norm_back(grad_hat, hat, inverse):
    first = jnp.mean(grad_hat, axis=-1, keepdims=True)
    second = jnp.mean(grad_hat * hat, axis=-1, keepdims=True)
    return inverse * (grad_hat - first - hat * second)


def rowsum(values):
    return jnp.sum(values, axis=0, keepdims=True)


UNROLL = 64
COST_SHARE = 100
CONV_PIXELS = 1024
MOVE_ROWS = 8
BACK_PIXELS = 2048


def by_chunks(total, size, body, carry=0, unroll=None):
    unroll = max(1, min(unroll or UNROLL, total // size))

    def step(k, inner):
        for u in range(unroll):
            out = body(pl.ds(pl.multiple_of((k * unroll + u) * size, size), size), inner)
            inner = inner if out is None else out
        return inner

    if unroll == total // size:
        return step(0, carry)
    return lax.fori_loop(0, total // size // unroll, step, carry)


def put_shards(source, keep_ref, send_ref, lanes, shards, first, core, sem):
    unit = source.shape[0] // shards
    for s in range(shards):
        at = first + s
        rows = pl.ds(pl.multiple_of(lax.div(at, 2) * unit, unit), unit)
        piece = source.at[pl.ds(s * unit, unit)]

        @pl.when(lax.rem(at, 2) == core)
        def _():
            pltpu.make_async_copy(piece, keep_ref.at[rows, lanes], sem).start()

        @pl.when(lax.rem(at, 2) != core)
        def _():
            pltpu.make_async_copy(piece, send_ref.at[rows, lanes], sem).start()


def wait_shards(source, sem):
    pltpu.make_async_copy(source, source, sem).wait()


def repeat(count, body):
    for k in range(count):
        body(k, 0)


def gelu_pair(values):
    half = 0.5 * (1.0 + lax.erf(values * SQRT_HALF))
    slope = half + values * (jnp.exp(-0.5 * values * values) * INV_SQRT_2PI)
    return values * half, slope


def shift_matrix(size, amount):
    out_at = lax.broadcasted_iota(jnp.int32, (size, size), 0)
    in_at = lax.broadcasted_iota(jnp.int32, (size, size), 1)
    return jnp.where(in_at == out_at + amount, 1.0, 0.0).astype(BF)


def weave_matrix(size, ways, inverse=False):
    out_at = lax.broadcasted_iota(jnp.int32, (size, size), 1 if inverse else 0)
    in_at = lax.broadcasted_iota(jnp.int32, (size, size), 0 if inverse else 1)
    source = lax.rem(out_at, ways) * (size // ways) + lax.div(out_at, ways)
    return jnp.where(in_at == source, 1.0, 0.0).astype(BF)


def qkv_kernel(first, x_ref, w_ref, p_ref, out_ref, n1_ref):
    @pl.when(pl.program_id(1) == 0)
    def _():
        def norm(sl, carry):
            hat, _ = stats(x_ref[sl, :].astype(F32))
            n1_ref[sl, :] = (hat * p_ref[0:1, :] + p_ref[2:3, :]).astype(BF)

        by_chunks(x_ref.shape[0], 32, norm)

    which = pl.program_id(1) + first
    bias = jnp.where(which == 0, p_ref[4:5, :], jnp.where(which == 2, p_ref[5:6, :], 0.0))
    out_ref[...] = (mm(n1_ref[...], w_ref[...]) + bias).astype(BF)


def qkv_call(tokens, weight, p768, first):
    rows, width = tokens.shape
    block = 512
    count = 3 - first
    return call(
        functools.partial(qkv_kernel, first),
        sds((rows, count * width), BF),
        grid=(rows // block, count),
        in_specs=[
            pl.BlockSpec((block, width), lambda i, j: (i, 0)),
            pl.BlockSpec((width, width), lambda i, j: (0, j + first)),
            whole(p768.shape),
        ],
        out_specs=pl.BlockSpec((block, width), lambda i, j: (i, j)),
        scratch=[pltpu.VMEM((block, width), BF)],
        flops=2 * rows * width * width * count,
        name="qkv",
    )(tokens, weight, p768)


def aug_layout(total_rows):
    low_at = 64 + total_rows
    if low_at + total_rows + 1 > 128:
        low_at = 128
    width = 128 * (2 + (low_at + total_rows) // 128)
    return low_at, width


def build_kaug(kaug_ref, k_refs, oh1_ref, oh2_ref, odd):
    lane = lax.broadcasted_iota(jnp.int32, (512, 128), 1)
    mine = (lane >= 64) if odd else (lane < 64)
    at = 0
    for k_ref in k_refs:
        for row in range(0, k_ref.shape[0], 512):
            keys = k_ref[row : row + 512, :].astype(F32)
            hot = oh1_ref[at : at + 512, :].astype(F32)
            kaug_ref[at : at + 512, 0:128] = jnp.where(mine, keys, hot).astype(BF)
            at += 512


def build_qaug(first_row, qp, tw_ref, tr_ref, qaug_ref, odd, total_rows, scale):
    low_at, width = aug_layout(total_rows)
    tokens = qp.shape[0]
    lane = lax.broadcasted_iota(jnp.int32, (64, 128), 1)
    mine = (lane >= 64) if odd else (lane < 64)
    lane_all = lax.broadcasted_iota(jnp.int32, (tokens, 128), 1)
    mine_all = (lane_all >= 64) if odd else (lane_all < 64)
    qf = qp.astype(F32)
    qm = jnp.where(mine_all, qf, 0.0).astype(BF)
    cols = mm(qm, tw_ref[...])
    rows = mm(qm, tr_ref[...])
    for i in range(tokens // 64):
        sl = slice(64 * i, 64 * i + 64)
        upper = pltpu.roll(cols[sl], 1, 1, stride=1, stride_axis=0)
        lower = pltpu.roll(cols[sl], 65, 1, stride=1, stride_axis=0)
        first = jnp.where(mine, qf[sl] * scale, lower if odd else upper)
        col_low = lower - lower.astype(BF).astype(F32)
        shift = lax.rem(first_row + i + (65 - total_rows + 128), 128)
        row_part = pltpu.roll(rows[sl], shift, 1)
        row_low = row_part - row_part.astype(BF).astype(F32)
        qaug_ref[sl, 0:128] = first.astype(BF)
        one_at = low_at + total_rows
        if low_at < 128:
            rest = jnp.where(lane == one_at, 1.0, 0.0)
            rest = jnp.where(
                (lane >= low_at) & (lane < one_at), pltpu.roll(row_low, total_rows, 1), rest
            )
            second = jnp.where(lane < 64, col_low, jnp.where(lane < low_at, row_part, rest))
            qaug_ref[sl, 128:256] = second.astype(BF)
        else:
            second = jnp.where(
                lane < 64, col_low, jnp.where(lane < 64 + total_rows, row_part, 0.0)
            )
            third = jnp.where(
                lane < total_rows,
                pltpu.roll(row_low, 64, 1),
                jnp.where(lane == total_rows, 1.0, 0.0),
            )
            qaug_ref[sl, 128:256] = second.astype(BF)
            qaug_ref[sl, 256:384] = third.astype(BF)


def attend_kernel(total_rows, scale, others, *refs):
    first_ref, q_ref, tw_ref, tr_ref, oh1_ref, oh2_ref = refs[:6]
    k_refs = refs[6 : 6 + others]
    v_refs = refs[6 + others : 6 + 2 * others]
    o_ref, qaug_out, lse_ref, kaug_ref, v_ref, p_ref, ot_ref, scores_ref = refs[6 + 2 * others :]
    first_row = first_ref[0]
    tokens = q_ref.shape[0]
    keys = kaug_ref.shape[0]

    @pl.when(pl.program_id(0) == 0)
    def _():
        kaug_ref[:, 128:] = oh2_ref[...]

    at = 0
    for ref in v_refs:
        v_ref[at : at + ref.shape[0], :] = ref[...]
        at += ref.shape[0]
    qp = q_ref[...]
    for odd in (0, 1):
        build_kaug(kaug_ref, k_refs, oh1_ref, oh2_ref, odd)
        build_qaug(first_row, qp, tw_ref, tr_ref, qaug_out.at[odd], odd, total_rows, scale)

        def queries(t, carry):
            sl = pl.ds(pl.multiple_of(t * 256, 256), 256)
            scores_ref[...] = mt(kaug_ref[...], qaug_out[odd, sl, :])

            def highest(rows, top):
                return jnp.maximum(top, jnp.max(scores_ref[rows, :], axis=0, keepdims=True))

            top = by_chunks(keys, 128, highest, jnp.full((1, 256), NEG, F32))

            def weigh(rows, total):
                weight = jnp.exp(scores_ref[rows, :] - top)
                p_ref[rows, :] = weight.astype(BF)
                return total + rowsum(weight)

            total = by_chunks(keys, 128, weigh, jnp.zeros((1, 256), F32))
            lse_ref[0, odd : odd + 1, sl] = top + jnp.log(total)
            out_t = tm(v_ref[...], p_ref[...])
            ot_ref[64 * odd : 64 * odd + 64, sl] = out_t[64 * odd : 64 * odd + 64] / total
            return carry

        repeat(tokens // 256, queries)
    o_ref[...] = ot_ref[...].T.astype(BF)


def attend_call(first, qkv_own, kv_others, tables, oh1, oh2, total_rows, heads):
    tokens = qkv_own.shape[0]
    width = qkv_own.shape[1] // 3
    keys = oh1.shape[0]
    aug = 128 + oh2.shape[1]
    pairs = width // 128
    tw, tr = tables
    parts = 1 + (1 if kv_others is not None else 0)
    in_specs = [
        pl.BlockSpec(memory_space=pltpu.SMEM),
        pl.BlockSpec((tokens, 128), lambda h: (0, h)),
        whole(tw.shape),
        whole(tr.shape),
        whole(oh1.shape),
        whole(oh2.shape),
    ]
    k_args, v_args, k_specs, v_specs = [qkv_own], [qkv_own], [], []
    k_specs.append(pl.BlockSpec((tokens, 128), lambda h: (0, h + pairs)))
    v_specs.append(pl.BlockSpec((tokens, 128), lambda h: (0, h + 2 * pairs)))
    if kv_others is not None:
        k_args.append(kv_others)
        v_args.append(kv_others)
        k_specs.append(pl.BlockSpec((keys - tokens, 128), lambda h: (0, h)))
        v_specs.append(pl.BlockSpec((keys - tokens, 128), lambda h: (0, h + pairs)))
    scale = (width // heads) ** -0.5
    return call(
        functools.partial(attend_kernel, total_rows, scale, parts),
        [
            sds((tokens, width), BF),
            sds((heads, tokens, aug), BF),
            sds((pairs, 2, tokens), F32),
        ],
        grid=(pairs,),
        in_specs=in_specs + k_specs + v_specs,
        out_specs=[
            pl.BlockSpec((tokens, 128), lambda h: (0, h)),
            pl.BlockSpec((2, tokens, aug), lambda h: (h, 0, 0)),
            pl.BlockSpec((1, 2, tokens), lambda h: (h, 0, 0)),
        ],
        scratch=[
            pltpu.VMEM((keys, aug), BF),
            pltpu.VMEM((keys, 128), BF),
            pltpu.VMEM((keys, 256), BF),
            pltpu.VMEM((128, tokens), F32),
            pltpu.VMEM((keys, 256), F32),
        ],
        flops=25e9,
        name="attend",
    )(first, qkv_own, tw, tr, oh1, oh2, *k_args, *v_args)


def mlp_kernel(
    x_ref, o_ref, wp_ref, w1_ref, b1_ref, w2_ref, p_ref, x1_ref, g_ref, gp_ref, y_ref, n2_ref, acc_ref,
    hidden_ref,
):
    step = pl.program_id(0)
    tokens = x_ref.shape[0]

    @pl.when(step == 0)
    def _():
        product = mm(o_ref[...], wp_ref[...])
        acc_ref[...] = product

        def norm(sl, carry):
            middle = x_ref[sl, :].astype(F32) + (acc_ref[sl, :] + p_ref[6:7, :])
            x1_ref[sl, :] = middle
            acc_ref[sl, :] = jnp.zeros_like(middle)
            hat, _ = stats(middle)
            n2_ref[sl, :] = (hat * p_ref[1:2, :] + p_ref[3:4, :]).astype(BF)

        by_chunks(tokens, 32, norm)

    hidden_ref[...] = mm(n2_ref[...], w1_ref[...])

    def act(sl, carry):
        value, slope = gelu_pair(hidden_ref[sl, :] + b1_ref[...])
        g_ref[sl, :] = value.astype(BF)
        gp_ref[sl, :] = slope.astype(BF)

    by_chunks(tokens, 32, act)
    acc_ref[...] += mm(g_ref[...], w2_ref[...])

    @pl.when(step == pl.num_programs(0) - 1)
    def _():
        y_ref[...] = (x1_ref[...] + (acc_ref[...] + p_ref[7:8, :])).astype(BF)


def mlp_call(tokens, attended, wp, w1, b1, w2, p768):
    rows, width = tokens.shape
    hidden = w1.shape[1]
    return call(
        mlp_kernel,
        [sds((rows, width), F32), sds((rows, hidden), BF), sds((rows, hidden), BF), sds((rows, width), BF)],
        grid=(hidden // width,),
        in_specs=[
            whole((rows, width)),
            whole((rows, width)),
            whole(wp.shape),
            pl.BlockSpec((width, width), lambda s: (0, s)),
            pl.BlockSpec((1, width), lambda s: (0, s)),
            pl.BlockSpec((width, width), lambda s: (s, 0)),
            whole(p768.shape),
        ],
        out_specs=[
            whole((rows, width)),
            pl.BlockSpec((rows, width), lambda s: (0, s)),
            pl.BlockSpec((rows, width), lambda s: (0, s)),
            whole((rows, width)),
        ],
        scratch=[
            pltpu.VMEM((rows, width), BF),
            pltpu.VMEM((rows, width), F32),
            pltpu.VMEM((rows, width), F32),
        ],
        flops=14e9,
        name="mlp",
    )(tokens, attended, wp, w1, b1, w2, p768)


def pool_matrix(a, b, rows, cols):
    count = rows * cols // 4
    out_at = lax.broadcasted_iota(jnp.int32, (count, rows * cols), 0)
    in_at = lax.broadcasted_iota(jnp.int32, (count, rows * cols), 1)
    half = cols // 2
    source = (2 * lax.div(out_at, half) + a) * cols + 2 * lax.rem(out_at, half) + b
    return jnp.where(in_at == source, 1.0, 0.0).astype(BF)


def lateral_norm(product_ref, count, gain, shift, write):
    def norm(sl, carry):
        hat, _ = stats(product_ref[sl, :])
        write(sl, (hat * gain + shift).astype(BF))

    by_chunks(count, 64, norm)


def pyramid_kernel(
    lr, cols, y_ref, ff_ref, fs_ref, mu_ref, lf_ref, lm_ref, lc0_ref, lc1_ref, p384_ref, fsb_ref, p256_ref,
    zf_ref, zm_ref, zb_ref, zc_ref, plane_ref, mplane_ref, f2_ref, first_ref, product_ref,
    third_ref, stack_ref,
):
    tokens = lr * cols
    half = mu_ref.shape[1] // 2
    quart = fs_ref.shape[0] // 4

    def offset(b, carry):
        columns = pl.ds(pl.multiple_of(b * half, half), half)
        first_ref[...] = mm(y_ref[...], ff_ref[:, columns])

        def norm(sl, inner):
            hat, _ = stats(first_ref[sl, :] + p384_ref[0:1, :])
            value = hat * p384_ref[1:2, :] + p384_ref[2:3, :]
            f2_ref[sl, :] = (0.5 * value * (1.0 + lax.erf(value * SQRT_HALF))).astype(BF)

        by_chunks(tokens, 64, norm)

        for k in range(4):
            third_ref[k * tokens : (k + 1) * tokens, :] = (
                mt(f2_ref[...], fs_ref[k * quart : (k + 1) * quart, :]) + fsb_ref[...]
            ).astype(BF)
        stack_ref[...] = mm(third_ref[...], lf_ref[...])
        for k in range(4):

            def write(sl, values):
                plane_ref[k // 2, 2 * b + k % 2, sl, :] = values

            part = stack_ref.at[k * tokens : (k + 1) * tokens]
            lateral_norm(part, tokens, p256_ref[0:1, :], p256_ref[8:9, :], write)
        middle = (mm(y_ref[...], mu_ref[:, columns]) + p384_ref[3:4, :]).astype(BF)
        product_ref[...] = mm(middle, lm_ref[...])

        def write_middle(sl, values):
            mplane_ref[b, sl, :] = values

        lateral_norm(product_ref, tokens, p256_ref[1:2, :], p256_ref[9:10, :], write_middle)
        return carry

    repeat(2, offset)
    weave4 = weave_matrix(4 * cols, 4)
    weave2 = weave_matrix(2 * cols, 2)

    def weave(i, carry):
        sl = pl.ds(pl.multiple_of(i * cols, cols), cols)
        for c in (0, 1):
            planes = jnp.concatenate([plane_ref[c, k, sl, :] for k in range(4)], axis=0)
            zf_ref[i, c] = mm(weave4, planes).astype(BF)
        planes = jnp.concatenate([mplane_ref[k, sl, :] for k in range(2)], axis=0)
        zm_ref[i, 0] = mm(weave2, planes).astype(BF)
        return carry

    repeat(lr, weave)

    @pl.when(pl.program_id(0) == 0)
    def _():
        product_ref[...] = mm(y_ref[...], lc0_ref[...])

        def write_base(sl, values):
            zb_ref[sl, :] = values

        lateral_norm(product_ref, tokens, p256_ref[2:3, :], p256_ref[10:11, :], write_base)
        pooled = pool_picks(y_ref, pick_ref=None, rows=lr, cols=cols)
        product_ref[0 : tokens // 4, :] = mm(pooled.astype(BF), lc1_ref[...])

        def write_coarse(sl, values):
            zc_ref[sl, :] = values

        lateral_norm(product_ref, tokens // 4, p256_ref[3:4, :], p256_ref[11:12, :], write_coarse)


def pool_picks(y_ref, pick_ref, rows, cols):
    def pick(k, top):
        values = mm(pool_matrix(k // 2, k % 2, rows, cols), y_ref[...])
        if pick_ref is not None:
            pick_ref[k] = values
        return jnp.maximum(top, values)

    low = jnp.full((rows * cols // 4, y_ref.shape[1]), -jnp.inf, F32)
    for k in range(4):
        low = pick(k, low)
    return low


def pyramid_call(y, lr, cols, ff, fs, mu, lf, lm, lc0, lc1, p384, fsb, p256):
    tokens, width = y.shape
    outs = lf.shape[1]
    half2 = ff.shape[1] // 2
    return call(
        functools.partial(pyramid_kernel, lr, cols),
        [
            sds((lr, 4, 4 * cols, outs), BF),
            sds((lr, 2, 2 * cols, outs), BF),
            sds((tokens, outs), BF),
            sds((tokens // 4, outs), BF),
        ],
        grid=(2,),
        in_specs=[
            whole(y.shape),
            pl.BlockSpec((width, half2), lambda a: (0, a)),
            whole(fs.shape),
            pl.BlockSpec((width, half2), lambda a: (0, a)),
            whole(lf.shape),
            whole(lm.shape),
            whole(lc0.shape),
            whole(lc1.shape),
            whole(p384.shape),
            whole(fsb.shape),
            whole(p256.shape),
        ],
        out_specs=[
            pl.BlockSpec((lr, 2, 4 * cols, outs), lambda a: (0, a, 0, 0)),
            pl.BlockSpec((lr, 1, 2 * cols, outs), lambda a: (0, a, 0, 0)),
            whole((tokens, outs)),
            whole((tokens // 4, outs)),
        ],
        scratch=[
            pltpu.VMEM((2, 4, tokens, outs), BF),
            pltpu.VMEM((2, tokens, outs), BF),
            pltpu.VMEM((tokens, half2 // 2), BF),
            pltpu.VMEM((tokens, half2 // 2), F32),
            pltpu.VMEM((tokens, outs), F32),
            pltpu.VMEM((4 * tokens, fs.shape[0] // 4), BF),
            pltpu.VMEM((4 * tokens, outs), F32),
        ],
        flops=20e9,
        name="pyramid",
    )(y, ff, fs, mu, lf, lm, lc0, lc1, p384, fsb, p256)


def fill_padded(step, block, src_ref, rim_ref, pad_ref, left, right):
    rows, cols, chan = src_ref.shape

    @pl.when(step == 0)
    def _():
        pad_ref[0, :, chan : 2 * chan] = rim_ref[0]
        pad_ref[rows + 1, :, chan : 2 * chan] = rim_ref[1]

        def copy(row, carry):
            pad_ref[row + 1, :, chan : 2 * chan] = src_ref[row]
            return carry

        lax.fori_loop(0, rows, copy, 0)

    def move(at):
        row = pad_ref[at, :, chan : 2 * chan]
        pad_ref[at, :, 0:chan] = mm(left, row).astype(BF)
        pad_ref[at, :, 2 * chan :] = mm(right, row).astype(BF)

    start = step * block
    group = min(block, MOVE_ROWS)

    @pl.when(step == 0)
    def _():
        move(0)
        move(1)

    def move_group(k, carry):
        for q in range(group):
            move(start + 2 + k * group + q)
        return carry

    lax.fori_loop(0, block // group, move_group, 0)


def conv_rows(rows, cols, block):
    return min(block, max(1, (CONV_PIXELS if rows * cols > 4096 else CONV_PIXELS // 2) // cols))


def conv_kernel(level, block, z_ref, rim_ref, w_ref, cot_ref, p_ref, *refs):
    map_ref, dr_ref, dw_ref, sums_ref, pad_ref, dwt_ref, gradt_ref = refs[-7:]
    step = pl.program_id(0)
    rows, cols, chan = z_ref.shape
    fill_padded(
        step, block, z_ref, rim_ref, pad_ref, shift_matrix(cols, -1), shift_matrix(cols, 1)
    )
    gain = p_ref[4 + level : 5 + level, :]
    shift = p_ref[12 + level : 13 + level, :]
    few = conv_rows(rows, cols, block)
    pixels = few * cols

    @pl.when(step == 0)
    def _():
        sums_ref[...] = jnp.zeros_like(sums_ref)
        dwt_ref[...] = jnp.zeros_like(dwt_ref)
        gradt_ref[...] = jnp.zeros_like(gradt_ref)

    def add_grad(row):
        for a in range(3):
            for b in range(3):
                window = pad_ref[pl.ds(row + a, few), :, b * chan : (b + 1) * chan]
                dwt_ref[3 * a + b] += mm(gradt_ref[...], window.reshape(pixels, chan))

    def forward(k, carry):
        sum_gain, sum_shift = carry
        row = step * block + k * few
        result = None
        for a in range(3):
            part = mm(pad_ref[pl.ds(row + a, few)].reshape(pixels, 3 * chan), w_ref[0, a])
            result = part if result is None else result + part
        base = pl.multiple_of(k * pixels, pixels)
        add_grad(jnp.maximum(row - few, 0))
        for q in range(0, pixels, 64):
            sl = pl.ds(base + q, 64)
            hat, inverse = stats(result[q : q + 64])
            map_ref[sl, :] = (hat * gain + shift).astype(BF)
            cot = cot_ref[sl, :].astype(F32)
            sum_gain = sum_gain + rowsum(cot * hat)
            sum_shift = sum_shift + rowsum(cot)
            dr_ref[sl, :] = norm_back(cot * gain, hat, inverse).astype(BF)
        gradt_ref[...] = dr_ref[pl.ds(base, pixels), :].T
        return sum_gain, sum_shift

    zero = jnp.zeros((1, chan), F32)
    sum_gain, sum_shift = lax.fori_loop(0, block // few, forward, (zero, zero))
    sums_ref[0:1, :] += sum_gain
    sums_ref[1:2, :] += sum_shift

    @pl.when(step == pl.num_programs(0) - 1)
    def _():
        add_grad(rows - few)

        def turn(k, carry):
            dw_ref[pl.ds(pl.multiple_of(k * chan, chan), chan), :] = dwt_ref[k].T.astype(BF)
            return carry

        lax.fori_loop(0, 9, turn, 0)


def conv_call(level, z, rims, weights, cot, p256, block, packed):
    rows, cols, chan = z.shape
    before = [] if packed is None else [packed]
    spec = pl.BlockSpec((block * cols, chan), lambda s: (s, 0))
    return call(
        functools.partial(conv_kernel, level, block),
        [
            sds((rows * cols, chan), BF),
            sds((rows * cols, chan), BF),
            sds((9 * chan, 4 * chan), BF),
            sds((8, chan), F32),
        ],
        grid=(rows // block,),
        in_specs=[
            whole(z.shape),
            whole(rims.shape),
            pl.BlockSpec((1, 3, 3 * chan, chan), lambda s: (level, 0, 0, 0)),
            spec,
            whole(p256.shape),
        ]
        + [pl.BlockSpec(memory_space=pl.ANY)] * len(before),
        out_specs=[
            spec,
            spec,
            pl.BlockSpec((9 * chan, chan), lambda s: (0, level)),
            whole((8, chan)),
        ],
        scratch=[
            pltpu.VMEM((rows + 2, cols, 3 * chan), BF),
            pltpu.VMEM((9, chan, chan), F32),
            pltpu.VMEM((chan, conv_rows(rows, cols, block) * cols), BF),
        ],
        flops=5 * 9 * rows * cols * chan * chan,
        name=f"conv{level}",
        aliases={5: 2} if before else {},
    )(z, rims, weights, cot.reshape(rows * cols, chan), p256, *before)


def conv_back_kernel(ways, block, dr_ref, rim_ref, w_ref, dz_ref, pad_ref):
    step = pl.program_id(0)
    rows, cols, chan = dr_ref.shape
    fill_padded(
        step, block, dr_ref, rim_ref, pad_ref, shift_matrix(cols, 1), shift_matrix(cols, -1)
    )
    few = min(block, max(1, BACK_PIXELS // cols))
    pixels = few * cols
    base = cols // ways
    unweave = weave_matrix(cols, ways, inverse=True)

    def back(k, carry):
        row = step * block + k * few
        result = None
        for a in range(3):
            for b in range(3):
                window = pad_ref[pl.ds(row + 2 - a, few), :, b * chan : (b + 1) * chan]
                part = mt(
                    window.reshape(pixels, chan), w_ref[0, a, b * chan : (b + 1) * chan, :]
                )
                result = part if result is None else result + part
        low = result.astype(BF)
        if ways == 1:
            dz_ref[pl.ds(pl.multiple_of(k * pixels, pixels), pixels), :] = low
            return carry
        for q in range(few):
            planes = mm(unweave, low[q * cols : (q + 1) * cols]).astype(BF)
            inner = k * few + q
            at = pl.ds(pl.multiple_of(lax.div(inner, ways) * base, base), base)
            for w in range(ways):
                dz_ref[lax.rem(inner, ways), w, at, :] = planes[w * base : (w + 1) * base]
        return carry

    lax.fori_loop(0, block // few, back, 0)


def conv_back_call(level, dr, rims, weights, ways, block):
    rows, cols, chan = dr.shape
    if ways == 1:
        out = sds((rows * cols, chan), BF)
        spec = pl.BlockSpec((block * cols, chan), lambda s: (s, 0))
    else:
        tokens = rows * cols // (ways * ways)
        out = sds((ways, ways, tokens, chan), BF)
        spec = pl.BlockSpec(
            (ways, ways, block * cols // (ways * ways), chan), lambda s: (0, 0, s, 0)
        )
    return call(
        functools.partial(conv_back_kernel, ways, block),
        out,
        grid=(rows // block,),
        in_specs=[
            whole(dr.shape),
            whole(rims.shape),
            pl.BlockSpec((1, 3, 3 * chan, chan), lambda s: (level, 0, 0, 0)),
        ],
        out_specs=spec,
        scratch=[pltpu.VMEM((rows + 2, cols, 3 * chan), BF)],
        flops=3 * 9 * rows * cols * chan * chan,
        name=f"conv_back{level}",
    )(dr, rims, weights)


def lateral_back(product_ref, count, read, gain, dl_ref):
    zero = jnp.zeros((1, product_ref.shape[1]), F32)

    def chunk(sl, carry):
        hat, inverse = stats(product_ref[sl, :])
        grad = read(sl)
        dl_ref[sl, :] = norm_back(grad * gain, hat, inverse).astype(BF)
        return carry[0] + rowsum(grad * hat), carry[1] + rowsum(grad)

    return by_chunks(count, 64, chunk, (zero, zero))


def pyramid_back_kernel(
    lr, cols, y_ref, ff_ref, fs_ref, mu_ref, lf_ref, lm_ref, lc0_ref, lc1_ref, p384_ref,
    fsb_ref, p256_ref, dzf_ref, dzm_ref, dzb_ref, dzc_ref, place_ref,
    dy_ref, pack_ref, s384_ref, s192_ref, s256_ref,
    yt_ref, hat_ref, slope_ref, inv_ref, f2_ref, df2_ref, df1_ref, dl_ref, fs_acc, lf_acc, lm_acc,
    dcol_ref, drest_ref, product_ref, pick_ref, third_ref, stack_ref, dls_ref, sem,
):
    step = pl.program_id(0)
    tokens = lr * cols
    quart = fs_ref.shape[0] // 4
    half = ff_ref.shape[1]
    chan = lf_ref.shape[1]

    rest = drest_ref.shape[1]

    def col_copy(at):
        lanes = pl.ds(pl.multiple_of(at * 2 * half, 2 * half), 2 * half)
        return pltpu.make_async_copy(dcol_ref.at[at], pack_ref.at[:, lanes], sem.at[at])

    rest_copy = pltpu.make_async_copy(drest_ref, pack_ref.at[:, pl.ds(8 * half, rest)], sem.at[4])

    @pl.when(step == 0)
    def _():
        yt_ref[...] = y_ref[...].T
        for ref in (fs_acc, lf_acc, lm_acc, s384_ref, s192_ref, s256_ref):
            ref[...] = jnp.zeros_like(ref)
        product_ref[...] = mm(y_ref[...], lc0_ref[...])
        sg, ss = lateral_back(
            product_ref, tokens, lambda sl: dzb_ref[sl, :].astype(F32), p256_ref[2:3, :], dl_ref
        )
        s256_ref[2:3, :] = sg
        s256_ref[10:11, :] = ss
        drest_ref[:, half : half + chan] = mm(yt_ref[...], dl_ref[...]).astype(BF)
        dy_ref[...] = mt(dl_ref[...], lc0_ref[...])
        top = pool_picks(y_ref, pick_ref, lr, cols)
        low = top.astype(BF)
        product_ref[0 : tokens // 4, :] = mm(low, lc1_ref[...])
        sg, ss = lateral_back(
            product_ref, tokens // 4, lambda sl: dzc_ref[sl, :].astype(F32), p256_ref[3:4, :], dl_ref
        )
        s256_ref[3:4, :] = sg
        s256_ref[11:12, :] = ss
        grad = dl_ref[0 : tokens // 4, :]
        drest_ref[:, half + chan : half + 2 * chan] = tm(low, grad).astype(BF)
        dtop = mt(grad, lc1_ref[...])
        hits = jnp.zeros_like(top)
        for k in range(4):
            hits = hits + jnp.where(pick_ref[k] == top, 1.0, 0.0)
        dtop = dtop / hits

        def share_out(k, carry):
            share = jnp.where(pick_ref[k] == top, dtop, 0.0)
            upper = share.astype(BF)
            lower = (share - upper.astype(F32)).astype(BF)
            spread = pool_matrix(k // 2, k % 2, lr, cols)
            dy_ref[...] += tm(spread, upper) + tm(spread, lower)
            return carry

        repeat(4, share_out)

    df2_ref[...] = mm(y_ref[...], ff_ref[...])

    def norm(sl, carry):
        hat, inverse = stats(df2_ref[sl, :] + p384_ref[0:1, :])
        hat_ref[sl, :] = hat
        inv_ref[sl, :] = jnp.broadcast_to(inverse, (64, 128))
        value, slope = gelu_pair(hat * p384_ref[1:2, :] + p384_ref[2:3, :])
        f2_ref[sl, :] = value.astype(BF)
        slope_ref[sl, :] = slope
        df2_ref[sl, :] = jnp.zeros_like(hat)

    by_chunks(tokens, 64, norm)

    for k in range(4):
        third_ref[k * tokens : (k + 1) * tokens, :] = (
            mt(f2_ref[...], fs_ref[k * quart : (k + 1) * quart, :]) + fsb_ref[...]
        ).astype(BF)
    stack_ref[...] = mm(third_ref[...], lf_ref[...])
    for k in range(4):
        sg, ss = lateral_back(
            stack_ref.at[k * tokens : (k + 1) * tokens],
            tokens,
            lambda sl: dzf_ref[0, k // 2, 0, k % 2, sl, :].astype(F32),
            p256_ref[0:1, :],
            dls_ref.at[k * tokens : (k + 1) * tokens],
        )
        s256_ref[0:1, :] += sg
        s256_ref[8:9, :] += ss
    lf_acc[...] += tm(third_ref[...], dls_ref[...])
    third_ref[...] = mt(dls_ref[...], lf_ref[...]).astype(BF)
    s192_ref[0:1, :] += rowsum(third_ref[...].astype(F32))
    for k in range(4):
        rows = slice(k * quart, (k + 1) * quart)
        fs_acc[rows, :] += tm(third_ref[k * tokens : (k + 1) * tokens, :], f2_ref[...])
        df2_ref[...] += mm(third_ref[k * tokens : (k + 1) * tokens, :], fs_ref[rows, :])
    zero = jnp.zeros((1, half), F32)

    def first_back(sl, carry):
        sum_gain, sum_shift, sum_bias = carry
        hat = hat_ref[sl, :]
        grad = df2_ref[sl, :] * slope_ref[sl, :]
        low = norm_back(grad * p384_ref[1:2, :], hat, inv_ref[sl, 0:1]).astype(BF)
        df1_ref[sl, :] = low
        return (
            sum_gain + rowsum(grad * hat),
            sum_shift + rowsum(grad),
            sum_bias + rowsum(low.astype(F32)),
        )

    sum_gain, sum_shift, sum_bias = by_chunks(tokens, 64, first_back, (zero, zero, zero))
    s384_ref[0:1, :] += sum_bias
    s384_ref[1:2, :] += sum_gain
    s384_ref[2:3, :] += sum_shift
    dcol_ref[step, :, 0:half] = mm(yt_ref[...], df1_ref[...]).astype(BF)
    dy_ref[...] += mt(df1_ref[...], ff_ref[...])

    f2_ref[...] = (mm(y_ref[...], mu_ref[...]) + p384_ref[3:4, :]).astype(BF)
    product_ref[...] = mm(f2_ref[...], lm_ref[...])
    sg, ss = lateral_back(
        product_ref, tokens, lambda sl: dzm_ref[0, 0, sl, :].astype(F32), p256_ref[1:2, :], dl_ref
    )
    s256_ref[1:2, :] += sg
    s256_ref[9:10, :] += ss
    lm_acc[...] += tm(f2_ref[...], dl_ref[...])
    df1_ref[...] = mt(dl_ref[...], lm_ref[...]).astype(BF)
    s384_ref[3:4, :] += rowsum(df1_ref[...].astype(F32))
    dcol_ref[step, :, half:] = mm(yt_ref[...], df1_ref[...]).astype(BF)
    col_copy(step).start()
    dy_ref[...] += mt(df1_ref[...], mu_ref[...])

    @pl.when(step == pl.num_programs(0) - 1)
    def _():
        drest_ref[:, 0:half] = fs_acc[...].astype(BF)
        laterals = jnp.concatenate([lf_acc[...], lm_acc[...]], axis=0).astype(BF)
        drest_ref[:, half + 2 * chan : half + 3 * chan] = mm(place_ref[...], laterals).astype(BF)
        rest_copy.start()
        for at in range(4):
            col_copy(at).wait()
        rest_copy.wait()


def pyramid_back_call(
    y, lr, cols, ff, fs, mu, lf, lm, lc0, lc1, p384, fsb, p256, dzf, dzm, dzb, dzc, place
):
    tokens, width = y.shape
    half = fs.shape[1]
    quart = fsb.shape[1]
    outs = lf.shape[1]
    col_block = pl.BlockSpec((width, half), lambda s: (0, s))
    return call(
        functools.partial(pyramid_back_kernel, lr, cols),
        [
            sds((tokens, width), F32),
            sds((width, 9 * half + 3 * outs), BF),
            sds((8, half), F32),
            sds((8, quart), F32),
            sds((16, outs), F32),
        ],
        grid=(4,),
        in_specs=[
            whole(y.shape),
            col_block,
            whole(fs.shape),
            col_block,
            whole(lf.shape),
            whole(lm.shape),
            whole(lc0.shape),
            whole(lc1.shape),
            whole(p384.shape),
            whole(fsb.shape),
            whole(p256.shape),
            pl.BlockSpec((1, 2, 1, 2, tokens, outs), lambda s: (s // 2, 0, s % 2, 0, 0, 0)),
            pl.BlockSpec((1, 1, tokens, outs), lambda s: (s // 2, s % 2, 0, 0)),
            whole(dzb.shape),
            whole(dzc.shape),
            whole(place.shape),
        ],
        out_specs=[
            whole((tokens, width)),
            pl.BlockSpec(memory_space=pl.ANY),
            whole((8, half)),
            whole((8, quart)),
            whole((16, outs)),
        ],
        scratch=[
            pltpu.VMEM((width, tokens), BF),
            pltpu.VMEM((tokens, half), F32),
            pltpu.VMEM((tokens, half), F32),
            pltpu.VMEM((tokens, 128), F32),
            pltpu.VMEM((tokens, half), BF),
            pltpu.VMEM((tokens, half), F32),
            pltpu.VMEM((tokens, half), BF),
            pltpu.VMEM((tokens, outs), BF),
            pltpu.VMEM(fs.shape, F32),
            pltpu.VMEM(lf.shape, F32),
            pltpu.VMEM(lm.shape, F32),
            pltpu.VMEM((4, width, 2 * half), BF),
            pltpu.VMEM((width, half + 3 * outs), BF),
            pltpu.VMEM((tokens, outs), F32),
            pltpu.VMEM((4, tokens // 4, width), F32),
            pltpu.VMEM((4 * tokens, quart), BF),
            pltpu.VMEM((4 * tokens, outs), F32),
            pltpu.VMEM((4 * tokens, outs), BF),
            pltpu.SemaphoreType.DMA((5,)),
        ],
        flops=45e9,
        name="pyramid_back",
    )(
        y, ff, fs, mu, lf, lm, lc0, lc1, p384, fsb, p256,
        dzf.reshape(2, 2, 2, 2, tokens, outs), dzm, dzb, dzc, place,
    )


def mlp_back_kernel(
    shards,
    core_ref, dy_ref, g_ref, gp_ref, w1_ref, w2_ref, x1_ref, o_ref, wp_ref, p_ref, s384_ref, s192_ref, s256_ref, levels_ref,
    hot256_ref, hot384_ref, hot192_ref,
    keep_ref, send_ref, keep2_ref, send2_ref, dx1_ref, do_ref,
    n2t_ref, d2_ref, dn2_ref, low_ref, sums_ref, vec_ref, dw1_ref, dw2_ref, rest_ref, temp_ref, sem,
):
    step = pl.program_id(0)
    steps = pl.num_programs(0)
    tokens, width = dy_ref.shape
    unit = width // shards
    hidden = 4 * width

    core = core_ref[0]

    @pl.when(step == 0)
    def _():
        sums_ref[...] = jnp.zeros_like(sums_ref)
        vec_ref[...] = jnp.zeros_like(vec_ref)
        dn2_ref[...] = jnp.zeros_like(dn2_ref)

        def norm(sl, total):
            hat, _ = stats(x1_ref[sl, :])
            low_ref[sl, :] = (hat * p_ref[1:2, :] + p_ref[3:4, :]).astype(BF)
            low = dy_ref[sl, :].astype(BF)
            d2_ref[sl, :] = low
            return total + rowsum(low.astype(F32))

        sums_ref[7:8, :] = by_chunks(tokens, 32, norm, jnp.zeros((1, width), F32))
        n2t_ref[...] = low_ref[...].T

    dw2_ref[step] = tm(g_ref[...], d2_ref[...]).astype(BF)
    put_shards(
        dw2_ref.at[step], keep2_ref, send2_ref, pl.ds(0, width), shards // 4, step * (shards // 4), core,
        sem.at[5 + step],
    )
    temp_ref[...] = mt(d2_ref[...], w2_ref[...])

    def act(sl, carry):
        low_ref[sl, :] = (temp_ref[sl, :] * gp_ref[sl, :].astype(F32)).astype(BF)

    by_chunks(tokens, 32, act)
    db1 = tm(low_ref[...], jnp.ones((tokens, 128), BF))
    lane = lax.broadcasted_iota(jnp.int32, (unit, 128), 1)
    for q in range(shards // 4):
        entry = jnp.zeros((unit, 128), F32)
        for k in range(4):
            sl = slice((4 * q + k) * unit, (4 * q + k + 1) * unit)
            entry = jnp.where(lane == 40 + k, db1[sl], entry)
        vec_ref[pl.ds(pl.multiple_of(step * (width // 4) + q * unit, 8), unit), :] += entry
    dw1_ref[step] = mm(n2t_ref[...], low_ref[...]).astype(BF)
    lanes = pl.ds(pl.multiple_of(step * width, width), width)
    put_shards(dw1_ref.at[step], keep_ref, send_ref, lanes, shards, 0, core, sem.at[step])
    dn2_ref[...] += mt(low_ref[...], w1_ref[...])

    @pl.when(step == steps - 1)
    def _():
        zero = jnp.zeros((1, width), F32)

        def back(sl, carry):
            hat, inverse = stats(x1_ref[sl, :])
            grad = dn2_ref[sl, :]
            dx1 = dy_ref[sl, :] + norm_back(grad * p_ref[1:2, :], hat, inverse)
            dx1_ref[sl, :] = dx1
            low = dx1.astype(BF)
            d2_ref[sl, :] = low
            return (
                carry[0] + rowsum(grad * hat),
                carry[1] + rowsum(grad),
                carry[2] + rowsum(low.astype(F32)),
            )

        sum_gain, sum_shift, sum_bias = by_chunks(tokens, 32, back, (zero, zero, zero))
        sums_ref[1:2, :] = sum_gain
        sums_ref[3:4, :] = sum_shift
        sums_ref[6:7, :] = sum_bias
        rest_ref[:, 0:width] = tm(o_ref[...], d2_ref[...]).astype(BF)
        do_ref[...] = mt(d2_ref[...], wp_ref[...]).astype(BF)

        def lanes_of(rows, before):
            after = 128 - before - rows.shape[0]
            parts = [jnp.zeros((before, rows.shape[1]), F32)] if before else []
            parts += [rows, jnp.zeros((after, rows.shape[1]), F32)]
            return jnp.concatenate(parts, axis=0)

        spread = mt(hot256_ref[...], lanes_of(s256_ref[...], 8).astype(BF))
        spread = spread + mt(hot256_ref[...], lanes_of(levels_ref[...], 24).astype(BF))
        spread = spread + mt(hot384_ref[...], lanes_of(s384_ref[...], 32).astype(BF))
        spread = spread + mt(hot192_ref[...], lanes_of(s192_ref[...], 48).astype(BF))
        spread = spread + lanes_of(sums_ref[...], 0).T
        rest_ref[:, width:] = (vec_ref[...] + spread).astype(BF)
        put_shards(
            rest_ref, keep_ref, send_ref, pl.ds(hidden, width + 128), shards, 0, core, sem.at[4]
        )
        for at in range(4):
            wait_shards(dw1_ref.at[at], sem.at[at])
            wait_shards(dw2_ref.at[at], sem.at[5 + at])
        wait_shards(rest_ref, sem.at[4])


def mlp_back_call(
    dy, g, gp, w1, w2, x1, attended, wp, p768, s384, s192, s256, levels, hots, core, shards
):
    rows, width = dy.shape
    hidden = g.shape[1]
    full = whole((rows, width))
    column = pl.BlockSpec((rows, width), lambda s: (0, s))
    smalls = [p768, s384, s192, s256, levels, *hots]
    return call(
        functools.partial(mlp_back_kernel, shards),
        [
            sds((width // 2, hidden + width + 128), BF),
            sds((width // 2, hidden + width + 128), BF),
            sds((hidden // 2, width), BF),
            sds((hidden // 2, width), BF),
            sds((rows, width), F32),
            sds((rows, width), BF),
        ],
        grid=(hidden // width,),
        in_specs=[
            pl.BlockSpec(memory_space=pltpu.SMEM),
            full,
            column,
            column,
            pl.BlockSpec((width, width), lambda s: (0, s)),
            pl.BlockSpec((width, width), lambda s: (s, 0)),
            full,
            full,
            whole((width, width)),
        ]
        + [whole(a.shape) for a in smalls],
        out_specs=[
            pl.BlockSpec(memory_space=pl.ANY),
            pl.BlockSpec(memory_space=pl.ANY),
            pl.BlockSpec(memory_space=pl.ANY),
            pl.BlockSpec(memory_space=pl.ANY),
            full,
            full,
        ],
        scratch=[
            pltpu.VMEM((width, rows), BF),
            pltpu.VMEM((rows, width), BF),
            pltpu.VMEM((rows, width), F32),
            pltpu.VMEM((rows, width), BF),
            pltpu.VMEM((8, width), F32),
            pltpu.VMEM((width, 128), F32),
            pltpu.VMEM((4, width, width), BF),
            pltpu.VMEM((4, width, width), BF),
            pltpu.VMEM((width, width + 128), BF),
            pltpu.VMEM((rows, width), F32),
            pltpu.SemaphoreType.DMA((9,)),
        ],
        flops=25e9,
        name="mlp_back",
    )(core, dy, g, gp, w1, w2, x1, attended, wp, *smalls)


def roll_back(values, amount):
    moved = jnp.concatenate(
        [
            pltpu.roll(values[8 * g : 8 * g + 8], (amount - 7 - 8 * g) % 128, 1)
            for g in range(values.shape[0] // 8)
        ],
        axis=0,
    )
    left = 7 - lax.rem(lax.broadcasted_iota(jnp.int32, values.shape, 0), 8)
    for step in (1, 2, 4):
        moved = jnp.where((left & step) > 0, pltpu.roll(moved, step, 1), moved)
    return moved


def attend_back_kernel(total_rows, scale, others, *refs):
    first_ref, q_ref, qaug_ref, do_ref, o_ref, lse_ref, tab_ref, oh1_ref, oh2_ref, before_ref = refs[:10]
    k_refs = refs[10 : 10 + others]
    v_refs = refs[10 + others : 10 + 2 * others]
    rest = refs[-15:]
    (
        dqkv_ref, dtab_ref, kaug_ref, v_ref, p_ref, ds_ref, dqt_ref, df_ref, qm_ref, dom_ref, delta_ref,
        scores_ref, dweight_ref, dk_acc, dv_acc,
    ) = rest
    first_row = first_ref[0]
    tokens = q_ref.shape[0]
    keys = kaug_ref.shape[0]

    @pl.when(pl.program_id(0) == 0)
    def _():
        kaug_ref[:, 128:] = oh2_ref[...]
        dtab_ref[...] = before_ref[...]

    at = 0
    for ref in v_refs:
        v_ref[at : at + ref.shape[0], :] = ref[...]
        at += ref.shape[0]
    lane_all = lax.broadcasted_iota(jnp.int32, (tokens, 128), 1)
    lane = lax.broadcasted_iota(jnp.int32, (64, 128), 1)
    qf = q_ref[...].astype(F32)
    dof = do_ref[...].astype(F32)
    delta_t = (dof * o_ref[...].astype(F32)).T
    dk_acc[...] = jnp.zeros_like(dk_acc)
    dv_acc[...] = jnp.zeros_like(dv_acc)
    dq = None
    for odd in (0, 1):
        mine_all = (lane_all >= 64) if odd else (lane_all < 64)
        other = (lane < 64) if odd else (lane >= 64)
        build_kaug(kaug_ref, k_refs, oh1_ref, oh2_ref, odd)
        qm = jnp.where(mine_all, qf, 0.0).astype(BF)
        dom = jnp.where(mine_all, dof, 0.0).astype(BF)
        delta = rowsum(delta_t[64 * odd : 64 * odd + 64])
        qm_ref[...] = qm
        dom_ref[...] = dom
        delta_ref[...] = delta

        def queries(t, carry):
            sl = pl.ds(pl.multiple_of(t * 256, 256), 256)
            scores_ref[...] = mt(kaug_ref[...], qaug_ref[odd, sl, :])
            dweight_ref[...] = mt(v_ref[...], dom_ref[sl, :])
            lse = lse_ref[0, odd : odd + 1, sl]
            shift = delta_ref[:, sl]

            def weigh(rows, inner):
                weight = jnp.exp(scores_ref[rows, :] - lse)
                p_ref[rows, :] = weight.astype(BF)
                ds_ref[rows, :] = (weight * (dweight_ref[rows, :] - shift)).astype(BF)

            by_chunks(keys, 128, weigh)
            dk_acc[...] += mm(ds_ref[...], qm_ref[sl, :])
            dv_acc[...] += mm(p_ref[...], dom_ref[sl, :])
            dqt_ref[:, sl] = tm(kaug_ref[...], ds_ref[...])
            return carry

        repeat(tokens // 256, queries)
        dqa = dqt_ref[0:256, :].T
        for i in range(tokens // 64):
            sl = slice(64 * i, 64 * i + 64)
            cols = roll_back(jnp.where(other, dqa[sl, 0:128], 0.0), 63 if odd else 127)
            shift = lax.rem(63 + total_rows - (first_row + i) + 128, 128)
            rows = pltpu.roll(
                jnp.where((lane >= 64) & (lane < 64 + total_rows), dqa[sl, 128:256], 0.0), shift, 1
            )
            df_ref[sl, 0:128] = cols.astype(BF)
            df_ref[sl, 128:256] = rows.astype(BF)
        from_tables = mt(df_ref[...], tab_ref[...])
        part = jnp.where(mine_all, dqa[:, 0:128] * scale + from_tables, 0.0)
        dq = part if dq is None else dq + part
        dtab_ref[...] += tm(qm, df_ref[...])
    dqkv_ref[0, 0:tokens, :] = dq.astype(BF)
    dqkv_ref[1] = (dk_acc[...] * scale).astype(BF)
    dqkv_ref[2] = dv_acc[...].astype(BF)


def attend_back_call(
    first, qkv_own, kv_others, qaug, dout, attended, lse, tab, oh1, oh2, dtab, total_rows, heads, part, parts, grads
):
    tokens = qkv_own.shape[0]
    width = qkv_own.shape[1] // 3
    keys = oh1.shape[0]
    aug = 128 + oh2.shape[1]
    pairs = width // 128
    count = pairs // parts
    base = part * count
    sources = 1 + (1 if kv_others is not None else 0)
    own = pl.BlockSpec((tokens, 128), lambda h: (0, h + base))
    in_specs = [
        pl.BlockSpec(memory_space=pltpu.SMEM),
        own,
        pl.BlockSpec((2, tokens, aug), lambda h: (h + base, 0, 0)),
        own,
        own,
        pl.BlockSpec((1, 2, tokens), lambda h: (h + base, 0, 0)),
        whole(tab.shape),
        whole(oh1.shape),
        whole(oh2.shape),
        whole(dtab.shape),
    ]
    k_args, v_args, k_specs, v_specs = [qkv_own], [qkv_own], [], []
    k_specs.append(pl.BlockSpec((tokens, 128), lambda h: (0, h + base + pairs)))
    v_specs.append(pl.BlockSpec((tokens, 128), lambda h: (0, h + base + 2 * pairs)))
    if kv_others is not None:
        k_args.append(kv_others)
        v_args.append(kv_others)
        k_specs.append(pl.BlockSpec((keys - tokens, 128), lambda h: (0, h + base)))
        v_specs.append(pl.BlockSpec((keys - tokens, 128), lambda h: (0, h + base + pairs)))
    scale = (width // heads) ** -0.5
    earlier = [] if grads is None else [grads]
    return call(
        functools.partial(attend_back_kernel, total_rows, scale, sources),
        [sds((3, keys, width), BF), sds((128, 256), F32)],
        grid=(count,),
        in_specs=in_specs + k_specs + v_specs + [pl.BlockSpec(memory_space=pl.ANY)] * len(earlier),
        out_specs=[pl.BlockSpec((3, keys, 128), lambda h: (0, 0, h + base)), whole((128, 256))],
        scratch=[
            pltpu.VMEM((keys, aug), BF),
            pltpu.VMEM((keys, 128), BF),
            pltpu.VMEM((keys, 256), BF),
            pltpu.VMEM((keys, 256), BF),
            pltpu.VMEM((aug, tokens), F32),
            pltpu.VMEM((tokens, 256), BF),
            pltpu.VMEM((tokens, 128), BF),
            pltpu.VMEM((tokens, 128), BF),
            pltpu.VMEM((1, tokens), F32),
            pltpu.VMEM((keys, 256), F32),
            pltpu.VMEM((keys, 256), F32),
            pltpu.VMEM((keys, 128), F32),
            pltpu.VMEM((keys, 128), F32),
        ],
        flops=30e9 / parts,
        name="attend_back",
        aliases={10 + 2 * sources: 0} if earlier else {},
    )(first, qkv_own, qaug, dout, attended, lse, tab, oh1, oh2, dtab, *k_args, *v_args, *earlier)


def qkv_back_kernel(
    x_ref, dqkv_ref, w_ref, dx1_ref, p_ref, dtab_ref, hot_ref,
    pack_ref, dx_ref, far_ref, nt_ref, low_ref, dn_ref, sums_ref, dw_ref, out_ref, extra_ref, sem,
):
    step = pl.program_id(0)
    tokens, width = x_ref.shape

    def w_copy(at):
        return pltpu.make_async_copy(
            out_ref.at[at], pack_ref.at[:, pl.ds(at * width, width)], sem.at[at]
        )

    extra_copy = pltpu.make_async_copy(extra_ref, pack_ref.at[:, pl.ds(3 * width, 384)], sem.at[3])

    def norm_chunk(sl, carry):
        hat, _ = stats(x_ref[sl, :].astype(F32))
        low_ref[sl, :] = (hat * p_ref[0:1, :] + p_ref[2:3, :]).astype(BF)

    by_chunks(tokens, 32, norm_chunk)
    nt_ref[...] = low_ref[...].T

    @pl.when(step == 0)
    def _():
        sums_ref[...] = jnp.zeros_like(sums_ref)
        sums_ref[4:5, :] = rowsum(dqkv_ref[0].astype(F32))
        both = dtab_ref[...]
        tables = (both[0:64] + both[64:128]).astype(BF)
        extra_ref[:, 128:384] = mm(hot_ref[...], tables).astype(BF)
        dw_ref[...] = jnp.zeros_like(dw_ref)

    dn_ref[...] = jnp.zeros_like(dn_ref)

    def product(at, carry):
        lanes = pl.ds(pl.multiple_of(at * width, width), width)
        dw_ref[at] += mm(nt_ref[...], dqkv_ref[at])
        dn_ref[...] += mt(dqkv_ref[at], w_ref[:, lanes])
        return carry

    lax.fori_loop(jnp.where(step == 0, 0, 1), 3, product, 0)
    sums_ref[5:6, :] += rowsum(dqkv_ref[2].astype(F32))

    def back_chunk(sl, carry):
        sum_gain, sum_shift = carry
        hat, inverse = stats(x_ref[sl, :].astype(F32))
        grad = dn_ref[sl, :]
        dn_ref[sl, :] = norm_back(grad * p_ref[0:1, :], hat, inverse)
        return sum_gain + rowsum(grad * hat), sum_shift + rowsum(grad)

    zero = jnp.zeros((1, width), F32)
    sum_gain, sum_shift = by_chunks(tokens, 32, back_chunk, (zero, zero))
    sums_ref[0:1, :] += sum_gain
    sums_ref[2:3, :] += sum_shift

    @pl.when(step == 0)
    def _():
        dx_ref[...] = dx1_ref[...] + dn_ref[...]

    far_ref[...] = dn_ref[...].astype(BF)

    @pl.when(step == pl.num_programs(0) - 1)
    def _():
        def put(at, carry):
            out_ref[at] = dw_ref[at].astype(BF)
            w_copy(at).start()
            return carry

        lax.fori_loop(0, 3, put, 0)
        padded = jnp.concatenate([sums_ref[...], jnp.zeros((120, width), F32)], axis=0)
        extra_ref[:, 0:128] = padded.T.astype(BF)
        extra_copy.start()
        for at in range(3):
            w_copy(at).wait()
        extra_copy.wait()


def qkv_back_call(tokens, dqkv, weight, dx1, p768, dtab, hot):
    rows, width = dx1.shape
    blocks = tokens.shape[0] // rows
    full = whole((rows, width))
    block = pl.BlockSpec((rows, width), lambda s: (s, 0))
    return call(
        qkv_back_kernel,
        [
            sds((width, 3 * width + 384), BF),
            sds((rows, width), F32),
            sds(((max(blocks, 2) - 1) * rows, width), BF),
        ],
        grid=(blocks,),
        in_specs=[
            block,
            pl.BlockSpec((3, rows, width), lambda s: (0, s, 0)),
            whole(weight.shape),
            full,
            whole(p768.shape),
            whole(dtab.shape),
            whole(hot.shape),
        ],
        out_specs=[
            pl.BlockSpec(memory_space=pl.ANY),
            full,
            pl.BlockSpec((rows, width), lambda s: (jnp.maximum(s - 1, 0), 0)),
        ],
        scratch=[
            pltpu.VMEM((width, rows), BF),
            pltpu.VMEM((rows, width), BF),
            pltpu.VMEM((rows, width), F32),
            pltpu.VMEM((8, width), F32),
            pltpu.VMEM((3, width, width), F32),
            pltpu.VMEM((3, width, width), BF),
            pltpu.VMEM((width, 384), BF),
            pltpu.SemaphoreType.DMA((4,)),
        ],
        flops=8e9,
        name="qkv_back",
    )(tokens, dqkv, weight, dx1, p768, dtab, hot)


def rim_exchange(levels, axis):
    peers = lax.axis_size(axis)
    chan = levels[0].shape[-1]
    counts = [level.shape[1] for level in levels]
    lasts = jnp.concatenate([level[-1] for level in levels], axis=0)
    firsts = jnp.concatenate([level[0] for level in levels], axis=0)
    if peers == 2:
        me = lax.axis_index(axis)
        got = lax.ppermute(jnp.where(me == 0, lasts, firsts), axis, [(0, 1), (1, 0)])
        nothing = jnp.zeros_like(got)
        before = jnp.where(me == 1, got, nothing)
        after = jnp.where(me == 0, got, nothing)
    else:
        before = lax.ppermute(lasts, axis, [(i, i + 1) for i in range(peers - 1)])
        after = lax.ppermute(firsts, axis, [(i + 1, i) for i in range(peers - 1)])
    both = jnp.stack([before, after])
    rims, at = [], 0
    for count in counts:
        rims.append(both[:, at : at + count])
        at += count
    return rims


class Halving:
    def __init__(self, keep, send):
        bits = lax.axis_size("img").bit_length() - 1
        self.left = list(range(1, bits))[::-1]
        self.shape = (2,) * (bits - 1) + (keep.shape[0] >> (bits - 1), keep.shape[1])
        self.keep, self.first = keep.reshape(self.shape), send.reshape(self.shape)

    def split(self, step):
        if step == 0:
            self.route = ("img", [(i, i ^ 1) for i in range(lax.axis_size("img"))])
            return self.first
        terms = self.terms
        if step == "y":
            at, mine, axis, pairs = len(self.left), lax.axis_index("seq"), "seq", [(0, 1), (1, 0)]
            shape = terms[0].shape
            terms = [t.reshape(shape[:-2] + (2, shape[-2] // 2, shape[-1])) for t in terms]
        else:
            at, mine, axis = self.left.index(step), (lax.axis_index("img") >> step) & 1, "img"
            pairs = [(i, i ^ (1 << step)) for i in range(lax.axis_size("img"))]
            self.left.remove(step)
        self.route = (axis, pairs)

        def half(which):
            parts = [lax.dynamic_index_in_dim(t, which, at, keepdims=False) for t in terms]
            return (parts[0].astype(F32) + parts[1].astype(F32)).astype(BF)

        self.keep = half(mine)
        return half(1 - mine)


def swap(steps, after=()):
    if lax.axis_size("seq") != 2:
        steps = [(h, step) for h, step in steps if step != "y"]
    sends = [h.split(step) for h, step in steps]
    keeps = [h.keep for h, _ in steps]
    sends, keeps, after = lax.optimization_barrier((sends, keeps, after))
    for (h, _), send, keep in zip(steps, sends, keeps):
        h.terms = [keep, lax.ppermute(flat(send), *h.route).reshape(send.shape)]
    return [h for h, _ in steps], after


def flat(values):
    return values.reshape(-1, values.shape[-1])


def last_swap(group):
    left = group[0].left
    count = 1 << len(left)
    base = left[-1]
    mine = (lax.axis_index("img") >> base) & (count - 1)
    shards = lax.axis_size("img")
    terms = [
        jnp.concatenate(
            [h.terms[k].reshape((count,) + h.terms[k].shape[len(left) :]) for h in group], axis=-1
        )
        for k in (0, 1)
    ]

    def part(which):
        parts = [lax.dynamic_index_in_dim(t, which, 0, keepdims=False) for t in terms]
        return (parts[0].astype(F32) + parts[1].astype(F32)).astype(BF)

    total = part(mine).astype(F32)
    for d in range(1, count):
        pairs = [(i, i ^ (d << base)) for i in range(shards)]
        total = total + lax.ppermute(part(mine ^ d), "img", pairs).astype(F32)
    grad = total.astype(BF)
    if lax.axis_size("seq") != 2:
        return lax.psum(grad, "seq").astype(F32)
    row = lax.axis_index("seq")
    other = lax.ppermute(grad, "seq", [(0, 1), (1, 0)])
    first = jnp.where(row == 0, grad, other)
    second = jnp.where(row == 0, other, grad)
    return jnp.concatenate([first, second], axis=0).astype(F32)


def settle(moving, done=()):
    terms, _ = lax.optimization_barrier(([h.terms for h in moving], done))
    for h, arrived in zip(moving, terms):
        h.terms = arrived


def seq_total(part):
    peers = lax.axis_size("seq")
    if peers == 2:
        other = lax.ppermute(part, "seq", [(0, 1), (1, 0)])
        return part.astype(F32) + other.astype(F32)
    return lax.psum(part, "seq").astype(F32)


def per_device(
    tokens, valid_rows, valid_cols, block_gains, block_shifts, qkv_weight, qv_bias, table_rows, table_cols,
    proj_weight, proj_bias, fc1_weight, fc1_bias, fc2_weight, fc2_bias, fine_first, fine_first_bias,
    fine_norm_gain, fine_norm_shift, fine_second, fine_second_bias, middle_up, middle_up_bias, lateral_fine,
    lateral_middle, lateral_coarse, level_gains, level_shifts, output_convs, cotan_fine, cotan_middle,
    cotan_base, cotan_coarse,
):
    lr, cols, width = tokens.shape[1:]
    head = table_rows.shape[0]
    heads = width // head
    peers = lax.axis_size("seq")
    shards = lax.axis_size("img")
    me = lax.axis_index("seq")
    total_rows = lr * peers
    count = lr * cols
    chan = lateral_fine.shape[1]
    first_row = me * lr
    first = first_row.astype(jnp.int32).reshape(1)
    own_tokens = tokens[0].reshape(count, width)

    far = [
        lax.ppermute(own_tokens, "seq", [(i, (i + d) % peers) for i in range(peers)])
        for d in range(1, peers)
    ]
    far_tokens = jnp.concatenate(far, axis=0) if len(far) > 1 else (far[0] if far else None)

    p768 = jnp.concatenate(
        [block_gains.T, block_shifts.T, qv_bias.T, proj_bias[None], fc2_bias[None]]
    ).astype(F32)
    qkv_own = qkv_call(own_tokens, qkv_weight, p768, 0)
    (
        fc1_bias, fine_first_bias, fine_norm_gain, fine_norm_shift, middle_up_bias, fine_second_bias, level_gains,
        level_shifts, table_cols, table_rows, valid_rows, qkv_own,
    ) = lax.optimization_barrier(
        (
            fc1_bias, fine_first_bias, fine_norm_gain, fine_norm_shift, middle_up_bias, fine_second_bias,
            level_gains, level_shifts, table_cols, table_rows, valid_rows, qkv_own,
        )
    )
    b1 = fc1_bias.astype(F32)[None]
    p384 = jnp.stack([fine_first_bias, fine_norm_gain, fine_norm_shift, middle_up_bias]).astype(F32)
    fsb = fine_second_bias.astype(F32)[None]
    p256 = jnp.concatenate([level_gains.T, level_shifts.T]).astype(F32)
    lc0, lc1 = lateral_coarse[:, 0, :], lateral_coarse[:, 1, :]

    def turned(table):
        back = table[:, ::-1]
        back = jnp.pad(back, ((0, 0), (0, 128 - back.shape[1])))
        return jnp.concatenate([back, back], axis=0)

    tw, tr = turned(table_cols), turned(table_rows)

    low_at, aug = aug_layout(total_rows)
    ranks = jnp.stack([(me - d) % peers for d in range(peers)])
    key_rows = (ranks[:, None] * lr + jnp.arange(lr)[None, :])[:, :, None]
    key_rows = jnp.broadcast_to(key_rows, (peers, lr, cols)).reshape(-1, 1)
    key_cols = jnp.broadcast_to(jnp.arange(cols)[None, None, :], (peers, lr, cols)).reshape(-1, 1)
    lane = jnp.arange(128)[None, :]
    oh1 = (lane % 64 == key_cols).astype(BF)
    lane = jnp.arange(aug - 128)[None, :]
    hot = (lane < 64) & (lane == key_cols)
    hot = hot | ((lane >= 64) & (lane < 64 + total_rows) & (lane - 64 == key_rows))
    off = low_at
    hot = hot | ((lane >= off) & (lane < off + total_rows) & (lane - off == key_rows))
    bad = (key_rows >= valid_rows[0]) | (key_cols >= valid_cols[0])
    oh2 = jnp.where(bad & (lane == off + total_rows), NEG, hot.astype(F32)).astype(BF)

    kv_far = qkv_call(far_tokens, qkv_weight, p768, 1) if far else None
    attended, qaug, lse = attend_call(
        first, qkv_own, kv_far, (tw, tr), oh1, oh2, total_rows, heads
    )
    x1, hidden, slope, y = mlp_call(own_tokens, attended, proj_weight, fc1_weight, b1, fc2_weight, p768)

    zf, zm, zb, zc = pyramid_call(
        y, lr, cols, fine_first, fine_second, middle_up, lateral_fine, lateral_middle, lc0, lc1, p384, fsb, p256
    )
    levels = [
        zf.reshape(4 * lr, 4 * cols, chan),
        zm.reshape(2 * lr, 2 * cols, chan),
        zb.reshape(lr, cols, chan),
        zc.reshape(lr // 2, cols // 2, chan),
    ]
    later, _ = lax.optimization_barrier((output_convs, zc))
    conv_weights = later.transpose(1, 0, 2).reshape(4, 3, 3 * chan, chan)
    rims = rim_exchange(levels, "seq")
    cots = [c[0] for c in (cotan_fine, cotan_middle, cotan_base, cotan_coarse)]
    maps, drs, level_sums = [None] * 4, [None] * 4, [None] * 4
    packed = None
    for level in (3, 2, 1, 0):
        z = levels[level]
        block = min(z.shape[0], max(1, 2048 // z.shape[1]))
        map_low, dr, packed, level_sums[level] = conv_call(
            level, z, rims[level], conv_weights, cots[level], p256, block, packed
        )
        maps[level], drs[level] = map_low.reshape(z.shape), dr.reshape(z.shape)

    conv_low = lax.psum_scatter(packed, "img", scatter_dimension=0, tiled=True)
    drims = rim_exchange(drs, "seq")
    unit = width // shards
    packed_row, _ = lax.optimization_barrier((jnp.arange(width)[:, None], level_sums[0]))
    shard_at, within = packed_row // unit, packed_row % unit

    def placed(size):
        own = size // shards
        at = jnp.arange(size)[None, :]
        return ((within < own) & (at == shard_at * own + within)).astype(BF)

    quart, half = lateral_fine.shape[0], lateral_middle.shape[0]
    own_q, own_h = quart // shards, half // shards
    at = jnp.arange(quart + half)[None, :]
    source = jnp.where(
        within < own_q,
        shard_at * own_q + within,
        jnp.where(within < own_q + own_h, quart + shard_at * own_h + within - own_q, -1),
    )
    place = (at == source).astype(BF)
    hots = (placed(chan), placed(half), placed(quart))
    all_tokens = jnp.concatenate([own_tokens] + far, axis=0)
    tables = jnp.concatenate([tw, tr], axis=1)
    level_rows = jnp.concatenate(
        [level_sums[k][0:1] for k in range(4)] + [level_sums[k][1:2] for k in range(4)]
    )
    drims, hots, place, all_tokens, tables, level_rows, head_hot = lax.optimization_barrier(
        (drims, hots, place, all_tokens, tables, level_rows, placed(head))
    )
    dzs = []
    for level, ways in enumerate((4, 2, 1, 1)):
        dr = drs[level]
        block = min(dr.shape[0], max(1, 2048 // dr.shape[1]))
        dzs.append(conv_back_call(level, dr, drims[level], conv_weights, ways, block))

    core = (lax.axis_index("img") & 1).astype(jnp.int32).reshape(1)
    dy, low_pack, s384, s192, s256 = pyramid_back_call(
        y, lr, cols, fine_first, fine_second, middle_up, lateral_fine, lateral_middle, lc0, lc1, p384, fsb, p256,
        *dzs, place,
    )
    low_pack, conv_low = lax.optimization_barrier((low_pack, conv_low))
    low_low = lax.psum_scatter(low_pack, "img", scatter_dimension=0, tiled=True)

    high_keep, high_send, keep2, send2, dx1, dout = mlp_back_call(
        dy, hidden, slope, fc1_weight, fc2_weight, x1, attended, proj_weight, p768,
        s384, s192, s256, level_rows, hots, core, shards,
    )
    three, four = Halving(high_keep, high_send), Halving(keep2, send2)

    def attend_part(dout_now, dtab, part, grads):
        return attend_back_call(
            first, qkv_own, kv_far, qaug, dout_now, attended, lse, tables, oh1, oh2, dtab,
            total_rows, heads, part, 2, grads,
        )

    _, dout = swap([(three, 0), (four, 0)], dout)
    dqkv, dtab = attend_part(dout, jnp.zeros((128, 256), F32), 0, None)
    settle([three, four], dtab)
    _, dtab = swap([(three, 1), (four, "y")], dtab)
    dqkv, dtab = attend_part(dout, dtab, 1, dqkv)
    last, dx, dx_far = qkv_back_call(
        all_tokens, dqkv, qkv_weight, dx1, p768, dtab, head_hot
    )
    last, low_low = lax.optimization_barrier((last, low_low))
    last_low = lax.psum_scatter(last, "img", scatter_dimension=0, tiled=True)
    settle([three, four], last)
    swap([(three, "y"), (four, 1)])
    settle([three, four])
    (dx_far, conv_low, low_low), _ = lax.optimization_barrier(
        ((dx_far, conv_low, low_low), [h.terms for h in (three, four)])
    )
    high_total, g_w2 = last_swap([three]), last_swap([four])
    for d in range(1, peers):
        part = dx_far[(d - 1) * count : d * count]
        dx = dx + lax.ppermute(part, "seq", [(i, (i - d) % peers) for i in range(peers)])
    conv_total, low_total = seq_total(conv_low), seq_total(low_low)
    last_low, _ = lax.optimization_barrier(
        (last_low, (conv_total, low_total, high_total, g_w2, dx))
    )
    last_total = seq_total(last_low)

    def taken(total, start, size):
        return total[:, start : start + size]

    g_ff = jnp.concatenate([taken(low_total, 2 * k * half, half) for k in range(4)], axis=1)
    g_mu = jnp.concatenate([taken(low_total, (2 * k + 1) * half, half) for k in range(4)], axis=1)
    g_fs = taken(low_total, 8 * half, half)
    g_lc = jnp.stack(
        [taken(low_total, 9 * half, chan), taken(low_total, 9 * half + chan, chan)], axis=1
    )
    laterals = taken(low_total, 9 * half + 2 * chan, chan)
    g_lf, g_lm = laterals[:own_q], laterals[own_q : own_q + own_h]
    g_w1 = taken(high_total, 0, 4 * width)
    g_wp = taken(high_total, 4 * width, width)
    vec = taken(high_total, 5 * width, 128)
    own_c = chan // shards
    g_lg = jnp.concatenate([vec[:own_c, 8:12], vec[:own_c, 24:28]], axis=1)
    g_ls = jnp.concatenate([vec[:own_c, 16:20], vec[:own_c, 28:32]], axis=1)
    g_ffb, g_fng, g_fns, g_mub = (vec[:own_h, 32 + k] for k in range(4))
    g_fsb = vec[:own_q, 48]
    g_b1 = vec[:, 40:44].T.reshape(-1)
    g_pb, g_b2 = vec[:, 6], vec[:, 7]
    g_qkv = last_total[:, : 3 * width]
    late = last_total[:, 3 * width : 3 * width + 128]
    g_bg = jnp.stack([late[:, 0], vec[:, 1]], axis=1)
    g_bs = jnp.stack([late[:, 2], vec[:, 3]], axis=1)
    g_qvb = late[:, 4:6]
    own_t = head // shards
    tabs = last_total[:own_t, 3 * width + 128 :]
    g_tc = tabs[:, : 2 * cols - 1][:, ::-1]
    g_tr = tabs[:, 128 : 128 + 2 * total_rows - 1][:, ::-1]
    g_conv = conv_total.reshape(-1, 4, chan)
    return (
        maps[0][None], maps[1][None], maps[2][None], maps[3][None],
        dx.reshape(1, lr, cols, width),
        g_bg, g_bs, g_qkv, g_qvb, g_tr, g_tc, g_wp, g_pb, g_w1, g_b1, g_w2, g_b2, g_ff, g_ffb, g_fng, g_fns,
        g_fs, g_fsb, g_mu, g_mub, g_lf, g_lm, g_lc, g_lg, g_ls, g_conv,
    )


def solution(mesh):
    image = P("img", "seq", None, None)
    in_specs = (image, P("img"), P("img")) + (P(),) * 26 + (image,) * 4
    ranks = (2, 2, 2, 2, 2, 2, 2, 1, 2, 1, 2, 1, 2, 1, 1, 1, 2, 1, 2, 1, 2, 2, 3, 2, 2, 3)
    out_specs = (image,) * 5 + tuple(P(*(("img",) + (None,) * (r - 1))) for r in ranks)
    return jax.shard_map(
        per_device, mesh=mesh, in_specs=in_specs, out_specs=out_specs, check_vma=False
    )
```

```python
import functools

import jax
import jax.numpy as jnp
from jax import lax
from jax.experimental import pallas as pl
from jax.experimental.pallas import tpu as pltpu
from jax.sharding import PartitionSpec as P

F32 = jnp.float32
BF = jnp.bfloat16
NEG = -1e30
EPS = 1e-6
SQRT_HALF = 0.7071067811865476
INV_SQRT_2PI = 0.3989422804014327
VMEM_LIMIT = 60 * 1024 * 1024


def mm(left, right):
    return lax.dot_general(left, right, (((1,), (0,)), ((), ())), preferred_element_type=F32)


def mt(left, right):
    return lax.dot_general(left, right, (((1,), (1,)), ((), ())), preferred_element_type=F32)


def tm(left, right):
    return lax.dot_general(left, right, (((0,), (0,)), ((), ())), preferred_element_type=F32)


def call(
    kernel, outs, grid=(), in_specs=None, out_specs=None, scratch=(), flops=0, name=None, aliases=None
):
    return pl.pallas_call(
        kernel,
        out_shape=outs,
        grid=grid,
        in_specs=in_specs,
        out_specs=out_specs,
        scratch_shapes=scratch,
        name=name,
        input_output_aliases=aliases or {},
        cost_estimate=pl.CostEstimate(flops=int(flops) // COST_SHARE, bytes_accessed=0, transcendentals=0),
        compiler_params=pltpu.CompilerParams(vmem_limit_bytes=VMEM_LIMIT),
    )


def whole(shape):
    return pl.BlockSpec(shape, lambda *_: (0,) * len(shape))


def sds(shape, dtype):
    return jax.ShapeDtypeStruct(shape, dtype)


def stats(values):
    average = jnp.mean(values, axis=-1, keepdims=True)
    centred = values - average
    spread = jnp.mean(centred * centred, axis=-1, keepdims=True)
    inverse = lax.rsqrt(spread + EPS)
    return centred * inverse, inverse


def norm_back(grad_hat, hat, inverse):
    first = jnp.mean(grad_hat, axis=-1, keepdims=True)
    second = jnp.mean(grad_hat * hat, axis=-1, keepdims=True)
    return inverse * (grad_hat - first - hat * second)


def rowsum(values):
    return jnp.sum(values, axis=0, keepdims=True)


UNROLL = 64
COST_SHARE = 100
CONV_PIXELS = 1024
MOVE_ROWS = 8
BACK_PIXELS = 2048


def by_chunks(total, size, body, carry=0, unroll=None):
    unroll = max(1, min(unroll or UNROLL, total // size))

    def step(k, inner):
        for u in range(unroll):
            out = body(pl.ds(pl.multiple_of((k * unroll + u) * size, size), size), inner)
            inner = inner if out is None else out
        return inner

    if unroll == total // size:
        return step(0, carry)
    return lax.fori_loop(0, total // size // unroll, step, carry)


def put_shards(source, keep_ref, send_ref, lanes, shards, first, core, sem):
    unit = source.shape[0] // shards
    for s in range(shards):
        at = first + s
        rows = pl.ds(pl.multiple_of(lax.div(at, 2) * unit, unit), unit)
        piece = source.at[pl.ds(s * unit, unit)]

        @pl.when(lax.rem(at, 2) == core)
        def _():
            pltpu.make_async_copy(piece, keep_ref.at[rows, lanes], sem).start()

        @pl.when(lax.rem(at, 2) != core)
        def _():
            pltpu.make_async_copy(piece, send_ref.at[rows, lanes], sem).start()


def wait_shards(source, sem):
    pltpu.make_async_copy(source, source, sem).wait()


def repeat(count, body):
    for k in range(count):
        body(k, 0)


def gelu_pair(values):
    half = 0.5 * (1.0 + lax.erf(values * SQRT_HALF))
    slope = half + values * (jnp.exp(-0.5 * values * values) * INV_SQRT_2PI)
    return values * half, slope


def shift_matrix(size, amount):
    out_at = lax.broadcasted_iota(jnp.int32, (size, size), 0)
    in_at = lax.broadcasted_iota(jnp.int32, (size, size), 1)
    return jnp.where(in_at == out_at + amount, 1.0, 0.0).astype(BF)


def weave_matrix(size, ways, inverse=False):
    out_at = lax.broadcasted_iota(jnp.int32, (size, size), 1 if inverse else 0)
    in_at = lax.broadcasted_iota(jnp.int32, (size, size), 0 if inverse else 1)
    source = lax.rem(out_at, ways) * (size // ways) + lax.div(out_at, ways)
    return jnp.where(in_at == source, 1.0, 0.0).astype(BF)


def qkv_kernel(first, x_ref, w_ref, p_ref, out_ref, n1_ref):
    @pl.when(pl.program_id(1) == 0)
    def _():
        def norm(sl, carry):
            hat, _ = stats(x_ref[sl, :].astype(F32))
            n1_ref[sl, :] = (hat * p_ref[0:1, :] + p_ref[2:3, :]).astype(BF)

        by_chunks(x_ref.shape[0], 32, norm)

    which = pl.program_id(1) + first
    bias = jnp.where(which == 0, p_ref[4:5, :], jnp.where(which == 2, p_ref[5:6, :], 0.0))
    out_ref[...] = (mm(n1_ref[...], w_ref[...]) + bias).astype(BF)


def qkv_call(tokens, weight, p768, first):
    rows, width = tokens.shape
    block = 512
    count = 3 - first
    return call(
        functools.partial(qkv_kernel, first),
        sds((rows, count * width), BF),
        grid=(rows // block, count),
        in_specs=[
            pl.BlockSpec((block, width), lambda i, j: (i, 0)),
            pl.BlockSpec((width, width), lambda i, j: (0, j + first)),
            whole(p768.shape),
        ],
        out_specs=pl.BlockSpec((block, width), lambda i, j: (i, j)),
        scratch=[pltpu.VMEM((block, width), BF)],
        flops=2 * rows * width * width * count,
        name="qkv",
    )(tokens, weight, p768)


def aug_layout(total_rows):
    low_at = 64 + total_rows
    if low_at + total_rows + 1 > 128:
        low_at = 128
    width = 128 * (2 + (low_at + total_rows) // 128)
    return low_at, width


def build_kaug(kaug_ref, k_refs, oh1_ref, oh2_ref, odd):
    lane = lax.broadcasted_iota(jnp.int32, (512, 128), 1)
    mine = (lane >= 64) if odd else (lane < 64)
    at = 0
    for k_ref in k_refs:
        for row in range(0, k_ref.shape[0], 512):
            keys = k_ref[row : row + 512, :].astype(F32)
            hot = oh1_ref[at : at + 512, :].astype(F32)
            kaug_ref[at : at + 512, 0:128] = jnp.where(mine, keys, hot).astype(BF)
            at += 512


def build_qaug(first_row, qp, tw_ref, tr_ref, qaug_ref, odd, total_rows, scale):
    low_at, width = aug_layout(total_rows)
    tokens = qp.shape[0]
    lane = lax.broadcasted_iota(jnp.int32, (64, 128), 1)
    mine = (lane >= 64) if odd else (lane < 64)
    lane_all = lax.broadcasted_iota(jnp.int32, (tokens, 128), 1)
    mine_all = (lane_all >= 64) if odd else (lane_all < 64)
    qf = qp.astype(F32)
    qm = jnp.where(mine_all, qf, 0.0).astype(BF)
    cols = mm(qm, tw_ref[...])
    rows = mm(qm, tr_ref[...])
    for i in range(tokens // 64):
        sl = slice(64 * i, 64 * i + 64)
        upper = pltpu.roll(cols[sl], 1, 1, stride=1, stride_axis=0)
        lower = pltpu.roll(cols[sl], 65, 1, stride=1, stride_axis=0)
        first = jnp.where(mine, qf[sl] * scale, lower if odd else upper)
        col_low = lower - lower.astype(BF).astype(F32)
        shift = lax.rem(first_row + i + (65 - total_rows + 128), 128)
        row_part = pltpu.roll(rows[sl], shift, 1)
        row_low = row_part - row_part.astype(BF).astype(F32)
        qaug_ref[sl, 0:128] = first.astype(BF)
        one_at = low_at + total_rows
        if low_at < 128:
            rest = jnp.where(lane == one_at, 1.0, 0.0)
            rest = jnp.where(
                (lane >= low_at) & (lane < one_at), pltpu.roll(row_low, total_rows, 1), rest
            )
            second = jnp.where(lane < 64, col_low, jnp.where(lane < low_at, row_part, rest))
            qaug_ref[sl, 128:256] = second.astype(BF)
        else:
            second = jnp.where(
                lane < 64, col_low, jnp.where(lane < 64 + total_rows, row_part, 0.0)
            )
            third = jnp.where(
                lane < total_rows,
                pltpu.roll(row_low, 64, 1),
                jnp.where(lane == total_rows, 1.0, 0.0),
            )
            qaug_ref[sl, 128:256] = second.astype(BF)
            qaug_ref[sl, 256:384] = third.astype(BF)


def attend_kernel(total_rows, scale, others, *refs):
    first_ref, q_ref, tw_ref, tr_ref, oh1_ref, oh2_ref = refs[:6]
    k_refs = refs[6 : 6 + others]
    v_refs = refs[6 + others : 6 + 2 * others]
    o_ref, qaug_out, lse_ref, kaug_ref, v_ref, p_ref, ot_ref, scores_ref = refs[6 + 2 * others :]
    first_row = first_ref[0]
    tokens = q_ref.shape[0]
    keys = kaug_ref.shape[0]

    @pl.when(pl.program_id(0) == 0)
    def _():
        kaug_ref[:, 128:] = oh2_ref[...]

    at = 0
    for ref in v_refs:
        v_ref[at : at + ref.shape[0], :] = ref[...]
        at += ref.shape[0]
    qp = q_ref[...]
    for odd in (0, 1):
        build_kaug(kaug_ref, k_refs, oh1_ref, oh2_ref, odd)
        build_qaug(first_row, qp, tw_ref, tr_ref, qaug_out.at[odd], odd, total_rows, scale)

        def queries(t, carry):
            sl = pl.ds(pl.multiple_of(t * 256, 256), 256)
            scores_ref[...] = mt(kaug_ref[...], qaug_out[odd, sl, :])

            def highest(rows, top):
                return jnp.maximum(top, jnp.max(scores_ref[rows, :], axis=0, keepdims=True))

            top = by_chunks(keys, 128, highest, jnp.full((1, 256), NEG, F32))

            def weigh(rows, total):
                weight = jnp.exp(scores_ref[rows, :] - top)
                p_ref[rows, :] = weight.astype(BF)
                return total + rowsum(weight)

            total = by_chunks(keys, 128, weigh, jnp.zeros((1, 256), F32))
            lse_ref[0, odd : odd + 1, sl] = top + jnp.log(total)
            out_t = tm(v_ref[...], p_ref[...])
            ot_ref[64 * odd : 64 * odd + 64, sl] = out_t[64 * odd : 64 * odd + 64] / total
            return carry

        repeat(tokens // 256, queries)
    o_ref[...] = ot_ref[...].T.astype(BF)


def attend_call(first, qkv_own, kv_others, tables, oh1, oh2, total_rows, heads):
    tokens = qkv_own.shape[0]
    width = qkv_own.shape[1] // 3
    keys = oh1.shape[0]
    aug = 128 + oh2.shape[1]
    pairs = width // 128
    tw, tr = tables
    parts = 1 + (1 if kv_others is not None else 0)
    in_specs = [
        pl.BlockSpec(memory_space=pltpu.SMEM),
        pl.BlockSpec((tokens, 128), lambda h: (0, h)),
        whole(tw.shape),
        whole(tr.shape),
        whole(oh1.shape),
        whole(oh2.shape),
    ]
    k_args, v_args, k_specs, v_specs = [qkv_own], [qkv_own], [], []
    k_specs.append(pl.BlockSpec((tokens, 128), lambda h: (0, h + pairs)))
    v_specs.append(pl.BlockSpec((tokens, 128), lambda h: (0, h + 2 * pairs)))
    if kv_others is not None:
        k_args.append(kv_others)
        v_args.append(kv_others)
        k_specs.append(pl.BlockSpec((keys - tokens, 128), lambda h: (0, h)))
        v_specs.append(pl.BlockSpec((keys - tokens, 128), lambda h: (0, h + pairs)))
    scale = (width // heads) ** -0.5
    return call(
        functools.partial(attend_kernel, total_rows, scale, parts),
        [
            sds((tokens, width), BF),
            sds((heads, tokens, aug), BF),
            sds((pairs, 2, tokens), F32),
        ],
        grid=(pairs,),
        in_specs=in_specs + k_specs + v_specs,
        out_specs=[
            pl.BlockSpec((tokens, 128), lambda h: (0, h)),
            pl.BlockSpec((2, tokens, aug), lambda h: (h, 0, 0)),
            pl.BlockSpec((1, 2, tokens), lambda h: (h, 0, 0)),
        ],
        scratch=[
            pltpu.VMEM((keys, aug), BF),
            pltpu.VMEM((keys, 128), BF),
            pltpu.VMEM((keys, 256), BF),
            pltpu.VMEM((128, tokens), F32),
            pltpu.VMEM((keys, 256), F32),
        ],
        flops=25e9,
        name="attend",
    )(first, qkv_own, tw, tr, oh1, oh2, *k_args, *v_args)


def mlp_kernel(
    x_ref, o_ref, wp_ref, w1_ref, b1_ref, w2_ref, p_ref, x1_ref, g_ref, gp_ref, y_ref, n2_ref, acc_ref,
    hidden_ref,
):
    step = pl.program_id(0)
    tokens = x_ref.shape[0]

    @pl.when(step == 0)
    def _():
        product = mm(o_ref[...], wp_ref[...])
        acc_ref[...] = product

        def norm(sl, carry):
            middle = x_ref[sl, :].astype(F32) + (acc_ref[sl, :] + p_ref[6:7, :])
            x1_ref[sl, :] = middle
            acc_ref[sl, :] = jnp.zeros_like(middle)
            hat, _ = stats(middle)
            n2_ref[sl, :] = (hat * p_ref[1:2, :] + p_ref[3:4, :]).astype(BF)

        by_chunks(tokens, 32, norm)

    hidden_ref[...] = mm(n2_ref[...], w1_ref[...])

    def act(sl, carry):
        value, slope = gelu_pair(hidden_ref[sl, :] + b1_ref[...])
        g_ref[sl, :] = value.astype(BF)
        gp_ref[sl, :] = slope.astype(BF)

    by_chunks(tokens, 32, act)
    acc_ref[...] += mm(g_ref[...], w2_ref[...])

    @pl.when(step == pl.num_programs(0) - 1)
    def _():
        y_ref[...] = (x1_ref[...] + (acc_ref[...] + p_ref[7:8, :])).astype(BF)


def mlp_call(tokens, attended, wp, w1, b1, w2, p768):
    rows, width = tokens.shape
    hidden = w1.shape[1]
    return call(
        mlp_kernel,
        [sds((rows, width), F32), sds((rows, hidden), BF), sds((rows, hidden), BF), sds((rows, width), BF)],
        grid=(hidden // width,),
        in_specs=[
            whole((rows, width)),
            whole((rows, width)),
            whole(wp.shape),
            pl.BlockSpec((width, width), lambda s: (0, s)),
            pl.BlockSpec((1, width), lambda s: (0, s)),
            pl.BlockSpec((width, width), lambda s: (s, 0)),
            whole(p768.shape),
        ],
        out_specs=[
            whole((rows, width)),
            pl.BlockSpec((rows, width), lambda s: (0, s)),
            pl.BlockSpec((rows, width), lambda s: (0, s)),
            whole((rows, width)),
        ],
        scratch=[
            pltpu.VMEM((rows, width), BF),
            pltpu.VMEM((rows, width), F32),
            pltpu.VMEM((rows, width), F32),
        ],
        flops=14e9,
        name="mlp",
    )(tokens, attended, wp, w1, b1, w2, p768)


def pool_matrix(a, b, rows, cols):
    count = rows * cols // 4
    out_at = lax.broadcasted_iota(jnp.int32, (count, rows * cols), 0)
    in_at = lax.broadcasted_iota(jnp.int32, (count, rows * cols), 1)
    half = cols // 2
    source = (2 * lax.div(out_at, half) + a) * cols + 2 * lax.rem(out_at, half) + b
    return jnp.where(in_at == source, 1.0, 0.0).astype(BF)


def lateral_norm(product_ref, count, gain, shift, write):
    def norm(sl, carry):
        hat, _ = stats(product_ref[sl, :])
        write(sl, (hat * gain + shift).astype(BF))

    by_chunks(count, 64, norm)


def pyramid_kernel(
    lr, cols, y_ref, ff_ref, fs_ref, mu_ref, lf_ref, lm_ref, lc0_ref, lc1_ref, p384_ref, fsb_ref, p256_ref,
    zf_ref, zm_ref, zb_ref, zc_ref, plane_ref, mplane_ref, f2_ref, first_ref, product_ref,
    third_ref, stack_ref,
):
    tokens = lr * cols
    half = mu_ref.shape[1] // 2
    quart = fs_ref.shape[0] // 4

    def offset(b, carry):
        columns = pl.ds(pl.multiple_of(b * half, half), half)
        first_ref[...] = mm(y_ref[...], ff_ref[:, columns])

        def norm(sl, inner):
            hat, _ = stats(first_ref[sl, :] + p384_ref[0:1, :])
            value = hat * p384_ref[1:2, :] + p384_ref[2:3, :]
            f2_ref[sl, :] = (0.5 * value * (1.0 + lax.erf(value * SQRT_HALF))).astype(BF)

        by_chunks(tokens, 64, norm)

        for k in range(4):
            third_ref[k * tokens : (k + 1) * tokens, :] = (
                mt(f2_ref[...], fs_ref[k * quart : (k + 1) * quart, :]) + fsb_ref[...]
            ).astype(BF)
        stack_ref[...] = mm(third_ref[...], lf_ref[...])
        for k in range(4):

            def write(sl, values):
                plane_ref[k // 2, 2 * b + k % 2, sl, :] = values

            part = stack_ref.at[k * tokens : (k + 1) * tokens]
            lateral_norm(part, tokens, p256_ref[0:1, :], p256_ref[8:9, :], write)
        middle = (mm(y_ref[...], mu_ref[:, columns]) + p384_ref[3:4, :]).astype(BF)
        product_ref[...] = mm(middle, lm_ref[...])

        def write_middle(sl, values):
            mplane_ref[b, sl, :] = values

        lateral_norm(product_ref, tokens, p256_ref[1:2, :], p256_ref[9:10, :], write_middle)
        return carry

    repeat(2, offset)
    weave4 = weave_matrix(4 * cols, 4)
    weave2 = weave_matrix(2 * cols, 2)

    def weave(i, carry):
        sl = pl.ds(pl.multiple_of(i * cols, cols), cols)
        for c in (0, 1):
            planes = jnp.concatenate([plane_ref[c, k, sl, :] for k in range(4)], axis=0)
            zf_ref[i, c] = mm(weave4, planes).astype(BF)
        planes = jnp.concatenate([mplane_ref[k, sl, :] for k in range(2)], axis=0)
        zm_ref[i, 0] = mm(weave2, planes).astype(BF)
        return carry

    repeat(lr, weave)

    @pl.when(pl.program_id(0) == 0)
    def _():
        product_ref[...] = mm(y_ref[...], lc0_ref[...])

        def write_base(sl, values):
            zb_ref[sl, :] = values

        lateral_norm(product_ref, tokens, p256_ref[2:3, :], p256_ref[10:11, :], write_base)
        pooled = pool_picks(y_ref, pick_ref=None, rows=lr, cols=cols)
        product_ref[0 : tokens // 4, :] = mm(pooled.astype(BF), lc1_ref[...])

        def write_coarse(sl, values):
            zc_ref[sl, :] = values

        lateral_norm(product_ref, tokens // 4, p256_ref[3:4, :], p256_ref[11:12, :], write_coarse)


def pool_picks(y_ref, pick_ref, rows, cols):
    def pick(k, top):
        values = mm(pool_matrix(k // 2, k % 2, rows, cols), y_ref[...])
        if pick_ref is not None:
            pick_ref[k] = values
        return jnp.maximum(top, values)

    low = jnp.full((rows * cols // 4, y_ref.shape[1]), -jnp.inf, F32)
    for k in range(4):
        low = pick(k, low)
    return low


def pyramid_call(y, lr, cols, ff, fs, mu, lf, lm, lc0, lc1, p384, fsb, p256):
    tokens, width = y.shape
    outs = lf.shape[1]
    half2 = ff.shape[1] // 2
    return call(
        functools.partial(pyramid_kernel, lr, cols),
        [
            sds((lr, 4, 4 * cols, outs), BF),
            sds((lr, 2, 2 * cols, outs), BF),
            sds((tokens, outs), BF),
            sds((tokens // 4, outs), BF),
        ],
        grid=(2,),
        in_specs=[
            whole(y.shape),
            pl.BlockSpec((width, half2), lambda a: (0, a)),
            whole(fs.shape),
            pl.BlockSpec((width, half2), lambda a: (0, a)),
            whole(lf.shape),
            whole(lm.shape),
            whole(lc0.shape),
            whole(lc1.shape),
            whole(p384.shape),
            whole(fsb.shape),
            whole(p256.shape),
        ],
        out_specs=[
            pl.BlockSpec((lr, 2, 4 * cols, outs), lambda a: (0, a, 0, 0)),
            pl.BlockSpec((lr, 1, 2 * cols, outs), lambda a: (0, a, 0, 0)),
            whole((tokens, outs)),
            whole((tokens // 4, outs)),
        ],
        scratch=[
            pltpu.VMEM((2, 4, tokens, outs), BF),
            pltpu.VMEM((2, tokens, outs), BF),
            pltpu.VMEM((tokens, half2 // 2), BF),
            pltpu.VMEM((tokens, half2 // 2), F32),
            pltpu.VMEM((tokens, outs), F32),
            pltpu.VMEM((4 * tokens, fs.shape[0] // 4), BF),
            pltpu.VMEM((4 * tokens, outs), F32),
        ],
        flops=20e9,
        name="pyramid",
    )(y, ff, fs, mu, lf, lm, lc0, lc1, p384, fsb, p256)


def fill_padded(step, block, src_ref, rim_ref, pad_ref, left, right):
    rows, cols, chan = src_ref.shape

    @pl.when(step == 0)
    def _():
        pad_ref[0, :, chan : 2 * chan] = rim_ref[0]
        pad_ref[rows + 1, :, chan : 2 * chan] = rim_ref[1]

        def copy(row, carry):
            pad_ref[row + 1, :, chan : 2 * chan] = src_ref[row]
            return carry

        lax.fori_loop(0, rows, copy, 0)

    def move(at):
        row = pad_ref[at, :, chan : 2 * chan]
        pad_ref[at, :, 0:chan] = mm(left, row).astype(BF)
        pad_ref[at, :, 2 * chan :] = mm(right, row).astype(BF)

    start = step * block
    group = min(block, MOVE_ROWS)

    @pl.when(step == 0)
    def _():
        move(0)
        move(1)

    def move_group(k, carry):
        for q in range(group):
            move(start + 2 + k * group + q)
        return carry

    lax.fori_loop(0, block // group, move_group, 0)


def conv_rows(rows, cols, block):
    return min(block, max(1, (CONV_PIXELS if rows * cols > 4096 else CONV_PIXELS // 2) // cols))


def conv_kernel(level, block, z_ref, rim_ref, w_ref, cot_ref, p_ref, *refs):
    map_ref, dr_ref, dw_ref, sums_ref, pad_ref, dwt_ref, gradt_ref = refs[-7:]
    step = pl.program_id(0)
    rows, cols, chan = z_ref.shape
    fill_padded(
        step, block, z_ref, rim_ref, pad_ref, shift_matrix(cols, -1), shift_matrix(cols, 1)
    )
    gain = p_ref[4 + level : 5 + level, :]
    shift = p_ref[12 + level : 13 + level, :]
    few = conv_rows(rows, cols, block)
    pixels = few * cols

    @pl.when(step == 0)
    def _():
        sums_ref[...] = jnp.zeros_like(sums_ref)
        dwt_ref[...] = jnp.zeros_like(dwt_ref)
        gradt_ref[...] = jnp.zeros_like(gradt_ref)

    def add_grad(row):
        for a in range(3):
            for b in range(3):
                window = pad_ref[pl.ds(row + a, few), :, b * chan : (b + 1) * chan]
                dwt_ref[3 * a + b] += mm(gradt_ref[...], window.reshape(pixels, chan))

    def forward(k, carry):
        sum_gain, sum_shift = carry
        row = step * block + k * few
        result = None
        for a in range(3):
            part = mm(pad_ref[pl.ds(row + a, few)].reshape(pixels, 3 * chan), w_ref[0, a])
            result = part if result is None else result + part
        base = pl.multiple_of(k * pixels, pixels)
        add_grad(jnp.maximum(row - few, 0))
        for q in range(0, pixels, 64):
            sl = pl.ds(base + q, 64)
            hat, inverse = stats(result[q : q + 64])
            map_ref[sl, :] = (hat * gain + shift).astype(BF)
            cot = cot_ref[sl, :].astype(F32)
            sum_gain = sum_gain + rowsum(cot * hat)
            sum_shift = sum_shift + rowsum(cot)
            dr_ref[sl, :] = norm_back(cot * gain, hat, inverse).astype(BF)
        gradt_ref[...] = dr_ref[pl.ds(base, pixels), :].T
        return sum_gain, sum_shift

    zero = jnp.zeros((1, chan), F32)
    sum_gain, sum_shift = lax.fori_loop(0, block // few, forward, (zero, zero))
    sums_ref[0:1, :] += sum_gain
    sums_ref[1:2, :] += sum_shift

    @pl.when(step == pl.num_programs(0) - 1)
    def _():
        add_grad(rows - few)

        def turn(k, carry):
            dw_ref[pl.ds(pl.multiple_of(k * chan, chan), chan), :] = dwt_ref[k].T.astype(BF)
            return carry

        lax.fori_loop(0, 9, turn, 0)


def conv_call(level, z, rims, weights, cot, p256, block, packed):
    rows, cols, chan = z.shape
    before = [] if packed is None else [packed]
    spec = pl.BlockSpec((block * cols, chan), lambda s: (s, 0))
    return call(
        functools.partial(conv_kernel, level, block),
        [
            sds((rows * cols, chan), BF),
            sds((rows * cols, chan), BF),
            sds((9 * chan, 4 * chan), BF),
            sds((8, chan), F32),
        ],
        grid=(rows // block,),
        in_specs=[
            whole(z.shape),
            whole(rims.shape),
            pl.BlockSpec((1, 3, 3 * chan, chan), lambda s: (level, 0, 0, 0)),
            spec,
            whole(p256.shape),
        ]
        + [pl.BlockSpec(memory_space=pl.ANY)] * len(before),
        out_specs=[
            spec,
            spec,
            pl.BlockSpec((9 * chan, chan), lambda s: (0, level)),
            whole((8, chan)),
        ],
        scratch=[
            pltpu.VMEM((rows + 2, cols, 3 * chan), BF),
            pltpu.VMEM((9, chan, chan), F32),
            pltpu.VMEM((chan, conv_rows(rows, cols, block) * cols), BF),
        ],
        flops=5 * 9 * rows * cols * chan * chan,
        name=f"conv{level}",
        aliases={5: 2} if before else {},
    )(z, rims, weights, cot.reshape(rows * cols, chan), p256, *before)


def conv_back_kernel(ways, block, dr_ref, rim_ref, w_ref, dz_ref, pad_ref):
    step = pl.program_id(0)
    rows, cols, chan = dr_ref.shape
    fill_padded(
        step, block, dr_ref, rim_ref, pad_ref, shift_matrix(cols, 1), shift_matrix(cols, -1)
    )
    few = min(block, max(1, BACK_PIXELS // cols))
    pixels = few * cols
    base = cols // ways
    unweave = weave_matrix(cols, ways, inverse=True)

    def back(k, carry):
        row = step * block + k * few
        result = None
        for a in range(3):
            for b in range(3):
                window = pad_ref[pl.ds(row + 2 - a, few), :, b * chan : (b + 1) * chan]
                part = mt(
                    window.reshape(pixels, chan), w_ref[0, a, b * chan : (b + 1) * chan, :]
                )
                result = part if result is None else result + part
        low = result.astype(BF)
        if ways == 1:
            dz_ref[pl.ds(pl.multiple_of(k * pixels, pixels), pixels), :] = low
            return carry
        for q in range(few):
            planes = mm(unweave, low[q * cols : (q + 1) * cols]).astype(BF)
            inner = k * few + q
            at = pl.ds(pl.multiple_of(lax.div(inner, ways) * base, base), base)
            for w in range(ways):
                dz_ref[lax.rem(inner, ways), w, at, :] = planes[w * base : (w + 1) * base]
        return carry

    lax.fori_loop(0, block // few, back, 0)


def conv_back_call(level, dr, rims, weights, ways, block):
    rows, cols, chan = dr.shape
    if ways == 1:
        out = sds((rows * cols, chan), BF)
        spec = pl.BlockSpec((block * cols, chan), lambda s: (s, 0))
    else:
        tokens = rows * cols // (ways * ways)
        out = sds((ways, ways, tokens, chan), BF)
        spec = pl.BlockSpec(
            (ways, ways, block * cols // (ways * ways), chan), lambda s: (0, 0, s, 0)
        )
    return call(
        functools.partial(conv_back_kernel, ways, block),
        out,
        grid=(rows // block,),
        in_specs=[
            whole(dr.shape),
            whole(rims.shape),
            pl.BlockSpec((1, 3, 3 * chan, chan), lambda s: (level, 0, 0, 0)),
        ],
        out_specs=spec,
        scratch=[pltpu.VMEM((rows + 2, cols, 3 * chan), BF)],
        flops=3 * 9 * rows * cols * chan * chan,
        name=f"conv_back{level}",
    )(dr, rims, weights)


def lateral_back(product_ref, count, read, gain, dl_ref):
    zero = jnp.zeros((1, product_ref.shape[1]), F32)

    def chunk(sl, carry):
        hat, inverse = stats(product_ref[sl, :])
        grad = read(sl)
        dl_ref[sl, :] = norm_back(grad * gain, hat, inverse).astype(BF)
        return carry[0] + rowsum(grad * hat), carry[1] + rowsum(grad)

    return by_chunks(count, 64, chunk, (zero, zero))


def pyramid_back_kernel(
    lr, cols, y_ref, ff_ref, fs_ref, mu_ref, lf_ref, lm_ref, lc0_ref, lc1_ref, p384_ref,
    fsb_ref, p256_ref, dzf_ref, dzm_ref, dzb_ref, dzc_ref, place_ref,
    dy_ref, pack_ref, s384_ref, s192_ref, s256_ref,
    yt_ref, hat_ref, slope_ref, inv_ref, f2_ref, df2_ref, df1_ref, dl_ref, fs_acc, lf_acc, lm_acc,
    dcol_ref, drest_ref, product_ref, pick_ref, third_ref, stack_ref, dls_ref, sem,
):
    step = pl.program_id(0)
    tokens = lr * cols
    quart = fs_ref.shape[0] // 4
    half = ff_ref.shape[1]
    chan = lf_ref.shape[1]

    rest = drest_ref.shape[1]

    def col_copy(at):
        lanes = pl.ds(pl.multiple_of(at * 2 * half, 2 * half), 2 * half)
        return pltpu.make_async_copy(dcol_ref.at[at], pack_ref.at[:, lanes], sem.at[at])

    rest_copy = pltpu.make_async_copy(drest_ref, pack_ref.at[:, pl.ds(8 * half, rest)], sem.at[4])

    @pl.when(step == 0)
    def _():
        yt_ref[...] = y_ref[...].T
        for ref in (fs_acc, lf_acc, lm_acc, s384_ref, s192_ref, s256_ref):
            ref[...] = jnp.zeros_like(ref)
        product_ref[...] = mm(y_ref[...], lc0_ref[...])
        sg, ss = lateral_back(
            product_ref, tokens, lambda sl: dzb_ref[sl, :].astype(F32), p256_ref[2:3, :], dl_ref
        )
        s256_ref[2:3, :] = sg
        s256_ref[10:11, :] = ss
        drest_ref[:, half : half + chan] = mm(yt_ref[...], dl_ref[...]).astype(BF)
        dy_ref[...] = mt(dl_ref[...], lc0_ref[...])
        top = pool_picks(y_ref, pick_ref, lr, cols)
        low = top.astype(BF)
        product_ref[0 : tokens // 4, :] = mm(low, lc1_ref[...])
        sg, ss = lateral_back(
            product_ref, tokens // 4, lambda sl: dzc_ref[sl, :].astype(F32), p256_ref[3:4, :], dl_ref
        )
        s256_ref[3:4, :] = sg
        s256_ref[11:12, :] = ss
        grad = dl_ref[0 : tokens // 4, :]
        drest_ref[:, half + chan : half + 2 * chan] = tm(low, grad).astype(BF)
        dtop = mt(grad, lc1_ref[...])
        hits = jnp.zeros_like(top)
        for k in range(4):
            hits = hits + jnp.where(pick_ref[k] == top, 1.0, 0.0)
        dtop = dtop / hits

        def share_out(k, carry):
            share = jnp.where(pick_ref[k] == top, dtop, 0.0)
            upper = share.astype(BF)
            lower = (share - upper.astype(F32)).astype(BF)
            spread = pool_matrix(k // 2, k % 2, lr, cols)
            dy_ref[...] += tm(spread, upper) + tm(spread, lower)
            return carry

        repeat(4, share_out)

    df2_ref[...] = mm(y_ref[...], ff_ref[...])

    def norm(sl, carry):
        hat, inverse = stats(df2_ref[sl, :] + p384_ref[0:1, :])
        hat_ref[sl, :] = hat
        inv_ref[sl, :] = jnp.broadcast_to(inverse, (64, 128))
        value, slope = gelu_pair(hat * p384_ref[1:2, :] + p384_ref[2:3, :])
        f2_ref[sl, :] = value.astype(BF)
        slope_ref[sl, :] = slope
        df2_ref[sl, :] = jnp.zeros_like(hat)

    by_chunks(tokens, 64, norm)

    for k in range(4):
        third_ref[k * tokens : (k + 1) * tokens, :] = (
            mt(f2_ref[...], fs_ref[k * quart : (k + 1) * quart, :]) + fsb_ref[...]
        ).astype(BF)
    stack_ref[...] = mm(third_ref[...], lf_ref[...])
    for k in range(4):
        sg, ss = lateral_back(
            stack_ref.at[k * tokens : (k + 1) * tokens],
            tokens,
            lambda sl: dzf_ref[0, k // 2, 0, k % 2, sl, :].astype(F32),
            p256_ref[0:1, :],
            dls_ref.at[k * tokens : (k + 1) * tokens],
        )
        s256_ref[0:1, :] += sg
        s256_ref[8:9, :] += ss
    lf_acc[...] += tm(third_ref[...], dls_ref[...])
    third_ref[...] = mt(dls_ref[...], lf_ref[...]).astype(BF)
    s192_ref[0:1, :] += rowsum(third_ref[...].astype(F32))
    for k in range(4):
        rows = slice(k * quart, (k + 1) * quart)
        fs_acc[rows, :] += tm(third_ref[k * tokens : (k + 1) * tokens, :], f2_ref[...])
        df2_ref[...] += mm(third_ref[k * tokens : (k + 1) * tokens, :], fs_ref[rows, :])
    zero = jnp.zeros((1, half), F32)

    def first_back(sl, carry):
        sum_gain, sum_shift, sum_bias = carry
        hat = hat_ref[sl, :]
        grad = df2_ref[sl, :] * slope_ref[sl, :]
        low = norm_back(grad * p384_ref[1:2, :], hat, inv_ref[sl, 0:1]).astype(BF)
        df1_ref[sl, :] = low
        return (
            sum_gain + rowsum(grad * hat),
            sum_shift + rowsum(grad),
            sum_bias + rowsum(low.astype(F32)),
        )

    sum_gain, sum_shift, sum_bias = by_chunks(tokens, 64, first_back, (zero, zero, zero))
    s384_ref[0:1, :] += sum_bias
    s384_ref[1:2, :] += sum_gain
    s384_ref[2:3, :] += sum_shift
    dcol_ref[step, :, 0:half] = mm(yt_ref[...], df1_ref[...]).astype(BF)
    dy_ref[...] += mt(df1_ref[...], ff_ref[...])

    f2_ref[...] = (mm(y_ref[...], mu_ref[...]) + p384_ref[3:4, :]).astype(BF)
    product_ref[...] = mm(f2_ref[...], lm_ref[...])
    sg, ss = lateral_back(
        product_ref, tokens, lambda sl: dzm_ref[0, 0, sl, :].astype(F32), p256_ref[1:2, :], dl_ref
    )
    s256_ref[1:2, :] += sg
    s256_ref[9:10, :] += ss
    lm_acc[...] += tm(f2_ref[...], dl_ref[...])
    df1_ref[...] = mt(dl_ref[...], lm_ref[...]).astype(BF)
    s384_ref[3:4, :] += rowsum(df1_ref[...].astype(F32))
    dcol_ref[step, :, half:] = mm(yt_ref[...], df1_ref[...]).astype(BF)
    col_copy(step).start()
    dy_ref[...] += mt(df1_ref[...], mu_ref[...])

    @pl.when(step == pl.num_programs(0) - 1)
    def _():
        drest_ref[:, 0:half] = fs_acc[...].astype(BF)
        laterals = jnp.concatenate([lf_acc[...], lm_acc[...]], axis=0).astype(BF)
        drest_ref[:, half + 2 * chan : half + 3 * chan] = mm(place_ref[...], laterals).astype(BF)
        rest_copy.start()
        for at in range(4):
            col_copy(at).wait()
        rest_copy.wait()


def pyramid_back_call(
    y, lr, cols, ff, fs, mu, lf, lm, lc0, lc1, p384, fsb, p256, dzf, dzm, dzb, dzc, place
):
    tokens, width = y.shape
    half = fs.shape[1]
    quart = fsb.shape[1]
    outs = lf.shape[1]
    col_block = pl.BlockSpec((width, half), lambda s: (0, s))
    return call(
        functools.partial(pyramid_back_kernel, lr, cols),
        [
            sds((tokens, width), F32),
            sds((width, 9 * half + 3 * outs), BF),
            sds((8, half), F32),
            sds((8, quart), F32),
            sds((16, outs), F32),
        ],
        grid=(4,),
        in_specs=[
            whole(y.shape),
            col_block,
            whole(fs.shape),
            col_block,
            whole(lf.shape),
            whole(lm.shape),
            whole(lc0.shape),
            whole(lc1.shape),
            whole(p384.shape),
            whole(fsb.shape),
            whole(p256.shape),
            pl.BlockSpec((1, 2, 1, 2, tokens, outs), lambda s: (s // 2, 0, s % 2, 0, 0, 0)),
            pl.BlockSpec((1, 1, tokens, outs), lambda s: (s // 2, s % 2, 0, 0)),
            whole(dzb.shape),
            whole(dzc.shape),
            whole(place.shape),
        ],
        out_specs=[
            whole((tokens, width)),
            pl.BlockSpec(memory_space=pl.ANY),
            whole((8, half)),
            whole((8, quart)),
            whole((16, outs)),
        ],
        scratch=[
            pltpu.VMEM((width, tokens), BF),
            pltpu.VMEM((tokens, half), F32),
            pltpu.VMEM((tokens, half), F32),
            pltpu.VMEM((tokens, 128), F32),
            pltpu.VMEM((tokens, half), BF),
            pltpu.VMEM((tokens, half), F32),
            pltpu.VMEM((tokens, half), BF),
            pltpu.VMEM((tokens, outs), BF),
            pltpu.VMEM(fs.shape, F32),
            pltpu.VMEM(lf.shape, F32),
            pltpu.VMEM(lm.shape, F32),
            pltpu.VMEM((4, width, 2 * half), BF),
            pltpu.VMEM((width, half + 3 * outs), BF),
            pltpu.VMEM((tokens, outs), F32),
            pltpu.VMEM((4, tokens // 4, width), F32),
            pltpu.VMEM((4 * tokens, quart), BF),
            pltpu.VMEM((4 * tokens, outs), F32),
            pltpu.VMEM((4 * tokens, outs), BF),
            pltpu.SemaphoreType.DMA((5,)),
        ],
        flops=45e9,
        name="pyramid_back",
    )(
        y, ff, fs, mu, lf, lm, lc0, lc1, p384, fsb, p256,
        dzf.reshape(2, 2, 2, 2, tokens, outs), dzm, dzb, dzc, place,
    )


def mlp_back_kernel(
    shards,
    core_ref, dy_ref, g_ref, gp_ref, w1_ref, w2_ref, x1_ref, o_ref, wp_ref, p_ref, s384_ref, s192_ref, s256_ref, levels_ref,
    hot256_ref, hot384_ref, hot192_ref,
    keep_ref, send_ref, keep2_ref, send2_ref, dx1_ref, do_ref,
    n2t_ref, d2_ref, dn2_ref, low_ref, sums_ref, vec_ref, dw1_ref, dw2_ref, rest_ref, temp_ref, sem,
):
    step = pl.program_id(0)
    steps = pl.num_programs(0)
    tokens, width = dy_ref.shape
    unit = width // shards
    hidden = 4 * width

    core = core_ref[0]

    @pl.when(step == 0)
    def _():
        sums_ref[...] = jnp.zeros_like(sums_ref)
        vec_ref[...] = jnp.zeros_like(vec_ref)
        dn2_ref[...] = jnp.zeros_like(dn2_ref)

        def norm(sl, total):
            hat, _ = stats(x1_ref[sl, :])
            low_ref[sl, :] = (hat * p_ref[1:2, :] + p_ref[3:4, :]).astype(BF)
            low = dy_ref[sl, :].astype(BF)
            d2_ref[sl, :] = low
            return total + rowsum(low.astype(F32))

        sums_ref[7:8, :] = by_chunks(tokens, 32, norm, jnp.zeros((1, width), F32))
        n2t_ref[...] = low_ref[...].T

    dw2_ref[step] = tm(g_ref[...], d2_ref[...]).astype(BF)
    put_shards(
        dw2_ref.at[step], keep2_ref, send2_ref, pl.ds(0, width), shards // 4, step * (shards // 4), core,
        sem.at[5 + step],
    )
    temp_ref[...] = mt(d2_ref[...], w2_ref[...])

    def act(sl, carry):
        low_ref[sl, :] = (temp_ref[sl, :] * gp_ref[sl, :].astype(F32)).astype(BF)

    by_chunks(tokens, 32, act)
    db1 = tm(low_ref[...], jnp.ones((tokens, 128), BF))
    lane = lax.broadcasted_iota(jnp.int32, (unit, 128), 1)
    for q in range(shards // 4):
        entry = jnp.zeros((unit, 128), F32)
        for k in range(4):
            sl = slice((4 * q + k) * unit, (4 * q + k + 1) * unit)
            entry = jnp.where(lane == 40 + k, db1[sl], entry)
        vec_ref[pl.ds(pl.multiple_of(step * (width // 4) + q * unit, 8), unit), :] += entry
    dw1_ref[step] = mm(n2t_ref[...], low_ref[...]).astype(BF)
    lanes = pl.ds(pl.multiple_of(step * width, width), width)
    put_shards(dw1_ref.at[step], keep_ref, send_ref, lanes, shards, 0, core, sem.at[step])
    dn2_ref[...] += mt(low_ref[...], w1_ref[...])

    @pl.when(step == steps - 1)
    def _():
        zero = jnp.zeros((1, width), F32)

        def back(sl, carry):
            hat, inverse = stats(x1_ref[sl, :])
            grad = dn2_ref[sl, :]
            dx1 = dy_ref[sl, :] + norm_back(grad * p_ref[1:2, :], hat, inverse)
            dx1_ref[sl, :] = dx1
            low = dx1.astype(BF)
            d2_ref[sl, :] = low
            return (
                carry[0] + rowsum(grad * hat),
                carry[1] + rowsum(grad),
                carry[2] + rowsum(low.astype(F32)),
            )

        sum_gain, sum_shift, sum_bias = by_chunks(tokens, 32, back, (zero, zero, zero))
        sums_ref[1:2, :] = sum_gain
        sums_ref[3:4, :] = sum_shift
        sums_ref[6:7, :] = sum_bias
        rest_ref[:, 0:width] = tm(o_ref[...], d2_ref[...]).astype(BF)
        do_ref[...] = mt(d2_ref[...], wp_ref[...]).astype(BF)

        def lanes_of(rows, before):
            after = 128 - before - rows.shape[0]
            parts = [jnp.zeros((before, rows.shape[1]), F32)] if before else []
            parts += [rows, jnp.zeros((after, rows.shape[1]), F32)]
            return jnp.concatenate(parts, axis=0)

        spread = mt(hot256_ref[...], lanes_of(s256_ref[...], 8).astype(BF))
        spread = spread + mt(hot256_ref[...], lanes_of(levels_ref[...], 24).astype(BF))
        spread = spread + mt(hot384_ref[...], lanes_of(s384_ref[...], 32).astype(BF))
        spread = spread + mt(hot192_ref[...], lanes_of(s192_ref[...], 48).astype(BF))
        spread = spread + lanes_of(sums_ref[...], 0).T
        rest_ref[:, width:] = (vec_ref[...] + spread).astype(BF)
        put_shards(
            rest_ref, keep_ref, send_ref, pl.ds(hidden, width + 128), shards, 0, core, sem.at[4]
        )
        for at in range(4):
            wait_shards(dw1_ref.at[at], sem.at[at])
            wait_shards(dw2_ref.at[at], sem.at[5 + at])
        wait_shards(rest_ref, sem.at[4])


def mlp_back_call(
    dy, g, gp, w1, w2, x1, attended, wp, p768, s384, s192, s256, levels, hots, core, shards
):
    rows, width = dy.shape
    hidden = g.shape[1]
    full = whole((rows, width))
    column = pl.BlockSpec((rows, width), lambda s: (0, s))
    smalls = [p768, s384, s192, s256, levels, *hots]
    return call(
        functools.partial(mlp_back_kernel, shards),
        [
            sds((width // 2, hidden + width + 128), BF),
            sds((width // 2, hidden + width + 128), BF),
            sds((hidden // 2, width), BF),
            sds((hidden // 2, width), BF),
            sds((rows, width), F32),
            sds((rows, width), BF),
        ],
        grid=(hidden // width,),
        in_specs=[
            pl.BlockSpec(memory_space=pltpu.SMEM),
            full,
            column,
            column,
            pl.BlockSpec((width, width), lambda s: (0, s)),
            pl.BlockSpec((width, width), lambda s: (s, 0)),
            full,
            full,
            whole((width, width)),
        ]
        + [whole(a.shape) for a in smalls],
        out_specs=[
            pl.BlockSpec(memory_space=pl.ANY),
            pl.BlockSpec(memory_space=pl.ANY),
            pl.BlockSpec(memory_space=pl.ANY),
            pl.BlockSpec(memory_space=pl.ANY),
            full,
            full,
        ],
        scratch=[
            pltpu.VMEM((width, rows), BF),
            pltpu.VMEM((rows, width), BF),
            pltpu.VMEM((rows, width), F32),
            pltpu.VMEM((rows, width), BF),
            pltpu.VMEM((8, width), F32),
            pltpu.VMEM((width, 128), F32),
            pltpu.VMEM((4, width, width), BF),
            pltpu.VMEM((4, width, width), BF),
            pltpu.VMEM((width, width + 128), BF),
            pltpu.VMEM((rows, width), F32),
            pltpu.SemaphoreType.DMA((9,)),
        ],
        flops=25e9,
        name="mlp_back",
    )(core, dy, g, gp, w1, w2, x1, attended, wp, *smalls)


def roll_back(values, amount):
    moved = jnp.concatenate(
        [
            pltpu.roll(values[8 * g : 8 * g + 8], (amount - 7 - 8 * g) % 128, 1)
            for g in range(values.shape[0] // 8)
        ],
        axis=0,
    )
    left = 7 - lax.rem(lax.broadcasted_iota(jnp.int32, values.shape, 0), 8)
    for step in (1, 2, 4):
        moved = jnp.where((left & step) > 0, pltpu.roll(moved, step, 1), moved)
    return moved


def attend_back_kernel(total_rows, scale, others, *refs):
    first_ref, q_ref, qaug_ref, do_ref, o_ref, lse_ref, tab_ref, oh1_ref, oh2_ref, before_ref = refs[:10]
    k_refs = refs[10 : 10 + others]
    v_refs = refs[10 + others : 10 + 2 * others]
    rest = refs[-15:]
    (
        dqkv_ref, dtab_ref, kaug_ref, v_ref, p_ref, ds_ref, dqt_ref, df_ref, qm_ref, dom_ref, delta_ref,
        scores_ref, dweight_ref, dk_acc, dv_acc,
    ) = rest
    first_row = first_ref[0]
    tokens = q_ref.shape[0]
    keys = kaug_ref.shape[0]

    @pl.when(pl.program_id(0) == 0)
    def _():
        kaug_ref[:, 128:] = oh2_ref[...]
        dtab_ref[...] = before_ref[...]

    at = 0
    for ref in v_refs:
        v_ref[at : at + ref.shape[0], :] = ref[...]
        at += ref.shape[0]
    lane_all = lax.broadcasted_iota(jnp.int32, (tokens, 128), 1)
    lane = lax.broadcasted_iota(jnp.int32, (64, 128), 1)
    qf = q_ref[...].astype(F32)
    dof = do_ref[...].astype(F32)
    delta_t = (dof * o_ref[...].astype(F32)).T
    dk_acc[...] = jnp.zeros_like(dk_acc)
    dv_acc[...] = jnp.zeros_like(dv_acc)
    dq = None
    for odd in (0, 1):
        mine_all = (lane_all >= 64) if odd else (lane_all < 64)
        other = (lane < 64) if odd else (lane >= 64)
        build_kaug(kaug_ref, k_refs, oh1_ref, oh2_ref, odd)
        qm = jnp.where(mine_all, qf, 0.0).astype(BF)
        dom = jnp.where(mine_all, dof, 0.0).astype(BF)
        delta = rowsum(delta_t[64 * odd : 64 * odd + 64])
        qm_ref[...] = qm
        dom_ref[...] = dom
        delta_ref[...] = delta

        def queries(t, carry):
            sl = pl.ds(pl.multiple_of(t * 256, 256), 256)
            scores_ref[...] = mt(kaug_ref[...], qaug_ref[odd, sl, :])
            dweight_ref[...] = mt(v_ref[...], dom_ref[sl, :])
            lse = lse_ref[0, odd : odd + 1, sl]
            shift = delta_ref[:, sl]

            def weigh(rows, inner):
                weight = jnp.exp(scores_ref[rows, :] - lse)
                p_ref[rows, :] = weight.astype(BF)
                ds_ref[rows, :] = (weight * (dweight_ref[rows, :] - shift)).astype(BF)

            by_chunks(keys, 128, weigh)
            dk_acc[...] += mm(ds_ref[...], qm_ref[sl, :])
            dv_acc[...] += mm(p_ref[...], dom_ref[sl, :])
            dqt_ref[:, sl] = tm(kaug_ref[...], ds_ref[...])
            return carry

        repeat(tokens // 256, queries)
        dqa = dqt_ref[0:256, :].T
        for i in range(tokens // 64):
            sl = slice(64 * i, 64 * i + 64)
            cols = roll_back(jnp.where(other, dqa[sl, 0:128], 0.0), 63 if odd else 127)
            shift = lax.rem(63 + total_rows - (first_row + i) + 128, 128)
            rows = pltpu.roll(
                jnp.where((lane >= 64) & (lane < 64 + total_rows), dqa[sl, 128:256], 0.0), shift, 1
            )
            df_ref[sl, 0:128] = cols.astype(BF)
            df_ref[sl, 128:256] = rows.astype(BF)
        from_tables = mt(df_ref[...], tab_ref[...])
        part = jnp.where(mine_all, dqa[:, 0:128] * scale + from_tables, 0.0)
        dq = part if dq is None else dq + part
        dtab_ref[...] += tm(qm, df_ref[...])
    dqkv_ref[0, 0:tokens, :] = dq.astype(BF)
    dqkv_ref[1] = (dk_acc[...] * scale).astype(BF)
    dqkv_ref[2] = dv_acc[...].astype(BF)


def attend_back_call(
    first, qkv_own, kv_others, qaug, dout, attended, lse, tab, oh1, oh2, dtab, total_rows, heads, part, parts, grads
):
    tokens = qkv_own.shape[0]
    width = qkv_own.shape[1] // 3
    keys = oh1.shape[0]
    aug = 128 + oh2.shape[1]
    pairs = width // 128
    count = pairs // parts
    base = part * count
    sources = 1 + (1 if kv_others is not None else 0)
    own = pl.BlockSpec((tokens, 128), lambda h: (0, h + base))
    in_specs = [
        pl.BlockSpec(memory_space=pltpu.SMEM),
        own,
        pl.BlockSpec((2, tokens, aug), lambda h: (h + base, 0, 0)),
        own,
        own,
        pl.BlockSpec((1, 2, tokens), lambda h: (h + base, 0, 0)),
        whole(tab.shape),
        whole(oh1.shape),
        whole(oh2.shape),
        whole(dtab.shape),
    ]
    k_args, v_args, k_specs, v_specs = [qkv_own], [qkv_own], [], []
    k_specs.append(pl.BlockSpec((tokens, 128), lambda h: (0, h + base + pairs)))
    v_specs.append(pl.BlockSpec((tokens, 128), lambda h: (0, h + base + 2 * pairs)))
    if kv_others is not None:
        k_args.append(kv_others)
        v_args.append(kv_others)
        k_specs.append(pl.BlockSpec((keys - tokens, 128), lambda h: (0, h + base)))
        v_specs.append(pl.BlockSpec((keys - tokens, 128), lambda h: (0, h + base + pairs)))
    scale = (width // heads) ** -0.5
    earlier = [] if grads is None else [grads]
    return call(
        functools.partial(attend_back_kernel, total_rows, scale, sources),
        [sds((3, keys, width), BF), sds((128, 256), F32)],
        grid=(count,),
        in_specs=in_specs + k_specs + v_specs + [pl.BlockSpec(memory_space=pl.ANY)] * len(earlier),
        out_specs=[pl.BlockSpec((3, keys, 128), lambda h: (0, 0, h + base)), whole((128, 256))],
        scratch=[
            pltpu.VMEM((keys, aug), BF),
            pltpu.VMEM((keys, 128), BF),
            pltpu.VMEM((keys, 256), BF),
            pltpu.VMEM((keys, 256), BF),
            pltpu.VMEM((aug, tokens), F32),
            pltpu.VMEM((tokens, 256), BF),
            pltpu.VMEM((tokens, 128), BF),
            pltpu.VMEM((tokens, 128), BF),
            pltpu.VMEM((1, tokens), F32),
            pltpu.VMEM((keys, 256), F32),
            pltpu.VMEM((keys, 256), F32),
            pltpu.VMEM((keys, 128), F32),
            pltpu.VMEM((keys, 128), F32),
        ],
        flops=30e9 / parts,
        name="attend_back",
        aliases={10 + 2 * sources: 0} if earlier else {},
    )(first, qkv_own, qaug, dout, attended, lse, tab, oh1, oh2, dtab, *k_args, *v_args, *earlier)


def qkv_back_kernel(
    x_ref, dqkv_ref, w_ref, dx1_ref, p_ref, dtab_ref, hot_ref,
    pack_ref, dx_ref, far_ref, nt_ref, low_ref, dn_ref, sums_ref, dw_ref, out_ref, extra_ref, sem,
):
    step = pl.program_id(0)
    tokens, width = x_ref.shape

    def w_copy(at):
        return pltpu.make_async_copy(
            out_ref.at[at], pack_ref.at[:, pl.ds(at * width, width)], sem.at[at]
        )

    extra_copy = pltpu.make_async_copy(extra_ref, pack_ref.at[:, pl.ds(3 * width, 384)], sem.at[3])

    def norm_chunk(sl, carry):
        hat, _ = stats(x_ref[sl, :].astype(F32))
        low_ref[sl, :] = (hat * p_ref[0:1, :] + p_ref[2:3, :]).astype(BF)

    by_chunks(tokens, 32, norm_chunk)
    nt_ref[...] = low_ref[...].T

    @pl.when(step == 0)
    def _():
        sums_ref[...] = jnp.zeros_like(sums_ref)
        sums_ref[4:5, :] = rowsum(dqkv_ref[0].astype(F32))
        both = dtab_ref[...]
        tables = (both[0:64] + both[64:128]).astype(BF)
        extra_ref[:, 128:384] = mm(hot_ref[...], tables).astype(BF)
        dw_ref[...] = jnp.zeros_like(dw_ref)

    dn_ref[...] = jnp.zeros_like(dn_ref)

    def product(at, carry):
        lanes = pl.ds(pl.multiple_of(at * width, width), width)
        dw_ref[at] += mm(nt_ref[...], dqkv_ref[at])
        dn_ref[...] += mt(dqkv_ref[at], w_ref[:, lanes])
        return carry

    lax.fori_loop(jnp.where(step == 0, 0, 1), 3, product, 0)
    sums_ref[5:6, :] += rowsum(dqkv_ref[2].astype(F32))

    def back_chunk(sl, carry):
        sum_gain, sum_shift = carry
        hat, inverse = stats(x_ref[sl, :].astype(F32))
        grad = dn_ref[sl, :]
        dn_ref[sl, :] = norm_back(grad * p_ref[0:1, :], hat, inverse)
        return sum_gain + rowsum(grad * hat), sum_shift + rowsum(grad)

    zero = jnp.zeros((1, width), F32)
    sum_gain, sum_shift = by_chunks(tokens, 32, back_chunk, (zero, zero))
    sums_ref[0:1, :] += sum_gain
    sums_ref[2:3, :] += sum_shift

    @pl.when(step == 0)
    def _():
        dx_ref[...] = dx1_ref[...] + dn_ref[...]

    far_ref[...] = dn_ref[...].astype(BF)

    @pl.when(step == pl.num_programs(0) - 1)
    def _():
        def put(at, carry):
            out_ref[at] = dw_ref[at].astype(BF)
            w_copy(at).start()
            return carry

        lax.fori_loop(0, 3, put, 0)
        padded = jnp.concatenate([sums_ref[...], jnp.zeros((120, width), F32)], axis=0)
        extra_ref[:, 0:128] = padded.T.astype(BF)
        extra_copy.start()
        for at in range(3):
            w_copy(at).wait()
        extra_copy.wait()


def qkv_back_call(tokens, dqkv, weight, dx1, p768, dtab, hot):
    rows, width = dx1.shape
    blocks = tokens.shape[0] // rows
    full = whole((rows, width))
    block = pl.BlockSpec((rows, width), lambda s: (s, 0))
    return call(
        qkv_back_kernel,
        [
            sds((width, 3 * width + 384), BF),
            sds((rows, width), F32),
            sds(((max(blocks, 2) - 1) * rows, width), BF),
        ],
        grid=(blocks,),
        in_specs=[
            block,
            pl.BlockSpec((3, rows, width), lambda s: (0, s, 0)),
            whole(weight.shape),
            full,
            whole(p768.shape),
            whole(dtab.shape),
            whole(hot.shape),
        ],
        out_specs=[
            pl.BlockSpec(memory_space=pl.ANY),
            full,
            pl.BlockSpec((rows, width), lambda s: (jnp.maximum(s - 1, 0), 0)),
        ],
        scratch=[
            pltpu.VMEM((width, rows), BF),
            pltpu.VMEM((rows, width), BF),
            pltpu.VMEM((rows, width), F32),
            pltpu.VMEM((8, width), F32),
            pltpu.VMEM((3, width, width), F32),
            pltpu.VMEM((3, width, width), BF),
            pltpu.VMEM((width, 384), BF),
            pltpu.SemaphoreType.DMA((4,)),
        ],
        flops=8e9,
        name="qkv_back",
    )(tokens, dqkv, weight, dx1, p768, dtab, hot)


def rim_exchange(levels, axis):
    peers = lax.axis_size(axis)
    chan = levels[0].shape[-1]
    counts = [level.shape[1] for level in levels]
    lasts = jnp.concatenate([level[-1] for level in levels], axis=0)
    firsts = jnp.concatenate([level[0] for level in levels], axis=0)
    if peers == 2:
        me = lax.axis_index(axis)
        got = lax.ppermute(jnp.where(me == 0, lasts, firsts), axis, [(0, 1), (1, 0)])
        nothing = jnp.zeros_like(got)
        before = jnp.where(me == 1, got, nothing)
        after = jnp.where(me == 0, got, nothing)
    else:
        before = lax.ppermute(lasts, axis, [(i, i + 1) for i in range(peers - 1)])
        after = lax.ppermute(firsts, axis, [(i + 1, i) for i in range(peers - 1)])
    both = jnp.stack([before, after])
    rims, at = [], 0
    for count in counts:
        rims.append(both[:, at : at + count])
        at += count
    return rims


class Halving:
    def __init__(self, keep, send):
        bits = lax.axis_size("img").bit_length() - 1
        self.left = list(range(1, bits))[::-1]
        self.shape = (2,) * (bits - 1) + (keep.shape[0] >> (bits - 1), keep.shape[1])
        self.keep, self.first = keep.reshape(self.shape), send.reshape(self.shape)

    def split(self, step):
        if step == 0:
            self.route = ("img", [(i, i ^ 1) for i in range(lax.axis_size("img"))])
            return self.first
        terms = self.terms
        if step == "y":
            at, mine, axis, pairs = len(self.left), lax.axis_index("seq"), "seq", [(0, 1), (1, 0)]
            shape = terms[0].shape
            terms = [t.reshape(shape[:-2] + (2, shape[-2] // 2, shape[-1])) for t in terms]
        else:
            at, mine, axis = self.left.index(step), (lax.axis_index("img") >> step) & 1, "img"
            pairs = [(i, i ^ (1 << step)) for i in range(lax.axis_size("img"))]
            self.left.remove(step)
        self.route = (axis, pairs)

        def half(which):
            parts = [lax.dynamic_index_in_dim(t, which, at, keepdims=False) for t in terms]
            return (parts[0].astype(F32) + parts[1].astype(F32)).astype(BF)

        self.keep = half(mine)
        return half(1 - mine)


def swap(steps, after=()):
    if lax.axis_size("seq") != 2:
        steps = [(h, step) for h, step in steps if step != "y"]
    sends = [h.split(step) for h, step in steps]
    keeps = [h.keep for h, _ in steps]
    sends, keeps, after = lax.optimization_barrier((sends, keeps, after))
    for (h, _), send, keep in zip(steps, sends, keeps):
        h.terms = [keep, lax.ppermute(flat(send), *h.route).reshape(send.shape)]
    return [h for h, _ in steps], after


def flat(values):
    return values.reshape(-1, values.shape[-1])


def last_swap(group):
    left = group[0].left
    count = 1 << len(left)
    base = left[-1]
    mine = (lax.axis_index("img") >> base) & (count - 1)
    shards = lax.axis_size("img")
    terms = [
        jnp.concatenate(
            [h.terms[k].reshape((count,) + h.terms[k].shape[len(left) :]) for h in group], axis=-1
        )
        for k in (0, 1)
    ]

    def part(which):
        parts = [lax.dynamic_index_in_dim(t, which, 0, keepdims=False) for t in terms]
        return (parts[0].astype(F32) + parts[1].astype(F32)).astype(BF)

    total = part(mine).astype(F32)
    for d in range(1, count):
        pairs = [(i, i ^ (d << base)) for i in range(shards)]
        total = total + lax.ppermute(part(mine ^ d), "img", pairs).astype(F32)
    grad = total.astype(BF)
    if lax.axis_size("seq") != 2:
        return lax.psum(grad, "seq").astype(F32)
    row = lax.axis_index("seq")
    other = lax.ppermute(grad, "seq", [(0, 1), (1, 0)])
    first = jnp.where(row == 0, grad, other)
    second = jnp.where(row == 0, other, grad)
    return jnp.concatenate([first, second], axis=0).astype(F32)


def settle(moving, done=()):
    terms, _ = lax.optimization_barrier(([h.terms for h in moving], done))
    for h, arrived in zip(moving, terms):
        h.terms = arrived


def seq_total(part):
    peers = lax.axis_size("seq")
    if peers == 2:
        other = lax.ppermute(part, "seq", [(0, 1), (1, 0)])
        return part.astype(F32) + other.astype(F32)
    return lax.psum(part, "seq").astype(F32)


def per_device(
    tokens, valid_rows, valid_cols, block_gains, block_shifts, qkv_weight, qv_bias, table_rows, table_cols,
    proj_weight, proj_bias, fc1_weight, fc1_bias, fc2_weight, fc2_bias, fine_first, fine_first_bias,
    fine_norm_gain, fine_norm_shift, fine_second, fine_second_bias, middle_up, middle_up_bias, lateral_fine,
    lateral_middle, lateral_coarse, level_gains, level_shifts, output_convs, cotan_fine, cotan_middle,
    cotan_base, cotan_coarse,
):
    lr, cols, width = tokens.shape[1:]
    head = table_rows.shape[0]
    heads = width // head
    peers = lax.axis_size("seq")
    shards = lax.axis_size("img")
    me = lax.axis_index("seq")
    total_rows = lr * peers
    count = lr * cols
    chan = lateral_fine.shape[1]
    first_row = me * lr
    first = first_row.astype(jnp.int32).reshape(1)
    own_tokens = tokens[0].reshape(count, width)

    far = [
        lax.ppermute(own_tokens, "seq", [(i, (i + d) % peers) for i in range(peers)])
        for d in range(1, peers)
    ]
    far_tokens = jnp.concatenate(far, axis=0) if len(far) > 1 else (far[0] if far else None)

    p768 = jnp.concatenate(
        [block_gains.T, block_shifts.T, qv_bias.T, proj_bias[None], fc2_bias[None]]
    ).astype(F32)
    qkv_own = qkv_call(own_tokens, qkv_weight, p768, 0)
    (
        fc1_bias, fine_first_bias, fine_norm_gain, fine_norm_shift, middle_up_bias, fine_second_bias, level_gains,
        level_shifts, table_cols, table_rows, valid_rows, qkv_own,
    ) = lax.optimization_barrier(
        (
            fc1_bias, fine_first_bias, fine_norm_gain, fine_norm_shift, middle_up_bias, fine_second_bias,
            level_gains, level_shifts, table_cols, table_rows, valid_rows, qkv_own,
        )
    )
    b1 = fc1_bias.astype(F32)[None]
    p384 = jnp.stack([fine_first_bias, fine_norm_gain, fine_norm_shift, middle_up_bias]).astype(F32)
    fsb = fine_second_bias.astype(F32)[None]
    p256 = jnp.concatenate([level_gains.T, level_shifts.T]).astype(F32)
    lc0, lc1 = lateral_coarse[:, 0, :], lateral_coarse[:, 1, :]

    def turned(table):
        back = table[:, ::-1]
        back = jnp.pad(back, ((0, 0), (0, 128 - back.shape[1])))
        return jnp.concatenate([back, back], axis=0)

    tw, tr = turned(table_cols), turned(table_rows)

    low_at, aug = aug_layout(total_rows)
    ranks = jnp.stack([(me - d) % peers for d in range(peers)])
    key_rows = (ranks[:, None] * lr + jnp.arange(lr)[None, :])[:, :, None]
    key_rows = jnp.broadcast_to(key_rows, (peers, lr, cols)).reshape(-1, 1)
    key_cols = jnp.broadcast_to(jnp.arange(cols)[None, None, :], (peers, lr, cols)).reshape(-1, 1)
    lane = jnp.arange(128)[None, :]
    oh1 = (lane % 64 == key_cols).astype(BF)
    lane = jnp.arange(aug - 128)[None, :]
    hot = (lane < 64) & (lane == key_cols)
    hot = hot | ((lane >= 64) & (lane < 64 + total_rows) & (lane - 64 == key_rows))
    off = low_at
    hot = hot | ((lane >= off) & (lane < off + total_rows) & (lane - off == key_rows))
    bad = (key_rows >= valid_rows[0]) | (key_cols >= valid_cols[0])
    oh2 = jnp.where(bad & (lane == off + total_rows), NEG, hot.astype(F32)).astype(BF)

    kv_far = qkv_call(far_tokens, qkv_weight, p768, 1) if far else None
    attended, qaug, lse = attend_call(
        first, qkv_own, kv_far, (tw, tr), oh1, oh2, total_rows, heads
    )
    x1, hidden, slope, y = mlp_call(own_tokens, attended, proj_weight, fc1_weight, b1, fc2_weight, p768)

    zf, zm, zb, zc = pyramid_call(
        y, lr, cols, fine_first, fine_second, middle_up, lateral_fine, lateral_middle, lc0, lc1, p384, fsb, p256
    )
    levels = [
        zf.reshape(4 * lr, 4 * cols, chan),
        zm.reshape(2 * lr, 2 * cols, chan),
        zb.reshape(lr, cols, chan),
        zc.reshape(lr // 2, cols // 2, chan),
    ]
    later, _ = lax.optimization_barrier((output_convs, zc))
    conv_weights = later.transpose(1, 0, 2).reshape(4, 3, 3 * chan, chan)
    rims = rim_exchange(levels, "seq")
    cots = [c[0] for c in (cotan_fine, cotan_middle, cotan_base, cotan_coarse)]
    maps, drs, level_sums = [None] * 4, [None] * 4, [None] * 4
    packed = None
    for level in (3, 2, 1, 0):
        z = levels[level]
        block = min(z.shape[0], max(1, 2048 // z.shape[1]))
        map_low, dr, packed, level_sums[level] = conv_call(
            level, z, rims[level], conv_weights, cots[level], p256, block, packed
        )
        maps[level], drs[level] = map_low.reshape(z.shape), dr.reshape(z.shape)

    conv_low = lax.psum_scatter(packed, "img", scatter_dimension=0, tiled=True)
    drims = rim_exchange(drs, "seq")
    unit = width // shards
    packed_row, _ = lax.optimization_barrier((jnp.arange(width)[:, None], level_sums[0]))
    shard_at, within = packed_row // unit, packed_row % unit

    def placed(size):
        own = size // shards
        at = jnp.arange(size)[None, :]
        return ((within < own) & (at == shard_at * own + within)).astype(BF)

    quart, half = lateral_fine.shape[0], lateral_middle.shape[0]
    own_q, own_h = quart // shards, half // shards
    at = jnp.arange(quart + half)[None, :]
    source = jnp.where(
        within < own_q,
        shard_at * own_q + within,
        jnp.where(within < own_q + own_h, quart + shard_at * own_h + within - own_q, -1),
    )
    place = (at == source).astype(BF)
    hots = (placed(chan), placed(half), placed(quart))
    all_tokens = jnp.concatenate([own_tokens] + far, axis=0)
    tables = jnp.concatenate([tw, tr], axis=1)
    level_rows = jnp.concatenate(
        [level_sums[k][0:1] for k in range(4)] + [level_sums[k][1:2] for k in range(4)]
    )
    drims, hots, place, all_tokens, tables, level_rows, head_hot = lax.optimization_barrier(
        (drims, hots, place, all_tokens, tables, level_rows, placed(head))
    )
    dzs = []
    for level, ways in enumerate((4, 2, 1, 1)):
        dr = drs[level]
        block = min(dr.shape[0], max(1, 2048 // dr.shape[1]))
        dzs.append(conv_back_call(level, dr, drims[level], conv_weights, ways, block))

    core = (lax.axis_index("img") & 1).astype(jnp.int32).reshape(1)
    dy, low_pack, s384, s192, s256 = pyramid_back_call(
        y, lr, cols, fine_first, fine_second, middle_up, lateral_fine, lateral_middle, lc0, lc1, p384, fsb, p256,
        *dzs, place,
    )
    low_pack, conv_low = lax.optimization_barrier((low_pack, conv_low))
    low_low = lax.psum_scatter(low_pack, "img", scatter_dimension=0, tiled=True)

    high_keep, high_send, keep2, send2, dx1, dout = mlp_back_call(
        dy, hidden, slope, fc1_weight, fc2_weight, x1, attended, proj_weight, p768,
        s384, s192, s256, level_rows, hots, core, shards,
    )
    three, four = Halving(high_keep, high_send), Halving(keep2, send2)

    def attend_part(dout_now, dtab, part, grads):
        return attend_back_call(
            first, qkv_own, kv_far, qaug, dout_now, attended, lse, tables, oh1, oh2, dtab,
            total_rows, heads, part, 2, grads,
        )

    _, dout = swap([(three, 0), (four, 0)], dout)
    dqkv, dtab = attend_part(dout, jnp.zeros((128, 256), F32), 0, None)
    settle([three, four], dtab)
    _, dtab = swap([(three, 1), (four, "y")], dtab)
    dqkv, dtab = attend_part(dout, dtab, 1, dqkv)
    last, dx, dx_far = qkv_back_call(
        all_tokens, dqkv, qkv_weight, dx1, p768, dtab, head_hot
    )
    last_low = lax.psum_scatter(last, "img", scatter_dimension=0, tiled=True)
    settle([three, four], last)
    swap([(three, "y"), (four, 1)])
    settle([three, four])
    (dx_far, conv_low, low_low), _ = lax.optimization_barrier(
        ((dx_far, conv_low, low_low), [h.terms for h in (three, four)])
    )
    high_total, g_w2 = last_swap([three]), last_swap([four])
    for d in range(1, peers):
        part = dx_far[(d - 1) * count : d * count]
        dx = dx + lax.ppermute(part, "seq", [(i, (i - d) % peers) for i in range(peers)])
    conv_total, low_total = seq_total(conv_low), seq_total(low_low)
    last_low, _ = lax.optimization_barrier(
        (last_low, (conv_total, low_total, high_total, g_w2, dx))
    )
    last_total = seq_total(last_low)

    def taken(total, start, size):
        return total[:, start : start + size]

    g_ff = jnp.concatenate([taken(low_total, 2 * k * half, half) for k in range(4)], axis=1)
    g_mu = jnp.concatenate([taken(low_total, (2 * k + 1) * half, half) for k in range(4)], axis=1)
    g_fs = taken(low_total, 8 * half, half)
    g_lc = jnp.stack(
        [taken(low_total, 9 * half, chan), taken(low_total, 9 * half + chan, chan)], axis=1
    )
    laterals = taken(low_total, 9 * half + 2 * chan, chan)
    g_lf, g_lm = laterals[:own_q], laterals[own_q : own_q + own_h]
    g_w1 = taken(high_total, 0, 4 * width)
    g_wp = taken(high_total, 4 * width, width)
    vec = taken(high_total, 5 * width, 128)
    own_c = chan // shards
    g_lg = jnp.concatenate([vec[:own_c, 8:12], vec[:own_c, 24:28]], axis=1)
    g_ls = jnp.concatenate([vec[:own_c, 16:20], vec[:own_c, 28:32]], axis=1)
    g_ffb, g_fng, g_fns, g_mub = (vec[:own_h, 32 + k] for k in range(4))
    g_fsb = vec[:own_q, 48]
    g_b1 = vec[:, 40:44].T.reshape(-1)
    g_pb, g_b2 = vec[:, 6], vec[:, 7]
    g_qkv = last_total[:, : 3 * width]
    late = last_total[:, 3 * width : 3 * width + 128]
    g_bg = jnp.stack([late[:, 0], vec[:, 1]], axis=1)
    g_bs = jnp.stack([late[:, 2], vec[:, 3]], axis=1)
    g_qvb = late[:, 4:6]
    own_t = head // shards
    tabs = last_total[:own_t, 3 * width + 128 :]
    g_tc = tabs[:, : 2 * cols - 1][:, ::-1]
    g_tr = tabs[:, 128 : 128 + 2 * total_rows - 1][:, ::-1]
    g_conv = conv_total.reshape(-1, 4, chan)
    return (
        maps[0][None], maps[1][None], maps[2][None], maps[3][None],
        dx.reshape(1, lr, cols, width),
        g_bg, g_bs, g_qkv, g_qvb, g_tr, g_tc, g_wp, g_pb, g_w1, g_b1, g_w2, g_b2, g_ff, g_ffb, g_fng, g_fns,
        g_fs, g_fsb, g_mu, g_mub, g_lf, g_lm, g_lc, g_lg, g_ls, g_conv,
    )


def solution(mesh):
    image = P("img", "seq", None, None)
    in_specs = (image, P("img"), P("img")) + (P(),) * 26 + (image,) * 4
    ranks = (2, 2, 2, 2, 2, 2, 2, 1, 2, 1, 2, 1, 2, 1, 1, 1, 2, 1, 2, 1, 2, 2, 3, 2, 2, 3)
    out_specs = (image,) * 5 + tuple(P(*(("img",) + (None,) * (r - 1))) for r in ranks)
    return jax.shard_map(
        per_device, mesh=mesh, in_specs=in_specs, out_specs=out_specs, check_vma=False
    )
```
